32 devices in a mesh: gz: 4 (over x, core), gy: 8 (over z, y).
Axes of the slice: x: 2, y: 2, z: 4, core: 2. Of those that a mesh axis runs over, the one named last changes fastest.
Arguments:
- flow_state: float32 [5, 8, 512, 512], P(None, None, 'gy', 'gz'), may hold values from -6 to 6
- velocity: float32 [8, 512, 512], P(None, 'gy', 'gz'), may hold values from -6 to 6
- metric_y: float32 [512], replicated, may hold values from 2000 to 4000
- metric_z: float32 [512], replicated, may hold values from 32000 to 64000
Outputs:
- correction: float32 [5, 8, 512, 512], P(None, None, 'gy', 'gz')
The draws below stay inside these ranges and needn't reach their ends.
All inputs are finite; a program needn't handle non-finite values.
Results may differ from the reference program's by a relative error of at most 0.0009.
Values sent between devices are 32-bit elements; how exact they have to be, the bound alone decides.
No kernel may reach another device: no remote copies, remote signals or barrier semaphores. Data moves between devices by JAX's collectives and lax.ppermute only.
A program may use at most 64 MiB of HBM per device.

```python
import math
import jax
import jax.numpy as jnp
from jax import lax

COMP = 5
Y = 512
X = 8
Z = 512


def slow_profile(key, line_length):
    offset_angle = jax.random.uniform(key, (), jnp.float32, 0.0, 2.0 * math.pi)
    position = jnp.arange(line_length, dtype=jnp.float32)
    return 1.0 + 0.3 * jnp.sin(2.0 * math.pi * position / 512.0 + offset_angle)


def whole_profile(key, line_length):
    offset_angle = jax.random.uniform(key, (), jnp.float32, 0.0, 2.0 * math.pi)
    position = jnp.arange(line_length, dtype=jnp.float32)
    return 1.0 + 0.5 * jnp.sin(2.0 * math.pi * position / line_length + offset_angle)


def alternating(line_length):
    position = jnp.arange(line_length, dtype=jnp.int32)
    return (1 - 2 * (position % 2)).astype(jnp.float32)


def smooth_scale():
    wave_z = 2.0 * math.pi / Z
    wave_y = 2.0 * math.pi / Y
    reach = (1.0 + 48000.0 * wave_z * wave_z) * (1.0 + 3000.0 * wave_y * wave_y)
    return min(0.5, reach / (524288.0 * wave_z))


def draw_flow_state(key, part):
    amp_key = jax.random.fold_in(jax.random.fold_in(key, 11), 0)
    profile_key = jax.random.fold_in(jax.random.fold_in(key, 11), 1)
    smooth_key = jax.random.fold_in(jax.random.fold_in(key, 11), 3)
    amplitude = jnp.clip(jax.random.normal(amp_key, (COMP, X, Y, 1), jnp.float32), -4.5, 4.5)
    shape_z = alternating(Z) * slow_profile(profile_key, Z)
    y_key, z_key, level_key = jax.random.split(smooth_key, 3)
    level = jax.random.uniform(level_key, (COMP, X, 1, 1), jnp.float32, 0.5, 1.5)
    smooth = smooth_scale() * level * whole_profile(y_key, Y)[None, None, :, None] * whole_profile(z_key, Z)[None, None, None, :]
    return jnp.clip(amplitude * shape_z[None, None, None, :] + smooth, -6.0, 6.0)


def draw_velocity(key, part):
    amp_key, profile_key = jax.random.split(jax.random.fold_in(key, 23), 2)
    amplitude = jnp.clip(jax.random.normal(amp_key, (X, Y, 1), jnp.float32), -4.5, 4.5)
    shape_z = slow_profile(profile_key, Z)
    return jnp.clip((amplitude + 1.0) * shape_z[None, None, :], -6.0, 6.0)


def setup_inputs(seed: int = 0) -> dict:
    streams_of = jax.random.split(jax.random.key(seed), 5)
    return {
        "flow_state": draw_flow_state(jax.random.fold_in(streams_of[4], 71), 0),
        "velocity": draw_velocity(jax.random.fold_in(streams_of[4], 71), 0),
        "metric_y": jnp.clip(jnp.exp(jax.random.uniform(streams_of[2], (Y,), jnp.float32, math.log(2000.0), math.log(4000.0))), 2000.0, 4000.0),
        "metric_z": jnp.clip(jnp.exp(jax.random.uniform(streams_of[3], (Z,), jnp.float32, math.log(32000.0), math.log(64000.0))), 32000.0, 64000.0),
    }


viscous = 0.25
explicit_fourth = 0.04
implicit_fourth = 0.05
time_step = 1048576.0

def shifted(source, step_x, step_y, step_z):
    size_x = source.shape[-3] - 2
    size_y = source.shape[-2] - 4
    size_z = source.shape[-1] - 4
    return source[..., 1 + step_x:1 + step_x + size_x, 2 + step_y:2 + step_y + size_y, 2 + step_z:2 + step_z + size_z]

def tendency(fields, speeds):
    flux = fields * speeds
    center = shifted(fields, 0, 0, 0)
    advect = shifted(flux, 1, 0, 0) - shifted(flux, -1, 0, 0)
    advect = advect + shifted(flux, 0, 1, 0) - shifted(flux, 0, -1, 0)
    advect = advect + shifted(flux, 0, 0, 1) - shifted(flux, 0, 0, -1)
    spread = shifted(fields, 1, 0, 0) + shifted(fields, -1, 0, 0)
    spread = spread + shifted(fields, 0, 1, 0) + shifted(fields, 0, -1, 0)
    spread = spread + shifted(fields, 0, 0, 1) + shifted(fields, 0, 0, -1)
    fourth_y = shifted(fields, 0, -2, 0) - 4.0 * shifted(fields, 0, -1, 0) + 6.0 * center - 4.0 * shifted(fields, 0, 1, 0) + shifted(fields, 0, 2, 0)
    fourth_z = shifted(fields, 0, 0, -2) - 4.0 * shifted(fields, 0, 0, -1) + 6.0 * center - 4.0 * shifted(fields, 0, 0, 1) + shifted(fields, 0, 0, 2)
    return time_step * (-0.5 * advect + viscous * spread - 6.0 * viscous * center - explicit_fourth * (fourth_y + fourth_z))

def band_values(metric):
    faces = 0.5 * (jnp.concatenate([metric[:1], metric]) + jnp.concatenate([metric, metric[-1:]]))
    diagonal = 1.0 + faces[:-1] + faces[1:] + 6.0 * implicit_fourth
    off_first = -faces[1:-1] - 4.0 * implicit_fourth
    return (diagonal, off_first)

def band_solve(diagonal, off_first, forcing):
    count = diagonal.shape[0]
    near = jnp.concatenate([jnp.zeros((1,), jnp.float32), off_first])
    far = jnp.concatenate([jnp.zeros((2,), jnp.float32), jnp.full((count - 2,), implicit_fourth, jnp.float32)])

    def factor_step(carry, inputs):
        last_main, older_main, last_near = carry
        entry_diag, entry_near, entry_far = inputs
        fac_far = entry_far / older_main
        fac_near = (entry_near - fac_far * last_near) / last_main
        fac_main = jnp.sqrt(entry_diag - fac_near * fac_near - fac_far * fac_far)
        return ((fac_main, last_main, fac_near), (fac_main, fac_near, fac_far))
    start = (jnp.ones((), jnp.float32), jnp.ones((), jnp.float32), jnp.zeros((), jnp.float32))
    _, (fac_main, fac_near, fac_far) = lax.scan(factor_step, start, (diagonal, near, far))

    def forward_step(carry, inputs):
        last_value, older_value = carry
        entry, main_entry, near_entry, far_entry = inputs
        value = (entry - near_entry * last_value - far_entry * older_value) / main_entry
        return ((value, last_value), value)
    zero_line = jnp.zeros(forcing.shape[1:], jnp.float32)
    _, interim = lax.scan(forward_step, (zero_line, zero_line), (forcing, fac_main, fac_near, fac_far))
    near_next = jnp.concatenate([fac_near[1:], jnp.zeros((1,), jnp.float32)])
    far_next = jnp.concatenate([fac_far[2:], jnp.zeros((2,), jnp.float32)])

    def backward_step(carry, inputs):
        next_value, later_value = carry
        entry, main_entry, near_entry, far_entry = inputs
        value = (entry - near_entry * next_value - far_entry * later_value) / main_entry
        return ((value, next_value), value)
    _, solved = lax.scan(backward_step, (zero_line, zero_line), (interim, fac_main, near_next, far_next), reverse=True)
    return solved

def reference(flow_state, velocity, metric_y, metric_z):
    speeds = jnp.pad(velocity, ((1, 1), (2, 2), (2, 2)))[None]
    diag_y, off_y = band_values(metric_y)
    diag_z, off_z = band_values(metric_z)

    def one_variable(single):
        padded = jnp.pad(single, ((1, 1), (2, 2), (2, 2)))[None]
        forcing = tendency(padded, speeds)[0]
        size_x, size_y, size_z = forcing.shape
        line_data = jnp.moveaxis(forcing, 1, 0).reshape(size_y, size_x * size_z)
        across = jnp.moveaxis(band_solve(diag_y, off_y, line_data).reshape(size_y, size_x, size_z), 0, 1)
        line_data = jnp.moveaxis(across, 2, 0).reshape(size_z, size_x * size_y)
        return jnp.moveaxis(band_solve(diag_z, off_z, line_data).reshape(size_z, size_x, size_y), 0, 2)
    return lax.map(one_variable, flow_state)
```

```python
import functools

import jax
import jax.numpy as jnp
from jax import lax
from jax.experimental import pallas as pl
from jax.experimental.pallas import tpu as pltpu
from jax.sharding import PartitionSpec as P

viscous = 0.25
explicit_fourth = 0.04
implicit_fourth = 0.05
time_step = 1048576.0
LANES = 128
EXTRA = 8
SWEEPS = 3
HIGHEST = lax.Precision.HIGHEST


def mm(a, b):
    return (
        a[0] * b[0] + a[1] * b[2],
        a[0] * b[1] + a[1] * b[3],
        a[2] * b[0] + a[3] * b[2],
        a[2] * b[1] + a[3] * b[3],
    )


def inverse_of_one_minus(a):
    p, q, r, s = 1.0 - a[0], -a[1], -a[2], 1.0 - a[3]
    d = 1.0 / (p * s - q * r)
    return (s * d, -q * d, -r * d, p * d)


def pick(condition, a, b):
    return tuple(jnp.where(condition, x, y) for x, y in zip(a, b))


def lane_roll(x, by):
    return pltpu.roll(x, by % LANES, 1)


def row_roll(x, by):
    by = by % x.shape[0]
    return jnp.concatenate([x[x.shape[0] - by :], x[: x.shape[0] - by]], axis=0)


def factor(metric, ny, nz, wy):
    rows = ny + nz
    lane = lax.broadcasted_iota(jnp.int32, (rows, LANES), 1)
    row = lax.broadcasted_iota(jnp.int32, (rows, LANES), 0)
    block = jnp.where(row < ny, row, row - ny)
    to_end = jnp.where(row < ny, ny, nz) - 1 - block
    even = (lane & 1) == 0

    def before(x, by):
        rolled = lane_roll(x, by)
        value = jnp.where(lane < by, row_roll(rolled, 1), rolled)
        return jnp.where((lane < by) & (block == 0), 0.0, value)

    def after(x, by):
        rolled = lane_roll(x, -by)
        value = jnp.where(lane >= LANES - by, row_roll(rolled, -1), rolled)
        return jnp.where((lane >= LANES - by) & (to_end == 0), 0.0, value)

    first = (lane == 0) & (block == 0)
    last = (lane == LANES - 1) & (to_end == 0)
    face_low = 0.5 * (jnp.where(first, metric, before(metric, 1)) + metric)
    face_high = 0.5 * (metric + jnp.where(last, metric, after(metric, 1)))
    ones = jnp.ones_like(metric)
    zeros = jnp.zeros_like(metric)

    def eliminate(sign):
        back = before if sign > 0 else after
        face_in, face_out = (face_low, face_high) if sign > 0 else (face_high, face_low)
        place = block if sign > 0 else to_end
        ratio, far = ones, zeros
        for _ in range(SWEEPS):
            eps = 4.0 * implicit_fourth - implicit_fourth * back(ratio, 1)
            mass = (1.0 + 6.0 * implicit_fourth) - implicit_fourth * back(far, 2) - 2.0 * eps
            eps_in = back(eps, 1)
            scale = 1.0 / (face_in + 2.0 * eps_in)
            m = ((mass + face_in) * scale, mass - eps_in * eps_in * scale, scale, ones)
            step = 1
            while step < LANES:
                inside = (lane >= step) if sign > 0 else (lane < LANES - step)
                m = pick(inside, mm(m, tuple(lane_roll(x, sign * step) for x in m)), m)
                step *= 2
            edge = LANES - 1 if sign > 0 else 0
            total = tuple(jnp.broadcast_to(x[:, edge : edge + 1], (rows, LANES)) for x in m)
            step = 1
            while step < max(ny, nz):
                total = pick(
                    place >= step, mm(total, tuple(row_roll(x, sign * step) for x in total)), total
                )
                step *= 2
            top = jnp.where(place >= 1, row_roll(total[0], sign), 1.0)
            low = jnp.where(place >= 1, row_roll(total[2], sign), 0.0)
            eta = (m[0] * top + m[1] * low) / (m[2] * top + m[3] * low)
            one_over = 1.0 / (face_out + (eta + 2.0 * eps))
            ratio = (face_out + eps) * one_over
            far = implicit_fourth * one_over
        return ratio, far, one_over

    near_l, far_l, pivot_l = eliminate(1)
    near_r, far_r, _ = eliminate(-1)
    near_l = jnp.where((to_end == 0) & (lane >= LANES - 1), 0.0, near_l)
    far_l = jnp.where((to_end == 0) & (lane >= LANES - 2), 0.0, far_l)
    near_r = jnp.where((block == 0) & (lane < 1), 0.0, near_r)
    far_r = jnp.where((block == 0) & (lane < 2), 0.0, far_r)

    def of_even(x):
        return jnp.where(even, x, lane_roll(x, 1))

    def of_odd(x):
        return jnp.where(even, lane_roll(x, -1), x)

    t0, t1, r0, r1 = of_even(near_l), of_odd(near_l), of_even(far_l), of_odd(far_l)
    from_right = (t0 * t1 - r0, -t0 * r1, t1, -r1)
    p1 = of_odd(pivot_l)
    left_inverse = (of_even(pivot_l) + t0 * t0 * p1, t0 * p1, t0 * p1, p1)
    s0, s1, q0, q1 = of_even(near_r), of_odd(near_r), of_even(far_r), of_odd(far_r)
    from_left = (-q0, s0, -s1 * q0, s1 * s0 - q1)
    from_left_after = tuple(after(x, 2) for x in from_left)
    from_right_before = tuple(before(x, 2) for x in from_right)
    diagonal = mm(inverse_of_one_minus(mm(from_right, from_left_after)), left_inverse)
    width = jnp.where(row < ny, wy, LANES)
    place = lane & (width - 1)
    to_right, to_left = from_right, from_left
    step = 2
    while step < LANES:
        to_right = pick(
            place + step < width, mm(to_right, tuple(lane_roll(x, -step) for x in to_right)), to_right
        )
        to_left = pick(place >= step, mm(to_left, tuple(lane_roll(x, step) for x in to_left)), to_left)
        step *= 2
    return from_right, from_left, diagonal, to_right, to_left, from_right_before, from_left_after


def cell_weights(chain, column, even):
    return jnp.where(even, chain[column], chain[2 + column])


def first_kernel(ny, nz, partners, flow, speed, metric_y, metric_z, *refs):
    sources, factors, chains = refs[:3]
    messages = refs[3 : 3 + partners]
    spread = refs[3 + partners]
    fields, planes_x, wy, _ = flow.shape
    rows = ny + nz
    core_rows = fields * planes_x * wy

    lane = lax.broadcasted_iota(jnp.int32, (wy, LANES), 1)
    extra_row = lax.broadcasted_iota(jnp.int32, (EXTRA, LANES), 0)
    for part in range(3):
        spread[part, 0:8, :] = jnp.zeros((8, LANES), jnp.float32)
        spread[part, wy + 8 : wy + 16, :] = jnp.zeros((8, LANES), jnp.float32)
    side = time_step * (viscous + 4.0 * explicit_fourth)
    half = time_step * 0.5
    centre = time_step * (-6.0 * viscous - 12.0 * explicit_fourth)
    fourth = -time_step * explicit_fourth

    def plane(index, carry):
        field, x = index // planes_x, index % planes_x
        u = flow[field, x]
        flux = u * speed[x]
        high, low = jnp.minimum(x + 1, planes_x - 1), jnp.maximum(x - 1, 0)
        has_high = jnp.where(x + 1 < planes_x, 1.0, 0.0)
        has_low = jnp.where(x > 0, 1.0, 0.0)
        u_high, u_low = flow[field, high] * has_high, flow[field, low] * has_low
        total = (
            centre * u
            + (time_step * viscous) * (u_high + u_low)
            - half * (u_high * speed[high] - u_low * speed[low])
        )
        onward = side * u + half * flux
        backward = side * u - half * flux
        far = fourth * u
        spread[0, 8 : wy + 8, :] = onward
        spread[1, 8 : wy + 8, :] = backward
        spread[2, 8 : wy + 8, :] = far
        total = total + (spread[0, 7 : wy + 7, :] + spread[1, 9 : wy + 9, :])
        total = total + (spread[2, 6 : wy + 6, :] + spread[2, 10 : wy + 10, :])
        a, b = lane_roll(onward, 1), lane_roll(backward, -1)
        c, d = lane_roll(far, 2), lane_roll(far, -2)
        ends = jnp.where(lane < 1, a, 0.0) + jnp.where(lane >= LANES - 1, b, 0.0)
        ends = ends + jnp.where(lane < 2, c, 0.0) + jnp.where(lane >= LANES - 2, d, 0.0)
        inner = jnp.where(lane < 1, 0.0, a) + jnp.where(lane >= LANES - 1, 0.0, b)
        inner = inner + jnp.where(lane < 2, 0.0, c) + jnp.where(lane >= LANES - 2, 0.0, d)
        start = pl.multiple_of(index * wy, 8)
        sources[pl.ds(start, wy), 0:LANES] = total + inner
        sources[pl.ds(start, wy), LANES : 2 * LANES] = ends
        above = spread[1, 7:15, :] + spread[2, 8:16, :]
        below = spread[0, wy + 5 : wy + 13, :] + spread[2, wy + 4 : wy + 12, :]
        extra = jnp.where(extra_row < 2, above, jnp.where(extra_row < 4, below, 0.0))
        start = pl.multiple_of(core_rows + index * EXTRA, 8)
        sources[pl.ds(start, EXTRA), 0:LANES] = extra
        sources[pl.ds(start, EXTRA), LANES : 2 * LANES] = jnp.zeros((EXTRA, LANES), jnp.float32)
        return carry

    lax.fori_loop(0, fields * planes_x, plane, 0)

    metric = jnp.concatenate([metric_y[...], metric_z[...]], axis=0)
    parts = factor(metric, ny, nz, wy)
    from_right, from_left, diagonal, to_right, to_left, before, after = parts
    for number, value in enumerate(v for part in parts for v in part):
        factors[number] = value
    for number, value in enumerate(to_right + to_left):
        chains[number] = value

    me = lax.axis_index("gz")
    mine = lax.broadcasted_iota(jnp.int32, (rows, LANES), 0) == ny + me
    even = (lax.broadcasted_iota(jnp.int32, (1, LANES), 1) & 1) == 0
    lane = lax.broadcasted_iota(jnp.int32, (1, LANES), 1)

    def own(values):
        return tuple(jnp.sum(jnp.where(mine, v, 0.0), axis=0, keepdims=True) for v in values)

    up, down = own(to_right), own(to_left)
    up_past, down_past = own(mm(before, to_right)), own(mm(after, to_left))
    unit = (1.0, 0.0, 0.0, 1.0)
    weights = []
    for column in range(2):
        same = jnp.where(even, unit[column], unit[2 + column])
        inside_up = cell_weights(up, column, even)
        inside_down = cell_weights(down, column, even)
        past_up = lane_roll(cell_weights(up_past, column, even), -2)
        past_down = lane_roll(cell_weights(down_past, column, even), 2)
        ends_up = jnp.where(lane < 2, same, jnp.where(lane >= LANES - 2, past_up, 0.0))
        ends_down = jnp.where(lane < 2, past_down, jnp.where(lane >= LANES - 2, same, 0.0))
        weights.append(
            (
                jnp.concatenate([inside_up, ends_up], axis=1),
                jnp.concatenate([inside_down, ends_down], axis=1),
            )
        )
    stack = []
    for k in range(1, partners + 1):
        upward = jnp.bitwise_xor(me, k) > me
        stack += [jnp.where(upward, w[0], w[1]) for w in weights]
    while len(stack) % 8:
        stack.append(jnp.zeros((1, 2 * LANES), jnp.float32))
    moments = lax.dot_general(
        jnp.concatenate(stack, axis=0),
        sources[...],
        (((1,), (1,)), ((), ())),
        precision=HIGHEST,
        preferred_element_type=jnp.float32,
    )
    for k in range(partners):
        messages[k][...] = moments[2 * k : 2 * k + 2]


def dense_inverse(columns, start, width, low_ref, high_ref):
    lane = lax.broadcasted_iota(jnp.int32, (1, LANES), 1)
    pairs = width // 2
    fits = width + 4 <= LANES

    def at(pair, number):
        return columns[pl.ds(start + 2 * pair, 1), number : number + 1]

    def two_by_two(pair, number):
        return tuple(at(pair, number + k) for k in range(4))

    def inject(pair, values, block, extra, extra_lane):
        top, bottom = values
        top = jnp.where(lane == 2 * pair, block[0], jnp.where(lane == 2 * pair + 1, block[1], top))
        bottom = jnp.where(lane == 2 * pair, block[2], jnp.where(lane == 2 * pair + 1, block[3], bottom))
        if extra is not None and fits:
            top = jnp.where(lane == extra_lane, extra[0], jnp.where(lane == extra_lane + 1, extra[1], top))
            bottom = jnp.where(
                lane == extra_lane, extra[2], jnp.where(lane == extra_lane + 1, extra[3], bottom)
            )
        return top, bottom

    zero = jnp.zeros((1, LANES), jnp.float32)
    low = high = (zero, zero)
    for step in range(pairs):
        i, j = step, pairs - 1 - step
        t = two_by_two(i, 4)
        low = (t[0] * low[0] + t[1] * low[1], t[2] * low[0] + t[3] * low[1])
        block = two_by_two(i, 8)
        extra = None
        if i == 0:
            b = two_by_two(0, 12)
            extra = mm(block, (b[0], b[2], b[1], b[3]))
        low = inject(i, low, block, extra, width)
        t = two_by_two(j, 0)
        high = (t[0] * high[0] + t[1] * high[1], t[2] * high[0] + t[3] * high[1])
        block = two_by_two(j, 8)
        extra = None
        if step == 0:
            b = two_by_two(pairs - 1, 16)
            extra = mm(block, (b[0], b[2], b[1], b[3]))
        high = inject(j, high, block, extra, width + 2)
        low_ref[2 * i : 2 * i + 1, :] = low[0]
        low_ref[2 * i + 1 : 2 * i + 2, :] = low[1]
        high_ref[2 * j : 2 * j + 1, :] = high[0]
        high_ref[2 * j + 1 : 2 * j + 2, :] = high[1]
    row = lax.broadcasted_iota(jnp.int32, (width, LANES), 0)
    column = lax.broadcasted_iota(jnp.int32, (width, LANES), 1)
    lower = (column <= row) | ((column >= width) & (column < width + 2))
    return jnp.where(lower, low_ref[0:width, :], high_ref[0:width, :])


def chain_product(chains, number, place, begin, end, reverse):
    def step(index, product):
        block = begin + end - 1 - index if reverse else index
        row, lane = place(block)
        return mm(product, tuple(chains[number + k, row, lane] for k in range(4)))

    one, zero = jnp.float32(1.0), jnp.float32(0.0)
    return lax.fori_loop(begin, end, step, (one, zero, zero, one))


def stage_plan(count):
    plan, stride = [], 1
    while stride < count:
        radix = 4 if count // stride >= 4 else 2
        plan.append((stride, radix))
        stride *= radix
    return plan


def second_kernel(
    ny, nz, count_y, wy, partners, chains, sources, factors, local, entering, inverse_y, weights_y, coefs, *scratch
):
    columns, low_ref, high_ref, spread = scratch
    me_z, me_y = lax.axis_index("gz"), lax.axis_index("gy")

    def transposed(row):
        rows = [factors[number, pl.ds(row, 1), :] for number in range(12)]
        rows += [factors[20 + number, pl.ds(row, 1), :] for number in range(8)]
        rows += [factors[12 + number, pl.ds(row, 1), :] for number in range(8)]
        rows.append(jnp.zeros((4, LANES), jnp.float32))
        return jnp.concatenate(rows, axis=0).T

    columns[...] = transposed(ny + me_z)
    inverse = dense_inverse(columns, 0, LANES, low_ref, high_ref)
    spread[0:LANES, :] = inverse
    spread[LANES : 2 * LANES, :] = jnp.zeros((LANES, LANES), jnp.float32)
    past = tuple(columns[LANES - 1 : LANES, 16 + k : 17 + k] for k in range(4))
    ahead = tuple(columns[0:1, 12 + k : 13 + k] for k in range(4))
    head0, head1 = spread[0:1, :], spread[1:2, :]
    tail0, tail1 = spread[LANES - 2 : LANES - 1, :], spread[LANES - 1 : LANES, :]
    for q in range(2):
        spread[LANES + q : LANES + q + 1, :] = past[2 * q] * tail0 + past[2 * q + 1] * tail1
        spread[2 * LANES - 2 + q : 2 * LANES - 1 + q, :] = ahead[2 * q] * head0 + ahead[2 * q + 1] * head1
    local[...] = jnp.dot(
        sources[...], spread[...], precision=HIGHEST, preferred_element_type=jnp.float32
    )

    entering[...] = jnp.zeros(entering.shape, jnp.float32)

    def place_z(block):
        return ny + block, 0

    def place_z_end(block):
        return ny + block, LANES - 1

    for k in range(1, partners + 1):
        other = jnp.bitwise_xor(me_z, k)
        lower = other < me_z
        up = chain_product(chains, 0, place_z, other + 1, me_z, False)
        down = chain_product(chains, 4, place_z_end, me_z + 1, other, True)
        for p in range(2):
            from_low = up[2 * p] * head0 + up[2 * p + 1] * head1
            from_high = down[2 * p] * tail0 + down[2 * p + 1] * tail1
            row = 2 * (k - 1) + p
            entering[row : row + 1, :] = jnp.where(lower, from_low, from_high)

    cell = me_y * wy
    columns[...] = transposed(cell // LANES)
    start = lax.rem(cell, LANES)
    inverse_y[...] = dense_inverse(columns, start, wy, low_ref, high_ref)
    row = lax.broadcasted_iota(jnp.int32, (wy, LANES), 0)
    extra_row = lax.broadcasted_iota(jnp.int32, (EXTRA, LANES), 0)
    unit = (1.0, 0.0, 0.0, 1.0)

    def head(number):
        return tuple(columns[pl.ds(start, 1), number + k : number + k + 1] for k in range(4))

    def tail(number):
        return tuple(columns[pl.ds(start + wy - 1, 1), number + k : number + k + 1] for k in range(4))

    past_up, past_down = mm(head(12), head(20)), mm(tail(16), tail(24))
    for column in range(2):
        for output, number in ((column, 20), (2 + column, 24)):
            even = columns[pl.ds(start, wy), number + column : number + column + 1]
            odd = columns[pl.ds(start, wy), number + 2 + column : number + 3 + column]
            weights_y[output, 0:wy, :] = jnp.where((row & 1) == 0, even, odd)
        for output, early, late in (
            (column, (past_up[column], past_up[2 + column]), (unit[column], unit[2 + column])),
            (2 + column, (unit[column], unit[2 + column]), (past_down[column], past_down[2 + column])),
        ):
            value = jnp.zeros((EXTRA, LANES), jnp.float32)
            for r, v in enumerate(early + late):
                value = jnp.where(extra_row == r, v, value)
            weights_y[output, wy : wy + EXTRA, :] = value

    def place_y(block):
        c = block * wy
        return c // LANES, lax.rem(c, LANES)

    def place_y_end(block):
        c = block * wy + wy - 1
        return c // LANES, lax.rem(c, LANES)

    base = 0
    for stride, radix in stage_plan(count_y):
        group = me_y // stride
        first = (group // radix) * radix
        for k in range(radix):
            other = first + jnp.bitwise_xor(group - first, k)
            entries = []
            if k > 0:
                up = chain_product(chains, 0, place_y, (other + 1) * stride, me_y, False)
                down = chain_product(chains, 4, place_y_end, me_y + 1, other * stride, True)
                is_low, is_high = other < group, other > group
                entries += [jnp.where(is_low, v, 0.0) for v in up]
                entries += [jnp.where(is_high, v, 0.0) for v in down]
            else:
                entries += [jnp.float32(0.0)] * 8
            entries += chain_product(
                chains, 0, place_y, (other + 1) * stride, (first + radix) * stride, False
            )
            entries += chain_product(chains, 4, place_y_end, first * stride, other * stride, True)
            for offset, value in enumerate(entries):
                coefs[base + offset] = value
            base += 16


def third_kernel(partners, wy, weights_y, local, entering, *refs):
    messages, (solved, carried) = refs[:partners], refs[partners:]
    planes = carried.shape[1]
    received = [m[...] for m in messages]
    padding = entering.shape[0] - 2 * partners
    if padding:
        received.append(jnp.zeros((padding, received[0].shape[1]), jnp.float32))
    received = jnp.concatenate(received, axis=0)
    solved[...] = local[...] + jnp.dot(
        received.T, entering[...], precision=HIGHEST, preferred_element_type=jnp.float32
    )

    def plane(index, carry):
        start = pl.multiple_of(index * wy, 8)
        core = solved[pl.ds(start, wy), :]
        start = pl.multiple_of(planes * wy + index * EXTRA, 8)
        extra = solved[pl.ds(start, EXTRA), :]
        for number in range(4):
            value = jnp.sum(core * weights_y[number, 0:wy, :], axis=0, keepdims=True)
            value = value + jnp.sum(extra * weights_y[number, wy : wy + EXTRA, :], axis=0, keepdims=True)
            carried[number, pl.ds(index, 1), :] = value
        return carry

    lax.fori_loop(0, planes, plane, 0)


def local_y_kernel(wy, solved, inverse_y, out):
    planes = out.shape[0]
    matrix = inverse_y[:, 0 : wy + EXTRA]

    def plane(index, carry):
        start = pl.multiple_of(index * wy, 8)
        core = solved[pl.ds(start, wy), :]
        start = pl.multiple_of(planes * wy + index * EXTRA, 8)
        both = jnp.concatenate([core, solved[pl.ds(start, EXTRA), :]], axis=0)
        out[index] = jnp.dot(matrix, both, precision=HIGHEST, preferred_element_type=jnp.float32)
        return carry

    lax.fori_loop(0, planes, plane, 0)


def combine(coefs, base, values, number):
    first = 0 if number in (0, 8) else 2
    out = [None, None]
    for k, value in values:
        for q in range(2):
            for p in range(2):
                term = coefs[base + 16 * k + number + 2 * p + q] * value[first + p]
                out[q] = term if out[q] is None else out[q] + term
    return out


def stage_kernel(base, stride, radix, narrow, has_entered, coefs, *refs):
    values = [(k, refs[k]) for k in range(radix)]
    position = radix
    entered = None
    if has_entered:
        entered = refs[position]
        position += 1
    message, entering = refs[position : position + 2]
    below = combine(coefs, base, values[1:], 0)
    above = combine(coefs, base, values[1:], 4)
    for row, value in enumerate(below + above):
        entering[row] = value if entered is None else value + entered[row]
    upward = combine(coefs, base, values, 8)
    downward = combine(coefs, base, values, 12)
    if narrow:
        group = lax.axis_index("gy") // (stride * radix)
        sends_up = lax.rem(group, 2) == 0
        for row in range(2):
            message[row] = jnp.where(sends_up, upward[row], downward[row])
    else:
        for row, value in enumerate(upward + downward):
            message[row] = value


def last_kernel(base, radix, narrow, wy, coefs, local, inverse_y, entered, *refs):
    messages, (out, st) = refs[: radix - 1], refs[radix - 1 :]
    values = [(k + 1, m) for k, m in enumerate(messages)]
    if narrow:
        values = [(k, (m[0], m[1], m[0], m[1])) for k, m in values]
    below = combine(coefs, base, values, 0)
    above = combine(coefs, base, values, 4)
    for row, value in enumerate(below + above):
        st[row] = value + entered[row]
    sides = [
        jnp.broadcast_to(inverse_y[:, c : c + 1], (wy, LANES)) for c in (0, 1, wy - 2, wy - 1)
    ]
    fields, planes_x = out.shape[:2]
    for field in range(fields):

        def plane(x, carry):
            index = field * planes_x + x
            value = local[index]
            for number in range(4):
                value = value + sides[number] * st[number, pl.ds(index, 1), :]
            out[field, x] = value
            return carry

        lax.fori_loop(0, planes_x, plane, 0)


VMEM = pl.BlockSpec(memory_space=pltpu.VMEM)
SMEM = pl.BlockSpec(memory_space=pltpu.SMEM)
PARAMS = pltpu.CompilerParams(vmem_limit_bytes=40 * 1024 * 1024)


def array(*shape):
    return jax.ShapeDtypeStruct(shape, jnp.float32)


def cost(flops, data):
    return pl.CostEstimate(flops=flops, bytes_accessed=data, transcendentals=0)


def on_device(mesh, flow, speed, metric_y, metric_z):
    fields, planes_x, wy, wz = flow.shape
    count_y, count_z = mesh.shape["gy"], mesh.shape["gz"]
    assert wz == LANES
    ny, nz = metric_y.shape[0] // LANES, metric_z.shape[0] // LANES
    planes = fields * planes_x
    rows = planes * (wy + EXTRA)
    partners = count_z - 1
    entering_rows = -(-2 * partners // 8) * 8
    outputs = pl.pallas_call(
        functools.partial(first_kernel, ny, nz, partners),
        out_shape=[array(rows, 2 * LANES), array(28, ny + nz, LANES), array(8, ny + nz, LANES)]
        + [array(2, rows)] * partners,
        in_specs=[VMEM] * 4,
        out_specs=[VMEM] * (3 + partners),
        scratch_shapes=[pltpu.VMEM((3, wy + 16, LANES), jnp.float32)],
        compiler_params=PARAMS,
        name="forcing_and_factor",
    )(flow, speed, metric_y.reshape(ny, LANES), metric_z.reshape(nz, LANES))
    sources, factors, chains = outputs[:3]

    def exchange(values, axis, count, stride, radix):
        received = []
        for k, value in zip(range(1, radix), values):
            pairs = [(i, i ^ (k * stride)) for i in range(count)]
            received.append(lax.ppermute(value, axis, pairs))
        return received

    received = exchange(outputs[3:], "gz", count_z, 1, count_z)
    plan = stage_plan(count_y)
    local, entering, inverse_y, weights_y, coefs = pl.pallas_call(
        functools.partial(second_kernel, ny, nz, count_y, wy, partners),
        out_shape=[
            array(rows, LANES),
            array(entering_rows, LANES),
            array(wy, LANES),
            array(4, wy + EXTRA, LANES),
            array(16 * sum(radix for _, radix in plan)),
        ],
        in_specs=[SMEM, VMEM, VMEM],
        out_specs=[VMEM] * 4 + [SMEM],
        scratch_shapes=[
            pltpu.VMEM((LANES, 32), jnp.float32),
            pltpu.VMEM((LANES, LANES), jnp.float32),
            pltpu.VMEM((LANES, LANES), jnp.float32),
            pltpu.VMEM((2 * LANES, LANES), jnp.float32),
        ],
        compiler_params=PARAMS,
        cost_estimate=cost(2 * rows * 256 * 128 * 6, 4 * rows * 384),
        name="local_z",
    )(chains, sources, factors)
    solved, carried = pl.pallas_call(
        functools.partial(third_kernel, partners, wy),
        out_shape=[array(rows, LANES), array(4, planes, LANES)],
        in_specs=[VMEM] * (3 + partners),
        out_specs=[VMEM] * 2,
        compiler_params=PARAMS,
        name="finish_z",
    )(weights_y, local, entering, *received)

    narrow = plan[-1][1] == 2 and len(plan) > 1
    base, entered, result = 0, None, None
    for number, (stride, radix) in enumerate(plan):
        received = exchange([carried] * (radix - 1), "gy", count_y, stride, radix)
        if number == 0:
            result = pl.pallas_call(
                functools.partial(local_y_kernel, wy),
                out_shape=array(planes, wy, LANES),
                in_specs=[VMEM] * 2,
                out_specs=VMEM,
                compiler_params=PARAMS,
                cost_estimate=cost(2 * rows * 128 * 128 * 6, 4 * rows * 256),
                name="local_y",
            )(solved, inverse_y)
        if number + 1 < len(plan):
            slim = narrow and number + 2 == len(plan)
            inputs = [carried] + received + ([entered] if entered is not None else [])
            carried, entered = pl.pallas_call(
                functools.partial(stage_kernel, base, stride, radix, slim, entered is not None),
                out_shape=[array(2 if slim else 4, planes, LANES), array(4, planes, LANES)],
                in_specs=[SMEM] + [VMEM] * len(inputs),
                out_specs=[VMEM] * 2,
                compiler_params=PARAMS,
                name="join_groups",
            )(coefs, *inputs)
            base += 16 * radix
        else:
            if entered is None:
                entered = jnp.zeros((4, planes, LANES), jnp.float32)
            return pl.pallas_call(
                functools.partial(last_kernel, base, radix, narrow, wy),
                out_shape=array(fields, planes_x, wy, wz),
                in_specs=[SMEM] + [VMEM] * (3 + len(received)),
                out_specs=VMEM,
                scratch_shapes=[pltpu.VMEM((4, planes, LANES), jnp.float32)],
                compiler_params=PARAMS,
                name="finish_y",
            )(coefs, result, inverse_y, entered, *received)


def solution(mesh):
    placed = (P(None, None, "gy", "gz"), P(None, "gy", "gz"), P(), P())
    return jax.shard_map(
        functools.partial(on_device, mesh),
        mesh=mesh,
        in_specs=placed,
        out_specs=P(None, None, "gy", "gz"),
        check_vma=False,
    )
```

```python
import functools

import jax
import jax.numpy as jnp
from jax import lax
from jax.experimental import pallas as pl
from jax.experimental.pallas import tpu as pltpu
from jax.sharding import PartitionSpec as P

viscous = 0.25
explicit_fourth = 0.04
implicit_fourth = 0.05
time_step = 1048576.0
LANES = 128
EXTRA = 8


def mm(a, b):
    return (
        a[0] * b[0] + a[1] * b[2],
        a[0] * b[1] + a[1] * b[3],
        a[2] * b[0] + a[3] * b[2],
        a[2] * b[1] + a[3] * b[3],
    )


def inverse_of_one_minus(a):
    p, q, r, s = 1.0 - a[0], -a[1], -a[2], 1.0 - a[3]
    d = 1.0 / (p * s - q * r)
    return (s * d, -q * d, -r * d, p * d)


def pick(condition, a, b):
    return tuple(jnp.where(condition, x, y) for x, y in zip(a, b))


def halves(x):
    high = x.astype(jnp.bfloat16)
    return high, (x - high.astype(jnp.float32)).astype(jnp.bfloat16)


def matmul(a, b, dims=(((1,), (0,)), ((), ()))):
    return lax.dot_general(a, b, dims, preferred_element_type=jnp.float32)


def lane_roll(x, by):
    return pltpu.roll(x, by % LANES, 1)


def row_roll(x, by):
    by = by % x.shape[0]
    return jnp.concatenate([x[x.shape[0] - by :], x[: x.shape[0] - by]], axis=0)


class Factor:
    def __init__(self, metric, ny, nz, wy):
        self.ny, self.nz, self.wy, self.rows = ny, nz, wy, ny + nz
        self.lane = lax.broadcasted_iota(jnp.int32, (self.rows, LANES), 1)
        self.row = lax.broadcasted_iota(jnp.int32, (self.rows, LANES), 0)
        self.block = jnp.where(self.row < ny, self.row, self.row - ny)
        self.to_end = jnp.where(self.row < ny, ny, nz) - 1 - self.block
        first = (self.lane == 0) & (self.block == 0)
        last = (self.lane == LANES - 1) & (self.to_end == 0)
        self.face_low = 0.5 * (jnp.where(first, metric, self.before(metric, 1)) + metric)
        self.face_high = 0.5 * (metric + jnp.where(last, metric, self.after(metric, 1)))

    def before(self, x, by):
        rolled = lane_roll(x, by)
        value = jnp.where(self.lane < by, row_roll(rolled, 1), rolled)
        return jnp.where((self.lane < by) & (self.block == 0), 0.0, value)

    def after(self, x, by):
        rolled = lane_roll(x, -by)
        value = jnp.where(self.lane >= LANES - by, row_roll(rolled, -1), rolled)
        return jnp.where((self.lane >= LANES - by) & (self.to_end == 0), 0.0, value)

    def sweep(self, sign, ratio, far):
        rows = self.rows
        back = self.before if sign > 0 else self.after
        if sign > 0:
            face_in, face_out, place = self.face_low, self.face_high, self.block
        else:
            face_in, face_out, place = self.face_high, self.face_low, self.to_end
        eps = 4.0 * implicit_fourth - implicit_fourth * back(ratio, 1)
        mass = (1.0 + 6.0 * implicit_fourth) - implicit_fourth * back(far, 2) - 2.0 * eps
        eps_in = back(eps, 1)
        scale = 1.0 / (face_in + 2.0 * eps_in)
        m = ((mass + face_in) * scale, mass - eps_in * eps_in * scale, scale, jnp.ones_like(scale))
        step = 1
        while step < LANES:
            inside = (self.lane >= step) if sign > 0 else (self.lane < LANES - step)
            m = pick(inside, mm(m, tuple(lane_roll(x, sign * step) for x in m)), m)
            step *= 2
        edge = LANES - 1 if sign > 0 else 0
        total = tuple(jnp.broadcast_to(x[:, edge : edge + 1], (rows, LANES)) for x in m)
        step = 1
        while step < max(self.ny, self.nz):
            total = pick(
                place >= step, mm(total, tuple(row_roll(x, sign * step) for x in total)), total
            )
            step *= 2
        top = jnp.where(place >= 1, row_roll(total[0], sign), 1.0)
        low = jnp.where(place >= 1, row_roll(total[2], sign), 0.0)
        eta = (m[0] * top + m[1] * low) / (m[2] * top + m[3] * low)
        one_over = 1.0 / (face_out + (eta + 2.0 * eps))
        return (face_out + eps) * one_over, implicit_fourth * one_over, one_over

    def finish(self, near_l, far_l, pivot_l, near_r, far_r):
        lane, block, to_end = self.lane, self.block, self.to_end
        even = (lane & 1) == 0
        near_l = jnp.where((to_end == 0) & (lane >= LANES - 1), 0.0, near_l)
        far_l = jnp.where((to_end == 0) & (lane >= LANES - 2), 0.0, far_l)
        near_r = jnp.where((block == 0) & (lane < 1), 0.0, near_r)
        far_r = jnp.where((block == 0) & (lane < 2), 0.0, far_r)

        def of_even(x):
            return jnp.where(even, x, lane_roll(x, 1))

        def of_odd(x):
            return jnp.where(even, lane_roll(x, -1), x)

        t0, t1, r0, r1 = of_even(near_l), of_odd(near_l), of_even(far_l), of_odd(far_l)
        from_right = (t0 * t1 - r0, -t0 * r1, t1, -r1)
        p1 = of_odd(pivot_l)
        left_inverse = (of_even(pivot_l) + t0 * t0 * p1, t0 * p1, t0 * p1, p1)
        s0, s1, q0, q1 = of_even(near_r), of_odd(near_r), of_even(far_r), of_odd(far_r)
        from_left = (-q0, s0, -s1 * q0, s1 * s0 - q1)
        from_left_after = tuple(self.after(x, 2) for x in from_left)
        from_right_before = tuple(self.before(x, 2) for x in from_right)
        diagonal = mm(inverse_of_one_minus(mm(from_right, from_left_after)), left_inverse)
        width = jnp.where(self.row < self.ny, self.wy, LANES)
        place = lane & (width - 1)
        right, left = from_right, from_left
        step = 2
        while step < LANES:
            right = pick(place + step < width, mm(right, tuple(lane_roll(x, -step) for x in right)), right)
            left = pick(place >= step, mm(left, tuple(lane_roll(x, step) for x in left)), left)
            step *= 2
        return from_right, from_left, diagonal, right, left, from_right_before, from_left_after


def cell_weights(chain, column, even):
    return jnp.where(even, chain[column], chain[2 + column])


def first_kernel(ny, nz, partners, flow_hbm, speed_hbm, metric_y, metric_z, *refs):
    high, low, factors, chains = refs[:4]
    messages = refs[4 : 4 + partners]
    flow, speed, metric, spread, arrived = refs[4 + partners :]
    fields, planes_x, wy, _ = flow.shape
    rows = ny + nz
    core_rows = fields * planes_x * wy

    copies = [
        pltpu.make_async_copy(metric_y, metric.at[0:ny], arrived.at[fields]),
        pltpu.make_async_copy(metric_z, metric.at[ny:rows], arrived.at[fields + 1]),
        pltpu.make_async_copy(speed_hbm, speed, arrived.at[fields + 2]),
    ]
    for copy in copies:
        copy.start()
    for field in range(fields):
        pltpu.make_async_copy(flow_hbm.at[field], flow.at[field], arrived.at[field]).start()

    lane = lax.broadcasted_iota(jnp.int32, (wy, LANES), 1)
    extra_row = lax.broadcasted_iota(jnp.int32, (EXTRA, LANES), 0)
    for slot in range(2):
        for part in range(3):
            spread[slot, part, 0:8, :] = jnp.zeros((8, LANES), jnp.float32)
            spread[slot, part, wy + 8 : wy + 16, :] = jnp.zeros((8, LANES), jnp.float32)
    side = time_step * (viscous + 4.0 * explicit_fourth)
    half = time_step * 0.5
    centre = time_step * (-6.0 * viscous - 12.0 * explicit_fourth)
    fourth = -time_step * explicit_fourth

    def store(start, column, value):
        first, second = halves(value)
        high[pl.ds(start, value.shape[0]), column : column + LANES] = first
        low[pl.ds(start, value.shape[0]), column : column + LANES] = second

    def one_field(field):
        values = [flow[field, x] for x in range(planes_x)]
        fluxes = [half * (values[x] * speed[x]) for x in range(planes_x)]
        extras = []
        for x in range(planes_x):
            u, flux, slot = values[x], fluxes[x], x % 2
            total = centre * u
            for other, sign in ((x + 1, -1), (x - 1, 1)):
                if 0 <= other < planes_x:
                    total = total + (time_step * viscous) * values[other]
                    total = total + fluxes[other] if sign > 0 else total - fluxes[other]
            scaled = side * u
            onward, backward, far = scaled + flux, scaled - flux, fourth * u
            spread[slot, 0, 8 : wy + 8, :] = onward
            spread[slot, 1, 8 : wy + 8, :] = backward
            spread[slot, 2, 8 : wy + 8, :] = far
            total = total + (spread[slot, 0, 7 : wy + 7, :] + spread[slot, 1, 9 : wy + 9, :])
            total = total + (spread[slot, 2, 6 : wy + 6, :] + spread[slot, 2, 10 : wy + 10, :])
            a, b = lane_roll(onward, 1), lane_roll(backward, -1)
            c, d = lane_roll(far, 2), lane_roll(far, -2)
            ends = jnp.where(lane < 2, c + jnp.where(lane < 1, a, 0.0), 0.0)
            ends = jnp.where(lane >= LANES - 2, d + jnp.where(lane >= LANES - 1, b, 0.0), ends)
            index = field * planes_x + x
            start = pl.multiple_of(index * wy, 16)
            store(start, 0, total + ((a + b) + (c + d) - ends))
            store(start, LANES, ends)
            above = spread[slot, 1, 7:15, :] + spread[slot, 2, 8:16, :]
            below = spread[slot, 0, wy + 5 : wy + 13, :] + spread[slot, 2, wy + 4 : wy + 12, :]
            extras.append(jnp.where(extra_row < 2, above, jnp.where(extra_row < 4, below, 0.0)))
            if len(extras) == 2:
                start = pl.multiple_of(core_rows + (index - 1) * EXTRA, 16)
                store(start, 0, jnp.concatenate(extras, axis=0))
                for ref in (high, low):
                    ref[pl.ds(start, 2 * EXTRA), LANES : 2 * LANES] = jnp.zeros(
                        (2 * EXTRA, LANES), jnp.bfloat16
                    )
                extras = []

    copies[0].wait()
    copies[1].wait()
    factor = Factor(metric[...], ny, nz, wy)
    copies[2].wait()

    def step(field, carry):
        pltpu.make_async_copy(flow_hbm.at[field], flow.at[field], arrived.at[field]).wait()
        left, right = carry
        left = factor.sweep(1, left[0], left[1])
        right = factor.sweep(-1, right[0], right[1])
        one_field(field)
        return left, right

    guess = (jnp.ones((rows, LANES), jnp.float32),) + (jnp.zeros((rows, LANES), jnp.float32),) * 2
    left, right = lax.fori_loop(0, fields, step, (guess, guess))

    parts = factor.finish(left[0], left[1], left[2], right[0], right[1])
    from_right, from_left, diagonal, to_right, to_left, before, after = parts
    for number, value in enumerate(v for part in parts for v in part):
        factors[number] = value
    for number, value in enumerate(to_right + to_left):
        chains[number] = value

    me = lax.axis_index("gz")
    mine = lax.broadcasted_iota(jnp.int32, (rows, LANES), 0) == ny + me
    even = (lax.broadcasted_iota(jnp.int32, (1, LANES), 1) & 1) == 0
    lane = lax.broadcasted_iota(jnp.int32, (1, LANES), 1)

    def own(values):
        return tuple(jnp.sum(jnp.where(mine, v, 0.0), axis=0, keepdims=True) for v in values)

    up, down = own(to_right), own(to_left)
    up_past, down_past = own(mm(before, to_right)), own(mm(after, to_left))
    unit = (1.0, 0.0, 0.0, 1.0)
    weights = []
    for column in range(2):
        same = jnp.where(even, unit[column], unit[2 + column])
        inside_up = cell_weights(up, column, even)
        inside_down = cell_weights(down, column, even)
        past_up = lane_roll(cell_weights(up_past, column, even), -2)
        past_down = lane_roll(cell_weights(down_past, column, even), 2)
        ends_up = jnp.where(lane < 2, same, jnp.where(lane >= LANES - 2, past_up, 0.0))
        ends_down = jnp.where(lane < 2, past_down, jnp.where(lane >= LANES - 2, same, 0.0))
        weights.append(
            (
                jnp.concatenate([inside_up, ends_up], axis=1),
                jnp.concatenate([inside_down, ends_down], axis=1),
            )
        )
    stack = []
    for k in range(1, partners + 1):
        upward = jnp.bitwise_xor(me, k) > me
        stack += [jnp.where(upward, w[0], w[1]) for w in weights]
    while len(stack) % 8:
        stack.append(jnp.zeros((1, 2 * LANES), jnp.float32))
    count = len(stack)
    stack = jnp.concatenate(stack, axis=0)
    first = stack.astype(jnp.bfloat16).astype(jnp.float32)
    both = jnp.concatenate([first, stack - first], axis=0).astype(jnp.bfloat16)
    across = (((1,), (1,)), ((), ()))
    on_high = matmul(both, high[...], across)
    on_low = matmul(both, low[...], across)
    moments = (on_high[:count] + on_high[count:]) + on_low[:count]
    for k in range(partners):
        messages[k][...] = moments[2 * k : 2 * k + 2]


def dense_inverse(columns, start, width, low_ref, high_ref):
    lane = lax.broadcasted_iota(jnp.int32, (1, LANES), 1)
    pairs = width // 2
    fits = width + 4 <= LANES

    def at(pair, number):
        return columns[pl.ds(start + 2 * pair, 1), number : number + 1]

    def two_by_two(pair, number):
        return tuple(at(pair, number + k) for k in range(4))

    def inject(pair, values, block, extra, extra_lane):
        top, bottom = values
        top = jnp.where(lane == 2 * pair, block[0], jnp.where(lane == 2 * pair + 1, block[1], top))
        bottom = jnp.where(lane == 2 * pair, block[2], jnp.where(lane == 2 * pair + 1, block[3], bottom))
        if extra is not None and fits:
            top = jnp.where(lane == extra_lane, extra[0], jnp.where(lane == extra_lane + 1, extra[1], top))
            bottom = jnp.where(
                lane == extra_lane, extra[2], jnp.where(lane == extra_lane + 1, extra[3], bottom)
            )
        return top, bottom

    zero = jnp.zeros((1, LANES), jnp.float32)
    low = high = (zero, zero)
    for step in range(pairs):
        i, j = step, pairs - 1 - step
        t = two_by_two(i, 4)
        low = (t[0] * low[0] + t[1] * low[1], t[2] * low[0] + t[3] * low[1])
        block = two_by_two(i, 8)
        extra = None
        if i == 0:
            b = two_by_two(0, 12)
            extra = mm(block, (b[0], b[2], b[1], b[3]))
        low = inject(i, low, block, extra, width)
        t = two_by_two(j, 0)
        high = (t[0] * high[0] + t[1] * high[1], t[2] * high[0] + t[3] * high[1])
        block = two_by_two(j, 8)
        extra = None
        if step == 0:
            b = two_by_two(pairs - 1, 16)
            extra = mm(block, (b[0], b[2], b[1], b[3]))
        high = inject(j, high, block, extra, width + 2)
        low_ref[2 * i : 2 * i + 1, :] = low[0]
        low_ref[2 * i + 1 : 2 * i + 2, :] = low[1]
        high_ref[2 * j : 2 * j + 1, :] = high[0]
        high_ref[2 * j + 1 : 2 * j + 2, :] = high[1]
    row = lax.broadcasted_iota(jnp.int32, (width, LANES), 0)
    column = lax.broadcasted_iota(jnp.int32, (width, LANES), 1)
    lower = (column <= row) | ((column >= width) & (column < width + 2))
    return jnp.where(lower, low_ref[0:width, :], high_ref[0:width, :])


def stage_plan(count):
    plan, stride = [], 1
    while stride < count:
        radix = 4 if count // stride >= 4 else 2
        plan.append((stride, radix))
        stride *= radix
    return plan


def transposed(factors, row):
    rows = [factors[number, pl.ds(row, 1), :] for number in range(12)]
    rows += [factors[20 + number, pl.ds(row, 1), :] for number in range(8)]
    rows += [factors[12 + number, pl.ds(row, 1), :] for number in range(8)]
    rows.append(jnp.zeros((4, LANES), jnp.float32))
    return jnp.concatenate(rows, axis=0).T


def chain_products(chains, number, place, blocks, begins, ends, masks, reverse):
    count = -(-len(begins) // 8) * 8
    row = lax.broadcasted_iota(jnp.int32, (count, LANES), 0)
    begin = jnp.zeros((count, LANES), jnp.int32)
    end, mask = begin, jnp.zeros((count, LANES), jnp.float32)
    for r, (b, e, m) in enumerate(zip(begins, ends, masks)):
        begin, end = jnp.where(row == r, b, begin), jnp.where(row == r, e, end)
        mask = jnp.where(row == r, m, mask)
    one, zero = jnp.ones((count, LANES), jnp.float32), jnp.zeros((count, LANES), jnp.float32)
    product = (one, zero, zero, one)
    for block in range(blocks - 1, -1, -1) if reverse else range(blocks):
        where = place(block)
        value = tuple(chains[number + k, where[0], where[1]] for k in range(4))
        product = pick((begin <= block) & (block < end), mm(product, value), product)
    return tuple(x * mask for x in product)


def truth(condition):
    return jnp.where(condition, 1.0, 0.0)


def second_kernel(ny, nz, count_z, wy, partners, chains, factors, matrix, entering, weights_y, *scratch):
    columns, low_ref, high_ref, rows_ref = scratch
    me_z, me_y = lax.axis_index("gz"), lax.axis_index("gy")

    columns[...] = transposed(factors, ny + me_z)
    inverse = dense_inverse(columns, 0, LANES, low_ref, high_ref)
    rows_ref[0:LANES, :] = inverse
    rows_ref[LANES : 2 * LANES, :] = jnp.zeros((LANES, LANES), jnp.float32)
    past = tuple(columns[LANES - 1 : LANES, 16 + k : 17 + k] for k in range(4))
    ahead = tuple(columns[0:1, 12 + k : 13 + k] for k in range(4))
    head0, head1 = rows_ref[0:1, :], rows_ref[1:2, :]
    tail0, tail1 = rows_ref[LANES - 2 : LANES - 1, :], rows_ref[LANES - 1 : LANES, :]
    for q in range(2):
        rows_ref[LANES + q : LANES + q + 1, :] = past[2 * q] * tail0 + past[2 * q + 1] * tail1
        rows_ref[2 * LANES - 2 + q : 2 * LANES - 1 + q, :] = ahead[2 * q] * head0 + ahead[2 * q + 1] * head1
    first, second = halves(rows_ref[...])
    matrix[0 : 2 * LANES, :] = first
    matrix[2 * LANES : 4 * LANES, :] = second
    matrix[4 * LANES : 6 * LANES, :] = first

    others = [jnp.bitwise_xor(me_z, k) for k in range(1, partners + 1)]
    always = [1.0] * partners
    up = chain_products(
        chains, 0, lambda b: (ny + b, 0), count_z, [o + 1 for o in others], [me_z] * partners, always, False
    )
    down = chain_products(
        chains, 4, lambda b: (ny + b, LANES - 1), count_z, [me_z + 1] * partners, others, always, True
    )
    stack = []
    for k, other in enumerate(others):
        for p in range(2):
            from_low = up[2 * p][k : k + 1] * head0 + up[2 * p + 1][k : k + 1] * head1
            from_high = down[2 * p][k : k + 1] * tail0 + down[2 * p + 1][k : k + 1] * tail1
            stack.append(jnp.where(other < me_z, from_low, from_high))
    while len(stack) % 8:
        stack.append(jnp.zeros((1, LANES), jnp.float32))
    stack = jnp.concatenate(stack, axis=0)
    first = stack.astype(jnp.bfloat16).astype(jnp.float32)
    entering[...] = jnp.concatenate([first, stack - first, first], axis=0)

    cell = me_y * wy
    columns[...] = transposed(factors, cell // LANES)
    start = lax.rem(cell, LANES)
    row = lax.broadcasted_iota(jnp.int32, (wy, LANES), 0)
    extra_row = lax.broadcasted_iota(jnp.int32, (EXTRA, LANES), 0)
    unit = (1.0, 0.0, 0.0, 1.0)

    def head(number):
        return tuple(columns[pl.ds(start, 1), number + k : number + k + 1] for k in range(4))

    def tail(number):
        return tuple(columns[pl.ds(start + wy - 1, 1), number + k : number + k + 1] for k in range(4))

    past_up, past_down = mm(head(12), head(20)), mm(tail(16), tail(24))
    for column in range(2):
        for output, number in ((column, 20), (2 + column, 24)):
            even = columns[pl.ds(start, wy), number + column : number + column + 1]
            odd = columns[pl.ds(start, wy), number + 2 + column : number + 3 + column]
            weights_y[output, 0:wy, :] = jnp.where((row & 1) == 0, even, odd)
        for output, early, late in (
            (column, (past_up[column], past_up[2 + column]), (unit[column], unit[2 + column])),
            (2 + column, (unit[column], unit[2 + column]), (past_down[column], past_down[2 + column])),
        ):
            value = jnp.zeros((EXTRA, LANES), jnp.float32)
            for r, v in enumerate(early + late):
                value = jnp.where(extra_row == r, v, value)
            weights_y[output, wy : wy + EXTRA, :] = value


def y_kernel(count_y, wy, chains, factors, unused, inverse_y, coefs, columns, low_ref, high_ref):
    me_y = lax.axis_index("gy")
    cell = me_y * wy
    columns[...] = transposed(factors, cell // LANES)
    start = lax.rem(cell, LANES)
    inverse_y[...] = dense_inverse(columns, start, wy, low_ref, high_ref)

    up, down = ([], [], []), ([], [], [])
    plan = stage_plan(count_y)
    for number, (stride, radix) in enumerate(plan):
        group = me_y // stride
        first = (group // radix) * radix
        others = [first + jnp.bitwise_xor(group - first, k) for k in range(radix)]
        for other in others[1:]:
            for lists, values in (
                (up, ((other + 1) * stride, me_y, truth(other < group))),
                (down, (me_y + 1, other * stride, truth(other > group))),
            ):
                for one, value in zip(lists, values):
                    one.append(value)
        if number + 1 < len(plan):
            for other in others:
                for lists, values in (
                    (up, ((other + 1) * stride, (first + radix) * stride, 1.0)),
                    (down, (first * stride, other * stride, 1.0)),
                ):
                    for one, value in zip(lists, values):
                        one.append(value)

    def place(block):
        return block * wy // LANES, block * wy % LANES

    def place_end(block):
        return place(block)[0], place(block)[1] + wy - 1

    for base, value in (
        (0, chain_products(chains, 0, place, count_y, *up, False)),
        (4, chain_products(chains, 4, place_end, count_y, *down, True)),
    ):
        for k in range(4):
            coefs[base + k] = value[k]


def third_kernel(partners, wy, weights_y, high, low, matrix, entering, *refs):
    messages, (solved, carried) = refs[:partners], refs[partners:]
    planes = carried.shape[1]
    received = [m[...] for m in messages]
    padding = entering.shape[0] // 3 - 2 * partners
    if padding:
        received.append(jnp.zeros((padding, received[0].shape[1]), jnp.float32))
    received = jnp.concatenate(received, axis=0)
    first = received.astype(jnp.bfloat16).astype(jnp.float32)
    received = jnp.concatenate([first, first, received - first], axis=0).T.astype(jnp.bfloat16)
    entered = entering[...].astype(jnp.bfloat16)
    parts = planes // 8
    total = planes * (wy + EXTRA)

    def solve(begin, size):
        rows = slice(begin, begin + size)
        left = jnp.concatenate([high[rows, :], high[rows, :], low[rows, :]], axis=1)
        return matmul(left, matrix[...]) + matmul(received[rows], entered)

    extra = solve(planes * wy, planes * EXTRA)
    solved[planes * wy : total, :] = extra
    for part in range(parts):
        core = solve(part * 8 * wy, 8 * wy)
        solved[part * 8 * wy : (part + 1) * 8 * wy, :] = core
        for number in range(4):
            lines = []
            for k in range(8):
                index = part * 8 + k
                value = jnp.sum(core[k * wy : (k + 1) * wy] * weights_y[number, 0:wy, :], axis=0, keepdims=True)
                past = extra[index * EXTRA : (index + 1) * EXTRA] * weights_y[number, wy : wy + EXTRA, :]
                lines.append(value + jnp.sum(past, axis=0, keepdims=True))
            carried[number, part * 8 : (part + 1) * 8, :] = jnp.concatenate(lines, axis=0)


def local_y_kernel(wy, solved, inverse_y, out):
    planes = out.shape[0]
    first, second = halves(inverse_y[:, 0 : wy + EXTRA])
    left = jnp.concatenate([first, second, first], axis=1)

    def part(index, carry):
        for k in range(8):
            number = index * 8 + k
            start = pl.multiple_of(number * wy, 8)
            core = solved[pl.ds(start, wy), :]
            start = pl.multiple_of(planes * wy + number * EXTRA, 8)
            both = jnp.concatenate([core, solved[pl.ds(start, EXTRA), :]], axis=0)
            top, rest = halves(both)
            out[number] = matmul(left, jnp.concatenate([top, top, rest], axis=0))
        return carry

    lax.fori_loop(0, planes // 8, part, 0)


def combine(coefs, side, row, values):
    first = 0 if side == 0 else 2
    out = [None, None]
    for k, value in enumerate(values):
        for q in range(2):
            for p in range(2):
                term = coefs[side + 2 * p + q, row + k : row + k + 1, :] * value[first + p]
                out[q] = term if out[q] is None else out[q] + term
    return out


def stage_kernel(base, stride, radix, narrow, has_entered, coefs, *refs):
    values = refs[:radix]
    position = radix
    entered = None
    if has_entered:
        entered = refs[position]
        position += 1
    message, entering = refs[position : position + 2]
    below = combine(coefs, 0, base, values[1:])
    above = combine(coefs, 4, base, values[1:])
    for row, value in enumerate(below + above):
        entering[row] = value if entered is None else value + entered[row]
    upward = combine(coefs, 0, base + radix - 1, values)
    downward = combine(coefs, 4, base + radix - 1, values)
    if narrow:
        group = lax.axis_index("gy") // (stride * radix)
        sends_up = lax.rem(group, 2) == 0
        for row in range(2):
            message[row] = jnp.where(sends_up, upward[row], downward[row])
    else:
        for row, value in enumerate(upward + downward):
            message[row] = value


def last_kernel(base, radix, narrow, wy, coefs, local, inverse_y, entered, *refs):
    messages, (out_hbm, out, sent) = refs[: radix - 1], refs[radix - 1 :]
    values = list(messages)
    if narrow:
        values = [(m[0], m[1], m[0], m[1]) for m in values]
    below = combine(coefs, 0, base, values)
    above = combine(coefs, 4, base, values)
    st = [value + entered[row] for row, value in enumerate(below + above)]
    sides = [
        jnp.broadcast_to(inverse_y[:, c : c + 1], (wy, LANES)) for c in (0, 1, wy - 2, wy - 1)
    ]
    fields, planes_x = out.shape[:2]
    copies = []
    for field in range(fields):
        for x in range(planes_x):
            index = field * planes_x + x
            value = local[index]
            for number in range(4):
                value = value + sides[number] * st[number][index : index + 1]
            out[field, x] = value
        copy = pltpu.make_async_copy(out.at[field], out_hbm.at[field], sent.at[field])
        copy.start()
        copies.append(copy)
    for copy in copies:
        copy.wait()


VMEM = pl.BlockSpec(memory_space=pltpu.VMEM)
HBM = pl.BlockSpec(memory_space=pltpu.HBM)
SMEM = pl.BlockSpec(memory_space=pltpu.SMEM)
PARAMS = pltpu.CompilerParams(vmem_limit_bytes=40 * 1024 * 1024)


def array(*shape):
    return jax.ShapeDtypeStruct(shape, jnp.float32)


def cost(flops, data):
    return pl.CostEstimate(flops=flops, bytes_accessed=data, transcendentals=0)


def on_device(mesh, flow, speed, metric_y, metric_z):
    fields, planes_x, wy, wz = flow.shape
    count_y, count_z = mesh.shape["gy"], mesh.shape["gz"]
    assert wz == LANES
    ny, nz = metric_y.shape[0] // LANES, metric_z.shape[0] // LANES
    planes = fields * planes_x
    rows = planes * (wy + EXTRA)
    partners = count_z - 1
    entering_rows = -(-2 * partners // 8) * 8
    half = jax.ShapeDtypeStruct((rows, 2 * LANES), jnp.bfloat16)
    outputs = pl.pallas_call(
        functools.partial(first_kernel, ny, nz, partners),
        out_shape=[half, half, array(28, ny + nz, LANES), array(8, ny + nz, LANES)]
        + [array(2, rows)] * partners,
        in_specs=[HBM] * 4,
        out_specs=[VMEM] * (4 + partners),
        scratch_shapes=[
            pltpu.VMEM(flow.shape, jnp.float32),
            pltpu.VMEM(speed.shape, jnp.float32),
            pltpu.VMEM((ny + nz, LANES), jnp.float32),
            pltpu.VMEM((2, 3, wy + 16, LANES), jnp.float32),
            pltpu.SemaphoreType.DMA((fields + 3,)),
        ],
        compiler_params=PARAMS,
        name="forcing_and_factor",
    )(flow, speed, metric_y.reshape(ny, LANES), metric_z.reshape(nz, LANES))
    high, low, factors, chains = outputs[:4]

    def exchange(values, axis, count, stride, radix):
        received = []
        for k, value in zip(range(1, radix), values):
            pairs = [(i, i ^ (k * stride)) for i in range(count)]
            received.append(lax.ppermute(value, axis, pairs))
        return received

    received = exchange(outputs[4:], "gz", count_z, 1, count_z)
    plan = stage_plan(count_y)
    work = [pltpu.VMEM((LANES, 32), jnp.float32)] + [pltpu.VMEM((LANES, LANES), jnp.float32)] * 2
    matrix, entering, weights_y = pl.pallas_call(
        functools.partial(second_kernel, ny, nz, count_z, wy, partners),
        out_shape=[
            jax.ShapeDtypeStruct((6 * LANES, LANES), jnp.bfloat16),
            array(3 * entering_rows, LANES),
            array(4, wy + EXTRA, LANES),
        ],
        in_specs=[SMEM, VMEM],
        out_specs=[VMEM] * 3,
        scratch_shapes=work + [pltpu.VMEM((2 * LANES, LANES), jnp.float32)],
        compiler_params=PARAMS,
        cost_estimate=cost(2 * rows * 256 * 128 * 6, 4 * rows * 384),
        name="inverse_z",
    )(chains, factors)
    solved, carried = pl.pallas_call(
        functools.partial(third_kernel, partners, wy),
        out_shape=[array(rows, LANES), array(4, planes, LANES)],
        in_specs=[VMEM] * (5 + partners),
        out_specs=[VMEM] * 2,
        compiler_params=PARAMS,
        name="finish_z",
    )(weights_y, high, low, matrix, entering, *received)

    narrow = plan[-1][1] == 2 and len(plan) > 1
    base, entered, result = 0, None, None
    for number, (stride, radix) in enumerate(plan):
        received = exchange([carried] * (radix - 1), "gy", count_y, stride, radix)
        if number == 0:
            entries = sum(2 * radix - 1 for _, radix in plan[:-1]) + plan[-1][1] - 1
            inverse_y, coefs = pl.pallas_call(
                functools.partial(y_kernel, count_y, wy),
                out_shape=[array(wy, LANES), array(8, -(-entries // 8) * 8, LANES)],
                in_specs=[SMEM, VMEM, HBM],
                out_specs=[VMEM] * 2,
                scratch_shapes=work,
                compiler_params=PARAMS,
                cost_estimate=cost(2 * rows * 128 * 128 * 6, 4 * rows * 256),
                name="inverse_y",
            )(chains, factors, carried)
            result = pl.pallas_call(
                functools.partial(local_y_kernel, wy),
                out_shape=array(planes, wy, LANES),
                in_specs=[VMEM] * 2,
                out_specs=VMEM,
                compiler_params=PARAMS,
                cost_estimate=cost(2 * rows * 128 * 128 * 6, 4 * rows * 256),
                name="local_y",
            )(solved, inverse_y)
        if number + 1 < len(plan):
            slim = narrow and number + 2 == len(plan)
            inputs = [carried] + received + ([entered] if entered is not None else [])
            carried, entered = pl.pallas_call(
                functools.partial(stage_kernel, base, stride, radix, slim, entered is not None),
                out_shape=[array(2 if slim else 4, planes, LANES), array(4, planes, LANES)],
                in_specs=[VMEM] * (1 + len(inputs)),
                out_specs=[VMEM] * 2,
                compiler_params=PARAMS,
                name="join_groups",
            )(coefs, *inputs)
            base += 2 * radix - 1
        else:
            if entered is None:
                entered = jnp.zeros((4, planes, LANES), jnp.float32)
            return pl.pallas_call(
                functools.partial(last_kernel, base, radix, narrow, wy),
                out_shape=array(fields, planes_x, wy, wz),
                in_specs=[VMEM] * (4 + len(received)),
                out_specs=HBM,
                scratch_shapes=[
                    pltpu.VMEM(flow.shape, jnp.float32),
                    pltpu.SemaphoreType.DMA((fields,)),
                ],
                compiler_params=PARAMS,
                name="finish_y",
            )(coefs, result, inverse_y, entered, *received)


def solution(mesh):
    placed = (P(None, None, "gy", "gz"), P(None, "gy", "gz"), P(), P())
    return jax.shard_map(
        functools.partial(on_device, mesh),
        mesh=mesh,
        in_specs=placed,
        out_specs=P(None, None, "gy", "gz"),
        check_vma=False,
    )
```

```python
import functools

import jax
import jax.numpy as jnp
from jax import lax
from jax.experimental import pallas as pl
from jax.experimental.pallas import tpu as pltpu
from jax.sharding import PartitionSpec as P

viscous = 0.25
explicit_fourth = 0.04
implicit_fourth = 0.05
time_step = 1048576.0
LANES = 128
EXTRA = 8


def mm(a, b):
    return (
        a[0] * b[0] + a[1] * b[2],
        a[0] * b[1] + a[1] * b[3],
        a[2] * b[0] + a[3] * b[2],
        a[2] * b[1] + a[3] * b[3],
    )


def inverse_of_one_minus(a):
    p, q, r, s = 1.0 - a[0], -a[1], -a[2], 1.0 - a[3]
    d = 1.0 / (p * s - q * r)
    return (s * d, -q * d, -r * d, p * d)


def pick(condition, a, b):
    return tuple(jnp.where(condition, x, y) for x, y in zip(a, b))


def halves(x):
    high = x.astype(jnp.bfloat16)
    return high, (x - high.astype(jnp.float32)).astype(jnp.bfloat16)


def matmul(a, b, dims=(((1,), (0,)), ((), ()))):
    return lax.dot_general(a, b, dims, preferred_element_type=jnp.float32)


def lane_roll(x, by):
    return pltpu.roll(x, by % LANES, 1)


def row_roll(x, by):
    by = by % x.shape[0]
    return jnp.concatenate([x[x.shape[0] - by :], x[: x.shape[0] - by]], axis=0)


class Factor:
    def __init__(self, metric, ny, nz, wy):
        self.ny, self.nz, self.wy, self.rows = ny, nz, wy, ny + nz
        self.lane = lax.broadcasted_iota(jnp.int32, (self.rows, LANES), 1)
        self.row = lax.broadcasted_iota(jnp.int32, (self.rows, LANES), 0)
        self.block = jnp.where(self.row < ny, self.row, self.row - ny)
        self.to_end = jnp.where(self.row < ny, ny, nz) - 1 - self.block
        first = (self.lane == 0) & (self.block == 0)
        last = (self.lane == LANES - 1) & (self.to_end == 0)
        self.face_low = 0.5 * (jnp.where(first, metric, self.before(metric, 1)) + metric)
        self.face_high = 0.5 * (metric + jnp.where(last, metric, self.after(metric, 1)))

    def before(self, x, by):
        rolled = lane_roll(x, by)
        value = jnp.where(self.lane < by, row_roll(rolled, 1), rolled)
        return jnp.where((self.lane < by) & (self.block == 0), 0.0, value)

    def after(self, x, by):
        rolled = lane_roll(x, -by)
        value = jnp.where(self.lane >= LANES - by, row_roll(rolled, -1), rolled)
        return jnp.where((self.lane >= LANES - by) & (self.to_end == 0), 0.0, value)

    def guess(self, sign):
        face = self.face_high if sign > 0 else self.face_low
        if sign > 0:
            cell = self.lane + LANES * self.block
        else:
            cell = LANES - 1 - self.lane + LANES * self.to_end
        near = face / (cell + 1).astype(jnp.float32)
        one_over = 1.0 / (face + jnp.sqrt(face + near * near))
        return face * one_over, implicit_fourth * one_over, one_over

    def sweep(self, sign, ratio, far):
        rows = self.rows
        back = self.before if sign > 0 else self.after
        if sign > 0:
            face_in, face_out, place = self.face_low, self.face_high, self.block
        else:
            face_in, face_out, place = self.face_high, self.face_low, self.to_end
        eps = 4.0 * implicit_fourth - implicit_fourth * back(ratio, 1)
        mass = (1.0 + 6.0 * implicit_fourth) - implicit_fourth * back(far, 2) - 2.0 * eps
        eps_in = back(eps, 1)
        scale = 1.0 / (face_in + 2.0 * eps_in)
        m = ((mass + face_in) * scale, mass - eps_in * eps_in * scale, scale, jnp.ones_like(scale))
        step = 1
        while step < LANES:
            inside = (self.lane >= step) if sign > 0 else (self.lane < LANES - step)
            m = pick(inside, mm(m, tuple(lane_roll(x, sign * step) for x in m)), m)
            step *= 2
        edge = LANES - 1 if sign > 0 else 0
        total = tuple(jnp.broadcast_to(x[:, edge : edge + 1], (rows, LANES)) for x in m)
        step = 1
        while step < max(self.ny, self.nz):
            total = pick(
                place >= step, mm(total, tuple(row_roll(x, sign * step) for x in total)), total
            )
            step *= 2
        top = jnp.where(place >= 1, row_roll(total[0], sign), 1.0)
        low = jnp.where(place >= 1, row_roll(total[2], sign), 0.0)
        eta = (m[0] * top + m[1] * low) / (m[2] * top + m[3] * low)
        one_over = 1.0 / (face_out + (eta + 2.0 * eps))
        return (face_out + eps) * one_over, implicit_fourth * one_over, one_over

    def finish(self, near_l, far_l, pivot_l, near_r, far_r):
        lane, block, to_end = self.lane, self.block, self.to_end
        even = (lane & 1) == 0
        near_l = jnp.where((to_end == 0) & (lane >= LANES - 1), 0.0, near_l)
        far_l = jnp.where((to_end == 0) & (lane >= LANES - 2), 0.0, far_l)
        near_r = jnp.where((block == 0) & (lane < 1), 0.0, near_r)
        far_r = jnp.where((block == 0) & (lane < 2), 0.0, far_r)

        def of_even(x):
            return jnp.where(even, x, lane_roll(x, 1))

        def of_odd(x):
            return jnp.where(even, lane_roll(x, -1), x)

        t0, t1, r0, r1 = of_even(near_l), of_odd(near_l), of_even(far_l), of_odd(far_l)
        from_right = (t0 * t1 - r0, -t0 * r1, t1, -r1)
        p1 = of_odd(pivot_l)
        left_inverse = (of_even(pivot_l) + t0 * t0 * p1, t0 * p1, t0 * p1, p1)
        s0, s1, q0, q1 = of_even(near_r), of_odd(near_r), of_even(far_r), of_odd(far_r)
        from_left = (-q0, s0, -s1 * q0, s1 * s0 - q1)
        from_left_after = tuple(self.after(x, 2) for x in from_left)
        from_right_before = tuple(self.before(x, 2) for x in from_right)
        diagonal = mm(inverse_of_one_minus(mm(from_right, from_left_after)), left_inverse)
        width = jnp.where(self.row < self.ny, self.wy, LANES)
        place = lane & (width - 1)
        right, left = from_right, from_left
        step = 2
        while step < LANES:
            right = pick(place + step < width, mm(right, tuple(lane_roll(x, -step) for x in right)), right)
            left = pick(place >= step, mm(left, tuple(lane_roll(x, step) for x in left)), left)
            step *= 2
        return from_right, from_left, diagonal, right, left, from_right_before, from_left_after


def cell_weights(chain, column, even):
    return jnp.where(even, chain[column], chain[2 + column])


def first_kernel(ny, nz, partners, flow_hbm, speed_hbm, metric_y, metric_z, *refs):
    high, low, factors, chains = refs[:4]
    messages = refs[4 : 4 + partners]
    flow, speed, metric, spread, arrived = refs[4 + partners :]
    fields, planes_x, wy, _ = flow.shape
    rows = ny + nz
    core_rows = fields * planes_x * wy

    copies = [
        pltpu.make_async_copy(metric_y, metric.at[0:ny], arrived.at[fields]),
        pltpu.make_async_copy(metric_z, metric.at[ny:rows], arrived.at[fields + 1]),
        pltpu.make_async_copy(speed_hbm, speed, arrived.at[fields + 2]),
    ]
    for copy in copies:
        copy.start()
    for field in range(fields):
        pltpu.make_async_copy(flow_hbm.at[field], flow.at[field], arrived.at[field]).start()

    lane = lax.broadcasted_iota(jnp.int32, (wy, LANES), 1)
    extra_row = lax.broadcasted_iota(jnp.int32, (EXTRA, LANES), 0)
    for slot in range(2):
        for part in range(3):
            spread[slot, part, 0:8, :] = jnp.zeros((8, LANES), jnp.float32)
            spread[slot, part, wy + 8 : wy + 16, :] = jnp.zeros((8, LANES), jnp.float32)
    side = time_step * (viscous + 4.0 * explicit_fourth)
    half = time_step * 0.5
    centre = time_step * (-6.0 * viscous - 12.0 * explicit_fourth)
    fourth = -time_step * explicit_fourth

    def store(start, column, value):
        first, second = halves(value)
        high[pl.ds(start, value.shape[0]), column : column + LANES] = first
        low[pl.ds(start, value.shape[0]), column : column + LANES] = second

    def one_field(field):
        values = [flow[field, x] for x in range(planes_x)]
        fluxes = [half * (values[x] * speed[x]) for x in range(planes_x)]
        extras = []
        for x in range(planes_x):
            u, flux, slot = values[x], fluxes[x], x % 2
            total = centre * u
            for other, sign in ((x + 1, -1), (x - 1, 1)):
                if 0 <= other < planes_x:
                    total = total + (time_step * viscous) * values[other]
                    total = total + fluxes[other] if sign > 0 else total - fluxes[other]
            scaled = side * u
            onward, backward, far = scaled + flux, scaled - flux, fourth * u
            spread[slot, 0, 8 : wy + 8, :] = onward
            spread[slot, 1, 8 : wy + 8, :] = backward
            spread[slot, 2, 8 : wy + 8, :] = far
            total = total + (spread[slot, 0, 7 : wy + 7, :] + spread[slot, 1, 9 : wy + 9, :])
            total = total + (spread[slot, 2, 6 : wy + 6, :] + spread[slot, 2, 10 : wy + 10, :])
            a, b = lane_roll(onward, 1), lane_roll(backward, -1)
            c, d = lane_roll(far, 2), lane_roll(far, -2)
            ends = jnp.where(lane < 2, c + jnp.where(lane < 1, a, 0.0), 0.0)
            ends = jnp.where(lane >= LANES - 2, d + jnp.where(lane >= LANES - 1, b, 0.0), ends)
            index = field * planes_x + x
            start = index * wy if isinstance(index, int) else pl.multiple_of(index * wy, 16)
            store(start, 0, total + ((a + b) + (c + d) - ends))
            store(start, LANES, ends)
            above = spread[slot, 1, 7:15, :] + spread[slot, 2, 8:16, :]
            below = spread[slot, 0, wy + 5 : wy + 13, :] + spread[slot, 2, wy + 4 : wy + 12, :]
            extras.append(jnp.where(extra_row < 2, above, jnp.where(extra_row < 4, below, 0.0)))
            if len(extras) == 2:
                start = core_rows + (index - 1) * EXTRA
                start = start if isinstance(index, int) else pl.multiple_of(start, 16)
                store(start, 0, jnp.concatenate(extras, axis=0))
                for ref in (high, low):
                    ref[pl.ds(start, 2 * EXTRA), LANES : 2 * LANES] = jnp.zeros(
                        (2 * EXTRA, LANES), jnp.bfloat16
                    )
                extras = []

    copies[0].wait()
    copies[1].wait()
    factor = Factor(metric[...], ny, nz, wy)
    copies[2].wait()

    def arrive(field):
        pltpu.make_async_copy(flow_hbm.at[field], flow.at[field], arrived.at[field]).wait()

    def step(index, carry):
        left, right = carry
        left = factor.sweep(1, left[0], left[1])
        right = factor.sweep(-1, right[0], right[1])
        for k in range(2):
            arrive(2 * index + k)
            one_field(2 * index + k)
        return left, right

    assert fields // 2 >= 2
    left, right = lax.fori_loop(0, fields // 2, step, (factor.guess(1), factor.guess(-1)))
    for field in range(fields // 2 * 2, fields):
        arrive(field)
        one_field(field)

    parts = factor.finish(left[0], left[1], left[2], right[0], right[1])
    from_right, from_left, diagonal, to_right, to_left, before, after = parts
    for number, value in enumerate(v for part in parts for v in part):
        factors[number] = value
    for number, value in enumerate(to_right + to_left):
        chains[number] = value

    me = lax.axis_index("gz")
    mine = lax.broadcasted_iota(jnp.int32, (rows, LANES), 0) == ny + me
    even = (lax.broadcasted_iota(jnp.int32, (1, LANES), 1) & 1) == 0
    lane = lax.broadcasted_iota(jnp.int32, (1, LANES), 1)

    def own(values):
        return tuple(jnp.sum(jnp.where(mine, v, 0.0), axis=0, keepdims=True) for v in values)

    up, down = own(to_right), own(to_left)
    up_past, down_past = own(mm(before, to_right)), own(mm(after, to_left))
    unit = (1.0, 0.0, 0.0, 1.0)
    weights = []
    for column in range(2):
        same = jnp.where(even, unit[column], unit[2 + column])
        inside_up = cell_weights(up, column, even)
        inside_down = cell_weights(down, column, even)
        past_up = lane_roll(cell_weights(up_past, column, even), -2)
        past_down = lane_roll(cell_weights(down_past, column, even), 2)
        ends_up = jnp.where(lane < 2, same, jnp.where(lane >= LANES - 2, past_up, 0.0))
        ends_down = jnp.where(lane < 2, past_down, jnp.where(lane >= LANES - 2, same, 0.0))
        weights.append(
            (
                jnp.concatenate([inside_up, ends_up], axis=1),
                jnp.concatenate([inside_down, ends_down], axis=1),
            )
        )
    stack = []
    for k in range(1, partners + 1):
        upward = jnp.bitwise_xor(me, k) > me
        stack += [jnp.where(upward, w[0], w[1]) for w in weights]
    while len(stack) % 8:
        stack.append(jnp.zeros((1, 2 * LANES), jnp.float32))
    count = len(stack)
    stack = jnp.concatenate(stack, axis=0)
    first = stack.astype(jnp.bfloat16).astype(jnp.float32)
    both = jnp.concatenate([first, stack - first], axis=0).astype(jnp.bfloat16)
    across = (((1,), (1,)), ((), ()))
    on_high = matmul(both, high[...], across)
    on_low = matmul(both, low[...], across)
    moments = (on_high[:count] + on_high[count:]) + on_low[:count]
    for k in range(partners):
        messages[k][...] = moments[2 * k : 2 * k + 2]


def dense_inverse(columns, start, width, stack):
    parts = 8
    steps = width // (2 * parts)
    lane = lax.broadcasted_iota(jnp.int32, (parts, LANES), 1)
    part = lax.broadcasted_iota(jnp.int32, (parts, LANES), 0)
    fits = width + 4 <= LANES
    values = [columns[pl.ds(start + 2 * i, parts, stride=2 * steps), :] for i in range(steps)]

    def wide(i, number):
        return tuple(
            jnp.broadcast_to(values[i][:, number + k : number + k + 1], (parts, LANES)) for k in range(4)
        )

    blocks = [wide(i, 8) for i in range(steps)]
    zero, one = jnp.zeros((parts, LANES), jnp.float32), jnp.ones((parts, LANES), jnp.float32)

    def put(rows, i, extra, extra_lane, owner):
        first = 2 * (part * steps + i)
        out = []
        for r in range(2):
            row = jnp.where(lane == first, blocks[i][2 * r], rows[r])
            row = jnp.where(lane == first + 1, blocks[i][2 * r + 1], row)
            if extra is not None and fits:
                row = jnp.where((part == owner) & (lane == extra_lane), extra[2 * r], row)
                row = jnp.where((part == owner) & (lane == extra_lane + 1), extra[2 * r + 1], row)
            out.append(row)
        return tuple(out)

    def run(order, number, ends, extra_lane, owner):
        rows, product, out = (zero, zero), (one, zero, zero, one), {}
        for i in order:
            t = wide(i, number)
            rows = (t[0] * rows[0] + t[1] * rows[1], t[2] * rows[0] + t[3] * rows[1])
            extra = None
            if i == order[0]:
                e = wide(i, ends)
                extra = mm(blocks[i], (e[0], e[2], e[1], e[3]))
            rows = put(rows, i, extra, extra_lane, owner)
            product = mm(t, product)
            out[i] = rows, product
        rows, product = out[order[-1]]
        entering, last = [None] * parts, (jnp.zeros((1, LANES), jnp.float32),) * 2
        sequence = range(parts) if number == 4 else range(parts - 1, -1, -1)
        for p in sequence:
            entering[p] = last
            own, across = [r[p : p + 1] for r in rows], [x[p : p + 1] for x in product]
            last = (
                own[0] + across[0] * last[0] + across[1] * last[1],
                own[1] + across[2] * last[0] + across[3] * last[1],
            )
        entering = [jnp.concatenate([e[r] for e in entering], axis=0) for r in range(2)]
        result = []
        for i in range(steps):
            rows, product = out[i]
            for r in range(2):
                result.append(rows[r] + product[2 * r] * entering[0] + product[2 * r + 1] * entering[1])
        return result

    low = run(list(range(steps)), 4, 12, width, 0)
    high = run(list(range(steps - 1, -1, -1)), 0, 16, width + 2, parts - 1)
    for k in range(2 * steps):
        lower = lane <= 2 * (part * steps + k // 2) + 1
        if fits:
            lower = lower & (lane < width) | ((lane >= width) & (lane < width + 2))
        stack[parts * k : parts * (k + 1), :] = jnp.where(lower, low[k], high[k])
    rows = [stack[pl.ds(p, 2 * steps, stride=parts), :] for p in range(parts)]
    return jnp.concatenate(rows, axis=0)


def stage_plan(count):
    plan, stride = [], 1
    while stride < count:
        radix = 4 if count // stride >= 4 else 2
        plan.append((stride, radix))
        stride *= radix
    return plan


def transposed(factors, row):
    rows = [factors[number, pl.ds(row, 1), :] for number in range(12)]
    rows += [factors[20 + number, pl.ds(row, 1), :] for number in range(8)]
    rows += [factors[12 + number, pl.ds(row, 1), :] for number in range(8)]
    rows.append(jnp.zeros((4, LANES), jnp.float32))
    return jnp.concatenate(rows, axis=0).T


def chain_products(chains, number, place, blocks, begins, ends, masks, reverse):
    count = -(-len(begins) // 8) * 8
    row = lax.broadcasted_iota(jnp.int32, (count, LANES), 0)
    begin = jnp.zeros((count, LANES), jnp.int32)
    end, mask = begin, jnp.zeros((count, LANES), jnp.float32)
    for r, (b, e, m) in enumerate(zip(begins, ends, masks)):
        begin, end = jnp.where(row == r, b, begin), jnp.where(row == r, e, end)
        mask = jnp.where(row == r, m, mask)
    one, zero = jnp.ones((count, LANES), jnp.float32), jnp.zeros((count, LANES), jnp.float32)
    product = (one, zero, zero, one)
    for block in range(blocks - 1, -1, -1) if reverse else range(blocks):
        where = place(block)
        value = tuple(chains[number + k, where[0], where[1]] for k in range(4))
        product = pick((begin <= block) & (block < end), mm(product, value), product)
    return tuple(x * mask for x in product)


def truth(condition):
    return jnp.where(condition, 1.0, 0.0)


def second_kernel(ny, nz, count_z, wy, partners, chains, factors, matrix, entering, weights_y, *scratch):
    columns, stacked, rows_ref = scratch
    me_z, me_y = lax.axis_index("gz"), lax.axis_index("gy")

    columns[0:LANES, 0:32] = transposed(factors, ny + me_z)
    inverse = dense_inverse(columns, 0, LANES, stacked)
    rows_ref[0:LANES, :] = inverse
    rows_ref[LANES : 2 * LANES, :] = jnp.zeros((LANES, LANES), jnp.float32)
    past = tuple(columns[LANES - 1 : LANES, 16 + k : 17 + k] for k in range(4))
    ahead = tuple(columns[0:1, 12 + k : 13 + k] for k in range(4))
    head0, head1 = rows_ref[0:1, :], rows_ref[1:2, :]
    tail0, tail1 = rows_ref[LANES - 2 : LANES - 1, :], rows_ref[LANES - 1 : LANES, :]
    for q in range(2):
        rows_ref[LANES + q : LANES + q + 1, :] = past[2 * q] * tail0 + past[2 * q + 1] * tail1
        rows_ref[2 * LANES - 2 + q : 2 * LANES - 1 + q, :] = ahead[2 * q] * head0 + ahead[2 * q + 1] * head1
    first, second = halves(rows_ref[...])
    matrix[0 : 2 * LANES, :] = first
    matrix[2 * LANES : 4 * LANES, :] = second
    matrix[4 * LANES : 6 * LANES, :] = first

    others = [jnp.bitwise_xor(me_z, k) for k in range(1, partners + 1)]
    always = [1.0] * partners
    up = chain_products(
        chains, 0, lambda b: (ny + b, 0), count_z, [o + 1 for o in others], [me_z] * partners, always, False
    )
    down = chain_products(
        chains, 4, lambda b: (ny + b, LANES - 1), count_z, [me_z + 1] * partners, others, always, True
    )
    stack = []
    for k, other in enumerate(others):
        for p in range(2):
            from_low = up[2 * p][k : k + 1] * head0 + up[2 * p + 1][k : k + 1] * head1
            from_high = down[2 * p][k : k + 1] * tail0 + down[2 * p + 1][k : k + 1] * tail1
            stack.append(jnp.where(other < me_z, from_low, from_high))
    while len(stack) % 8:
        stack.append(jnp.zeros((1, LANES), jnp.float32))
    stack = jnp.concatenate(stack, axis=0)
    first = stack.astype(jnp.bfloat16).astype(jnp.float32)
    entering[...] = jnp.concatenate([first, stack - first, first], axis=0)

    cell = me_y * wy
    columns[0:LANES, 0:32] = transposed(factors, cell // LANES)
    start = lax.rem(cell, LANES)
    row = lax.broadcasted_iota(jnp.int32, (wy, LANES), 0)
    extra_row = lax.broadcasted_iota(jnp.int32, (EXTRA, LANES), 0)
    unit = (1.0, 0.0, 0.0, 1.0)

    def head(number):
        return tuple(columns[pl.ds(start, 1), number + k : number + k + 1] for k in range(4))

    def tail(number):
        return tuple(columns[pl.ds(start + wy - 1, 1), number + k : number + k + 1] for k in range(4))

    past_up, past_down = mm(head(12), head(20)), mm(tail(16), tail(24))
    for column in range(2):
        for output, number in ((column, 20), (2 + column, 24)):
            even = columns[pl.ds(start, wy), number + column : number + column + 1]
            odd = columns[pl.ds(start, wy), number + 2 + column : number + 3 + column]
            weights_y[output, 0:wy, :] = jnp.where((row & 1) == 0, even, odd)
        for output, early, late in (
            (column, (past_up[column], past_up[2 + column]), (unit[column], unit[2 + column])),
            (2 + column, (unit[column], unit[2 + column]), (past_down[column], past_down[2 + column])),
        ):
            value = jnp.zeros((EXTRA, LANES), jnp.float32)
            for r, v in enumerate(early + late):
                value = jnp.where(extra_row == r, v, value)
            weights_y[output, wy : wy + EXTRA, :] = value


def y_kernel(count_y, wy, chains, factors, unused, inverse_y, coefs, columns, stacked):
    me_y = lax.axis_index("gy")
    cell = me_y * wy
    columns[0:LANES, 0:32] = transposed(factors, cell // LANES)
    start = lax.rem(cell, LANES)
    inverse_y[...] = dense_inverse(columns, start, wy, stacked)

    up, down = ([], [], []), ([], [], [])
    plan = stage_plan(count_y)
    for number, (stride, radix) in enumerate(plan):
        group = me_y // stride
        first = (group // radix) * radix
        others = [first + jnp.bitwise_xor(group - first, k) for k in range(radix)]
        for other in others[1:]:
            for lists, values in (
                (up, ((other + 1) * stride, me_y, truth(other < group))),
                (down, (me_y + 1, other * stride, truth(other > group))),
            ):
                for one, value in zip(lists, values):
                    one.append(value)
        if number + 1 < len(plan):
            for other in others:
                for lists, values in (
                    (up, ((other + 1) * stride, (first + radix) * stride, 1.0)),
                    (down, (first * stride, other * stride, 1.0)),
                ):
                    for one, value in zip(lists, values):
                        one.append(value)

    def place(block):
        return block * wy // LANES, block * wy % LANES

    def place_end(block):
        return place(block)[0], place(block)[1] + wy - 1

    for base, value in (
        (0, chain_products(chains, 0, place, count_y, *up, False)),
        (4, chain_products(chains, 4, place_end, count_y, *down, True)),
    ):
        for k in range(4):
            coefs[base + k] = value[k]


def third_kernel(partners, wy, weights_y, high, low, matrix, entering, *refs):
    messages, (solved, carried) = refs[:partners], refs[partners:]
    planes = carried.shape[1]
    received = [m[...] for m in messages]
    padding = entering.shape[0] // 3 - 2 * partners
    if padding:
        received.append(jnp.zeros((padding, received[0].shape[1]), jnp.float32))
    received = jnp.concatenate(received, axis=0)
    first = received.astype(jnp.bfloat16).astype(jnp.float32)
    received = jnp.concatenate([first, first, received - first], axis=0).T.astype(jnp.bfloat16)
    entered = entering[...].astype(jnp.bfloat16)
    parts = planes // 8
    total = planes * (wy + EXTRA)

    def solve(begin, size):
        rows = slice(begin, begin + size)
        left = jnp.concatenate([high[rows, :], high[rows, :], low[rows, :]], axis=1)
        return matmul(left, matrix[...]) + matmul(received[rows], entered)

    extra = solve(planes * wy, planes * EXTRA)
    solved[planes * wy : total, :] = extra
    for part in range(parts):
        core = solve(part * 8 * wy, 8 * wy)
        solved[part * 8 * wy : (part + 1) * 8 * wy, :] = core
        for number in range(4):
            lines = []
            for k in range(8):
                index = part * 8 + k
                value = jnp.sum(core[k * wy : (k + 1) * wy] * weights_y[number, 0:wy, :], axis=0, keepdims=True)
                past = extra[index * EXTRA : (index + 1) * EXTRA] * weights_y[number, wy : wy + EXTRA, :]
                lines.append(value + jnp.sum(past, axis=0, keepdims=True))
            carried[number, part * 8 : (part + 1) * 8, :] = jnp.concatenate(lines, axis=0)


def local_y_kernel(wy, solved, inverse_y, out):
    planes = out.shape[0]
    first, second = halves(inverse_y[:, 0 : wy + EXTRA])
    left = jnp.concatenate([first, second, first], axis=1)

    def part(index, carry):
        for k in range(8):
            number = index * 8 + k
            start = pl.multiple_of(number * wy, 8)
            core = solved[pl.ds(start, wy), :]
            start = pl.multiple_of(planes * wy + number * EXTRA, 8)
            both = jnp.concatenate([core, solved[pl.ds(start, EXTRA), :]], axis=0)
            top, rest = halves(both)
            out[number] = matmul(left, jnp.concatenate([top, top, rest], axis=0))
        return carry

    lax.fori_loop(0, planes // 8, part, 0)


def combine(coefs, side, row, values):
    first = 0 if side == 0 else 2
    out = [None, None]
    for k, value in enumerate(values):
        for q in range(2):
            for p in range(2):
                term = coefs[side + 2 * p + q, row + k : row + k + 1, :] * value[first + p]
                out[q] = term if out[q] is None else out[q] + term
    return out


def stage_kernel(base, stride, radix, narrow, has_entered, coefs, *refs):
    values = refs[:radix]
    position = radix
    entered = None
    if has_entered:
        entered = refs[position]
        position += 1
    message, entering = refs[position : position + 2]
    below = combine(coefs, 0, base, values[1:])
    above = combine(coefs, 4, base, values[1:])
    for row, value in enumerate(below + above):
        entering[row] = value if entered is None else value + entered[row]
    upward = combine(coefs, 0, base + radix - 1, values)
    downward = combine(coefs, 4, base + radix - 1, values)
    if narrow:
        group = lax.axis_index("gy") // (stride * radix)
        sends_up = lax.rem(group, 2) == 0
        for row in range(2):
            message[row] = jnp.where(sends_up, upward[row], downward[row])
    else:
        for row, value in enumerate(upward + downward):
            message[row] = value


def last_kernel(base, radix, narrow, wy, coefs, local, inverse_y, entered, *refs):
    messages, (out_hbm, out, sent) = refs[: radix - 1], refs[radix - 1 :]
    values = list(messages)
    if narrow:
        values = [(m[0], m[1], m[0], m[1]) for m in values]
    below = combine(coefs, 0, base, values)
    above = combine(coefs, 4, base, values)
    st = [value + entered[row] for row, value in enumerate(below + above)]
    sides = [
        jnp.broadcast_to(inverse_y[:, c : c + 1], (wy, LANES)) for c in (0, 1, wy - 2, wy - 1)
    ]
    fields, planes_x = out.shape[:2]
    copies = []
    for field in range(fields):
        for x in range(planes_x):
            index = field * planes_x + x
            value = local[index]
            for number in range(4):
                value = value + sides[number] * st[number][index : index + 1]
            out[field, x] = value
        copy = pltpu.make_async_copy(out.at[field], out_hbm.at[field], sent.at[field])
        copy.start()
        copies.append(copy)
    for copy in copies:
        copy.wait()


VMEM = pl.BlockSpec(memory_space=pltpu.VMEM)
HBM = pl.BlockSpec(memory_space=pltpu.HBM)
SMEM = pl.BlockSpec(memory_space=pltpu.SMEM)
PARAMS = pltpu.CompilerParams(vmem_limit_bytes=40 * 1024 * 1024)


def array(*shape):
    return jax.ShapeDtypeStruct(shape, jnp.float32)


def in_hbm(x):
    return pltpu.with_memory_space_constraint(x, pltpu.HBM)


def cost(flops, data):
    return pl.CostEstimate(flops=flops, bytes_accessed=data, transcendentals=0)


def on_device(mesh, flow, speed, metric_y, metric_z):
    fields, planes_x, wy, wz = flow.shape
    count_y, count_z = mesh.shape["gy"], mesh.shape["gz"]
    assert wz == LANES
    ny, nz = metric_y.shape[0] // LANES, metric_z.shape[0] // LANES
    planes = fields * planes_x
    rows = planes * (wy + EXTRA)
    partners = count_z - 1
    entering_rows = -(-2 * partners // 8) * 8
    half = jax.ShapeDtypeStruct((rows, 2 * LANES), jnp.bfloat16)
    outputs = pl.pallas_call(
        functools.partial(first_kernel, ny, nz, partners),
        out_shape=[half, half, array(28, ny + nz, LANES), array(8, ny + nz, LANES)]
        + [array(2, rows)] * partners,
        in_specs=[HBM] * 4,
        out_specs=[VMEM] * (4 + partners),
        scratch_shapes=[
            pltpu.VMEM(flow.shape, jnp.float32),
            pltpu.VMEM(speed.shape, jnp.float32),
            pltpu.VMEM((ny + nz, LANES), jnp.float32),
            pltpu.VMEM((2, 3, wy + 16, LANES), jnp.float32),
            pltpu.SemaphoreType.DMA((fields + 3,)),
        ],
        compiler_params=PARAMS,
        name="forcing_and_factor",
    )(*(in_hbm(x) for x in (flow, speed, metric_y.reshape(ny, LANES), metric_z.reshape(nz, LANES))))
    high, low, factors, chains = outputs[:4]

    def exchange(values, axis, count, stride, radix):
        received = []
        for k, value in zip(range(1, radix), values):
            pairs = [(i, i ^ (k * stride)) for i in range(count)]
            received.append(lax.ppermute(value, axis, pairs))
        return received

    received = exchange(outputs[4:], "gz", count_z, 1, count_z)
    plan = stage_plan(count_y)
    work = [pltpu.VMEM((LANES + 16, LANES), jnp.float32)] * 2
    matrix, entering, weights_y = pl.pallas_call(
        functools.partial(second_kernel, ny, nz, count_z, wy, partners),
        out_shape=[
            jax.ShapeDtypeStruct((6 * LANES, LANES), jnp.bfloat16),
            array(3 * entering_rows, LANES),
            array(4, wy + EXTRA, LANES),
        ],
        in_specs=[SMEM, VMEM],
        out_specs=[VMEM] * 3,
        scratch_shapes=work + [pltpu.VMEM((2 * LANES, LANES), jnp.float32)],
        compiler_params=PARAMS,
        cost_estimate=cost(2 * rows * 256 * 128 * 6, 4 * rows * 384),
        name="inverse_z",
    )(chains, factors)
    solved, carried = pl.pallas_call(
        functools.partial(third_kernel, partners, wy),
        out_shape=[array(rows, LANES), array(4, planes, LANES)],
        in_specs=[VMEM] * (5 + partners),
        out_specs=[VMEM] * 2,
        compiler_params=PARAMS,
        name="finish_z",
    )(weights_y, high, low, matrix, entering, *received)

    narrow = plan[-1][1] == 2 and len(plan) > 1
    base, entered, result = 0, None, None
    for number, (stride, radix) in enumerate(plan):
        received = exchange([carried] * (radix - 1), "gy", count_y, stride, radix)
        if number == 0:
            entries = sum(2 * radix - 1 for _, radix in plan[:-1]) + plan[-1][1] - 1
            inverse_y, coefs = pl.pallas_call(
                functools.partial(y_kernel, count_y, wy),
                out_shape=[array(wy, LANES), array(8, -(-entries // 8) * 8, LANES)],
                in_specs=[SMEM, VMEM, HBM],
                out_specs=[VMEM] * 2,
                scratch_shapes=work,
                compiler_params=PARAMS,
                cost_estimate=cost(2 * rows * 128 * 128 * 6, 4 * rows * 256),
                name="inverse_y",
            )(chains, factors, carried)
            result = pl.pallas_call(
                functools.partial(local_y_kernel, wy),
                out_shape=array(planes, wy, LANES),
                in_specs=[VMEM] * 2,
                out_specs=VMEM,
                compiler_params=PARAMS,
                cost_estimate=cost(2 * rows * 128 * 128 * 6, 4 * rows * 256),
                name="local_y",
            )(solved, inverse_y)
        if number + 1 < len(plan):
            slim = narrow and number + 2 == len(plan)
            inputs = [carried] + received + ([entered] if entered is not None else [])
            carried, entered = pl.pallas_call(
                functools.partial(stage_kernel, base, stride, radix, slim, entered is not None),
                out_shape=[array(2 if slim else 4, planes, LANES), array(4, planes, LANES)],
                in_specs=[VMEM] * (1 + len(inputs)),
                out_specs=[VMEM] * 2,
                compiler_params=PARAMS,
                name="join_groups",
            )(coefs, *inputs)
            base += 2 * radix - 1
        else:
            if entered is None:
                entered = jnp.zeros((4, planes, LANES), jnp.float32)
            return pl.pallas_call(
                functools.partial(last_kernel, base, radix, narrow, wy),
                out_shape=array(fields, planes_x, wy, wz),
                in_specs=[VMEM] * (4 + len(received)),
                out_specs=HBM,
                scratch_shapes=[
                    pltpu.VMEM(flow.shape, jnp.float32),
                    pltpu.SemaphoreType.DMA((fields,)),
                ],
                compiler_params=PARAMS,
                name="finish_y",
            )(coefs, result, inverse_y, entered, *received)


def solution(mesh):
    placed = (P(None, None, "gy", "gz"), P(None, "gy", "gz"), P(), P())
    return jax.shard_map(
        functools.partial(on_device, mesh),
        mesh=mesh,
        in_specs=placed,
        out_specs=P(None, None, "gy", "gz"),
        check_vma=False,
    )
```

```python
import functools

import jax
import jax.numpy as jnp
from jax import lax
from jax.experimental import pallas as pl
from jax.experimental.pallas import tpu as pltpu
from jax.sharding import PartitionSpec as P

viscous = 0.25
explicit_fourth = 0.04
implicit_fourth = 0.05
time_step = 1048576.0
LANES = 128
EXTRA = 8


def mm(a, b):
    return (
        a[0] * b[0] + a[1] * b[2],
        a[0] * b[1] + a[1] * b[3],
        a[2] * b[0] + a[3] * b[2],
        a[2] * b[1] + a[3] * b[3],
    )


def inverse_of_one_minus(a):
    p, q, r, s = 1.0 - a[0], -a[1], -a[2], 1.0 - a[3]
    d = 1.0 / (p * s - q * r)
    return (s * d, -q * d, -r * d, p * d)


def pick(condition, a, b):
    return tuple(jnp.where(condition, x, y) for x, y in zip(a, b))


def halves(x):
    high = x.astype(jnp.bfloat16)
    return high, (x - high.astype(jnp.float32)).astype(jnp.bfloat16)


def matmul(a, b, dims=(((1,), (0,)), ((), ()))):
    return lax.dot_general(a, b, dims, preferred_element_type=jnp.float32)


def lane_roll(x, by):
    return pltpu.roll(x, by % LANES, 1)


def row_roll(x, by):
    by = by % x.shape[0]
    return jnp.concatenate([x[x.shape[0] - by :], x[: x.shape[0] - by]], axis=0)


class Factor:
    def __init__(self, metric, ny, nz, wy):
        self.ny, self.nz, self.wy, self.rows = ny, nz, wy, ny + nz
        self.lane = lax.broadcasted_iota(jnp.int32, (self.rows, LANES), 1)
        self.row = lax.broadcasted_iota(jnp.int32, (self.rows, LANES), 0)
        self.block = jnp.where(self.row < ny, self.row, self.row - ny)
        self.to_end = jnp.where(self.row < ny, ny, nz) - 1 - self.block
        first = (self.lane == 0) & (self.block == 0)
        last = (self.lane == LANES - 1) & (self.to_end == 0)
        self.face_low = 0.5 * (jnp.where(first, metric, self.before(metric, 1)) + metric)
        self.face_high = 0.5 * (metric + jnp.where(last, metric, self.after(metric, 1)))

    def before(self, x, by):
        rolled = lane_roll(x, by)
        value = jnp.where(self.lane < by, row_roll(rolled, 1), rolled)
        return jnp.where((self.lane < by) & (self.block == 0), 0.0, value)

    def after(self, x, by):
        rolled = lane_roll(x, -by)
        value = jnp.where(self.lane >= LANES - by, row_roll(rolled, -1), rolled)
        return jnp.where((self.lane >= LANES - by) & (self.to_end == 0), 0.0, value)

    def guess(self, sign):
        face = self.face_high if sign > 0 else self.face_low
        if sign > 0:
            cell = self.lane + LANES * self.block
        else:
            cell = LANES - 1 - self.lane + LANES * self.to_end
        near = face / (cell + 1).astype(jnp.float32)
        one_over = 1.0 / (face + jnp.sqrt(face + near * near))
        return face * one_over, implicit_fourth * one_over, one_over

    def sweep(self, sign, ratio, far):
        rows = self.rows
        back = self.before if sign > 0 else self.after
        if sign > 0:
            face_in, face_out, place = self.face_low, self.face_high, self.block
        else:
            face_in, face_out, place = self.face_high, self.face_low, self.to_end
        eps = 4.0 * implicit_fourth - implicit_fourth * back(ratio, 1)
        mass = (1.0 + 6.0 * implicit_fourth) - implicit_fourth * back(far, 2) - 2.0 * eps
        eps_in = back(eps, 1)
        scale = 1.0 / (face_in + 2.0 * eps_in)
        m = ((mass + face_in) * scale, mass - eps_in * eps_in * scale, scale, jnp.ones_like(scale))
        step = 1
        while step < LANES:
            inside = (self.lane >= step) if sign > 0 else (self.lane < LANES - step)
            m = pick(inside, mm(m, tuple(lane_roll(x, sign * step) for x in m)), m)
            step *= 2
        edge = LANES - 1 if sign > 0 else 0
        total = tuple(jnp.broadcast_to(x[:, edge : edge + 1], (rows, LANES)) for x in m)
        step = 1
        while step < max(self.ny, self.nz):
            total = pick(
                place >= step, mm(total, tuple(row_roll(x, sign * step) for x in total)), total
            )
            step *= 2
        top = jnp.where(place >= 1, row_roll(total[0], sign), 1.0)
        low = jnp.where(place >= 1, row_roll(total[2], sign), 0.0)
        eta = (m[0] * top + m[1] * low) / (m[2] * top + m[3] * low)
        one_over = 1.0 / (face_out + (eta + 2.0 * eps))
        return (face_out + eps) * one_over, implicit_fourth * one_over, one_over

    def finish(self, near_l, far_l, pivot_l, near_r, far_r):
        lane, block, to_end = self.lane, self.block, self.to_end
        even = (lane & 1) == 0
        near_l = jnp.where((to_end == 0) & (lane >= LANES - 1), 0.0, near_l)
        far_l = jnp.where((to_end == 0) & (lane >= LANES - 2), 0.0, far_l)
        near_r = jnp.where((block == 0) & (lane < 1), 0.0, near_r)
        far_r = jnp.where((block == 0) & (lane < 2), 0.0, far_r)

        def of_even(x):
            return jnp.where(even, x, lane_roll(x, 1))

        def of_odd(x):
            return jnp.where(even, lane_roll(x, -1), x)

        t0, t1, r0, r1 = of_even(near_l), of_odd(near_l), of_even(far_l), of_odd(far_l)
        from_right = (t0 * t1 - r0, -t0 * r1, t1, -r1)
        p1 = of_odd(pivot_l)
        left_inverse = (of_even(pivot_l) + t0 * t0 * p1, t0 * p1, t0 * p1, p1)
        s0, s1, q0, q1 = of_even(near_r), of_odd(near_r), of_even(far_r), of_odd(far_r)
        from_left = (-q0, s0, -s1 * q0, s1 * s0 - q1)
        from_left_after = tuple(self.after(x, 2) for x in from_left)
        from_right_before = tuple(self.before(x, 2) for x in from_right)
        diagonal = mm(inverse_of_one_minus(mm(from_right, from_left_after)), left_inverse)
        width = jnp.where(self.row < self.ny, self.wy, LANES)
        place = lane & (width - 1)
        right, left = from_right, from_left
        step = 2
        while step < LANES:
            right = pick(place + step < width, mm(right, tuple(lane_roll(x, -step) for x in right)), right)
            left = pick(place >= step, mm(left, tuple(lane_roll(x, step) for x in left)), left)
            step *= 2
        return from_right, from_left, diagonal, right, left, from_right_before, from_left_after


def cell_weights(chain, column, even):
    return jnp.where(even, chain[column], chain[2 + column])


def first_kernel(ny, nz, partners, paired, flow_hbm, speed_hbm, metric_y, metric_z, *refs):
    high, low, factors, chains = refs[:4]
    count = 1 if paired else partners
    messages = refs[4 : 4 + count]
    flow, speed, metric, spread, arrived = refs[4 + count :]
    fields, planes_x, wy, _ = flow.shape
    rows = ny + nz
    core_rows = fields * planes_x * wy

    copies = [
        pltpu.make_async_copy(metric_y, metric.at[0:ny], arrived.at[fields]),
        pltpu.make_async_copy(metric_z, metric.at[ny:rows], arrived.at[fields + 1]),
        pltpu.make_async_copy(speed_hbm, speed, arrived.at[fields + 2]),
    ]
    for copy in copies:
        copy.start()
    for field in range(fields):
        pltpu.make_async_copy(flow_hbm.at[field], flow.at[field], arrived.at[field]).start()

    lane = lax.broadcasted_iota(jnp.int32, (wy, LANES), 1)
    extra_row = lax.broadcasted_iota(jnp.int32, (EXTRA, LANES), 0)
    for slot in range(2):
        for part in range(3):
            spread[slot, part, 0:8, :] = jnp.zeros((8, LANES), jnp.float32)
            spread[slot, part, wy + 8 : wy + 16, :] = jnp.zeros((8, LANES), jnp.float32)
    side = time_step * (viscous + 4.0 * explicit_fourth)
    half = time_step * 0.5
    centre = time_step * (-6.0 * viscous - 12.0 * explicit_fourth)
    fourth = -time_step * explicit_fourth

    def store(start, column, value):
        first, second = halves(value)
        high[pl.ds(start, value.shape[0]), column : column + LANES] = first
        low[pl.ds(start, value.shape[0]), column : column + LANES] = second

    def one_field(field):
        values = [flow[field, x] for x in range(planes_x)]
        fluxes = [half * (values[x] * speed[x]) for x in range(planes_x)]
        extras = []
        for x in range(planes_x):
            u, flux, slot = values[x], fluxes[x], x % 2
            total = centre * u
            for other, sign in ((x + 1, -1), (x - 1, 1)):
                if 0 <= other < planes_x:
                    total = total + (time_step * viscous) * values[other]
                    total = total + fluxes[other] if sign > 0 else total - fluxes[other]
            scaled = side * u
            onward, backward, far = scaled + flux, scaled - flux, fourth * u
            spread[slot, 0, 8 : wy + 8, :] = onward
            spread[slot, 1, 8 : wy + 8, :] = backward
            spread[slot, 2, 8 : wy + 8, :] = far
            total = total + (spread[slot, 0, 7 : wy + 7, :] + spread[slot, 1, 9 : wy + 9, :])
            total = total + (spread[slot, 2, 6 : wy + 6, :] + spread[slot, 2, 10 : wy + 10, :])
            a, b = lane_roll(onward, 1), lane_roll(backward, -1)
            c, d = lane_roll(far, 2), lane_roll(far, -2)
            ends = jnp.where(lane < 2, c + jnp.where(lane < 1, a, 0.0), 0.0)
            ends = jnp.where(lane >= LANES - 2, d + jnp.where(lane >= LANES - 1, b, 0.0), ends)
            index = field * planes_x + x
            start = index * wy
            store(start, 0, total + ((a + b) + (c + d) - ends))
            store(start, LANES, ends)
            above = spread[slot, 1, 7:15, :] + spread[slot, 2, 8:16, :]
            below = spread[slot, 0, wy + 5 : wy + 13, :] + spread[slot, 2, wy + 4 : wy + 12, :]
            extras.append(jnp.where(extra_row < 2, above, jnp.where(extra_row < 4, below, 0.0)))
            if len(extras) == 2:
                start = core_rows + (index - 1) * EXTRA
                store(start, 0, jnp.concatenate(extras, axis=0))
                for ref in (high, low):
                    ref[pl.ds(start, 2 * EXTRA), LANES : 2 * LANES] = jnp.zeros(
                        (2 * EXTRA, LANES), jnp.bfloat16
                    )
                extras = []

    copies[0].wait()
    copies[1].wait()
    factor = Factor(metric[...], ny, nz, wy)

    guess_l, guess_r = factor.guess(1), factor.guess(-1)
    left, right = factor.sweep(1, *guess_l[:2]), factor.sweep(-1, *guess_r[:2])
    copies[2].wait()
    for field in range(fields):
        pltpu.make_async_copy(flow_hbm.at[field], flow.at[field], arrived.at[field]).wait()
    left, right = factor.sweep(1, *left[:2]), factor.sweep(-1, *right[:2])
    for field in range(fields // 2):
        one_field(field)
    parts = factor.finish(*left, *right[:2])
    from_right, from_left, diagonal, to_right, to_left, before, after = parts
    for number, value in enumerate(v for part in parts for v in part):
        factors[number] = value
    for number, value in enumerate(to_right + to_left):
        chains[number] = value
    for field in range(fields // 2, fields):
        one_field(field)

    me = lax.axis_index("gz")
    mine = lax.broadcasted_iota(jnp.int32, (rows, LANES), 0) == ny + me
    even = (lax.broadcasted_iota(jnp.int32, (1, LANES), 1) & 1) == 0
    lane = lax.broadcasted_iota(jnp.int32, (1, LANES), 1)

    def own(values):
        return tuple(jnp.sum(jnp.where(mine, v, 0.0), axis=0, keepdims=True) for v in values)

    up, down = own(to_right), own(to_left)
    up_past, down_past = own(mm(before, to_right)), own(mm(after, to_left))
    unit = (1.0, 0.0, 0.0, 1.0)
    weights = []
    for column in range(2):
        same = jnp.where(even, unit[column], unit[2 + column])
        inside_up = cell_weights(up, column, even)
        inside_down = cell_weights(down, column, even)
        past_up = lane_roll(cell_weights(up_past, column, even), -2)
        past_down = lane_roll(cell_weights(down_past, column, even), 2)
        ends_up = jnp.where(lane < 2, same, jnp.where(lane >= LANES - 2, past_up, 0.0))
        ends_down = jnp.where(lane < 2, past_down, jnp.where(lane >= LANES - 2, same, 0.0))
        weights.append(
            (
                jnp.concatenate([inside_up, ends_up], axis=1),
                jnp.concatenate([inside_down, ends_down], axis=1),
            )
        )
    if paired:
        lower = (me & 1) == 0
        stack = [jnp.where(lower, w[0], w[1]) for w in weights]
        peer = lax.broadcasted_iota(jnp.int32, (rows, LANES), 0) == ny + jnp.bitwise_xor(me, 1)

        def of_peer(values, place):
            chosen = tuple(jnp.sum(jnp.where(peer, v, 0.0), axis=0, keepdims=True) for v in values)
            return tuple(jnp.broadcast_to(v[:, place : place + 1], (1, 2 * LANES)) for v in chosen)

        over, under = of_peer(to_right, 0), of_peer(to_left, LANES - 1)
        (up0, down0), (up1, down1) = weights
        for q in range(2):
            upward = jnp.where(lower, over[q] * up0 + over[2 + q] * up1, weights[q][0])
            downward = jnp.where(lower, weights[q][1], under[q] * down0 + under[2 + q] * down1)
            stack.append(jnp.where(me < 2, upward, downward))
    else:
        stack = []
        for k in range(1, partners + 1):
            upward = jnp.bitwise_xor(me, k) > me
            stack += [jnp.where(upward, w[0], w[1]) for w in weights]
    while len(stack) % 8:
        stack.append(jnp.zeros((1, 2 * LANES), jnp.float32))
    count = len(stack)
    stack = jnp.concatenate(stack, axis=0)
    first = stack.astype(jnp.bfloat16).astype(jnp.float32)
    both = jnp.concatenate([first, stack - first], axis=0).astype(jnp.bfloat16)
    across = (((1,), (1,)), ((), ()))
    total = high.shape[0]
    size = planes_x * wy
    for begin in range(0, total, size):
        rows = slice(begin, min(begin + size, total))
        on_high = matmul(both, high[rows, :], across)
        on_low = matmul(both, low[rows, :], across)
        moments = (on_high[:count] + on_high[count:]) + on_low[:count]
        if paired:
            messages[0][:, rows] = moments[0:4]
        else:
            for k in range(partners):
                messages[k][:, rows] = moments[2 * k : 2 * k + 2]


def dense_inverse(columns, start, width, stack):
    parts = 8
    steps = width // (2 * parts)
    lane = lax.broadcasted_iota(jnp.int32, (parts, LANES), 1)
    part = lax.broadcasted_iota(jnp.int32, (parts, LANES), 0)
    fits = width + 4 <= LANES
    values = [columns[pl.ds(start + 2 * i, parts, stride=2 * steps), :] for i in range(steps)]

    def wide(i, number):
        return tuple(
            jnp.broadcast_to(values[i][:, number + k : number + k + 1], (parts, LANES)) for k in range(4)
        )

    blocks = [wide(i, 8) for i in range(steps)]
    zero, one = jnp.zeros((parts, LANES), jnp.float32), jnp.ones((parts, LANES), jnp.float32)

    def put(rows, i, extra, extra_lane, owner):
        first = 2 * (part * steps + i)
        out = []
        for r in range(2):
            row = jnp.where(lane == first, blocks[i][2 * r], rows[r])
            row = jnp.where(lane == first + 1, blocks[i][2 * r + 1], row)
            if extra is not None and fits:
                row = jnp.where((part == owner) & (lane == extra_lane), extra[2 * r], row)
                row = jnp.where((part == owner) & (lane == extra_lane + 1), extra[2 * r + 1], row)
            out.append(row)
        return tuple(out)

    def run(order, number, ends, extra_lane, owner):
        rows, product, out = (zero, zero), (one, zero, zero, one), {}
        for i in order:
            t = wide(i, number)
            rows = (t[0] * rows[0] + t[1] * rows[1], t[2] * rows[0] + t[3] * rows[1])
            extra = None
            if i == order[0]:
                e = wide(i, ends)
                extra = mm(blocks[i], (e[0], e[2], e[1], e[3]))
            rows = put(rows, i, extra, extra_lane, owner)
            product = mm(t, product)
            out[i] = rows, product
        rows, product = out[order[-1]]
        entering, last = [None] * parts, (jnp.zeros((1, LANES), jnp.float32),) * 2
        sequence = range(parts) if number == 4 else range(parts - 1, -1, -1)
        for p in sequence:
            entering[p] = last
            own, across = [r[p : p + 1] for r in rows], [x[p : p + 1] for x in product]
            last = (
                own[0] + across[0] * last[0] + across[1] * last[1],
                own[1] + across[2] * last[0] + across[3] * last[1],
            )
        entering = [jnp.concatenate([e[r] for e in entering], axis=0) for r in range(2)]
        result = []
        for i in range(steps):
            rows, product = out[i]
            for r in range(2):
                result.append(rows[r] + product[2 * r] * entering[0] + product[2 * r + 1] * entering[1])
        return result

    low = run(list(range(steps)), 4, 12, width, 0)
    high = run(list(range(steps - 1, -1, -1)), 0, 16, width + 2, parts - 1)
    for k in range(2 * steps):
        lower = lane <= 2 * (part * steps + k // 2) + 1
        if fits:
            lower = lower & (lane < width) | ((lane >= width) & (lane < width + 2))
        stack[parts * k : parts * (k + 1), :] = jnp.where(lower, low[k], high[k])
    rows = [stack[pl.ds(p, 2 * steps, stride=parts), :] for p in range(parts)]
    return jnp.concatenate(rows, axis=0)


def stage_plan(count):
    plan, stride = [], 1
    while stride < count:
        plan.append((stride, 2))
        stride *= 2
    return plan


def transposed(factors, row):
    rows = [factors[number, pl.ds(row, 1), :] for number in range(12)]
    rows += [factors[20 + number, pl.ds(row, 1), :] for number in range(8)]
    rows += [factors[12 + number, pl.ds(row, 1), :] for number in range(8)]
    rows.append(jnp.zeros((4, LANES), jnp.float32))
    return jnp.concatenate(rows, axis=0).T


def chain_products(chains, number, place, blocks, begins, ends, masks, reverse):
    count = -(-len(begins) // 8) * 8
    row = lax.broadcasted_iota(jnp.int32, (count, LANES), 0)
    begin = jnp.zeros((count, LANES), jnp.int32)
    end, mask = begin, jnp.zeros((count, LANES), jnp.float32)
    for r, (b, e, m) in enumerate(zip(begins, ends, masks)):
        begin, end = jnp.where(row == r, b, begin), jnp.where(row == r, e, end)
        mask = jnp.where(row == r, m, mask)
    one, zero = jnp.ones((count, LANES), jnp.float32), jnp.zeros((count, LANES), jnp.float32)
    product = (one, zero, zero, one)
    for block in range(blocks - 1, -1, -1) if reverse else range(blocks):
        where = place(block)
        value = tuple(chains[number + k, where[0], where[1]] for k in range(4))
        product = pick((begin <= block) & (block < end), mm(product, value), product)
    return tuple(x * mask for x in product)


def truth(condition):
    return jnp.where(condition, 1.0, 0.0)


def second_kernel(ny, nz, count_z, wy, partners, paired, chains, factors, matrix, entering, weights_y, *scratch):
    columns, stacked, rows_ref = scratch
    me_z, me_y = lax.axis_index("gz"), lax.axis_index("gy")

    columns[0:LANES, 0:32] = transposed(factors, ny + me_z)
    inverse = dense_inverse(columns, 0, LANES, stacked)
    rows_ref[0:LANES, :] = inverse
    rows_ref[LANES : 2 * LANES, :] = jnp.zeros((LANES, LANES), jnp.float32)
    past = tuple(columns[LANES - 1 : LANES, 16 + k : 17 + k] for k in range(4))
    ahead = tuple(columns[0:1, 12 + k : 13 + k] for k in range(4))
    head0, head1 = rows_ref[0:1, :], rows_ref[1:2, :]
    tail0, tail1 = rows_ref[LANES - 2 : LANES - 1, :], rows_ref[LANES - 1 : LANES, :]
    for q in range(2):
        rows_ref[LANES + q : LANES + q + 1, :] = past[2 * q] * tail0 + past[2 * q + 1] * tail1
        rows_ref[2 * LANES - 2 + q : 2 * LANES - 1 + q, :] = ahead[2 * q] * head0 + ahead[2 * q + 1] * head1
    first, second = halves(rows_ref[...])
    matrix[0 : 2 * LANES, :] = first
    matrix[2 * LANES : 4 * LANES, :] = second
    matrix[4 * LANES : 6 * LANES, :] = first

    if paired:
        pair = me_z // 2 * 2
        begins, ends = [me_z, pair], [me_z + 1, pair + 2]
        lowers = [me_z % 2 == 1, pair > 0]
    else:
        others = [jnp.bitwise_xor(me_z, k) for k in range(1, partners + 1)]
        begins, ends = [other + 1 for other in others], others
        lowers = [other < me_z for other in others]
    size = len(begins)
    up = chain_products(
        chains, 0, lambda b: (ny + b, 0), count_z, begins, [me_z] * size, [1.0] * size, False
    )
    down = chain_products(
        chains, 4, lambda b: (ny + b, LANES - 1), count_z, [me_z + 1] * size, ends, [1.0] * size, True
    )
    stack = []
    for k, lower in enumerate(lowers):
        for p in range(2):
            from_low = up[2 * p][k : k + 1] * head0 + up[2 * p + 1][k : k + 1] * head1
            from_high = down[2 * p][k : k + 1] * tail0 + down[2 * p + 1][k : k + 1] * tail1
            stack.append(jnp.where(lower, from_low, from_high))
    while len(stack) % 8:
        stack.append(jnp.zeros((1, LANES), jnp.float32))
    stack = jnp.concatenate(stack, axis=0)
    first = stack.astype(jnp.bfloat16).astype(jnp.float32)
    entering[...] = jnp.concatenate([first, stack - first, first], axis=0)

    cell = me_y * wy
    columns[0:LANES, 0:32] = transposed(factors, cell // LANES)
    start = lax.rem(cell, LANES)
    row = lax.broadcasted_iota(jnp.int32, (wy, LANES), 0)
    extra_row = lax.broadcasted_iota(jnp.int32, (EXTRA, LANES), 0)
    unit = (1.0, 0.0, 0.0, 1.0)

    def head(number):
        return tuple(columns[pl.ds(start, 1), number + k : number + k + 1] for k in range(4))

    def tail(number):
        return tuple(columns[pl.ds(start + wy - 1, 1), number + k : number + k + 1] for k in range(4))

    past_up, past_down = mm(head(12), head(20)), mm(tail(16), tail(24))
    for column in range(2):
        for output, number in ((column, 20), (2 + column, 24)):
            even = columns[pl.ds(start, wy), number + column : number + column + 1]
            odd = columns[pl.ds(start, wy), number + 2 + column : number + 3 + column]
            weights_y[output, 0:wy, :] = jnp.where((row & 1) == 0, even, odd)
        for output, early, late in (
            (column, (past_up[column], past_up[2 + column]), (unit[column], unit[2 + column])),
            (2 + column, (unit[column], unit[2 + column]), (past_down[column], past_down[2 + column])),
        ):
            value = jnp.zeros((EXTRA, LANES), jnp.float32)
            for r, v in enumerate(early + late):
                value = jnp.where(extra_row == r, v, value)
            weights_y[output, wy : wy + EXTRA, :] = value


def y_kernel(count_y, wy, chains, factors, unused, inverse_y, coefs, columns, stacked):
    me_y = lax.axis_index("gy")
    cell = me_y * wy
    columns[0:LANES, 0:32] = transposed(factors, cell // LANES)
    start = lax.rem(cell, LANES)
    inverse_y[...] = dense_inverse(columns, start, wy, stacked)

    up, down = ([], [], []), ([], [], [])
    plan = stage_plan(count_y)
    for number, (stride, radix) in enumerate(plan):
        group = me_y // stride
        first = (group // radix) * radix
        others = [first + jnp.bitwise_xor(group - first, k) for k in range(radix)]
        for other in others[1:]:
            for lists, values in (
                (up, ((other + 1) * stride, me_y, truth(other < group))),
                (down, (me_y + 1, other * stride, truth(other > group))),
            ):
                for one, value in zip(lists, values):
                    one.append(value)
        if number + 1 < len(plan):
            for other in others:
                for lists, values in (
                    (up, ((other + 1) * stride, (first + radix) * stride, 1.0)),
                    (down, (first * stride, other * stride, 1.0)),
                ):
                    for one, value in zip(lists, values):
                        one.append(value)

    def place(block):
        return block * wy // LANES, block * wy % LANES

    def place_end(block):
        return place(block)[0], place(block)[1] + wy - 1

    for base, value in (
        (0, chain_products(chains, 0, place, count_y, *up, False)),
        (4, chain_products(chains, 4, place_end, count_y, *down, True)),
    ):
        for k in range(4):
            coefs[base + k] = value[k]


def pair_kernel(own, received, total):
    total[...] = own[2:4] + received[2:4]


def third_kernel(partners, wy, weights_y, high, low, matrix, entering, *refs):
    messages, (solved, carried) = refs[:partners], refs[partners:]
    planes = carried.shape[1]
    received = [m[0:2] for m in messages]
    padding = entering.shape[0] // 3 - 2 * partners
    if padding:
        received.append(jnp.zeros((padding, received[0].shape[1]), jnp.float32))
    received = jnp.concatenate(received, axis=0)
    first = received.astype(jnp.bfloat16).astype(jnp.float32)
    received = jnp.concatenate([first, first, received - first], axis=0).T.astype(jnp.bfloat16)
    entered = entering[...].astype(jnp.bfloat16)
    parts = planes // 8
    total = planes * (wy + EXTRA)

    def solve(begin, size):
        rows = slice(begin, begin + size)
        left = jnp.concatenate([high[rows, :], high[rows, :], low[rows, :]], axis=1)
        return matmul(left, matrix[...]) + matmul(received[rows], entered)

    extra = solve(planes * wy, planes * EXTRA)
    solved[planes * wy : total, :] = extra
    for part in range(parts):
        core = solve(part * 8 * wy, 8 * wy)
        solved[part * 8 * wy : (part + 1) * 8 * wy, :] = core
        for number in range(4):
            lines = []
            for k in range(8):
                index = part * 8 + k
                value = jnp.sum(core[k * wy : (k + 1) * wy] * weights_y[number, 0:wy, :], axis=0, keepdims=True)
                past = extra[index * EXTRA : (index + 1) * EXTRA] * weights_y[number, wy : wy + EXTRA, :]
                lines.append(value + jnp.sum(past, axis=0, keepdims=True))
            carried[number, part * 8 : (part + 1) * 8, :] = jnp.concatenate(lines, axis=0)


def local_y_kernel(wy, solved, inverse_y, unused, out):
    planes = out.shape[0]
    first, second = halves(inverse_y[:, 0 : wy + EXTRA])
    left = jnp.concatenate([first, second, first], axis=1)

    def part(index, carry):
        for k in range(8):
            number = index * 8 + k
            start = pl.multiple_of(number * wy, 8)
            core = solved[pl.ds(start, wy), :]
            start = pl.multiple_of(planes * wy + number * EXTRA, 8)
            both = jnp.concatenate([core, solved[pl.ds(start, EXTRA), :]], axis=0)
            top, rest = halves(both)
            out[number] = matmul(left, jnp.concatenate([top, top, rest], axis=0))
        return carry

    lax.fori_loop(0, planes // 8, part, 0)


def combine(coefs, side, row, values):
    first = 0 if side == 0 else 2
    out = [None, None]
    for k, value in enumerate(values):
        for q in range(2):
            for p in range(2):
                term = coefs[side + 2 * p + q, row + k : row + k + 1, :] * value[first + p]
                out[q] = term if out[q] is None else out[q] + term
    return out


def stage_kernel(base, stride, radix, narrow, has_entered, coefs, *refs):
    values = refs[:radix]
    position = radix
    entered = None
    if has_entered:
        entered = refs[position]
        position += 1
    message, entering = refs[position : position + 2]
    below = combine(coefs, 0, base, values[1:])
    above = combine(coefs, 4, base, values[1:])
    for row, value in enumerate(below + above):
        entering[row] = value if entered is None else value + entered[row]
    upward = combine(coefs, 0, base + radix - 1, values)
    downward = combine(coefs, 4, base + radix - 1, values)
    if narrow:
        group = lax.axis_index("gy") // (stride * radix)
        sends_up = lax.rem(group, 2) == 0
        for row in range(2):
            message[row] = jnp.where(sends_up, upward[row], downward[row])
    else:
        for row, value in enumerate(upward + downward):
            message[row] = value


def last_kernel(base, radix, narrow, wy, coefs, local, inverse_y, entered, *refs):
    messages, (out_hbm, out, sent) = refs[: radix - 1], refs[radix - 1 :]
    values = list(messages)
    if narrow:
        values = [(m[0], m[1], m[0], m[1]) for m in values]
    below = combine(coefs, 0, base, values)
    above = combine(coefs, 4, base, values)
    st = [value + entered[row] for row, value in enumerate(below + above)]
    sides = [
        jnp.broadcast_to(inverse_y[:, c : c + 1], (wy, LANES)) for c in (0, 1, wy - 2, wy - 1)
    ]
    fields, planes_x = out.shape[:2]
    copies = []
    for field in range(fields):
        for x in range(planes_x):
            index = field * planes_x + x
            value = local[index]
            for number in range(4):
                value = value + sides[number] * st[number][index : index + 1]
            out[field, x] = value
        copy = pltpu.make_async_copy(out.at[field], out_hbm.at[field], sent.at[field])
        copy.start()
        copies.append(copy)
    for copy in copies:
        copy.wait()


VMEM = pl.BlockSpec(memory_space=pltpu.VMEM)
HBM = pl.BlockSpec(memory_space=pltpu.HBM)
SMEM = pl.BlockSpec(memory_space=pltpu.SMEM)
PARAMS = pltpu.CompilerParams(vmem_limit_bytes=40 * 1024 * 1024)


def array(*shape):
    return jax.ShapeDtypeStruct(shape, jnp.float32)


def in_hbm(x):
    return pltpu.with_memory_space_constraint(x, pltpu.HBM)


def cost(flops, data):
    return pl.CostEstimate(flops=flops, bytes_accessed=data, transcendentals=0)


def on_device(mesh, flow, speed, metric_y, metric_z):
    fields, planes_x, wy, wz = flow.shape
    count_y, count_z = mesh.shape["gy"], mesh.shape["gz"]
    assert wz == LANES
    ny, nz = metric_y.shape[0] // LANES, metric_z.shape[0] // LANES
    planes = fields * planes_x
    rows = planes * (wy + EXTRA)
    partners = count_z - 1
    paired = count_z == 4
    arrivals = 2 if paired else partners
    entering_rows = -(-2 * arrivals // 8) * 8
    half = jax.ShapeDtypeStruct((rows, 2 * LANES), jnp.bfloat16)
    outputs = pl.pallas_call(
        functools.partial(first_kernel, ny, nz, partners, paired),
        out_shape=[half, half, array(28, ny + nz, LANES), array(8, ny + nz, LANES)]
        + ([array(4, rows)] if paired else [array(2, rows)] * partners),
        in_specs=[HBM] * 4,
        out_specs=[VMEM] * (5 if paired else 4 + partners),
        scratch_shapes=[
            pltpu.VMEM(flow.shape, jnp.float32),
            pltpu.VMEM(speed.shape, jnp.float32),
            pltpu.VMEM((ny + nz, LANES), jnp.float32),
            pltpu.VMEM((2, 3, wy + 16, LANES), jnp.float32),
            pltpu.SemaphoreType.DMA((fields + 3,)),
        ],
        compiler_params=PARAMS,
        name="forcing_and_factor",
    )(*(in_hbm(x) for x in (flow, speed, metric_y.reshape(ny, LANES), metric_z.reshape(nz, LANES))))
    high, low, factors, chains = outputs[:4]

    def exchange(values, axis, count, stride, radix):
        received = []
        for k, value in zip(range(1, radix), values):
            pairs = [(i, i ^ (k * stride)) for i in range(count)]
            received.append(lax.ppermute(value, axis, pairs))
        return received

    if paired:
        near = exchange(outputs[4:], "gz", count_z, 1, 2)
        total = pl.pallas_call(
            pair_kernel,
            out_shape=array(2, rows),
            in_specs=[VMEM] * 2,
            out_specs=VMEM,
            compiler_params=PARAMS,
            name="join_pair",
        )(outputs[4], near[0])
        received = near + exchange([total], "gz", count_z, 2, 2)
    else:
        received = exchange(outputs[4:], "gz", count_z, 1, count_z)
    plan = stage_plan(count_y)
    work = [pltpu.VMEM((LANES + 16, LANES), jnp.float32)] * 2
    matrix, entering, weights_y = pl.pallas_call(
        functools.partial(second_kernel, ny, nz, count_z, wy, partners, paired),
        out_shape=[
            jax.ShapeDtypeStruct((6 * LANES, LANES), jnp.bfloat16),
            array(3 * entering_rows, LANES),
            array(4, wy + EXTRA, LANES),
        ],
        in_specs=[SMEM, VMEM],
        out_specs=[VMEM] * 3,
        scratch_shapes=work + [pltpu.VMEM((2 * LANES, LANES), jnp.float32)],
        compiler_params=PARAMS,
        cost_estimate=cost(2 * rows * 256 * 128 * 6, 4 * rows * 384),
        name="inverse_z",
    )(chains, factors)
    solved, carried = pl.pallas_call(
        functools.partial(third_kernel, arrivals, wy),
        out_shape=[array(rows, LANES), array(4, planes, LANES)],
        in_specs=[VMEM] * (5 + arrivals),
        out_specs=[VMEM] * 2,
        compiler_params=PARAMS,
        name="finish_z",
    )(weights_y, high, low, matrix, entering, *received)

    narrow = plan[-1][1] == 2 and len(plan) > 1
    base, entered, result = 0, None, None
    for number, (stride, radix) in enumerate(plan):
        received = exchange([carried] * (radix - 1), "gy", count_y, stride, radix)
        if number == 0:
            entries = sum(2 * radix - 1 for _, radix in plan[:-1]) + plan[-1][1] - 1
            inverse_y, coefs = pl.pallas_call(
                functools.partial(y_kernel, count_y, wy),
                out_shape=[array(wy, LANES), array(8, -(-entries // 8) * 8, LANES)],
                in_specs=[SMEM, VMEM, HBM],
                out_specs=[VMEM] * 2,
                scratch_shapes=work,
                compiler_params=PARAMS,
                cost_estimate=cost(2 * rows * 128 * 128 * 6, 4 * rows * 256),
                name="inverse_y",
            )(chains, factors, carried)
        if number + 1 < len(plan):
            slim = narrow and number + 2 == len(plan)
            inputs = [carried] + received + ([entered] if entered is not None else [])
            carried, entered = pl.pallas_call(
                functools.partial(stage_kernel, base, stride, radix, slim, entered is not None),
                out_shape=[array(2 if slim else 4, planes, LANES), array(4, planes, LANES)],
                in_specs=[VMEM] * (1 + len(inputs)),
                out_specs=[VMEM] * 2,
                compiler_params=PARAMS,
                name="join_groups",
            )(coefs, *inputs)
            base += 2 * radix - 1
            if number == 0:
                result = pl.pallas_call(
                    functools.partial(local_y_kernel, wy),
                    out_shape=array(planes, wy, LANES),
                    in_specs=[VMEM] * 2 + [HBM],
                    out_specs=VMEM,
                    compiler_params=PARAMS,
                    cost_estimate=cost(2 * rows * 128 * 128 * 6, 4 * rows * 256),
                    name="local_y",
                )(solved, inverse_y, entered)
        else:
            return pl.pallas_call(
                functools.partial(last_kernel, base, radix, narrow, wy),
                out_shape=array(fields, planes_x, wy, wz),
                in_specs=[VMEM] * (4 + len(received)),
                out_specs=HBM,
                scratch_shapes=[
                    pltpu.VMEM(flow.shape, jnp.float32),
                    pltpu.SemaphoreType.DMA((fields,)),
                ],
                compiler_params=PARAMS,
                name="finish_y",
            )(coefs, result, inverse_y, entered, *received)


def solution(mesh):
    placed = (P(None, None, "gy", "gz"), P(None, "gy", "gz"), P(), P())
    return jax.shard_map(
        functools.partial(on_device, mesh),
        mesh=mesh,
        in_specs=placed,
        out_specs=P(None, None, "gy", "gz"),
        check_vma=False,
    )
```

```python
import functools

import jax
import jax.numpy as jnp
from jax import lax
from jax.experimental import pallas as pl
from jax.experimental.pallas import tpu as pltpu
from jax.sharding import PartitionSpec as P

viscous = 0.25
explicit_fourth = 0.04
implicit_fourth = 0.05
time_step = 1048576.0
LANES = 128
EXTRA = 8


def mm(a, b):
    return (
        a[0] * b[0] + a[1] * b[2],
        a[0] * b[1] + a[1] * b[3],
        a[2] * b[0] + a[3] * b[2],
        a[2] * b[1] + a[3] * b[3],
    )


def inverse_of_one_minus(a):
    p, q, r, s = 1.0 - a[0], -a[1], -a[2], 1.0 - a[3]
    d = 1.0 / (p * s - q * r)
    return (s * d, -q * d, -r * d, p * d)


def pick(condition, a, b):
    return tuple(jnp.where(condition, x, y) for x, y in zip(a, b))


def halves(x):
    high = x.astype(jnp.bfloat16)
    return high, (x - high.astype(jnp.float32)).astype(jnp.bfloat16)


def matmul(a, b, dims=(((1,), (0,)), ((), ()))):
    return lax.dot_general(a, b, dims, preferred_element_type=jnp.float32)


def lane_roll(x, by):
    return pltpu.roll(x, by % LANES, 1)


def row_roll(x, by):
    by = by % x.shape[0]
    return jnp.concatenate([x[x.shape[0] - by :], x[: x.shape[0] - by]], axis=0)


class Factor:
    def __init__(self, metric, ny, nz, wy):
        self.ny, self.nz, self.wy, self.rows = ny, nz, wy, ny + nz
        self.lane = lax.broadcasted_iota(jnp.int32, (self.rows, LANES), 1)
        self.row = lax.broadcasted_iota(jnp.int32, (self.rows, LANES), 0)
        self.block = jnp.where(self.row < ny, self.row, self.row - ny)
        self.to_end = jnp.where(self.row < ny, ny, nz) - 1 - self.block
        first = (self.lane == 0) & (self.block == 0)
        last = (self.lane == LANES - 1) & (self.to_end == 0)
        self.face_low = 0.5 * (jnp.where(first, metric, self.before(metric, 1)) + metric)
        self.face_high = 0.5 * (metric + jnp.where(last, metric, self.after(metric, 1)))

    def before(self, x, by):
        rolled = lane_roll(x, by)
        value = jnp.where(self.lane < by, row_roll(rolled, 1), rolled)
        return jnp.where((self.lane < by) & (self.block == 0), 0.0, value)

    def after(self, x, by):
        rolled = lane_roll(x, -by)
        value = jnp.where(self.lane >= LANES - by, row_roll(rolled, -1), rolled)
        return jnp.where((self.lane >= LANES - by) & (self.to_end == 0), 0.0, value)

    def guess(self, sign):
        face = self.face_high if sign > 0 else self.face_low
        if sign > 0:
            cell = self.lane + LANES * self.block
        else:
            cell = LANES - 1 - self.lane + LANES * self.to_end
        near = face / (cell + 1).astype(jnp.float32)
        one_over = 1.0 / (face + jnp.sqrt(face + near * near))
        return face * one_over, implicit_fourth * one_over, one_over

    def sweep(self, sign, ratio, far):
        rows = self.rows
        back = self.before if sign > 0 else self.after
        if sign > 0:
            face_in, face_out, place = self.face_low, self.face_high, self.block
        else:
            face_in, face_out, place = self.face_high, self.face_low, self.to_end
        eps = 4.0 * implicit_fourth - implicit_fourth * back(ratio, 1)
        mass = (1.0 + 6.0 * implicit_fourth) - implicit_fourth * back(far, 2) - 2.0 * eps
        eps_in = back(eps, 1)
        scale = 1.0 / (face_in + 2.0 * eps_in)
        m = ((mass + face_in) * scale, mass - eps_in * eps_in * scale, scale, jnp.ones_like(scale))
        step = 1
        while step < LANES:
            inside = (self.lane >= step) if sign > 0 else (self.lane < LANES - step)
            m = pick(inside, mm(m, tuple(lane_roll(x, sign * step) for x in m)), m)
            step *= 2
        edge = LANES - 1 if sign > 0 else 0
        total = tuple(jnp.broadcast_to(x[:, edge : edge + 1], (rows, LANES)) for x in m)
        step = 1
        while step < max(self.ny, self.nz):
            total = pick(
                place >= step, mm(total, tuple(row_roll(x, sign * step) for x in total)), total
            )
            step *= 2
        top = jnp.where(place >= 1, row_roll(total[0], sign), 1.0)
        low = jnp.where(place >= 1, row_roll(total[2], sign), 0.0)
        eta = (m[0] * top + m[1] * low) / (m[2] * top + m[3] * low)
        one_over = 1.0 / (face_out + (eta + 2.0 * eps))
        return (face_out + eps) * one_over, implicit_fourth * one_over, one_over

    def finish(self, near_l, far_l, pivot_l, near_r, far_r):
        lane, block, to_end = self.lane, self.block, self.to_end
        even = (lane & 1) == 0
        near_l = jnp.where((to_end == 0) & (lane >= LANES - 1), 0.0, near_l)
        far_l = jnp.where((to_end == 0) & (lane >= LANES - 2), 0.0, far_l)
        near_r = jnp.where((block == 0) & (lane < 1), 0.0, near_r)
        far_r = jnp.where((block == 0) & (lane < 2), 0.0, far_r)

        def of_even(x):
            return jnp.where(even, x, lane_roll(x, 1))

        def of_odd(x):
            return jnp.where(even, lane_roll(x, -1), x)

        t0, t1, r0, r1 = of_even(near_l), of_odd(near_l), of_even(far_l), of_odd(far_l)
        from_right = (t0 * t1 - r0, -t0 * r1, t1, -r1)
        p1 = of_odd(pivot_l)
        left_inverse = (of_even(pivot_l) + t0 * t0 * p1, t0 * p1, t0 * p1, p1)
        s0, s1, q0, q1 = of_even(near_r), of_odd(near_r), of_even(far_r), of_odd(far_r)
        from_left = (-q0, s0, -s1 * q0, s1 * s0 - q1)
        from_left_after = tuple(self.after(x, 2) for x in from_left)
        from_right_before = tuple(self.before(x, 2) for x in from_right)
        diagonal = mm(inverse_of_one_minus(mm(from_right, from_left_after)), left_inverse)
        width = jnp.where(self.row < self.ny, self.wy, LANES)
        place = lane & (width - 1)
        right, left = from_right, from_left
        step = 2
        while step < LANES:
            right = pick(place + step < width, mm(right, tuple(lane_roll(x, -step) for x in right)), right)
            left = pick(place >= step, mm(left, tuple(lane_roll(x, step) for x in left)), left)
            step *= 2
        return from_right, from_left, diagonal, right, left, from_right_before, from_left_after


def cell_weights(chain, column, even):
    return jnp.where(even, chain[column], chain[2 + column])


def first_kernel(ny, nz, partners, paired, flow_hbm, speed_hbm, metric_y, metric_z, *refs):
    high, low, factors, chains = refs[:4]
    count = 1 if paired else partners
    messages = refs[4 : 4 + count]
    flow, speed, metric, spread, arrived = refs[4 + count :]
    fields, planes_x, wy, _ = flow.shape
    rows = ny + nz
    core_rows = fields * planes_x * wy

    copies = [
        pltpu.make_async_copy(metric_y, metric.at[0:ny], arrived.at[fields]),
        pltpu.make_async_copy(metric_z, metric.at[ny:rows], arrived.at[fields + 1]),
        pltpu.make_async_copy(speed_hbm, speed, arrived.at[fields + 2]),
    ]
    for copy in copies:
        copy.start()
    for field in range(fields):
        pltpu.make_async_copy(flow_hbm.at[field], flow.at[field], arrived.at[field]).start()

    lane = lax.broadcasted_iota(jnp.int32, (wy, LANES), 1)
    extra_row = lax.broadcasted_iota(jnp.int32, (EXTRA, LANES), 0)
    for slot in range(2):
        for part in range(3):
            spread[slot, part, 0:8, :] = jnp.zeros((8, LANES), jnp.float32)
            spread[slot, part, wy + 8 : wy + 16, :] = jnp.zeros((8, LANES), jnp.float32)
    side = time_step * (viscous + 4.0 * explicit_fourth)
    half = time_step * 0.5
    centre = time_step * (-6.0 * viscous - 12.0 * explicit_fourth)
    fourth = -time_step * explicit_fourth

    def store(start, column, value):
        first, second = halves(value)
        high[pl.ds(start, value.shape[0]), column : column + LANES] = first
        low[pl.ds(start, value.shape[0]), column : column + LANES] = second

    def one_field(field):
        values = [flow[field, x] for x in range(planes_x)]
        fluxes = [half * (values[x] * speed[x]) for x in range(planes_x)]
        extras = []
        for x in range(planes_x):
            u, flux, slot = values[x], fluxes[x], x % 2
            total = centre * u
            for other, sign in ((x + 1, -1), (x - 1, 1)):
                if 0 <= other < planes_x:
                    total = total + (time_step * viscous) * values[other]
                    total = total + fluxes[other] if sign > 0 else total - fluxes[other]
            scaled = side * u
            onward, backward, far = scaled + flux, scaled - flux, fourth * u
            spread[slot, 0, 8 : wy + 8, :] = onward
            spread[slot, 1, 8 : wy + 8, :] = backward
            spread[slot, 2, 8 : wy + 8, :] = far
            total = total + (spread[slot, 0, 7 : wy + 7, :] + spread[slot, 1, 9 : wy + 9, :])
            total = total + (spread[slot, 2, 6 : wy + 6, :] + spread[slot, 2, 10 : wy + 10, :])
            a, b = lane_roll(onward, 1), lane_roll(backward, -1)
            c, d = lane_roll(far, 2), lane_roll(far, -2)
            ends = jnp.where(lane < 2, c + jnp.where(lane < 1, a, 0.0), 0.0)
            ends = jnp.where(lane >= LANES - 2, d + jnp.where(lane >= LANES - 1, b, 0.0), ends)
            index = field * planes_x + x
            start = index * wy
            store(start, 0, total + ((a + b) + (c + d) - ends))
            store(start, LANES, ends)
            above = spread[slot, 1, 7:15, :] + spread[slot, 2, 8:16, :]
            below = spread[slot, 0, wy + 5 : wy + 13, :] + spread[slot, 2, wy + 4 : wy + 12, :]
            extras.append(jnp.where(extra_row < 2, above, jnp.where(extra_row < 4, below, 0.0)))
            if len(extras) == 2:
                start = core_rows + (index - 1) * EXTRA
                store(start, 0, jnp.concatenate(extras, axis=0))
                for ref in (high, low):
                    ref[pl.ds(start, 2 * EXTRA), LANES : 2 * LANES] = jnp.zeros(
                        (2 * EXTRA, LANES), jnp.bfloat16
                    )
                extras = []

    copies[0].wait()
    copies[1].wait()
    factor = Factor(metric[...], ny, nz, wy)

    guess_l, guess_r = factor.guess(1), factor.guess(-1)
    left, right = factor.sweep(1, *guess_l[:2]), factor.sweep(-1, *guess_r[:2])
    copies[2].wait()
    for field in range(fields):
        pltpu.make_async_copy(flow_hbm.at[field], flow.at[field], arrived.at[field]).wait()
    left, right = factor.sweep(1, *left[:2]), factor.sweep(-1, *right[:2])
    for field in range(fields // 2):
        one_field(field)
    parts = factor.finish(*left, *right[:2])
    from_right, from_left, diagonal, to_right, to_left, before, after = parts
    for number, value in enumerate(v for part in parts for v in part):
        factors[number] = value
    for number, value in enumerate(to_right + to_left):
        chains[number] = value
    for field in range(fields // 2, fields):
        one_field(field)

    me = lax.axis_index("gz")
    mine = lax.broadcasted_iota(jnp.int32, (rows, LANES), 0) == ny + me
    even = (lax.broadcasted_iota(jnp.int32, (1, LANES), 1) & 1) == 0
    lane = lax.broadcasted_iota(jnp.int32, (1, LANES), 1)

    def own(values):
        return tuple(jnp.sum(jnp.where(mine, v, 0.0), axis=0, keepdims=True) for v in values)

    up, down = own(to_right), own(to_left)
    up_past, down_past = own(mm(before, to_right)), own(mm(after, to_left))
    unit = (1.0, 0.0, 0.0, 1.0)
    weights = []
    for column in range(2):
        same = jnp.where(even, unit[column], unit[2 + column])
        inside_up = cell_weights(up, column, even)
        inside_down = cell_weights(down, column, even)
        past_up = lane_roll(cell_weights(up_past, column, even), -2)
        past_down = lane_roll(cell_weights(down_past, column, even), 2)
        ends_up = jnp.where(lane < 2, same, jnp.where(lane >= LANES - 2, past_up, 0.0))
        ends_down = jnp.where(lane < 2, past_down, jnp.where(lane >= LANES - 2, same, 0.0))
        weights.append(
            (
                jnp.concatenate([inside_up, ends_up], axis=1),
                jnp.concatenate([inside_down, ends_down], axis=1),
            )
        )
    if paired:
        lower = (me & 1) == 0
        stack = [jnp.where(lower, w[0], w[1]) for w in weights]
        peer = lax.broadcasted_iota(jnp.int32, (rows, LANES), 0) == ny + jnp.bitwise_xor(me, 1)

        def of_peer(values, place):
            chosen = tuple(jnp.sum(jnp.where(peer, v, 0.0), axis=0, keepdims=True) for v in values)
            return tuple(jnp.broadcast_to(v[:, place : place + 1], (1, 2 * LANES)) for v in chosen)

        over, under = of_peer(to_right, 0), of_peer(to_left, LANES - 1)
        (up0, down0), (up1, down1) = weights
        for q in range(2):
            upward = jnp.where(lower, over[q] * up0 + over[2 + q] * up1, weights[q][0])
            downward = jnp.where(lower, weights[q][1], under[q] * down0 + under[2 + q] * down1)
            stack.append(jnp.where(me < 2, upward, downward))
    else:
        stack = []
        for k in range(1, partners + 1):
            upward = jnp.bitwise_xor(me, k) > me
            stack += [jnp.where(upward, w[0], w[1]) for w in weights]
    while len(stack) % 8:
        stack.append(jnp.zeros((1, 2 * LANES), jnp.float32))
    count = len(stack)
    stack = jnp.concatenate(stack, axis=0)
    first = stack.astype(jnp.bfloat16).astype(jnp.float32)
    both = jnp.concatenate([first, stack - first], axis=0).astype(jnp.bfloat16)
    across = (((1,), (1,)), ((), ()))
    total = high.shape[0]
    size = planes_x * wy
    for begin in range(0, total, size):
        rows = slice(begin, min(begin + size, total))
        on_high = matmul(both, high[rows, :], across)
        on_low = matmul(both, low[rows, :], across)
        moments = (on_high[:count] + on_high[count:]) + on_low[:count]
        if paired:
            messages[0][:, rows] = moments[0:4]
        else:
            for k in range(partners):
                messages[k][:, rows] = moments[2 * k : 2 * k + 2]


def dense_inverse(columns, start, width, stack):
    parts = 8
    steps = width // (2 * parts)
    lane = lax.broadcasted_iota(jnp.int32, (parts, LANES), 1)
    part = lax.broadcasted_iota(jnp.int32, (parts, LANES), 0)
    fits = width + 4 <= LANES
    values = [columns[pl.ds(start + 2 * i, parts, stride=2 * steps), :] for i in range(steps)]

    def wide(i, number):
        return tuple(
            jnp.broadcast_to(values[i][:, number + k : number + k + 1], (parts, LANES)) for k in range(4)
        )

    blocks = [wide(i, 8) for i in range(steps)]
    zero, one = jnp.zeros((parts, LANES), jnp.float32), jnp.ones((parts, LANES), jnp.float32)

    def put(rows, i, extra, extra_lane, owner):
        first = 2 * (part * steps + i)
        out = []
        for r in range(2):
            row = jnp.where(lane == first, blocks[i][2 * r], rows[r])
            row = jnp.where(lane == first + 1, blocks[i][2 * r + 1], row)
            if extra is not None and fits:
                row = jnp.where((part == owner) & (lane == extra_lane), extra[2 * r], row)
                row = jnp.where((part == owner) & (lane == extra_lane + 1), extra[2 * r + 1], row)
            out.append(row)
        return tuple(out)

    def run(order, number, ends, extra_lane, owner):
        rows, product, out = (zero, zero), (one, zero, zero, one), {}
        for i in order:
            t = wide(i, number)
            rows = (t[0] * rows[0] + t[1] * rows[1], t[2] * rows[0] + t[3] * rows[1])
            extra = None
            if i == order[0]:
                e = wide(i, ends)
                extra = mm(blocks[i], (e[0], e[2], e[1], e[3]))
            rows = put(rows, i, extra, extra_lane, owner)
            product = mm(t, product)
            out[i] = rows, product
        rows, product = out[order[-1]]
        entering, last = [None] * parts, (jnp.zeros((1, LANES), jnp.float32),) * 2
        sequence = range(parts) if number == 4 else range(parts - 1, -1, -1)
        for p in sequence:
            entering[p] = last
            own, across = [r[p : p + 1] for r in rows], [x[p : p + 1] for x in product]
            last = (
                own[0] + across[0] * last[0] + across[1] * last[1],
                own[1] + across[2] * last[0] + across[3] * last[1],
            )
        entering = [jnp.concatenate([e[r] for e in entering], axis=0) for r in range(2)]
        result = []
        for i in range(steps):
            rows, product = out[i]
            for r in range(2):
                result.append(rows[r] + product[2 * r] * entering[0] + product[2 * r + 1] * entering[1])
        return result

    low = run(list(range(steps)), 4, 12, width, 0)
    high = run(list(range(steps - 1, -1, -1)), 0, 16, width + 2, parts - 1)
    for k in range(2 * steps):
        lower = lane <= 2 * (part * steps + k // 2) + 1
        if fits:
            lower = lower & (lane < width) | ((lane >= width) & (lane < width + 2))
        stack[parts * k : parts * (k + 1), :] = jnp.where(lower, low[k], high[k])
    rows = [stack[pl.ds(p, 2 * steps, stride=parts), :] for p in range(parts)]
    return jnp.concatenate(rows, axis=0)


def stage_plan(count):
    plan, stride = [], 1
    while stride < count:
        radix = 4 if count // stride >= 4 else 2
        plan.append((stride, radix))
        stride *= radix
    return plan


def transposed(factors, row):
    rows = [factors[number, pl.ds(row, 1), :] for number in range(12)]
    rows += [factors[20 + number, pl.ds(row, 1), :] for number in range(8)]
    rows += [factors[12 + number, pl.ds(row, 1), :] for number in range(8)]
    rows.append(jnp.zeros((4, LANES), jnp.float32))
    return jnp.concatenate(rows, axis=0).T


def chain_products(chains, number, place, blocks, begins, ends, masks, reverse):
    count = -(-len(begins) // 8) * 8
    row = lax.broadcasted_iota(jnp.int32, (count, LANES), 0)
    begin = jnp.zeros((count, LANES), jnp.int32)
    end, mask = begin, jnp.zeros((count, LANES), jnp.float32)
    for r, (b, e, m) in enumerate(zip(begins, ends, masks)):
        begin, end = jnp.where(row == r, b, begin), jnp.where(row == r, e, end)
        mask = jnp.where(row == r, m, mask)
    one, zero = jnp.ones((count, LANES), jnp.float32), jnp.zeros((count, LANES), jnp.float32)
    product = (one, zero, zero, one)
    for block in range(blocks - 1, -1, -1) if reverse else range(blocks):
        where = place(block)
        value = tuple(chains[number + k, where[0], where[1]] for k in range(4))
        product = pick((begin <= block) & (block < end), mm(product, value), product)
    return tuple(x * mask for x in product)


def truth(condition):
    return jnp.where(condition, 1.0, 0.0)


def second_kernel(ny, nz, count_z, wy, partners, paired, chains, factors, matrix, entering, weights_y, *scratch):
    columns, stacked, rows_ref = scratch
    me_z, me_y = lax.axis_index("gz"), lax.axis_index("gy")

    columns[0:LANES, 0:32] = transposed(factors, ny + me_z)
    inverse = dense_inverse(columns, 0, LANES, stacked)
    rows_ref[0:LANES, :] = inverse
    rows_ref[LANES : 2 * LANES, :] = jnp.zeros((LANES, LANES), jnp.float32)
    past = tuple(columns[LANES - 1 : LANES, 16 + k : 17 + k] for k in range(4))
    ahead = tuple(columns[0:1, 12 + k : 13 + k] for k in range(4))
    head0, head1 = rows_ref[0:1, :], rows_ref[1:2, :]
    tail0, tail1 = rows_ref[LANES - 2 : LANES - 1, :], rows_ref[LANES - 1 : LANES, :]
    for q in range(2):
        rows_ref[LANES + q : LANES + q + 1, :] = past[2 * q] * tail0 + past[2 * q + 1] * tail1
        rows_ref[2 * LANES - 2 + q : 2 * LANES - 1 + q, :] = ahead[2 * q] * head0 + ahead[2 * q + 1] * head1
    first, second = halves(rows_ref[...])
    matrix[0 : 2 * LANES, :] = first
    matrix[2 * LANES : 4 * LANES, :] = second
    matrix[4 * LANES : 6 * LANES, :] = first

    if paired:
        pair = me_z // 2 * 2
        begins, ends = [me_z, pair], [me_z + 1, pair + 2]
        lowers = [me_z % 2 == 1, pair > 0]
    else:
        others = [jnp.bitwise_xor(me_z, k) for k in range(1, partners + 1)]
        begins, ends = [other + 1 for other in others], others
        lowers = [other < me_z for other in others]
    size = len(begins)
    up = chain_products(
        chains, 0, lambda b: (ny + b, 0), count_z, begins, [me_z] * size, [1.0] * size, False
    )
    down = chain_products(
        chains, 4, lambda b: (ny + b, LANES - 1), count_z, [me_z + 1] * size, ends, [1.0] * size, True
    )
    stack = []
    for k, lower in enumerate(lowers):
        for p in range(2):
            from_low = up[2 * p][k : k + 1] * head0 + up[2 * p + 1][k : k + 1] * head1
            from_high = down[2 * p][k : k + 1] * tail0 + down[2 * p + 1][k : k + 1] * tail1
            stack.append(jnp.where(lower, from_low, from_high))
    while len(stack) % 8:
        stack.append(jnp.zeros((1, LANES), jnp.float32))
    stack = jnp.concatenate(stack, axis=0)
    first = stack.astype(jnp.bfloat16).astype(jnp.float32)
    entering[...] = jnp.concatenate([first, stack - first, first], axis=0)

    cell = me_y * wy
    columns[0:LANES, 0:32] = transposed(factors, cell // LANES)
    start = lax.rem(cell, LANES)
    row = lax.broadcasted_iota(jnp.int32, (wy, LANES), 0)
    extra_row = lax.broadcasted_iota(jnp.int32, (EXTRA, LANES), 0)
    unit = (1.0, 0.0, 0.0, 1.0)

    def head(number):
        return tuple(columns[pl.ds(start, 1), number + k : number + k + 1] for k in range(4))

    def tail(number):
        return tuple(columns[pl.ds(start + wy - 1, 1), number + k : number + k + 1] for k in range(4))

    past_up, past_down = mm(head(12), head(20)), mm(tail(16), tail(24))
    for column in range(2):
        for output, number in ((column, 20), (2 + column, 24)):
            even = columns[pl.ds(start, wy), number + column : number + column + 1]
            odd = columns[pl.ds(start, wy), number + 2 + column : number + 3 + column]
            weights_y[output, 0:wy, :] = jnp.where((row & 1) == 0, even, odd)
        for output, early, late in (
            (column, (past_up[column], past_up[2 + column]), (unit[column], unit[2 + column])),
            (2 + column, (unit[column], unit[2 + column]), (past_down[column], past_down[2 + column])),
        ):
            value = jnp.zeros((EXTRA, LANES), jnp.float32)
            for r, v in enumerate(early + late):
                value = jnp.where(extra_row == r, v, value)
            weights_y[output, wy : wy + EXTRA, :] = value


def y_kernel(count_y, wy, chains, factors, unused, inverse_y, coefs, columns, stacked):
    me_y = lax.axis_index("gy")
    cell = me_y * wy
    columns[0:LANES, 0:32] = transposed(factors, cell // LANES)
    start = lax.rem(cell, LANES)
    inverse_y[...] = dense_inverse(columns, start, wy, stacked)

    up, down = ([], [], []), ([], [], [])
    plan = stage_plan(count_y)
    for number, (stride, radix) in enumerate(plan):
        group = me_y // stride
        first = (group // radix) * radix
        others = [first + jnp.bitwise_xor(group - first, k) for k in range(radix)]
        for other in others[1:]:
            for lists, values in (
                (up, ((other + 1) * stride, me_y, truth(other < group))),
                (down, (me_y + 1, other * stride, truth(other > group))),
            ):
                for one, value in zip(lists, values):
                    one.append(value)
        if number + 1 < len(plan):
            for other in others:
                for lists, values in (
                    (up, ((other + 1) * stride, (first + radix) * stride, 1.0)),
                    (down, (first * stride, other * stride, 1.0)),
                ):
                    for one, value in zip(lists, values):
                        one.append(value)

    def place(block):
        return block * wy // LANES, block * wy % LANES

    def place_end(block):
        return place(block)[0], place(block)[1] + wy - 1

    for base, value in (
        (0, chain_products(chains, 0, place, count_y, *up, False)),
        (4, chain_products(chains, 4, place_end, count_y, *down, True)),
    ):
        for k in range(4):
            coefs[base + k] = value[k]


def pair_kernel(own, received, total):
    total[...] = own[2:4] + received[2:4]


def third_kernel(partners, wy, weights_y, high, low, matrix, entering, *refs):
    messages, (solved, carried) = refs[:partners], refs[partners:]
    planes = carried.shape[1]
    received = [m[0:2] for m in messages]
    padding = entering.shape[0] // 3 - 2 * partners
    if padding:
        received.append(jnp.zeros((padding, received[0].shape[1]), jnp.float32))
    received = jnp.concatenate(received, axis=0)
    first = received.astype(jnp.bfloat16).astype(jnp.float32)
    received = jnp.concatenate([first, first, received - first], axis=0).T.astype(jnp.bfloat16)
    entered = entering[...].astype(jnp.bfloat16)
    parts = planes // 8
    total = planes * (wy + EXTRA)

    def solve(begin, size):
        rows = slice(begin, begin + size)
        left = jnp.concatenate([high[rows, :], high[rows, :], low[rows, :]], axis=1)
        return matmul(left, matrix[...]) + matmul(received[rows], entered)

    extra = solve(planes * wy, planes * EXTRA)
    solved[planes * wy : total, :] = extra
    for part in range(parts):
        core = solve(part * 8 * wy, 8 * wy)
        solved[part * 8 * wy : (part + 1) * 8 * wy, :] = core
        for number in range(4):
            lines = []
            for k in range(8):
                index = part * 8 + k
                value = jnp.sum(core[k * wy : (k + 1) * wy] * weights_y[number, 0:wy, :], axis=0, keepdims=True)
                past = extra[index * EXTRA : (index + 1) * EXTRA] * weights_y[number, wy : wy + EXTRA, :]
                lines.append(value + jnp.sum(past, axis=0, keepdims=True))
            carried[number, part * 8 : (part + 1) * 8, :] = jnp.concatenate(lines, axis=0)


def local_y_kernel(wy, solved, inverse_y, unused, out):
    planes = out.shape[0]
    first, second = halves(inverse_y[:, 0 : wy + EXTRA])
    left = jnp.concatenate([first, second, first], axis=1)

    def part(index, carry):
        for k in range(8):
            number = index * 8 + k
            start = pl.multiple_of(number * wy, 8)
            core = solved[pl.ds(start, wy), :]
            start = pl.multiple_of(planes * wy + number * EXTRA, 8)
            both = jnp.concatenate([core, solved[pl.ds(start, EXTRA), :]], axis=0)
            top, rest = halves(both)
            out[number] = matmul(left, jnp.concatenate([top, top, rest], axis=0))
        return carry

    lax.fori_loop(0, planes // 8, part, 0)


def combine(coefs, side, row, values):
    first = 0 if side == 0 else 2
    out = [None, None]
    for k, value in enumerate(values):
        for q in range(2):
            for p in range(2):
                term = coefs[side + 2 * p + q, row + k : row + k + 1, :] * value[first + p]
                out[q] = term if out[q] is None else out[q] + term
    return out


def stage_kernel(base, stride, radix, narrow, has_entered, coefs, *refs):
    values = refs[:radix]
    position = radix
    entered = None
    if has_entered:
        entered = refs[position]
        position += 1
    message, entering = refs[position : position + 2]
    below = combine(coefs, 0, base, values[1:])
    above = combine(coefs, 4, base, values[1:])
    for row, value in enumerate(below + above):
        entering[row] = value if entered is None else value + entered[row]
    upward = combine(coefs, 0, base + radix - 1, values)
    downward = combine(coefs, 4, base + radix - 1, values)
    if narrow:
        group = lax.axis_index("gy") // (stride * radix)
        sends_up = lax.rem(group, 2) == 0
        for row in range(2):
            message[row] = jnp.where(sends_up, upward[row], downward[row])
    else:
        for row, value in enumerate(upward + downward):
            message[row] = value


def last_kernel(base, radix, narrow, wy, coefs, local, inverse_y, entered, *refs):
    messages, (out_hbm, out, sent) = refs[: radix - 1], refs[radix - 1 :]
    values = list(messages)
    if narrow:
        values = [(m[0], m[1], m[0], m[1]) for m in values]
    below = combine(coefs, 0, base, values)
    above = combine(coefs, 4, base, values)
    st = [value + entered[row] for row, value in enumerate(below + above)]
    sides = [
        jnp.broadcast_to(inverse_y[:, c : c + 1], (wy, LANES)) for c in (0, 1, wy - 2, wy - 1)
    ]
    fields, planes_x = out.shape[:2]
    copies = []
    for field in range(fields):
        for x in range(planes_x):
            index = field * planes_x + x
            value = local[index]
            for number in range(4):
                value = value + sides[number] * st[number][index : index + 1]
            out[field, x] = value
        copy = pltpu.make_async_copy(out.at[field], out_hbm.at[field], sent.at[field])
        copy.start()
        copies.append(copy)
    for copy in copies:
        copy.wait()


VMEM = pl.BlockSpec(memory_space=pltpu.VMEM)
HBM = pl.BlockSpec(memory_space=pltpu.HBM)
SMEM = pl.BlockSpec(memory_space=pltpu.SMEM)
PARAMS = pltpu.CompilerParams(vmem_limit_bytes=40 * 1024 * 1024)


def array(*shape):
    return jax.ShapeDtypeStruct(shape, jnp.float32)


def in_hbm(x):
    return pltpu.with_memory_space_constraint(x, pltpu.HBM)


def cost(flops, data):
    return pl.CostEstimate(flops=flops, bytes_accessed=data, transcendentals=0)


def on_device(mesh, flow, speed, metric_y, metric_z):
    fields, planes_x, wy, wz = flow.shape
    count_y, count_z = mesh.shape["gy"], mesh.shape["gz"]
    assert wz == LANES
    ny, nz = metric_y.shape[0] // LANES, metric_z.shape[0] // LANES
    planes = fields * planes_x
    rows = planes * (wy + EXTRA)
    partners = count_z - 1
    paired = count_z == 4
    arrivals = 2 if paired else partners
    entering_rows = -(-2 * arrivals // 8) * 8
    half = jax.ShapeDtypeStruct((rows, 2 * LANES), jnp.bfloat16)
    outputs = pl.pallas_call(
        functools.partial(first_kernel, ny, nz, partners, paired),
        out_shape=[half, half, array(28, ny + nz, LANES), array(8, ny + nz, LANES)]
        + ([array(4, rows)] if paired else [array(2, rows)] * partners),
        in_specs=[HBM] * 4,
        out_specs=[VMEM] * (5 if paired else 4 + partners),
        scratch_shapes=[
            pltpu.VMEM(flow.shape, jnp.float32),
            pltpu.VMEM(speed.shape, jnp.float32),
            pltpu.VMEM((ny + nz, LANES), jnp.float32),
            pltpu.VMEM((2, 3, wy + 16, LANES), jnp.float32),
            pltpu.SemaphoreType.DMA((fields + 3,)),
        ],
        compiler_params=PARAMS,
        name="forcing_and_factor",
    )(*(in_hbm(x) for x in (flow, speed, metric_y.reshape(ny, LANES), metric_z.reshape(nz, LANES))))
    high, low, factors, chains = outputs[:4]

    def exchange(values, axis, count, stride, radix):
        received = []
        for k, value in zip(range(1, radix), values):
            pairs = [(i, i ^ (k * stride)) for i in range(count)]
            received.append(lax.ppermute(value, axis, pairs))
        return received

    if paired:
        near = exchange(outputs[4:], "gz", count_z, 1, 2)
        total = pl.pallas_call(
            pair_kernel,
            out_shape=array(2, rows),
            in_specs=[VMEM] * 2,
            out_specs=VMEM,
            compiler_params=PARAMS,
            name="join_pair",
        )(outputs[4], near[0])
        received = near + exchange([total], "gz", count_z, 2, 2)
    else:
        received = exchange(outputs[4:], "gz", count_z, 1, count_z)
    plan = stage_plan(count_y)
    work = [pltpu.VMEM((LANES + 16, LANES), jnp.float32)] * 2
    matrix, entering, weights_y = pl.pallas_call(
        functools.partial(second_kernel, ny, nz, count_z, wy, partners, paired),
        out_shape=[
            jax.ShapeDtypeStruct((6 * LANES, LANES), jnp.bfloat16),
            array(3 * entering_rows, LANES),
            array(4, wy + EXTRA, LANES),
        ],
        in_specs=[SMEM, VMEM],
        out_specs=[VMEM] * 3,
        scratch_shapes=work + [pltpu.VMEM((2 * LANES, LANES), jnp.float32)],
        compiler_params=PARAMS,
        cost_estimate=cost(2 * rows * 256 * 128 * 6, 4 * rows * 384),
        name="inverse_z",
    )(chains, factors)
    solved, carried = pl.pallas_call(
        functools.partial(third_kernel, arrivals, wy),
        out_shape=[array(rows, LANES), array(4, planes, LANES)],
        in_specs=[VMEM] * (5 + arrivals),
        out_specs=[VMEM] * 2,
        compiler_params=PARAMS,
        name="finish_z",
    )(weights_y, high, low, matrix, entering, *received)

    narrow = plan[-1][1] == 2 and len(plan) > 1
    base, entered, result = 0, None, None
    for number, (stride, radix) in enumerate(plan):
        received = exchange([carried] * (radix - 1), "gy", count_y, stride, radix)
        if number == 0:
            entries = sum(2 * radix - 1 for _, radix in plan[:-1]) + plan[-1][1] - 1
            inverse_y, coefs = pl.pallas_call(
                functools.partial(y_kernel, count_y, wy),
                out_shape=[array(wy, LANES), array(8, -(-entries // 8) * 8, LANES)],
                in_specs=[SMEM, VMEM, HBM],
                out_specs=[VMEM] * 2,
                scratch_shapes=work,
                compiler_params=PARAMS,
                cost_estimate=cost(2 * rows * 128 * 128 * 6, 4 * rows * 256),
                name="inverse_y",
            )(chains, factors, carried)
        if number + 1 < len(plan):
            slim = narrow and number + 2 == len(plan)
            inputs = [carried] + received + ([entered] if entered is not None else [])
            carried, entered = pl.pallas_call(
                functools.partial(stage_kernel, base, stride, radix, slim, entered is not None),
                out_shape=[array(2 if slim else 4, planes, LANES), array(4, planes, LANES)],
                in_specs=[VMEM] * (1 + len(inputs)),
                out_specs=[VMEM] * 2,
                compiler_params=PARAMS,
                name="join_groups",
            )(coefs, *inputs)
            base += 2 * radix - 1
            if number == 0:
                result = pl.pallas_call(
                    functools.partial(local_y_kernel, wy),
                    out_shape=array(planes, wy, LANES),
                    in_specs=[VMEM] * 2 + [HBM],
                    out_specs=VMEM,
                    compiler_params=PARAMS,
                    cost_estimate=cost(2 * rows * 128 * 128 * 6, 4 * rows * 256),
                    name="local_y",
                )(solved, inverse_y, entered)
        else:
            return pl.pallas_call(
                functools.partial(last_kernel, base, radix, narrow, wy),
                out_shape=array(fields, planes_x, wy, wz),
                in_specs=[VMEM] * (4 + len(received)),
                out_specs=HBM,
                scratch_shapes=[
                    pltpu.VMEM(flow.shape, jnp.float32),
                    pltpu.SemaphoreType.DMA((fields,)),
                ],
                compiler_params=PARAMS,
                name="finish_y",
            )(coefs, result, inverse_y, entered, *received)


def solution(mesh):
    placed = (P(None, None, "gy", "gz"), P(None, "gy", "gz"), P(), P())
    return jax.shard_map(
        functools.partial(on_device, mesh),
        mesh=mesh,
        in_specs=placed,
        out_specs=P(None, None, "gy", "gz"),
        check_vma=False,
    )
```

```python
import functools

import jax
import jax.numpy as jnp
from jax import lax
from jax.experimental import pallas as pl
from jax.experimental.pallas import tpu as pltpu
from jax.sharding import PartitionSpec as P

viscous = 0.25
explicit_fourth = 0.04
implicit_fourth = 0.05
time_step = 1048576.0
LANES = 128
EXTRA = 8


def mm(a, b):
    return (
        a[0] * b[0] + a[1] * b[2],
        a[0] * b[1] + a[1] * b[3],
        a[2] * b[0] + a[3] * b[2],
        a[2] * b[1] + a[3] * b[3],
    )


def inverse_of_one_minus(a):
    p, q, r, s = 1.0 - a[0], -a[1], -a[2], 1.0 - a[3]
    d = 1.0 / (p * s - q * r)
    return (s * d, -q * d, -r * d, p * d)


def pick(condition, a, b):
    return tuple(jnp.where(condition, x, y) for x, y in zip(a, b))


def halves(x):
    high = x.astype(jnp.bfloat16)
    return high, (x - high.astype(jnp.float32)).astype(jnp.bfloat16)


def matmul(a, b, dims=(((1,), (0,)), ((), ()))):
    return lax.dot_general(a, b, dims, preferred_element_type=jnp.float32)


def lane_roll(x, by):
    return pltpu.roll(x, by % LANES, 1)


def row_roll(x, by):
    by = by % x.shape[0]
    return jnp.concatenate([x[x.shape[0] - by :], x[: x.shape[0] - by]], axis=0)


class Factor:
    def __init__(self, metric, ny, nz, wy):
        self.ny, self.nz, self.wy, self.rows = ny, nz, wy, ny + nz
        self.lane = lax.broadcasted_iota(jnp.int32, (self.rows, LANES), 1)
        self.row = lax.broadcasted_iota(jnp.int32, (self.rows, LANES), 0)
        self.block = jnp.where(self.row < ny, self.row, self.row - ny)
        self.to_end = jnp.where(self.row < ny, ny, nz) - 1 - self.block
        first = (self.lane == 0) & (self.block == 0)
        last = (self.lane == LANES - 1) & (self.to_end == 0)
        self.face_low = 0.5 * (jnp.where(first, metric, self.before(metric, 1)) + metric)
        self.face_high = 0.5 * (metric + jnp.where(last, metric, self.after(metric, 1)))

    def before(self, x, by):
        rolled = lane_roll(x, by)
        value = jnp.where(self.lane < by, row_roll(rolled, 1), rolled)
        return jnp.where((self.lane < by) & (self.block == 0), 0.0, value)

    def after(self, x, by):
        rolled = lane_roll(x, -by)
        value = jnp.where(self.lane >= LANES - by, row_roll(rolled, -1), rolled)
        return jnp.where((self.lane >= LANES - by) & (self.to_end == 0), 0.0, value)

    def guess(self, sign):
        face = self.face_high if sign > 0 else self.face_low
        if sign > 0:
            cell = self.lane + LANES * self.block
        else:
            cell = LANES - 1 - self.lane + LANES * self.to_end
        near = face / (cell + 1).astype(jnp.float32)
        one_over = 1.0 / (face + jnp.sqrt(face + near * near))
        return face * one_over, implicit_fourth * one_over, one_over

    def sweep(self, sign, ratio, far):
        rows = self.rows
        back = self.before if sign > 0 else self.after
        if sign > 0:
            face_in, face_out, place = self.face_low, self.face_high, self.block
        else:
            face_in, face_out, place = self.face_high, self.face_low, self.to_end
        eps = 4.0 * implicit_fourth - implicit_fourth * back(ratio, 1)
        mass = (1.0 + 6.0 * implicit_fourth) - implicit_fourth * back(far, 2) - 2.0 * eps
        eps_in = back(eps, 1)
        scale = 1.0 / (face_in + 2.0 * eps_in)
        m = ((mass + face_in) * scale, mass - eps_in * eps_in * scale, scale, jnp.ones_like(scale))
        step = 1
        while step < LANES:
            inside = (self.lane >= step) if sign > 0 else (self.lane < LANES - step)
            m = pick(inside, mm(m, tuple(lane_roll(x, sign * step) for x in m)), m)
            step *= 2
        edge = LANES - 1 if sign > 0 else 0
        total = tuple(jnp.broadcast_to(x[:, edge : edge + 1], (rows, LANES)) for x in m)
        step = 1
        while step < max(self.ny, self.nz):
            total = pick(
                place >= step, mm(total, tuple(row_roll(x, sign * step) for x in total)), total
            )
            step *= 2
        top = jnp.where(place >= 1, row_roll(total[0], sign), 1.0)
        low = jnp.where(place >= 1, row_roll(total[2], sign), 0.0)
        eta = (m[0] * top + m[1] * low) / (m[2] * top + m[3] * low)
        one_over = 1.0 / (face_out + (eta + 2.0 * eps))
        return (face_out + eps) * one_over, implicit_fourth * one_over, one_over

    def finish(self, near_l, far_l, pivot_l, near_r, far_r):
        lane, block, to_end = self.lane, self.block, self.to_end
        even = (lane & 1) == 0
        near_l = jnp.where((to_end == 0) & (lane >= LANES - 1), 0.0, near_l)
        far_l = jnp.where((to_end == 0) & (lane >= LANES - 2), 0.0, far_l)
        near_r = jnp.where((block == 0) & (lane < 1), 0.0, near_r)
        far_r = jnp.where((block == 0) & (lane < 2), 0.0, far_r)

        def of_even(x):
            return jnp.where(even, x, lane_roll(x, 1))

        def of_odd(x):
            return jnp.where(even, lane_roll(x, -1), x)

        t0, t1, r0, r1 = of_even(near_l), of_odd(near_l), of_even(far_l), of_odd(far_l)
        from_right = (t0 * t1 - r0, -t0 * r1, t1, -r1)
        p1 = of_odd(pivot_l)
        left_inverse = (of_even(pivot_l) + t0 * t0 * p1, t0 * p1, t0 * p1, p1)
        s0, s1, q0, q1 = of_even(near_r), of_odd(near_r), of_even(far_r), of_odd(far_r)
        from_left = (-q0, s0, -s1 * q0, s1 * s0 - q1)
        from_left_after = tuple(self.after(x, 2) for x in from_left)
        from_right_before = tuple(self.before(x, 2) for x in from_right)
        diagonal = mm(inverse_of_one_minus(mm(from_right, from_left_after)), left_inverse)
        width = jnp.where(self.row < self.ny, self.wy, LANES)
        place = lane & (width - 1)
        right, left = from_right, from_left
        step = 2
        while step < LANES:
            right = pick(place + step < width, mm(right, tuple(lane_roll(x, -step) for x in right)), right)
            left = pick(place >= step, mm(left, tuple(lane_roll(x, step) for x in left)), left)
            step *= 2
        return from_right, from_left, diagonal, right, left, from_right_before, from_left_after


def cell_weights(chain, column, even):
    return jnp.where(even, chain[column], chain[2 + column])


def first_kernel(ny, nz, partners, paired, flow_hbm, speed_hbm, metric_y, metric_z, *refs):
    high, low, factors, chains = refs[:4]
    count = 1 if paired else partners
    messages = refs[4 : 4 + count]
    flow, speed, metric, spread, arrived = refs[4 + count :]
    fields, planes_x, wy, _ = flow.shape
    rows = ny + nz
    core_rows = fields * planes_x * wy

    copies = [
        pltpu.make_async_copy(metric_y, metric.at[0:ny], arrived.at[fields]),
        pltpu.make_async_copy(metric_z, metric.at[ny:rows], arrived.at[fields + 1]),
        pltpu.make_async_copy(speed_hbm, speed, arrived.at[fields + 2]),
    ]
    for copy in copies:
        copy.start()
    for field in range(fields):
        pltpu.make_async_copy(flow_hbm.at[field], flow.at[field], arrived.at[field]).start()

    lane = lax.broadcasted_iota(jnp.int32, (wy, LANES), 1)
    extra_row = lax.broadcasted_iota(jnp.int32, (EXTRA, LANES), 0)
    for slot in range(planes_x):
        for part in range(3):
            spread[slot, part, 0:8, :] = jnp.zeros((8, LANES), jnp.float32)
            spread[slot, part, wy + 8 : wy + 16, :] = jnp.zeros((8, LANES), jnp.float32)
    side = time_step * (viscous + 4.0 * explicit_fourth)
    half = time_step * 0.5
    centre = time_step * (-6.0 * viscous - 12.0 * explicit_fourth)
    fourth = -time_step * explicit_fourth

    def store(start, column, value):
        first, second = halves(value)
        high[pl.ds(start, value.shape[0]), column : column + LANES] = first
        low[pl.ds(start, value.shape[0]), column : column + LANES] = second

    def one_field(field):
        values = [flow[field, x] for x in range(planes_x)]
        fluxes = [half * (values[x] * speed[x]) for x in range(planes_x)]
        extras = []
        for x in range(planes_x):
            u, flux, slot = values[x], fluxes[x], x
            total = centre * u
            for other, sign in ((x + 1, -1), (x - 1, 1)):
                if 0 <= other < planes_x:
                    total = total + (time_step * viscous) * values[other]
                    total = total + fluxes[other] if sign > 0 else total - fluxes[other]
            scaled = side * u
            onward, backward, far = scaled + flux, scaled - flux, fourth * u
            spread[slot, 0, 8 : wy + 8, :] = onward
            spread[slot, 1, 8 : wy + 8, :] = backward
            spread[slot, 2, 8 : wy + 8, :] = far
            total = total + (spread[slot, 0, 7 : wy + 7, :] + spread[slot, 1, 9 : wy + 9, :])
            total = total + (spread[slot, 2, 6 : wy + 6, :] + spread[slot, 2, 10 : wy + 10, :])
            a, b = lane_roll(onward, 1), lane_roll(backward, -1)
            c, d = lane_roll(far, 2), lane_roll(far, -2)
            ends = jnp.where(lane < 2, c + jnp.where(lane < 1, a, 0.0), 0.0)
            ends = jnp.where(lane >= LANES - 2, d + jnp.where(lane >= LANES - 1, b, 0.0), ends)
            index = field * planes_x + x
            start = index * wy
            store(start, 0, total + ((a + b) + (c + d) - ends))
            store(start, LANES, ends)
            above = spread[slot, 1, 7:15, :] + spread[slot, 2, 8:16, :]
            below = spread[slot, 0, wy + 5 : wy + 13, :] + spread[slot, 2, wy + 4 : wy + 12, :]
            extras.append(jnp.where(extra_row < 2, above, jnp.where(extra_row < 4, below, 0.0)))
            if len(extras) == 2:
                start = core_rows + (index - 1) * EXTRA
                store(start, 0, jnp.concatenate(extras, axis=0))
                for ref in (high, low):
                    ref[pl.ds(start, 2 * EXTRA), LANES : 2 * LANES] = jnp.zeros(
                        (2 * EXTRA, LANES), jnp.bfloat16
                    )
                extras = []

    copies[0].wait()
    copies[1].wait()
    factor = Factor(metric[...], ny, nz, wy)

    guess_l, guess_r = factor.guess(1), factor.guess(-1)
    left, right = factor.sweep(1, *guess_l[:2]), factor.sweep(-1, *guess_r[:2])
    copies[2].wait()
    for field in range(fields):
        pltpu.make_async_copy(flow_hbm.at[field], flow.at[field], arrived.at[field]).wait()
    left, right = factor.sweep(1, *left[:2]), factor.sweep(-1, *right[:2])
    for field in range(fields // 2):
        one_field(field)
    parts = factor.finish(*left, *right[:2])
    from_right, from_left, diagonal, to_right, to_left, before, after = parts
    for number, value in enumerate(v for part in parts for v in part):
        factors[number] = value
    for number, value in enumerate(to_right + to_left):
        chains[number] = value
    for field in range(fields // 2, fields):
        one_field(field)

    me = lax.axis_index("gz")
    mine = lax.broadcasted_iota(jnp.int32, (rows, LANES), 0) == ny + me
    even = (lax.broadcasted_iota(jnp.int32, (1, LANES), 1) & 1) == 0
    lane = lax.broadcasted_iota(jnp.int32, (1, LANES), 1)

    def own(values):
        return tuple(jnp.sum(jnp.where(mine, v, 0.0), axis=0, keepdims=True) for v in values)

    up, down = own(to_right), own(to_left)
    up_past, down_past = own(mm(before, to_right)), own(mm(after, to_left))
    unit = (1.0, 0.0, 0.0, 1.0)
    weights = []
    for column in range(2):
        same = jnp.where(even, unit[column], unit[2 + column])
        inside_up = cell_weights(up, column, even)
        inside_down = cell_weights(down, column, even)
        past_up = lane_roll(cell_weights(up_past, column, even), -2)
        past_down = lane_roll(cell_weights(down_past, column, even), 2)
        ends_up = jnp.where(lane < 2, same, jnp.where(lane >= LANES - 2, past_up, 0.0))
        ends_down = jnp.where(lane < 2, past_down, jnp.where(lane >= LANES - 2, same, 0.0))
        weights.append(
            (
                jnp.concatenate([inside_up, ends_up], axis=1),
                jnp.concatenate([inside_down, ends_down], axis=1),
            )
        )
    if paired:
        lower = (me & 1) == 0
        stack = [jnp.where(lower, w[0], w[1]) for w in weights]
        peer = lax.broadcasted_iota(jnp.int32, (rows, LANES), 0) == ny + jnp.bitwise_xor(me, 1)

        def of_peer(values, place):
            chosen = tuple(jnp.sum(jnp.where(peer, v, 0.0), axis=0, keepdims=True) for v in values)
            return tuple(jnp.broadcast_to(v[:, place : place + 1], (1, 2 * LANES)) for v in chosen)

        over, under = of_peer(to_right, 0), of_peer(to_left, LANES - 1)
        (up0, down0), (up1, down1) = weights
        for q in range(2):
            upward = jnp.where(lower, over[q] * up0 + over[2 + q] * up1, weights[q][0])
            downward = jnp.where(lower, weights[q][1], under[q] * down0 + under[2 + q] * down1)
            stack.append(jnp.where(me < 2, upward, downward))
    else:
        stack = []
        for k in range(1, partners + 1):
            upward = jnp.bitwise_xor(me, k) > me
            stack += [jnp.where(upward, w[0], w[1]) for w in weights]
    while len(stack) % 8:
        stack.append(jnp.zeros((1, 2 * LANES), jnp.float32))
    count = len(stack)
    stack = jnp.concatenate(stack, axis=0)
    first = stack.astype(jnp.bfloat16).astype(jnp.float32)
    both = jnp.concatenate([first, stack - first], axis=0).astype(jnp.bfloat16)
    across = (((1,), (1,)), ((), ()))
    total = high.shape[0]
    size = planes_x * wy
    for begin in range(0, total, size):
        rows = slice(begin, min(begin + size, total))
        on_high = matmul(both, high[rows, :], across)
        on_low = matmul(both, low[rows, :], across)
        moments = (on_high[:count] + on_high[count:]) + on_low[:count]
        if paired:
            messages[0][:, rows] = moments[0:4]
        else:
            for k in range(partners):
                messages[k][:, rows] = moments[2 * k : 2 * k + 2]


def dense_inverse(columns, start, width, stack):
    parts = 8
    steps = width // (2 * parts)
    lane = lax.broadcasted_iota(jnp.int32, (parts, LANES), 1)
    part = lax.broadcasted_iota(jnp.int32, (parts, LANES), 0)
    fits = width + 4 <= LANES
    values = [columns[pl.ds(start + 2 * i, parts, stride=2 * steps), :] for i in range(steps)]

    def wide(i, number):
        return tuple(
            jnp.broadcast_to(values[i][:, number + k : number + k + 1], (parts, LANES)) for k in range(4)
        )

    blocks = [wide(i, 8) for i in range(steps)]
    zero, one = jnp.zeros((parts, LANES), jnp.float32), jnp.ones((parts, LANES), jnp.float32)

    def put(rows, i, extra, extra_lane, owner):
        first = 2 * (part * steps + i)
        out = []
        for r in range(2):
            row = jnp.where(lane == first, blocks[i][2 * r], rows[r])
            row = jnp.where(lane == first + 1, blocks[i][2 * r + 1], row)
            if extra is not None and fits:
                row = jnp.where((part == owner) & (lane == extra_lane), extra[2 * r], row)
                row = jnp.where((part == owner) & (lane == extra_lane + 1), extra[2 * r + 1], row)
            out.append(row)
        return tuple(out)

    def run(order, number, ends, extra_lane, owner):
        rows, product, out = (zero, zero), (one, zero, zero, one), {}
        for i in order:
            t = wide(i, number)
            rows = (t[0] * rows[0] + t[1] * rows[1], t[2] * rows[0] + t[3] * rows[1])
            extra = None
            if i == order[0]:
                e = wide(i, ends)
                extra = mm(blocks[i], (e[0], e[2], e[1], e[3]))
            rows = put(rows, i, extra, extra_lane, owner)
            product = mm(t, product)
            out[i] = rows, product
        rows, product = out[order[-1]]
        entering, last = [None] * parts, (jnp.zeros((1, LANES), jnp.float32),) * 2
        sequence = range(parts) if number == 4 else range(parts - 1, -1, -1)
        for p in sequence:
            entering[p] = last
            own, across = [r[p : p + 1] for r in rows], [x[p : p + 1] for x in product]
            last = (
                own[0] + across[0] * last[0] + across[1] * last[1],
                own[1] + across[2] * last[0] + across[3] * last[1],
            )
        entering = [jnp.concatenate([e[r] for e in entering], axis=0) for r in range(2)]
        result = []
        for i in range(steps):
            rows, product = out[i]
            for r in range(2):
                result.append(rows[r] + product[2 * r] * entering[0] + product[2 * r + 1] * entering[1])
        return result

    low = run(list(range(steps)), 4, 12, width, 0)
    high = run(list(range(steps - 1, -1, -1)), 0, 16, width + 2, parts - 1)
    for k in range(2 * steps):
        lower = lane <= 2 * (part * steps + k // 2) + 1
        if fits:
            lower = lower & (lane < width) | ((lane >= width) & (lane < width + 2))
        stack[parts * k : parts * (k + 1), :] = jnp.where(lower, low[k], high[k])
    rows = [stack[pl.ds(p, 2 * steps, stride=parts), :] for p in range(parts)]
    return jnp.concatenate(rows, axis=0)


def stage_plan(count):
    plan, stride = [], 1
    while stride < count:
        radix = 4 if count // stride >= 4 else 2
        plan.append((stride, radix))
        stride *= radix
    return plan


def transposed(factors, row):
    rows = [factors[number, pl.ds(row, 1), :] for number in range(12)]
    rows += [factors[20 + number, pl.ds(row, 1), :] for number in range(8)]
    rows += [factors[12 + number, pl.ds(row, 1), :] for number in range(8)]
    rows.append(jnp.zeros((4, LANES), jnp.float32))
    return jnp.concatenate(rows, axis=0).T


def chain_products(chains, number, place, blocks, begins, ends, masks, reverse):
    count = -(-len(begins) // 8) * 8
    row = lax.broadcasted_iota(jnp.int32, (count, LANES), 0)
    begin = jnp.zeros((count, LANES), jnp.int32)
    end, mask = begin, jnp.zeros((count, LANES), jnp.float32)
    for r, (b, e, m) in enumerate(zip(begins, ends, masks)):
        begin, end = jnp.where(row == r, b, begin), jnp.where(row == r, e, end)
        mask = jnp.where(row == r, m, mask)
    one, zero = jnp.ones((count, LANES), jnp.float32), jnp.zeros((count, LANES), jnp.float32)
    product = (one, zero, zero, one)
    for block in range(blocks - 1, -1, -1) if reverse else range(blocks):
        where = place(block)
        value = tuple(chains[number + k, where[0], where[1]] for k in range(4))
        product = pick((begin <= block) & (block < end), mm(product, value), product)
    return tuple(x * mask for x in product)


def truth(condition):
    return jnp.where(condition, 1.0, 0.0)


def inverse_z_kernel(ny, factors, matrix, columns, stacked, rows_ref):
    me_z = lax.axis_index("gz")
    columns[0:LANES, 0:32] = transposed(factors, ny + me_z)
    inverse = dense_inverse(columns, 0, LANES, stacked)
    rows_ref[0:LANES, :] = inverse
    rows_ref[LANES : 2 * LANES, :] = jnp.zeros((LANES, LANES), jnp.float32)
    past = tuple(columns[LANES - 1 : LANES, 16 + k : 17 + k] for k in range(4))
    ahead = tuple(columns[0:1, 12 + k : 13 + k] for k in range(4))
    head0, head1 = rows_ref[0:1, :], rows_ref[1:2, :]
    tail0, tail1 = rows_ref[LANES - 2 : LANES - 1, :], rows_ref[LANES - 1 : LANES, :]
    for q in range(2):
        rows_ref[LANES + q : LANES + q + 1, :] = past[2 * q] * tail0 + past[2 * q + 1] * tail1
        rows_ref[2 * LANES - 2 + q : 2 * LANES - 1 + q, :] = ahead[2 * q] * head0 + ahead[2 * q + 1] * head1
    first, second = halves(rows_ref[...])
    matrix[:, 0:LANES] = first
    matrix[:, LANES : 2 * LANES] = second


def whole_rows(matrix, row):
    start = row // 16 * 16
    both = matrix[start : start + 16, :].astype(jnp.float32)
    value = both[:, 0:LANES] + both[:, LANES : 2 * LANES]
    return value[row - start : row - start + 1]


def second_kernel(
    ny, nz, count_z, wy, partners, paired, chains, factors, matrix, high, low, local, moments, entering, spread_high, spread_low, *scratch
):
    columns, weights_y = scratch
    me_z, me_y = lax.axis_index("gz"), lax.axis_index("gy")
    planes = moments.shape[0] // 4
    head0, head1 = whole_rows(matrix, 0), whole_rows(matrix, 1)
    tail0, tail1 = whole_rows(matrix, LANES - 2), whole_rows(matrix, LANES - 1)

    if paired:
        pair = me_z // 2 * 2
        begins, ends = [me_z, pair], [me_z + 1, pair + 2]
        lowers = [me_z % 2 == 1, pair > 0]
    else:
        others = [jnp.bitwise_xor(me_z, k) for k in range(1, partners + 1)]
        begins, ends = [other + 1 for other in others], others
        lowers = [other < me_z for other in others]
    size = len(begins)
    up = chain_products(
        chains, 0, lambda b: (ny + b, 0), count_z, begins, [me_z] * size, [1.0] * size, False
    )
    down = chain_products(
        chains, 4, lambda b: (ny + b, LANES - 1), count_z, [me_z + 1] * size, ends, [1.0] * size, True
    )
    stack = []
    for k, lower in enumerate(lowers):
        for p in range(2):
            from_low = up[2 * p][k : k + 1] * head0 + up[2 * p + 1][k : k + 1] * head1
            from_high = down[2 * p][k : k + 1] * tail0 + down[2 * p + 1][k : k + 1] * tail1
            stack.append(jnp.where(lower, from_low, from_high))
    while len(stack) % 8:
        stack.append(jnp.zeros((1, LANES), jnp.float32))
    stack = jnp.concatenate(stack, axis=0)
    first = stack.astype(jnp.bfloat16).astype(jnp.float32)
    entering[...] = jnp.concatenate([first, stack - first, first], axis=0)

    cell = me_y * wy
    columns[0:LANES, 0:32] = transposed(factors, cell // LANES)
    start = lax.rem(cell, LANES)
    row = lax.broadcasted_iota(jnp.int32, (wy, LANES), 0)
    extra_row = lax.broadcasted_iota(jnp.int32, (EXTRA, LANES), 0)
    unit = (1.0, 0.0, 0.0, 1.0)

    def head(number):
        return tuple(columns[pl.ds(start, 1), number + k : number + k + 1] for k in range(4))

    def tail(number):
        return tuple(columns[pl.ds(start + wy - 1, 1), number + k : number + k + 1] for k in range(4))

    past_up, past_down = mm(head(12), head(20)), mm(tail(16), tail(24))
    for column in range(2):
        for output, number in ((column, 20), (2 + column, 24)):
            even = columns[pl.ds(start, wy), number + column : number + column + 1]
            odd = columns[pl.ds(start, wy), number + 2 + column : number + 3 + column]
            weights_y[output, 0:wy, :] = jnp.where((row & 1) == 0, even, odd)
        for output, early, late in (
            (column, (past_up[column], past_up[2 + column]), (unit[column], unit[2 + column])),
            (2 + column, (unit[column], unit[2 + column]), (past_down[column], past_down[2 + column])),
        ):
            value = jnp.zeros((EXTRA, LANES), jnp.float32)
            for r, v in enumerate(early + late):
                value = jnp.where(extra_row == r, v, value)
            weights_y[output, wy : wy + EXTRA, :] = value

    total = planes * (wy + EXTRA)

    def solve(begin, size):
        rows = slice(begin, begin + size)
        both = matmul(high[rows, :], matrix[...])
        value = both[:, 0:LANES] + (both[:, LANES : 2 * LANES] + matmul(low[rows, :], matrix[:, 0:LANES]))
        local[rows, :] = value
        return value

    extra = solve(planes * wy, planes * EXTRA)
    for part in range(planes // 8):
        core = solve(part * 8 * wy, 8 * wy)
        for number in range(4):
            lines = []
            for k in range(8):
                index = part * 8 + k
                value = jnp.sum(core[k * wy : (k + 1) * wy] * weights_y[number, 0:wy, :], axis=0, keepdims=True)
                past = extra[index * EXTRA : (index + 1) * EXTRA] * weights_y[number, wy : wy + EXTRA, :]
                lines.append(value + jnp.sum(past, axis=0, keepdims=True))
            start = number * planes + part * 8
            moments[start : start + 8, :] = jnp.concatenate(lines, axis=0)

    row = cell // LANES
    lane = lax.broadcasted_iota(jnp.int32, (1, LANES), 1)
    even = (lane & 1) == 0

    def chain(number):
        return tuple(factors[number + k, pl.ds(row, 1), :] for k in range(4))

    def turned(x, by):
        return pltpu.roll(x, lax.rem(by + 2 * LANES, LANES), 1)

    def tiled(x, period):
        x = jnp.where(lane < period, x, 0.0)
        while period < LANES:
            x = x + lane_roll(x, period)
            period *= 2
        return x

    up, down, before, after = chain(12), chain(16), chain(20), chain(24)
    past_up, past_down = mm(before, up), mm(after, down)
    plane_row = lax.broadcasted_iota(jnp.int32, (planes, LANES), 0)
    wide_lane = lax.broadcasted_iota(jnp.int32, (planes, LANES), 1)
    for column in range(2):
        same = jnp.where(even, unit[column], unit[2 + column])
        for number, inside, early, late in (
            (column, up, turned(cell_weights(past_up, column, even), -start_y(cell)), same),
            (
                2 + column,
                down,
                same,
                turned(cell_weights(past_down, column, even), 4 - wy - start_y(cell)),
            ),
        ):
            inside = tiled(turned(cell_weights(inside, column, even), -start_y(cell)), wy)
            past = jnp.where(lane < 2, early, jnp.where(lane < 4, late, 0.0))
            past = tiled(past, EXTRA)
            rows = slice(number * planes, (number + 1) * planes)
            for begin in range(0, total, LANES):
                if begin < planes * wy:
                    owner, value = (begin + wide_lane) // wy, inside
                else:
                    owner, value = (begin - planes * wy + wide_lane) // EXTRA, past
                size = min(LANES, total - begin)
                first, second = halves(jnp.where(plane_row == owner, value, 0.0))
                spread_high[rows, begin : begin + size] = first[:, 0:size]
                spread_low[rows, begin : begin + size] = second[:, 0:size]


def start_y(cell):
    return lax.rem(cell, LANES)


def y_kernel(count_y, wy, chains, factors, unused, inverse_y, coefs, columns, stacked):
    me_y = lax.axis_index("gy")
    cell = me_y * wy
    columns[0:LANES, 0:32] = transposed(factors, cell // LANES)
    start = lax.rem(cell, LANES)
    inverse_y[...] = dense_inverse(columns, start, wy, stacked)

    up, down = ([], [], []), ([], [], [])
    plan = stage_plan(count_y)
    for number, (stride, radix) in enumerate(plan):
        group = me_y // stride
        first = (group // radix) * radix
        others = [first + jnp.bitwise_xor(group - first, k) for k in range(radix)]
        for other in others[1:]:
            for lists, values in (
                (up, ((other + 1) * stride, me_y, truth(other < group))),
                (down, (me_y + 1, other * stride, truth(other > group))),
            ):
                for one, value in zip(lists, values):
                    one.append(value)
        if number + 1 < len(plan):
            for other in others:
                for lists, values in (
                    (up, ((other + 1) * stride, (first + radix) * stride, 1.0)),
                    (down, (first * stride, other * stride, 1.0)),
                ):
                    for one, value in zip(lists, values):
                        one.append(value)

    def place(block):
        return block * wy // LANES, block * wy % LANES

    def place_end(block):
        return place(block)[0], place(block)[1] + wy - 1

    for base, value in (
        (0, chain_products(chains, 0, place, count_y, *up, False)),
        (4, chain_products(chains, 4, place_end, count_y, *down, True)),
    ):
        for k in range(4):
            coefs[base + k] = value[k]


def pair_kernel(own, received, unused, total):
    total[...] = own[2:4] + received[2:4]


def arrived_rows(messages, count):
    rows = [m[0:2] for m in messages]
    if count > 2 * len(messages):
        rows.append(jnp.zeros((count - 2 * len(messages), rows[0].shape[1]), jnp.float32))
    return jnp.concatenate(rows, axis=0)


def third_kernel(moments, spread_high, spread_low, entering, *refs):
    messages, carried = refs[:-1], refs[-1]
    count = entering.shape[0] // 3
    received = arrived_rows(messages, count)
    first = received.astype(jnp.bfloat16).astype(jnp.float32)
    both = jnp.concatenate([first, received - first], axis=0).astype(jnp.bfloat16)
    top = jnp.concatenate([first, jnp.zeros_like(first)], axis=0).astype(jnp.bfloat16)
    across = (((1,), (1,)), ((), ()))
    corner = matmul(spread_high[...], both, across) + matmul(spread_low[...], top, across)
    values = entering[0:count, :] + entering[count : 2 * count, :]
    added = lax.dot_general(
        corner,
        jnp.concatenate([values, values], axis=0),
        (((1,), (0,)), ((), ())),
        precision=lax.Precision.HIGHEST,
        preferred_element_type=jnp.float32,
    )
    planes = carried.shape[1]
    for number in range(4):
        rows = slice(number * planes, (number + 1) * planes)
        carried[number] = moments[rows, :] + added[rows]


def local_y_kernel(wy, local, entering, inverse_y, unused, *refs):
    messages, (out, solved) = refs[:-2], refs[-2:]
    planes = out.shape[0]
    count = entering.shape[0] // 3
    received = arrived_rows(messages, count)
    first = received.astype(jnp.bfloat16).astype(jnp.float32)
    received = jnp.concatenate([first, first, received - first], axis=0).T.astype(jnp.bfloat16)
    solved[...] = local[...] + matmul(received, entering[...].astype(jnp.bfloat16))
    first, second = halves(inverse_y[:, 0 : wy + EXTRA])
    left = jnp.concatenate([first, second, first], axis=1)

    def part(index, carry):
        for k in range(8):
            number = index * 8 + k
            start = pl.multiple_of(number * wy, 8)
            core = solved[pl.ds(start, wy), :]
            start = pl.multiple_of(planes * wy + number * EXTRA, 8)
            both = jnp.concatenate([core, solved[pl.ds(start, EXTRA), :]], axis=0)
            top, rest = halves(both)
            out[number] = matmul(left, jnp.concatenate([top, top, rest], axis=0))
        return carry

    lax.fori_loop(0, planes // 8, part, 0)


def combine(coefs, side, row, values):
    first = 0 if side == 0 else 2
    out = [None, None]
    for k, value in enumerate(values):
        for q in range(2):
            for p in range(2):
                term = coefs[side + 2 * p + q, row + k : row + k + 1, :] * value[first + p]
                out[q] = term if out[q] is None else out[q] + term
    return out


def stage_kernel(base, stride, radix, narrow, has_entered, coefs, *refs):
    values = refs[:radix]
    position = radix
    entered = None
    if has_entered:
        entered = refs[position]
        position += 1
    message, entering = refs[position : position + 2]
    below = combine(coefs, 0, base, values[1:])
    above = combine(coefs, 4, base, values[1:])
    for row, value in enumerate(below + above):
        entering[row] = value if entered is None else value + entered[row]
    upward = combine(coefs, 0, base + radix - 1, values)
    downward = combine(coefs, 4, base + radix - 1, values)
    if narrow:
        group = lax.axis_index("gy") // (stride * radix)
        sends_up = lax.rem(group, 2) == 0
        for row in range(2):
            message[row] = jnp.where(sends_up, upward[row], downward[row])
    else:
        for row, value in enumerate(upward + downward):
            message[row] = value


def last_kernel(base, radix, narrow, wy, coefs, local, inverse_y, entered, *refs):
    messages, (out_hbm, out, sent) = refs[: radix - 1], refs[radix - 1 :]
    values = list(messages)
    if narrow:
        values = [(m[0], m[1], m[0], m[1]) for m in values]
    below = combine(coefs, 0, base, values)
    above = combine(coefs, 4, base, values)
    st = [value + entered[row] for row, value in enumerate(below + above)]
    sides = [
        jnp.broadcast_to(inverse_y[:, c : c + 1], (wy, LANES)) for c in (0, 1, wy - 2, wy - 1)
    ]
    fields, planes_x = out.shape[:2]
    copies = []
    for field in range(fields):
        for x in range(planes_x):
            index = field * planes_x + x
            value = local[index]
            for number in range(4):
                value = value + sides[number] * st[number][index : index + 1]
            out[field, x] = value
            if (x + 1) % 4 == 0:
                part = (field, pl.ds(x - 3, 4))
                copy = pltpu.make_async_copy(out.at[part], out_hbm.at[part], sent.at[len(copies)])
                copy.start()
                copies.append(copy)
    for copy in copies:
        copy.wait()


VMEM = pl.BlockSpec(memory_space=pltpu.VMEM)
HBM = pl.BlockSpec(memory_space=pltpu.HBM)
SMEM = pl.BlockSpec(memory_space=pltpu.SMEM)
PARAMS = pltpu.CompilerParams(vmem_limit_bytes=40 * 1024 * 1024)


def array(*shape):
    return jax.ShapeDtypeStruct(shape, jnp.float32)


def in_hbm(x):
    return pltpu.with_memory_space_constraint(x, pltpu.HBM)


def cost(flops, data):
    return pl.CostEstimate(flops=flops, bytes_accessed=data, transcendentals=0)


def on_device(mesh, flow, speed, metric_y, metric_z):
    fields, planes_x, wy, wz = flow.shape
    count_y, count_z = mesh.shape["gy"], mesh.shape["gz"]
    assert wz == LANES
    ny, nz = metric_y.shape[0] // LANES, metric_z.shape[0] // LANES
    planes = fields * planes_x
    rows = planes * (wy + EXTRA)
    partners = count_z - 1
    paired = count_z == 4
    arrivals = 2 if paired else partners
    entering_rows = -(-2 * arrivals // 8) * 8
    half = jax.ShapeDtypeStruct((rows, 2 * LANES), jnp.bfloat16)
    outputs = pl.pallas_call(
        functools.partial(first_kernel, ny, nz, partners, paired),
        out_shape=[half, half, array(28, ny + nz, LANES), array(8, ny + nz, LANES)]
        + ([array(4, rows)] if paired else [array(2, rows)] * partners),
        in_specs=[HBM] * 4,
        out_specs=[VMEM] * (5 if paired else 4 + partners),
        scratch_shapes=[
            pltpu.VMEM(flow.shape, jnp.float32),
            pltpu.VMEM(speed.shape, jnp.float32),
            pltpu.VMEM((ny + nz, LANES), jnp.float32),
            pltpu.VMEM((planes_x, 3, wy + 16, LANES), jnp.float32),
            pltpu.SemaphoreType.DMA((fields + 3,)),
        ],
        compiler_params=PARAMS,
        name="forcing_and_factor",
    )(*(in_hbm(x) for x in (flow, speed, metric_y.reshape(ny, LANES), metric_z.reshape(nz, LANES))))
    high, low, factors, chains = outputs[:4]

    def exchange(values, axis, count, stride, radix):
        received = []
        for k, value in zip(range(1, radix), values):
            pairs = [(i, i ^ (k * stride)) for i in range(count)]
            received.append(lax.ppermute(value, axis, pairs))
        return received

    plan = stage_plan(count_y)
    work = [pltpu.VMEM((LANES + 16, LANES), jnp.float32)] * 2
    matrix = pl.pallas_call(
        functools.partial(inverse_z_kernel, ny),
        out_shape=jax.ShapeDtypeStruct((2 * LANES, 2 * LANES), jnp.bfloat16),
        in_specs=[VMEM],
        out_specs=VMEM,
        scratch_shapes=work + [pltpu.VMEM((2 * LANES, LANES), jnp.float32)],
        compiler_params=PARAMS,
        cost_estimate=cost(rows * 1024, 4 * rows * 64),
        name="inverse_z",
    )(factors)
    if paired:
        near = exchange(outputs[4:], "gz", count_z, 1, 2)
        total = pl.pallas_call(
            pair_kernel,
            out_shape=array(2, rows),
            in_specs=[VMEM] * 2 + [HBM],
            out_specs=VMEM,
            compiler_params=PARAMS,
            name="join_pair",
        )(outputs[4], near[0], matrix)
        received = near + exchange([total], "gz", count_z, 2, 2)
    else:
        received = exchange(outputs[4:], "gz", count_z, 1, count_z)
    spread = jax.ShapeDtypeStruct((4 * planes, rows), jnp.bfloat16)
    local, moments, entering, spread_high, spread_low = pl.pallas_call(
        functools.partial(second_kernel, ny, nz, count_z, wy, partners, paired),
        out_shape=[
            array(rows, LANES),
            array(4 * planes, LANES),
            array(3 * entering_rows, LANES),
            spread,
            spread,
        ],
        in_specs=[SMEM] + [VMEM] * 4,
        out_specs=[VMEM] * 5,
        scratch_shapes=[
            pltpu.VMEM((LANES + 16, LANES), jnp.float32),
            pltpu.VMEM((4, wy + EXTRA, LANES), jnp.float32),
        ],
        compiler_params=PARAMS,
        cost_estimate=cost(2 * rows * 256 * 128 * 6, 4 * rows * 384),
        name="local_z",
    )(chains, factors, matrix, high, low)
    carried = pl.pallas_call(
        third_kernel,
        out_shape=array(4, planes, LANES),
        in_specs=[VMEM] * (4 + arrivals),
        out_specs=VMEM,
        compiler_params=PARAMS,
        name="carried_y",
    )(moments, spread_high, spread_low, entering, *received)
    arrived = received

    narrow = plan[-1][1] == 2 and len(plan) > 1
    base, entered, result = 0, None, None
    for number, (stride, radix) in enumerate(plan):
        received = exchange([carried] * (radix - 1), "gy", count_y, stride, radix)
        if number == 0:
            entries = sum(2 * radix - 1 for _, radix in plan[:-1]) + plan[-1][1] - 1
            inverse_y, coefs = pl.pallas_call(
                functools.partial(y_kernel, count_y, wy),
                out_shape=[array(wy, LANES), array(8, -(-entries // 8) * 8, LANES)],
                in_specs=[SMEM, VMEM, HBM],
                out_specs=[VMEM] * 2,
                scratch_shapes=work,
                compiler_params=PARAMS,
                cost_estimate=cost(2 * rows * 128 * 128 * 6, 4 * rows * 256),
                name="inverse_y",
            )(chains, factors, carried)
        if number + 1 < len(plan):
            slim = narrow and number + 2 == len(plan)
            inputs = [carried] + received + ([entered] if entered is not None else [])
            carried, entered = pl.pallas_call(
                functools.partial(stage_kernel, base, stride, radix, slim, entered is not None),
                out_shape=[array(2 if slim else 4, planes, LANES), array(4, planes, LANES)],
                in_specs=[VMEM] * (1 + len(inputs)),
                out_specs=[VMEM] * 2,
                compiler_params=PARAMS,
                name="join_groups",
            )(coefs, *inputs)
            base += 2 * radix - 1
            if number == 0:
                result = pl.pallas_call(
                    functools.partial(local_y_kernel, wy),
                    out_shape=array(planes, wy, LANES),
                    in_specs=[VMEM] * 3 + [HBM] + [VMEM] * arrivals,
                    out_specs=VMEM,
                    scratch_shapes=[pltpu.VMEM((rows, LANES), jnp.float32)],
                    compiler_params=PARAMS,
                    cost_estimate=cost(2 * rows * 128 * 128 * 6, 4 * rows * 256),
                    name="local_y",
                )(local, entering, inverse_y, entered, *arrived)
        else:
            return pl.pallas_call(
                functools.partial(last_kernel, base, radix, narrow, wy),
                out_shape=array(fields, planes_x, wy, wz),
                in_specs=[VMEM] * (4 + len(received)),
                out_specs=HBM,
                scratch_shapes=[
                    pltpu.VMEM(flow.shape, jnp.float32),
                    pltpu.SemaphoreType.DMA((planes // 4,)),
                ],
                compiler_params=PARAMS,
                name="finish_y",
            )(coefs, result, inverse_y, entered, *received)


def solution(mesh):
    placed = (P(None, None, "gy", "gz"), P(None, "gy", "gz"), P(), P())
    return jax.shard_map(
        functools.partial(on_device, mesh),
        mesh=mesh,
        in_specs=placed,
        out_specs=P(None, None, "gy", "gz"),
        check_vma=False,
    )
```

```python
import functools

import jax
import jax.numpy as jnp
from jax import lax
from jax.experimental import pallas as pl
from jax.experimental.pallas import tpu as pltpu
from jax.sharding import PartitionSpec as P

viscous = 0.25
explicit_fourth = 0.04
implicit_fourth = 0.05
time_step = 1048576.0
LANES = 128
EXTRA = 8


def mm(a, b):
    return (
        a[0] * b[0] + a[1] * b[2],
        a[0] * b[1] + a[1] * b[3],
        a[2] * b[0] + a[3] * b[2],
        a[2] * b[1] + a[3] * b[3],
    )


def inverse_of_one_minus(a):
    p, q, r, s = 1.0 - a[0], -a[1], -a[2], 1.0 - a[3]
    d = 1.0 / (p * s - q * r)
    return (s * d, -q * d, -r * d, p * d)


def pick(condition, a, b):
    return tuple(jnp.where(condition, x, y) for x, y in zip(a, b))


def halves(x):
    high = x.astype(jnp.bfloat16)
    return high, (x - high.astype(jnp.float32)).astype(jnp.bfloat16)


def matmul(a, b, dims=(((1,), (0,)), ((), ()))):
    return lax.dot_general(a, b, dims, preferred_element_type=jnp.float32)


def lane_roll(x, by):
    return pltpu.roll(x, by % LANES, 1)


def row_roll(x, by):
    by = by % x.shape[0]
    return jnp.concatenate([x[x.shape[0] - by :], x[: x.shape[0] - by]], axis=0)


class Factor:
    def __init__(self, metric, ny, nz, wy):
        self.ny, self.nz, self.wy, self.rows = ny, nz, wy, ny + nz
        self.lane = lax.broadcasted_iota(jnp.int32, (self.rows, LANES), 1)
        self.row = lax.broadcasted_iota(jnp.int32, (self.rows, LANES), 0)
        self.block = jnp.where(self.row < ny, self.row, self.row - ny)
        self.to_end = jnp.where(self.row < ny, ny, nz) - 1 - self.block
        first = (self.lane == 0) & (self.block == 0)
        last = (self.lane == LANES - 1) & (self.to_end == 0)
        self.face_low = 0.5 * (jnp.where(first, metric, self.before(metric, 1)) + metric)
        self.face_high = 0.5 * (metric + jnp.where(last, metric, self.after(metric, 1)))

    def before(self, x, by):
        rolled = lane_roll(x, by)
        value = jnp.where(self.lane < by, row_roll(rolled, 1), rolled)
        return jnp.where((self.lane < by) & (self.block == 0), 0.0, value)

    def after(self, x, by):
        rolled = lane_roll(x, -by)
        value = jnp.where(self.lane >= LANES - by, row_roll(rolled, -1), rolled)
        return jnp.where((self.lane >= LANES - by) & (self.to_end == 0), 0.0, value)

    def guess(self, sign):
        face = self.face_high if sign > 0 else self.face_low
        if sign > 0:
            cell = self.lane + LANES * self.block
        else:
            cell = LANES - 1 - self.lane + LANES * self.to_end
        near = face / (cell + 1).astype(jnp.float32)
        one_over = 1.0 / (face + jnp.sqrt(face + near * near))
        return face * one_over, implicit_fourth * one_over, one_over

    def sweep(self, sign, ratio, far):
        rows = self.rows
        back = self.before if sign > 0 else self.after
        if sign > 0:
            face_in, face_out, place = self.face_low, self.face_high, self.block
        else:
            face_in, face_out, place = self.face_high, self.face_low, self.to_end
        eps = 4.0 * implicit_fourth - implicit_fourth * back(ratio, 1)
        mass = (1.0 + 6.0 * implicit_fourth) - implicit_fourth * back(far, 2) - 2.0 * eps
        eps_in = back(eps, 1)
        scale = 1.0 / (face_in + 2.0 * eps_in)
        m = ((mass + face_in) * scale, mass - eps_in * eps_in * scale, scale, jnp.ones_like(scale))
        step = 1
        while step < LANES:
            inside = (self.lane >= step) if sign > 0 else (self.lane < LANES - step)
            m = pick(inside, mm(m, tuple(lane_roll(x, sign * step) for x in m)), m)
            step *= 2
        edge = LANES - 1 if sign > 0 else 0
        total = tuple(jnp.broadcast_to(x[:, edge : edge + 1], (rows, LANES)) for x in m)
        step = 1
        while step < max(self.ny, self.nz):
            total = pick(
                place >= step, mm(total, tuple(row_roll(x, sign * step) for x in total)), total
            )
            step *= 2
        top = jnp.where(place >= 1, row_roll(total[0], sign), 1.0)
        low = jnp.where(place >= 1, row_roll(total[2], sign), 0.0)
        eta = (m[0] * top + m[1] * low) / (m[2] * top + m[3] * low)
        one_over = 1.0 / (face_out + (eta + 2.0 * eps))
        return (face_out + eps) * one_over, implicit_fourth * one_over, one_over

    def finish(self, near_l, far_l, pivot_l, near_r, far_r):
        lane, block, to_end = self.lane, self.block, self.to_end
        even = (lane & 1) == 0
        near_l = jnp.where((to_end == 0) & (lane >= LANES - 1), 0.0, near_l)
        far_l = jnp.where((to_end == 0) & (lane >= LANES - 2), 0.0, far_l)
        near_r = jnp.where((block == 0) & (lane < 1), 0.0, near_r)
        far_r = jnp.where((block == 0) & (lane < 2), 0.0, far_r)

        def of_even(x):
            return jnp.where(even, x, lane_roll(x, 1))

        def of_odd(x):
            return jnp.where(even, lane_roll(x, -1), x)

        t0, t1, r0, r1 = of_even(near_l), of_odd(near_l), of_even(far_l), of_odd(far_l)
        from_right = (t0 * t1 - r0, -t0 * r1, t1, -r1)
        p1 = of_odd(pivot_l)
        left_inverse = (of_even(pivot_l) + t0 * t0 * p1, t0 * p1, t0 * p1, p1)
        s0, s1, q0, q1 = of_even(near_r), of_odd(near_r), of_even(far_r), of_odd(far_r)
        from_left = (-q0, s0, -s1 * q0, s1 * s0 - q1)
        from_left_after = tuple(self.after(x, 2) for x in from_left)
        from_right_before = tuple(self.before(x, 2) for x in from_right)
        diagonal = mm(inverse_of_one_minus(mm(from_right, from_left_after)), left_inverse)
        width = jnp.where(self.row < self.ny, self.wy, LANES)
        place = lane & (width - 1)
        right, left = from_right, from_left
        step = 2
        while step < LANES:
            right = pick(place + step < width, mm(right, tuple(lane_roll(x, -step) for x in right)), right)
            left = pick(place >= step, mm(left, tuple(lane_roll(x, step) for x in left)), left)
            step *= 2
        return from_right, from_left, diagonal, right, left, from_right_before, from_left_after


def cell_weights(chain, column, even):
    return jnp.where(even, chain[column], chain[2 + column])


def first_kernel(ny, nz, partners, paired, flow_hbm, speed_hbm, metric_y, metric_z, *refs):
    high, low, factors, chains = refs[:4]
    count = 1 if paired else partners
    messages = refs[4 : 4 + count]
    flow, speed, metric, spread, arrived = refs[4 + count :]
    fields, planes_x, wy, _ = flow.shape
    rows = ny + nz
    core_rows = fields * planes_x * wy

    copies = [
        pltpu.make_async_copy(metric_y, metric.at[0:ny], arrived.at[fields]),
        pltpu.make_async_copy(metric_z, metric.at[ny:rows], arrived.at[fields + 1]),
        pltpu.make_async_copy(speed_hbm, speed, arrived.at[fields + 2]),
    ]
    for copy in copies:
        copy.start()
    for field in range(fields):
        pltpu.make_async_copy(flow_hbm.at[field], flow.at[field], arrived.at[field]).start()

    lane = lax.broadcasted_iota(jnp.int32, (wy, LANES), 1)
    extra_row = lax.broadcasted_iota(jnp.int32, (EXTRA, LANES), 0)
    for slot in range(planes_x):
        for part in range(3):
            spread[slot, part, 0:8, :] = jnp.zeros((8, LANES), jnp.float32)
            spread[slot, part, wy + 8 : wy + 16, :] = jnp.zeros((8, LANES), jnp.float32)
    side = time_step * (viscous + 4.0 * explicit_fourth)
    half = time_step * 0.5
    centre = time_step * (-6.0 * viscous - 12.0 * explicit_fourth)
    fourth = -time_step * explicit_fourth

    def store(start, column, value):
        first, second = halves(value)
        high[pl.ds(start, value.shape[0]), column : column + LANES] = first
        low[pl.ds(start, value.shape[0]), column : column + LANES] = second

    def one_field(field):
        values = [flow[field, x] for x in range(planes_x)]
        fluxes = [half * (values[x] * speed[x]) for x in range(planes_x)]
        extras = []
        for x in range(planes_x):
            u, flux, slot = values[x], fluxes[x], x
            total = centre * u
            for other, sign in ((x + 1, -1), (x - 1, 1)):
                if 0 <= other < planes_x:
                    total = total + (time_step * viscous) * values[other]
                    total = total + fluxes[other] if sign > 0 else total - fluxes[other]
            scaled = side * u
            onward, backward, far = scaled + flux, scaled - flux, fourth * u
            spread[slot, 0, 8 : wy + 8, :] = onward
            spread[slot, 1, 8 : wy + 8, :] = backward
            spread[slot, 2, 8 : wy + 8, :] = far
            total = total + (spread[slot, 0, 7 : wy + 7, :] + spread[slot, 1, 9 : wy + 9, :])
            total = total + (spread[slot, 2, 6 : wy + 6, :] + spread[slot, 2, 10 : wy + 10, :])
            a, b = lane_roll(onward, 1), lane_roll(backward, -1)
            c, d = lane_roll(far, 2), lane_roll(far, -2)
            ends = jnp.where(lane < 2, c + jnp.where(lane < 1, a, 0.0), 0.0)
            ends = jnp.where(lane >= LANES - 2, d + jnp.where(lane >= LANES - 1, b, 0.0), ends)
            index = field * planes_x + x
            start = index * wy
            store(start, 0, total + ((a + b) + (c + d) - ends))
            store(start, LANES, ends)
            above = spread[slot, 1, 7:15, :] + spread[slot, 2, 8:16, :]
            below = spread[slot, 0, wy + 5 : wy + 13, :] + spread[slot, 2, wy + 4 : wy + 12, :]
            extras.append(jnp.where(extra_row < 2, above, jnp.where(extra_row < 4, below, 0.0)))
            if len(extras) == 2:
                start = core_rows + (index - 1) * EXTRA
                store(start, 0, jnp.concatenate(extras, axis=0))
                for ref in (high, low):
                    ref[pl.ds(start, 2 * EXTRA), LANES : 2 * LANES] = jnp.zeros(
                        (2 * EXTRA, LANES), jnp.bfloat16
                    )
                extras = []

    copies[0].wait()
    copies[1].wait()
    factor = Factor(metric[...], ny, nz, wy)

    guess_l, guess_r = factor.guess(1), factor.guess(-1)
    left, right = factor.sweep(1, *guess_l[:2]), factor.sweep(-1, *guess_r[:2])
    copies[2].wait()
    for field in range(fields):
        pltpu.make_async_copy(flow_hbm.at[field], flow.at[field], arrived.at[field]).wait()
    left, right = factor.sweep(1, *left[:2]), factor.sweep(-1, *right[:2])
    for field in range(fields // 2):
        one_field(field)
    parts = factor.finish(*left, *right[:2])
    from_right, from_left, diagonal, to_right, to_left, before, after = parts
    for number, value in enumerate(v for part in parts for v in part):
        factors[number] = value
    for number, value in enumerate(to_right + to_left):
        chains[number] = value
    for field in range(fields // 2, fields):
        one_field(field)

    me = lax.axis_index("gz")
    mine = lax.broadcasted_iota(jnp.int32, (rows, LANES), 0) == ny + me
    even = (lax.broadcasted_iota(jnp.int32, (1, LANES), 1) & 1) == 0
    lane = lax.broadcasted_iota(jnp.int32, (1, LANES), 1)

    def own(values):
        return tuple(jnp.sum(jnp.where(mine, v, 0.0), axis=0, keepdims=True) for v in values)

    up, down = own(to_right), own(to_left)
    up_past, down_past = own(mm(before, to_right)), own(mm(after, to_left))
    unit = (1.0, 0.0, 0.0, 1.0)
    weights = []
    for column in range(2):
        same = jnp.where(even, unit[column], unit[2 + column])
        inside_up = cell_weights(up, column, even)
        inside_down = cell_weights(down, column, even)
        past_up = lane_roll(cell_weights(up_past, column, even), -2)
        past_down = lane_roll(cell_weights(down_past, column, even), 2)
        ends_up = jnp.where(lane < 2, same, jnp.where(lane >= LANES - 2, past_up, 0.0))
        ends_down = jnp.where(lane < 2, past_down, jnp.where(lane >= LANES - 2, same, 0.0))
        weights.append(
            (
                jnp.concatenate([inside_up, ends_up], axis=1),
                jnp.concatenate([inside_down, ends_down], axis=1),
            )
        )
    if paired:
        lower = (me & 1) == 0
        stack = [jnp.where(lower, w[0], w[1]) for w in weights]
        peer = lax.broadcasted_iota(jnp.int32, (rows, LANES), 0) == ny + jnp.bitwise_xor(me, 1)

        def of_peer(values, place):
            chosen = tuple(jnp.sum(jnp.where(peer, v, 0.0), axis=0, keepdims=True) for v in values)
            return tuple(jnp.broadcast_to(v[:, place : place + 1], (1, 2 * LANES)) for v in chosen)

        over, under = of_peer(to_right, 0), of_peer(to_left, LANES - 1)
        (up0, down0), (up1, down1) = weights
        for q in range(2):
            upward = jnp.where(lower, over[q] * up0 + over[2 + q] * up1, weights[q][0])
            downward = jnp.where(lower, weights[q][1], under[q] * down0 + under[2 + q] * down1)
            stack.append(jnp.where(me < 2, upward, downward))
    else:
        stack = []
        for k in range(1, partners + 1):
            upward = jnp.bitwise_xor(me, k) > me
            stack += [jnp.where(upward, w[0], w[1]) for w in weights]
    while len(stack) % 8:
        stack.append(jnp.zeros((1, 2 * LANES), jnp.float32))
    count = len(stack)
    stack = jnp.concatenate(stack, axis=0)
    first = stack.astype(jnp.bfloat16).astype(jnp.float32)
    both = jnp.concatenate([first, stack - first], axis=0).astype(jnp.bfloat16)
    across = (((1,), (1,)), ((), ()))
    total = high.shape[0]
    size = planes_x * wy
    for begin in range(0, total, size):
        rows = slice(begin, min(begin + size, total))
        on_high = matmul(both, high[rows, :], across)
        on_low = matmul(both, low[rows, :], across)
        moments = (on_high[:count] + on_high[count:]) + on_low[:count]
        if paired:
            messages[0][:, rows] = moments[0:4]
        else:
            for k in range(partners):
                messages[k][:, rows] = moments[2 * k : 2 * k + 2]


def dense_inverse(columns, start, width, stack):
    parts = 8
    steps = width // (2 * parts)
    lane = lax.broadcasted_iota(jnp.int32, (parts, LANES), 1)
    part = lax.broadcasted_iota(jnp.int32, (parts, LANES), 0)
    fits = width + 4 <= LANES
    values = [columns[pl.ds(start + 2 * i, parts, stride=2 * steps), :] for i in range(steps)]

    def wide(i, number):
        return tuple(
            jnp.broadcast_to(values[i][:, number + k : number + k + 1], (parts, LANES)) for k in range(4)
        )

    blocks = [wide(i, 8) for i in range(steps)]
    zero, one = jnp.zeros((parts, LANES), jnp.float32), jnp.ones((parts, LANES), jnp.float32)

    def put(rows, i, extra, extra_lane, owner):
        first = 2 * (part * steps + i)
        out = []
        for r in range(2):
            row = jnp.where(lane == first, blocks[i][2 * r], rows[r])
            row = jnp.where(lane == first + 1, blocks[i][2 * r + 1], row)
            if extra is not None and fits:
                row = jnp.where((part == owner) & (lane == extra_lane), extra[2 * r], row)
                row = jnp.where((part == owner) & (lane == extra_lane + 1), extra[2 * r + 1], row)
            out.append(row)
        return tuple(out)

    def run(order, number, ends, extra_lane, owner):
        rows, product, out = (zero, zero), (one, zero, zero, one), {}
        for i in order:
            t = wide(i, number)
            rows = (t[0] * rows[0] + t[1] * rows[1], t[2] * rows[0] + t[3] * rows[1])
            extra = None
            if i == order[0]:
                e = wide(i, ends)
                extra = mm(blocks[i], (e[0], e[2], e[1], e[3]))
            rows = put(rows, i, extra, extra_lane, owner)
            product = mm(t, product)
            out[i] = rows, product
        rows, product = out[order[-1]]
        entering, last = [None] * parts, (jnp.zeros((1, LANES), jnp.float32),) * 2
        sequence = range(parts) if number == 4 else range(parts - 1, -1, -1)
        for p in sequence:
            entering[p] = last
            own, across = [r[p : p + 1] for r in rows], [x[p : p + 1] for x in product]
            last = (
                own[0] + across[0] * last[0] + across[1] * last[1],
                own[1] + across[2] * last[0] + across[3] * last[1],
            )
        entering = [jnp.concatenate([e[r] for e in entering], axis=0) for r in range(2)]
        result = []
        for i in range(steps):
            rows, product = out[i]
            for r in range(2):
                result.append(rows[r] + product[2 * r] * entering[0] + product[2 * r + 1] * entering[1])
        return result

    low = run(list(range(steps)), 4, 12, width, 0)
    high = run(list(range(steps - 1, -1, -1)), 0, 16, width + 2, parts - 1)
    for k in range(2 * steps):
        lower = lane <= 2 * (part * steps + k // 2) + 1
        if fits:
            lower = lower & (lane < width) | ((lane >= width) & (lane < width + 2))
        stack[parts * k : parts * (k + 1), :] = jnp.where(lower, low[k], high[k])
    rows = [stack[pl.ds(p, 2 * steps, stride=parts), :] for p in range(parts)]
    return jnp.concatenate(rows, axis=0)


def stage_plan(count):
    plan, stride = [], 1
    while stride < count:
        radix = 4 if count // stride >= 4 else 2
        plan.append((stride, radix))
        stride *= radix
    return plan


def transposed(factors, row):
    rows = [factors[number, pl.ds(row, 1), :] for number in range(12)]
    rows += [factors[20 + number, pl.ds(row, 1), :] for number in range(8)]
    rows += [factors[12 + number, pl.ds(row, 1), :] for number in range(8)]
    rows.append(jnp.zeros((4, LANES), jnp.float32))
    return jnp.concatenate(rows, axis=0).T


def chain_products(chains, number, place, blocks, begins, ends, masks, reverse):
    count = -(-len(begins) // 8) * 8
    row = lax.broadcasted_iota(jnp.int32, (count, LANES), 0)
    begin = jnp.zeros((count, LANES), jnp.int32)
    end, mask = begin, jnp.zeros((count, LANES), jnp.float32)
    for r, (b, e, m) in enumerate(zip(begins, ends, masks)):
        begin, end = jnp.where(row == r, b, begin), jnp.where(row == r, e, end)
        mask = jnp.where(row == r, m, mask)
    one, zero = jnp.ones((count, LANES), jnp.float32), jnp.zeros((count, LANES), jnp.float32)
    product = (one, zero, zero, one)
    for block in range(blocks - 1, -1, -1) if reverse else range(blocks):
        where = place(block)
        value = tuple(chains[number + k, where[0], where[1]] for k in range(4))
        product = pick((begin <= block) & (block < end), mm(product, value), product)
    return tuple(x * mask for x in product)


def truth(condition):
    return jnp.where(condition, 1.0, 0.0)


def inverse_z_kernel(ny, planes, wy, factors, matrix, spread_high, spread_low, columns, stacked, rows_ref):
    me_z = lax.axis_index("gz")
    columns[0:LANES, 0:32] = transposed(factors, ny + me_z)
    inverse = dense_inverse(columns, 0, LANES, stacked)
    rows_ref[0:LANES, :] = inverse
    rows_ref[LANES : 2 * LANES, :] = jnp.zeros((LANES, LANES), jnp.float32)
    past = tuple(columns[LANES - 1 : LANES, 16 + k : 17 + k] for k in range(4))
    ahead = tuple(columns[0:1, 12 + k : 13 + k] for k in range(4))
    head0, head1 = rows_ref[0:1, :], rows_ref[1:2, :]
    tail0, tail1 = rows_ref[LANES - 2 : LANES - 1, :], rows_ref[LANES - 1 : LANES, :]
    for q in range(2):
        rows_ref[LANES + q : LANES + q + 1, :] = past[2 * q] * tail0 + past[2 * q + 1] * tail1
        rows_ref[2 * LANES - 2 + q : 2 * LANES - 1 + q, :] = ahead[2 * q] * head0 + ahead[2 * q + 1] * head1
    first, second = halves(rows_ref[...])
    matrix[:, 0:LANES] = first
    matrix[:, LANES : 2 * LANES] = second

    cell = lax.axis_index("gy") * wy
    row = cell // LANES
    total = planes * (wy + EXTRA)
    unit = (1.0, 0.0, 0.0, 1.0)
    lane = lax.broadcasted_iota(jnp.int32, (1, LANES), 1)
    even = (lane & 1) == 0

    def chain(number):
        return tuple(factors[number + k, pl.ds(row, 1), :] for k in range(4))

    def turned(x, by):
        return pltpu.roll(x, lax.rem(by + 2 * LANES, LANES), 1)

    def tiled(x, period):
        x = jnp.where(lane < period, x, 0.0)
        while period < LANES:
            x = x + lane_roll(x, period)
            period *= 2
        return x

    up, down, before, after = chain(12), chain(16), chain(20), chain(24)
    past_up, past_down = mm(before, up), mm(after, down)
    plane_row = lax.broadcasted_iota(jnp.int32, (planes, LANES), 0)
    wide_lane = lax.broadcasted_iota(jnp.int32, (planes, LANES), 1)
    for column in range(2):
        same = jnp.where(even, unit[column], unit[2 + column])
        for number, inside, early, late in (
            (column, up, turned(cell_weights(past_up, column, even), -start_y(cell)), same),
            (
                2 + column,
                down,
                same,
                turned(cell_weights(past_down, column, even), 4 - wy - start_y(cell)),
            ),
        ):
            inside = tiled(turned(cell_weights(inside, column, even), -start_y(cell)), wy)
            past = jnp.where(lane < 2, early, jnp.where(lane < 4, late, 0.0))
            past = tiled(past, EXTRA)
            rows = slice(number * planes, (number + 1) * planes)
            for begin in range(0, total, LANES):
                if begin < planes * wy:
                    owner, value = (begin + wide_lane) // wy, inside
                else:
                    owner, value = (begin - planes * wy + wide_lane) // EXTRA, past
                size = min(LANES, total - begin)
                first, second = halves(jnp.where(plane_row == owner, value, 0.0))
                spread_high[rows, begin : begin + size] = first[:, 0:size]
                spread_low[rows, begin : begin + size] = second[:, 0:size]


def whole_rows(matrix, row):
    start = row // 16 * 16
    both = matrix[start : start + 16, :].astype(jnp.float32)
    value = both[:, 0:LANES] + both[:, LANES : 2 * LANES]
    return value[row - start : row - start + 1]


def second_kernel(
    ny, nz, count_z, wy, partners, paired, chains, factors, matrix, high, low, local, moments, entering, *scratch
):
    columns, weights_y = scratch
    me_z, me_y = lax.axis_index("gz"), lax.axis_index("gy")
    planes = moments.shape[0] // 4
    head0, head1 = whole_rows(matrix, 0), whole_rows(matrix, 1)
    tail0, tail1 = whole_rows(matrix, LANES - 2), whole_rows(matrix, LANES - 1)

    if paired:
        pair = me_z // 2 * 2
        begins, ends = [me_z, pair], [me_z + 1, pair + 2]
        lowers = [me_z % 2 == 1, pair > 0]
    else:
        others = [jnp.bitwise_xor(me_z, k) for k in range(1, partners + 1)]
        begins, ends = [other + 1 for other in others], others
        lowers = [other < me_z for other in others]
    size = len(begins)
    up = chain_products(
        chains, 0, lambda b: (ny + b, 0), count_z, begins, [me_z] * size, [1.0] * size, False
    )
    down = chain_products(
        chains, 4, lambda b: (ny + b, LANES - 1), count_z, [me_z + 1] * size, ends, [1.0] * size, True
    )
    stack = []
    for k, lower in enumerate(lowers):
        for p in range(2):
            from_low = up[2 * p][k : k + 1] * head0 + up[2 * p + 1][k : k + 1] * head1
            from_high = down[2 * p][k : k + 1] * tail0 + down[2 * p + 1][k : k + 1] * tail1
            stack.append(jnp.where(lower, from_low, from_high))
    while len(stack) % 8:
        stack.append(jnp.zeros((1, LANES), jnp.float32))
    stack = jnp.concatenate(stack, axis=0)
    first = stack.astype(jnp.bfloat16).astype(jnp.float32)
    entering[...] = jnp.concatenate([first, stack - first, first], axis=0)

    cell = me_y * wy
    columns[0:LANES, 0:32] = transposed(factors, cell // LANES)
    start = lax.rem(cell, LANES)
    row = lax.broadcasted_iota(jnp.int32, (wy, LANES), 0)
    extra_row = lax.broadcasted_iota(jnp.int32, (EXTRA, LANES), 0)
    unit = (1.0, 0.0, 0.0, 1.0)

    def head(number):
        return tuple(columns[pl.ds(start, 1), number + k : number + k + 1] for k in range(4))

    def tail(number):
        return tuple(columns[pl.ds(start + wy - 1, 1), number + k : number + k + 1] for k in range(4))

    past_up, past_down = mm(head(12), head(20)), mm(tail(16), tail(24))
    for column in range(2):
        for output, number in ((column, 20), (2 + column, 24)):
            even = columns[pl.ds(start, wy), number + column : number + column + 1]
            odd = columns[pl.ds(start, wy), number + 2 + column : number + 3 + column]
            weights_y[output, 0:wy, :] = jnp.where((row & 1) == 0, even, odd)
        for output, early, late in (
            (column, (past_up[column], past_up[2 + column]), (unit[column], unit[2 + column])),
            (2 + column, (unit[column], unit[2 + column]), (past_down[column], past_down[2 + column])),
        ):
            value = jnp.zeros((EXTRA, LANES), jnp.float32)
            for r, v in enumerate(early + late):
                value = jnp.where(extra_row == r, v, value)
            weights_y[output, wy : wy + EXTRA, :] = value

    total = planes * (wy + EXTRA)

    def solve(begin, size):
        rows = slice(begin, begin + size)
        both = matmul(high[rows, :], matrix[...])
        value = both[:, 0:LANES] + (both[:, LANES : 2 * LANES] + matmul(low[rows, :], matrix[:, 0:LANES]))
        local[rows, :] = value
        return value

    extra = solve(planes * wy, planes * EXTRA)
    for part in range(planes // 8):
        core = solve(part * 8 * wy, 8 * wy)
        for number in range(4):
            lines = []
            for k in range(8):
                index = part * 8 + k
                value = jnp.sum(core[k * wy : (k + 1) * wy] * weights_y[number, 0:wy, :], axis=0, keepdims=True)
                past = extra[index * EXTRA : (index + 1) * EXTRA] * weights_y[number, wy : wy + EXTRA, :]
                lines.append(value + jnp.sum(past, axis=0, keepdims=True))
            start = number * planes + part * 8
            moments[start : start + 8, :] = jnp.concatenate(lines, axis=0)


def start_y(cell):
    return lax.rem(cell, LANES)


def y_kernel(count_y, wy, chains, factors, unused, inverse_y, coefs, columns, stacked):
    me_y = lax.axis_index("gy")
    cell = me_y * wy
    columns[0:LANES, 0:32] = transposed(factors, cell // LANES)
    start = lax.rem(cell, LANES)
    inverse_y[...] = dense_inverse(columns, start, wy, stacked)

    up, down = ([], [], []), ([], [], [])
    plan = stage_plan(count_y)
    for number, (stride, radix) in enumerate(plan):
        group = me_y // stride
        first = (group // radix) * radix
        others = [first + jnp.bitwise_xor(group - first, k) for k in range(radix)]
        for other in others[1:]:
            for lists, values in (
                (up, ((other + 1) * stride, me_y, truth(other < group))),
                (down, (me_y + 1, other * stride, truth(other > group))),
            ):
                for one, value in zip(lists, values):
                    one.append(value)
        if number + 1 < len(plan):
            for other in others:
                for lists, values in (
                    (up, ((other + 1) * stride, (first + radix) * stride, 1.0)),
                    (down, (first * stride, other * stride, 1.0)),
                ):
                    for one, value in zip(lists, values):
                        one.append(value)

    def place(block):
        return block * wy // LANES, block * wy % LANES

    def place_end(block):
        return place(block)[0], place(block)[1] + wy - 1

    for base, value in (
        (0, chain_products(chains, 0, place, count_y, *up, False)),
        (4, chain_products(chains, 4, place_end, count_y, *down, True)),
    ):
        for k in range(4):
            coefs[base + k] = value[k]


def pair_kernel(own, received, unused, total):
    total[...] = own[2:4] + received[2:4]


def arrived_rows(messages, count):
    rows = [m[0:2] for m in messages]
    if count > 2 * len(messages):
        rows.append(jnp.zeros((count - 2 * len(messages), rows[0].shape[1]), jnp.float32))
    return jnp.concatenate(rows, axis=0)


def third_kernel(moments, spread_high, spread_low, entering, *refs):
    messages, carried = refs[:-1], refs[-1]
    count = entering.shape[0] // 3
    received = arrived_rows(messages, count)
    first = received.astype(jnp.bfloat16).astype(jnp.float32)
    both = jnp.concatenate([first, received - first], axis=0).astype(jnp.bfloat16)
    top = jnp.concatenate([first, jnp.zeros_like(first)], axis=0).astype(jnp.bfloat16)
    across = (((1,), (1,)), ((), ()))
    corner = matmul(spread_high[...], both, across) + matmul(spread_low[...], top, across)
    values = entering[0:count, :] + entering[count : 2 * count, :]
    added = lax.dot_general(
        corner,
        jnp.concatenate([values, values], axis=0),
        (((1,), (0,)), ((), ())),
        precision=lax.Precision.HIGHEST,
        preferred_element_type=jnp.float32,
    )
    planes = carried.shape[1]
    for number in range(4):
        rows = slice(number * planes, (number + 1) * planes)
        carried[number] = moments[rows, :] + added[rows]


def local_y_kernel(wy, local, entering, inverse_y, unused, *refs):
    messages, (out, solved) = refs[:-2], refs[-2:]
    planes = out.shape[0]
    count = entering.shape[0] // 3
    received = arrived_rows(messages, count)
    first = received.astype(jnp.bfloat16).astype(jnp.float32)
    received = jnp.concatenate([first, first, received - first], axis=0).T.astype(jnp.bfloat16)
    solved[...] = local[...] + matmul(received, entering[...].astype(jnp.bfloat16))
    first, second = halves(inverse_y[:, 0 : wy + EXTRA])
    left = jnp.concatenate([first, second, first], axis=1)

    def part(index, carry):
        for k in range(8):
            number = index * 8 + k
            start = pl.multiple_of(number * wy, 8)
            core = solved[pl.ds(start, wy), :]
            start = pl.multiple_of(planes * wy + number * EXTRA, 8)
            both = jnp.concatenate([core, solved[pl.ds(start, EXTRA), :]], axis=0)
            top, rest = halves(both)
            out[number] = matmul(left, jnp.concatenate([top, top, rest], axis=0))
        return carry

    lax.fori_loop(0, planes // 8, part, 0)


def combine(coefs, side, row, values):
    first = 0 if side == 0 else 2
    out = [None, None]
    for k, value in enumerate(values):
        for q in range(2):
            for p in range(2):
                term = coefs[side + 2 * p + q, row + k : row + k + 1, :] * value[first + p]
                out[q] = term if out[q] is None else out[q] + term
    return out


def stage_kernel(base, stride, radix, narrow, has_entered, coefs, *refs):
    values = (refs[0],) + tuple(refs[1:radix][::-1])
    position = radix
    entered = None
    if has_entered:
        entered = refs[position]
        position += 1
    message, entering = refs[position : position + 2]
    below = combine(coefs, 0, base, values[1:])
    above = combine(coefs, 4, base, values[1:])
    for row, value in enumerate(below + above):
        entering[row] = value if entered is None else value + entered[row]
    upward = combine(coefs, 0, base + radix - 1, values)
    downward = combine(coefs, 4, base + radix - 1, values)
    if narrow:
        group = lax.axis_index("gy") // (stride * radix)
        sends_up = lax.rem(group, 2) == 0
        for row in range(2):
            message[row] = jnp.where(sends_up, upward[row], downward[row])
    else:
        for row, value in enumerate(upward + downward):
            message[row] = value


def last_kernel(base, radix, narrow, wy, coefs, local, inverse_y, entered, *refs):
    messages, (out_hbm, out, sent) = refs[: radix - 1], refs[radix - 1 :]
    values = list(messages)
    if narrow:
        values = [(m[0], m[1], m[0], m[1]) for m in values]
    below = combine(coefs, 0, base, values)
    above = combine(coefs, 4, base, values)
    st = [value + entered[row] for row, value in enumerate(below + above)]
    sides = [
        jnp.broadcast_to(inverse_y[:, c : c + 1], (wy, LANES)) for c in (0, 1, wy - 2, wy - 1)
    ]
    fields, planes_x = out.shape[:2]
    copies = []
    for field in range(fields):
        for x in range(planes_x):
            index = field * planes_x + x
            value = local[index]
            for number in range(4):
                value = value + sides[number] * st[number][index : index + 1]
            out[field, x] = value
            if (x + 1) % 4 == 0:
                part = (field, pl.ds(x - 3, 4))
                copy = pltpu.make_async_copy(out.at[part], out_hbm.at[part], sent.at[len(copies)])
                copy.start()
                copies.append(copy)
    for copy in copies:
        copy.wait()


VMEM = pl.BlockSpec(memory_space=pltpu.VMEM)
HBM = pl.BlockSpec(memory_space=pltpu.HBM)
SMEM = pl.BlockSpec(memory_space=pltpu.SMEM)
PARAMS = pltpu.CompilerParams(vmem_limit_bytes=40 * 1024 * 1024)


def array(*shape):
    return jax.ShapeDtypeStruct(shape, jnp.float32)


def in_hbm(x):
    return pltpu.with_memory_space_constraint(x, pltpu.HBM)


def cost(flops, data):
    return pl.CostEstimate(flops=flops, bytes_accessed=data, transcendentals=0)


def on_device(mesh, flow, speed, metric_y, metric_z):
    fields, planes_x, wy, wz = flow.shape
    count_y, count_z = mesh.shape["gy"], mesh.shape["gz"]
    assert wz == LANES
    ny, nz = metric_y.shape[0] // LANES, metric_z.shape[0] // LANES
    planes = fields * planes_x
    rows = planes * (wy + EXTRA)
    partners = count_z - 1
    paired = count_z == 4
    arrivals = 2 if paired else partners
    entering_rows = -(-2 * arrivals // 8) * 8
    half = jax.ShapeDtypeStruct((rows, 2 * LANES), jnp.bfloat16)
    outputs = pl.pallas_call(
        functools.partial(first_kernel, ny, nz, partners, paired),
        out_shape=[half, half, array(28, ny + nz, LANES), array(8, ny + nz, LANES)]
        + ([array(4, rows)] if paired else [array(2, rows)] * partners),
        in_specs=[HBM] * 4,
        out_specs=[VMEM] * (5 if paired else 4 + partners),
        scratch_shapes=[
            pltpu.VMEM(flow.shape, jnp.float32),
            pltpu.VMEM(speed.shape, jnp.float32),
            pltpu.VMEM((ny + nz, LANES), jnp.float32),
            pltpu.VMEM((planes_x, 3, wy + 16, LANES), jnp.float32),
            pltpu.SemaphoreType.DMA((fields + 3,)),
        ],
        compiler_params=PARAMS,
        name="forcing_and_factor",
    )(*(in_hbm(x) for x in (flow, speed, metric_y.reshape(ny, LANES), metric_z.reshape(nz, LANES))))
    high, low, factors, chains = outputs[:4]

    def exchange(values, axis, count, stride, radix):
        received = {}
        for k in reversed(range(1, radix)):
            pairs = [(i, i ^ (k * stride)) for i in range(count)]
            received[k] = lax.ppermute(values[k - 1], axis, pairs)
        return [received[k] for k in range(1, radix)]

    plan = stage_plan(count_y)
    work = [pltpu.VMEM((LANES + 16, LANES), jnp.float32)] * 2
    spread = jax.ShapeDtypeStruct((4 * planes, rows), jnp.bfloat16)
    matrix, spread_high, spread_low = pl.pallas_call(
        functools.partial(inverse_z_kernel, ny, planes, wy),
        out_shape=[jax.ShapeDtypeStruct((2 * LANES, 2 * LANES), jnp.bfloat16), spread, spread],
        in_specs=[VMEM],
        out_specs=[VMEM] * 3,
        scratch_shapes=work + [pltpu.VMEM((2 * LANES, LANES), jnp.float32)],
        compiler_params=PARAMS,
        cost_estimate=cost(rows * 1024, 4 * rows * 64),
        name="inverse_z",
    )(factors)
    if paired:
        near = exchange(outputs[4:], "gz", count_z, 1, 2)
        total = pl.pallas_call(
            pair_kernel,
            out_shape=array(2, rows),
            in_specs=[VMEM] * 2 + [HBM],
            out_specs=VMEM,
            compiler_params=PARAMS,
            name="join_pair",
        )(outputs[4], near[0], matrix)
        received = near + exchange([total], "gz", count_z, 2, 2)
    else:
        received = exchange(outputs[4:], "gz", count_z, 1, count_z)
    local, moments, entering = pl.pallas_call(
        functools.partial(second_kernel, ny, nz, count_z, wy, partners, paired),
        out_shape=[
            array(rows, LANES),
            array(4 * planes, LANES),
            array(3 * entering_rows, LANES),
        ],
        in_specs=[SMEM] + [VMEM] * 4,
        out_specs=[VMEM] * 3,
        scratch_shapes=[
            pltpu.VMEM((LANES + 16, LANES), jnp.float32),
            pltpu.VMEM((4, wy + EXTRA, LANES), jnp.float32),
        ],
        compiler_params=PARAMS,
        cost_estimate=cost(2 * rows * 256 * 128 * 6, 4 * rows * 384),
        name="local_z",
    )(chains, factors, matrix, high, low)
    carried = pl.pallas_call(
        third_kernel,
        out_shape=array(4, planes, LANES),
        in_specs=[VMEM] * (4 + arrivals),
        out_specs=VMEM,
        compiler_params=PARAMS,
        name="carried_y",
    )(moments, spread_high, spread_low, entering, *received)
    arrived = received

    narrow = plan[-1][1] == 2 and len(plan) > 1
    base, entered, result = 0, None, None
    for number, (stride, radix) in enumerate(plan):
        received = exchange([carried] * (radix - 1), "gy", count_y, stride, radix)
        if number == 0:
            entries = sum(2 * radix - 1 for _, radix in plan[:-1]) + plan[-1][1] - 1
            inverse_y, coefs = pl.pallas_call(
                functools.partial(y_kernel, count_y, wy),
                out_shape=[array(wy, LANES), array(8, -(-entries // 8) * 8, LANES)],
                in_specs=[SMEM, VMEM, HBM],
                out_specs=[VMEM] * 2,
                scratch_shapes=work,
                compiler_params=PARAMS,
                cost_estimate=cost(2 * rows * 128 * 128 * 6, 4 * rows * 256),
                name="inverse_y",
            )(chains, factors, carried)
        if number + 1 < len(plan):
            slim = narrow and number + 2 == len(plan)
            inputs = [carried] + received[::-1] + ([entered] if entered is not None else [])
            carried, entered = pl.pallas_call(
                functools.partial(stage_kernel, base, stride, radix, slim, entered is not None),
                out_shape=[array(2 if slim else 4, planes, LANES), array(4, planes, LANES)],
                in_specs=[VMEM] * (1 + len(inputs)),
                out_specs=[VMEM] * 2,
                compiler_params=PARAMS,
                name="join_groups",
            )(coefs, *inputs)
            base += 2 * radix - 1
            if number == 0:
                result = pl.pallas_call(
                    functools.partial(local_y_kernel, wy),
                    out_shape=array(planes, wy, LANES),
                    in_specs=[VMEM] * 3 + [HBM] + [VMEM] * arrivals,
                    out_specs=VMEM,
                    scratch_shapes=[pltpu.VMEM((rows, LANES), jnp.float32)],
                    compiler_params=PARAMS,
                    cost_estimate=cost(2 * rows * 128 * 128 * 6, 4 * rows * 256),
                    name="local_y",
                )(local, entering, inverse_y, entered, *arrived)
        else:
            return pl.pallas_call(
                functools.partial(last_kernel, base, radix, narrow, wy),
                out_shape=array(fields, planes_x, wy, wz),
                in_specs=[VMEM] * (4 + len(received)),
                out_specs=HBM,
                scratch_shapes=[
                    pltpu.VMEM(flow.shape, jnp.float32),
                    pltpu.SemaphoreType.DMA((planes // 4,)),
                ],
                compiler_params=PARAMS,
                name="finish_y",
            )(coefs, result, inverse_y, entered, *received)


def solution(mesh):
    placed = (P(None, None, "gy", "gz"), P(None, "gy", "gz"), P(), P())
    return jax.shard_map(
        functools.partial(on_device, mesh),
        mesh=mesh,
        in_specs=placed,
        out_specs=P(None, None, "gy", "gz"),
        check_vma=False,
    )
```

```python
import functools

import jax
import jax.numpy as jnp
from jax import lax
from jax.experimental import pallas as pl
from jax.experimental.pallas import tpu as pltpu
from jax.sharding import PartitionSpec as P

viscous = 0.25
explicit_fourth = 0.04
implicit_fourth = 0.05
time_step = 1048576.0
LANES = 128
EXTRA = 8


def mm(a, b):
    return (
        a[0] * b[0] + a[1] * b[2],
        a[0] * b[1] + a[1] * b[3],
        a[2] * b[0] + a[3] * b[2],
        a[2] * b[1] + a[3] * b[3],
    )


def inverse_of_one_minus(a):
    p, q, r, s = 1.0 - a[0], -a[1], -a[2], 1.0 - a[3]
    d = 1.0 / (p * s - q * r)
    return (s * d, -q * d, -r * d, p * d)


def pick(condition, a, b):
    return tuple(jnp.where(condition, x, y) for x, y in zip(a, b))


def halves(x):
    high = x.astype(jnp.bfloat16)
    return high, (x - high.astype(jnp.float32)).astype(jnp.bfloat16)


def matmul(a, b, dims=(((1,), (0,)), ((), ()))):
    return lax.dot_general(a, b, dims, preferred_element_type=jnp.float32)


def scan(m, ahead, count, step, shift, product):
    unit = (1.0, 0.0, 0.0, 1.0)

    def moved(by):
        return tuple(jnp.where(ahead >= by, shift(x, by), u) for x, u in zip(m, unit))

    while step < count:
        if 2 * step < count:
            m = product(product(m, moved(step)), product(moved(2 * step), moved(3 * step)))
            step *= 4
        else:
            m = product(m, moved(step))
            step *= 2
    return m


def lane_roll(x, by):
    return pltpu.roll(x, by % LANES, 1)


def row_roll(x, by):
    by = by % x.shape[0]
    return jnp.concatenate([x[x.shape[0] - by :], x[: x.shape[0] - by]], axis=0)


class Factor:
    def __init__(self, metric, ny, nz, wy):
        self.ny, self.nz, self.wy, self.rows = ny, nz, wy, ny + nz
        self.lane = lax.broadcasted_iota(jnp.int32, (self.rows, LANES), 1)
        self.row = lax.broadcasted_iota(jnp.int32, (self.rows, LANES), 0)
        self.block = jnp.where(self.row < ny, self.row, self.row - ny)
        self.to_end = jnp.where(self.row < ny, ny, nz) - 1 - self.block
        first = (self.lane == 0) & (self.block == 0)
        last = (self.lane == LANES - 1) & (self.to_end == 0)
        self.face_low = 0.5 * (jnp.where(first, metric, self.before(metric, 1)) + metric)
        self.face_high = 0.5 * (metric + jnp.where(last, metric, self.after(metric, 1)))

    def before(self, x, by):
        rolled = lane_roll(x, by)
        value = jnp.where(self.lane < by, row_roll(rolled, 1), rolled)
        return jnp.where((self.lane < by) & (self.block == 0), 0.0, value)

    def after(self, x, by):
        rolled = lane_roll(x, -by)
        value = jnp.where(self.lane >= LANES - by, row_roll(rolled, -1), rolled)
        return jnp.where((self.lane >= LANES - by) & (self.to_end == 0), 0.0, value)

    def guess(self, sign):
        face = self.face_high if sign > 0 else self.face_low
        if sign > 0:
            cell = self.lane + LANES * self.block
        else:
            cell = LANES - 1 - self.lane + LANES * self.to_end
        near = face / (cell + 1).astype(jnp.float32)
        one_over = 1.0 / (face + jnp.sqrt(face + near * near))
        return face * one_over, implicit_fourth * one_over, one_over

    def sweep(self, sign, ratio, far):
        rows = self.rows
        back = self.before if sign > 0 else self.after
        if sign > 0:
            face_in, face_out, place = self.face_low, self.face_high, self.block
        else:
            face_in, face_out, place = self.face_high, self.face_low, self.to_end
        eps = 4.0 * implicit_fourth - implicit_fourth * back(ratio, 1)
        mass = (1.0 + 6.0 * implicit_fourth) - implicit_fourth * back(far, 2) - 2.0 * eps
        eps_in = back(eps, 1)
        scale = 1.0 / (face_in + 2.0 * eps_in)
        m = ((mass + face_in) * scale, mass - eps_in * eps_in * scale, scale, jnp.ones_like(scale))
        ahead = self.lane if sign > 0 else LANES - 1 - self.lane
        m = scan(m, ahead, LANES, 1, lambda x, by: lane_roll(x, sign * by), mm)
        edge = LANES - 1 if sign > 0 else 0
        total = tuple(jnp.broadcast_to(x[:, edge : edge + 1], (rows, LANES)) for x in m)
        total = scan(
            total, place, max(self.ny, self.nz), 1, lambda x, by: row_roll(x, sign * by), mm
        )
        top = jnp.where(place >= 1, row_roll(total[0], sign), 1.0)
        low = jnp.where(place >= 1, row_roll(total[2], sign), 0.0)
        eta = (m[0] * top + m[1] * low) / (m[2] * top + m[3] * low)
        one_over = 1.0 / (face_out + (eta + 2.0 * eps))
        return (face_out + eps) * one_over, implicit_fourth * one_over, one_over

    def finish(self, near_l, far_l, pivot_l, near_r, far_r):
        lane, block, to_end = self.lane, self.block, self.to_end
        even = (lane & 1) == 0
        near_l = jnp.where((to_end == 0) & (lane >= LANES - 1), 0.0, near_l)
        far_l = jnp.where((to_end == 0) & (lane >= LANES - 2), 0.0, far_l)
        near_r = jnp.where((block == 0) & (lane < 1), 0.0, near_r)
        far_r = jnp.where((block == 0) & (lane < 2), 0.0, far_r)

        def of_even(x):
            return jnp.where(even, x, lane_roll(x, 1))

        def of_odd(x):
            return jnp.where(even, lane_roll(x, -1), x)

        t0, t1, r0, r1 = of_even(near_l), of_odd(near_l), of_even(far_l), of_odd(far_l)
        from_right = (t0 * t1 - r0, -t0 * r1, t1, -r1)
        p1 = of_odd(pivot_l)
        left_inverse = (of_even(pivot_l) + t0 * t0 * p1, t0 * p1, t0 * p1, p1)
        s0, s1, q0, q1 = of_even(near_r), of_odd(near_r), of_even(far_r), of_odd(far_r)
        from_left = (-q0, s0, -s1 * q0, s1 * s0 - q1)
        from_left_after = tuple(self.after(x, 2) for x in from_left)
        from_right_before = tuple(self.before(x, 2) for x in from_right)
        diagonal = mm(inverse_of_one_minus(mm(from_right, from_left_after)), left_inverse)
        width = jnp.where(self.row < self.ny, self.wy, LANES)
        place = lane & (width - 1)
        right = scan(from_right, width - 1 - place, LANES, 2, lambda x, by: lane_roll(x, -by), mm)
        left = scan(from_left, place, LANES, 2, lane_roll, mm)
        return from_right, from_left, diagonal, right, left, from_right_before, from_left_after


def cell_weights(chain, column, even):
    return jnp.where(even, chain[column], chain[2 + column])


def first_kernel(ny, nz, partners, paired, flow_hbm, speed_hbm, metric_y, metric_z, *refs):
    high, low, factors, chains = refs[:4]
    count = 1 if paired else partners
    messages = refs[4 : 4 + count]
    flow, speed, metric, spread, arrived = refs[4 + count :]
    fields, planes_x, wy, _ = flow.shape
    rows = ny + nz
    core_rows = fields * planes_x * wy

    copies = [
        pltpu.make_async_copy(metric_y, metric.at[0:ny], arrived.at[fields]),
        pltpu.make_async_copy(metric_z, metric.at[ny:rows], arrived.at[fields + 1]),
        pltpu.make_async_copy(speed_hbm, speed, arrived.at[fields + 2]),
    ]
    for copy in copies:
        copy.start()
    for field in range(fields):
        pltpu.make_async_copy(flow_hbm.at[field], flow.at[field], arrived.at[field]).start()

    lane = lax.broadcasted_iota(jnp.int32, (wy, LANES), 1)
    extra_row = lax.broadcasted_iota(jnp.int32, (EXTRA, LANES), 0)
    for slot in range(planes_x):
        for part in range(3):
            spread[slot, part, 0:8, :] = jnp.zeros((8, LANES), jnp.float32)
            spread[slot, part, wy + 8 : wy + 16, :] = jnp.zeros((8, LANES), jnp.float32)
    side = time_step * (viscous + 4.0 * explicit_fourth)
    half = time_step * 0.5
    centre = time_step * (-6.0 * viscous - 12.0 * explicit_fourth)
    fourth = -time_step * explicit_fourth

    def store(start, column, value):
        first, second = halves(value)
        high[pl.ds(start, value.shape[0]), column : column + LANES] = first
        low[pl.ds(start, value.shape[0]), column : column + LANES] = second

    def one_field(field):
        values = [flow[field, x] for x in range(planes_x)]
        fluxes = [values[x] * speed[x] for x in range(planes_x)]
        aside = [(time_step * viscous) * u for u in values]
        extras = []
        for x in range(planes_x):
            u, flux, slot = values[x], fluxes[x], x
            total = centre * u
            if x + 1 < planes_x:
                total = total + (aside[x + 1] - fluxes[x + 1])
            if x > 0:
                total = total + (aside[x - 1] + fluxes[x - 1])
            scaled = side * u
            onward, backward, far = scaled + flux, scaled - flux, fourth * u
            spread[slot, 0, 8 : wy + 8, :] = onward
            spread[slot, 1, 8 : wy + 8, :] = backward
            spread[slot, 2, 8 : wy + 8, :] = far
            total = total + (spread[slot, 0, 7 : wy + 7, :] + spread[slot, 1, 9 : wy + 9, :])
            total = total + (spread[slot, 2, 6 : wy + 6, :] + spread[slot, 2, 10 : wy + 10, :])
            a, b = lane_roll(onward, 1), lane_roll(backward, -1)
            c, d = lane_roll(far, 2), lane_roll(far, -2)
            from_low, from_high = a + c, b + d
            ends = jnp.where(lane == 0, from_low, jnp.where(lane == 1, c, 0.0))
            ends = jnp.where(lane == LANES - 1, from_high, jnp.where(lane == LANES - 2, d, ends))
            index = field * planes_x + x
            start = index * wy
            store(start, 0, total + (from_low + from_high))
            store(start, LANES, ends)
            above = spread[slot, 1, 7:15, :] + spread[slot, 2, 8:16, :]
            below = spread[slot, 0, wy + 5 : wy + 13, :] + spread[slot, 2, wy + 4 : wy + 12, :]
            extras.append(jnp.where(extra_row < 2, above, jnp.where(extra_row < 4, below, 0.0)))
            if len(extras) == 2:
                start = core_rows + (index - 1) * EXTRA
                store(start, 0, jnp.concatenate(extras, axis=0))
                for ref in (high, low):
                    ref[pl.ds(start, 2 * EXTRA), LANES : 2 * LANES] = jnp.zeros(
                        (2 * EXTRA, LANES), jnp.bfloat16
                    )
                extras = []

    copies[0].wait()
    copies[1].wait()
    factor = Factor(metric[...], ny, nz, wy)

    guess_l, guess_r = factor.guess(1), factor.guess(-1)
    left, right = factor.sweep(1, *guess_l[:2]), factor.sweep(-1, *guess_r[:2])
    copies[2].wait()
    for x in range(planes_x):
        speed[x] = half * speed[x]
    for field in range(fields):
        pltpu.make_async_copy(flow_hbm.at[field], flow.at[field], arrived.at[field]).wait()
    left, right = factor.sweep(1, *left[:2]), factor.sweep(-1, *right[:2])
    for field in range(fields // 2):
        one_field(field)
    parts = factor.finish(*left, *right[:2])
    from_right, from_left, diagonal, to_right, to_left, before, after = parts
    for number, value in enumerate(v for part in parts for v in part):
        factors[number] = value
    for number, value in enumerate(to_right + to_left):
        chains[number] = value
    for field in range(fields // 2, fields):
        one_field(field)

    me = lax.axis_index("gz")
    mine = lax.broadcasted_iota(jnp.int32, (rows, LANES), 0) == ny + me
    even = (lax.broadcasted_iota(jnp.int32, (1, LANES), 1) & 1) == 0
    lane = lax.broadcasted_iota(jnp.int32, (1, LANES), 1)

    def own(values):
        return tuple(jnp.sum(jnp.where(mine, v, 0.0), axis=0, keepdims=True) for v in values)

    up, down = own(to_right), own(to_left)
    up_past, down_past = own(mm(before, to_right)), own(mm(after, to_left))
    unit = (1.0, 0.0, 0.0, 1.0)
    weights = []
    for column in range(2):
        same = jnp.where(even, unit[column], unit[2 + column])
        inside_up = cell_weights(up, column, even)
        inside_down = cell_weights(down, column, even)
        past_up = lane_roll(cell_weights(up_past, column, even), -2)
        past_down = lane_roll(cell_weights(down_past, column, even), 2)
        ends_up = jnp.where(lane < 2, same, past_up) - inside_up
        ends_down = jnp.where(lane < 2, past_down, same) - inside_down
        at_end = (lane < 2) | (lane >= LANES - 2)
        ends_up, ends_down = jnp.where(at_end, ends_up, 0.0), jnp.where(at_end, ends_down, 0.0)
        weights.append(
            (
                jnp.concatenate([inside_up, ends_up], axis=1),
                jnp.concatenate([inside_down, ends_down], axis=1),
            )
        )
    if paired:
        lower = (me & 1) == 0
        stack = [jnp.where(lower, w[0], w[1]) for w in weights]
        peer = lax.broadcasted_iota(jnp.int32, (rows, LANES), 0) == ny + jnp.bitwise_xor(me, 1)

        def of_peer(values, place):
            chosen = tuple(jnp.sum(jnp.where(peer, v, 0.0), axis=0, keepdims=True) for v in values)
            return tuple(jnp.broadcast_to(v[:, place : place + 1], (1, 2 * LANES)) for v in chosen)

        over, under = of_peer(to_right, 0), of_peer(to_left, LANES - 1)
        (up0, down0), (up1, down1) = weights
        for q in range(2):
            upward = jnp.where(lower, over[q] * up0 + over[2 + q] * up1, weights[q][0])
            downward = jnp.where(lower, weights[q][1], under[q] * down0 + under[2 + q] * down1)
            stack.append(jnp.where(me < 2, upward, downward))
    else:
        stack = []
        for k in range(1, partners + 1):
            upward = jnp.bitwise_xor(me, k) > me
            stack += [jnp.where(upward, w[0], w[1]) for w in weights]
    while len(stack) % 8:
        stack.append(jnp.zeros((1, 2 * LANES), jnp.float32))
    count = len(stack)
    stack = jnp.concatenate(stack, axis=0)
    first = stack.astype(jnp.bfloat16).astype(jnp.float32)
    both = jnp.concatenate([first, stack - first], axis=0).astype(jnp.bfloat16)
    across = (((1,), (1,)), ((), ()))
    total = high.shape[0]
    size = planes_x * wy
    for begin in range(0, total, size):
        rows = slice(begin, min(begin + size, total))
        on_high = matmul(both, high[rows, :], across)
        on_low = matmul(both, low[rows, :], across)
        moments = (on_high[:count] + on_high[count:]) + on_low[:count]
        if paired:
            messages[0][:, rows] = moments[0:4]
        else:
            for k in range(partners):
                messages[k][:, rows] = moments[2 * k : 2 * k + 2]


def dense_inverse(columns, start, width, stack):
    parts = 8
    steps = width // (2 * parts)
    lane = lax.broadcasted_iota(jnp.int32, (parts, LANES), 1)
    part = lax.broadcasted_iota(jnp.int32, (parts, LANES), 0)
    fits = width + 4 <= LANES
    values = [columns[pl.ds(start + 2 * i, parts, stride=2 * steps), :] for i in range(steps)]

    def wide(i, number):
        return tuple(
            jnp.broadcast_to(values[i][:, number + k : number + k + 1], (parts, LANES)) for k in range(4)
        )

    blocks = [wide(i, 8) for i in range(steps)]
    zero, one = jnp.zeros((parts, LANES), jnp.float32), jnp.ones((parts, LANES), jnp.float32)

    def put(rows, i, extra, extra_lane, owner):
        first = 2 * (part * steps + i)
        out = []
        for r in range(2):
            row = jnp.where(lane == first, blocks[i][2 * r], rows[r])
            row = jnp.where(lane == first + 1, blocks[i][2 * r + 1], row)
            if extra is not None and fits:
                row = jnp.where((part == owner) & (lane == extra_lane), extra[2 * r], row)
                row = jnp.where((part == owner) & (lane == extra_lane + 1), extra[2 * r + 1], row)
            out.append(row)
        return tuple(out)

    def run(order, number, ends, extra_lane, owner):
        rows, product, out = (zero, zero), (one, zero, zero, one), {}
        for i in order:
            t = wide(i, number)
            rows = (t[0] * rows[0] + t[1] * rows[1], t[2] * rows[0] + t[3] * rows[1])
            extra = None
            if i == order[0]:
                e = wide(i, ends)
                extra = mm(blocks[i], (e[0], e[2], e[1], e[3]))
            rows = put(rows, i, extra, extra_lane, owner)
            product = mm(t, product)
            out[i] = rows, product
        rows, product = out[order[-1]]
        entering, last = [None] * parts, (jnp.zeros((1, LANES), jnp.float32),) * 2
        sequence = range(parts) if number == 4 else range(parts - 1, -1, -1)
        for p in sequence:
            entering[p] = last
            own, across = [r[p : p + 1] for r in rows], [x[p : p + 1] for x in product]
            last = (
                own[0] + across[0] * last[0] + across[1] * last[1],
                own[1] + across[2] * last[0] + across[3] * last[1],
            )
        entering = [jnp.concatenate([e[r] for e in entering], axis=0) for r in range(2)]
        result = []
        for i in range(steps):
            rows, product = out[i]
            for r in range(2):
                result.append(rows[r] + product[2 * r] * entering[0] + product[2 * r + 1] * entering[1])
        return result

    low = run(list(range(steps)), 4, 12, width, 0)
    high = run(list(range(steps - 1, -1, -1)), 0, 16, width + 2, parts - 1)
    for k in range(2 * steps):
        lower = lane <= 2 * (part * steps + k // 2) + 1
        if fits:
            lower = lower & (lane < width) | ((lane >= width) & (lane < width + 2))
        stack[parts * k : parts * (k + 1), :] = jnp.where(lower, low[k], high[k])
    rows = [stack[pl.ds(p, 2 * steps, stride=parts), :] for p in range(parts)]
    return jnp.concatenate(rows, axis=0)


def stage_plan(count):
    plan, stride = [], 1
    while stride < count:
        radix = 4 if count // stride >= 4 else 2
        plan.append((stride, radix))
        stride *= radix
    return plan


def transposed(factors, row):
    rows = [factors[number, pl.ds(row, 1), :] for number in range(12)]
    rows += [factors[20 + number, pl.ds(row, 1), :] for number in range(8)]
    rows += [factors[12 + number, pl.ds(row, 1), :] for number in range(8)]
    rows.append(jnp.zeros((4, LANES), jnp.float32))
    return jnp.concatenate(rows, axis=0).T


def chain_products(chains, number, place, blocks, begins, ends, masks, reverse):
    count = -(-len(begins) // 8) * 8
    row = lax.broadcasted_iota(jnp.int32, (count, LANES), 0)
    begin = jnp.zeros((count, LANES), jnp.int32)
    end, mask = begin, jnp.zeros((count, LANES), jnp.float32)
    for r, (b, e, m) in enumerate(zip(begins, ends, masks)):
        begin, end = jnp.where(row == r, b, begin), jnp.where(row == r, e, end)
        mask = jnp.where(row == r, m, mask)
    one, zero = jnp.ones((count, LANES), jnp.float32), jnp.zeros((count, LANES), jnp.float32)
    product = (one, zero, zero, one)
    for block in range(blocks - 1, -1, -1) if reverse else range(blocks):
        where = place(block)
        value = tuple(chains[number + k, where[0], where[1]] for k in range(4))
        product = pick((begin <= block) & (block < end), mm(product, value), product)
    return tuple(x * mask for x in product)


def truth(condition):
    return jnp.where(condition, 1.0, 0.0)


def inverse_z_kernel(ny, planes, wy, factors, matrix, spread_high, spread_low, columns, stacked, rows_ref):
    me_z = lax.axis_index("gz")
    columns[0:LANES, 0:32] = transposed(factors, ny + me_z)
    inverse = dense_inverse(columns, 0, LANES, stacked)
    rows_ref[0:LANES, :] = inverse
    rows_ref[LANES : 2 * LANES, :] = jnp.zeros((LANES, LANES), jnp.float32)
    past = tuple(columns[LANES - 1 : LANES, 16 + k : 17 + k] for k in range(4))
    ahead = tuple(columns[0:1, 12 + k : 13 + k] for k in range(4))
    head0, head1 = rows_ref[0:1, :], rows_ref[1:2, :]
    tail0, tail1 = rows_ref[LANES - 2 : LANES - 1, :], rows_ref[LANES - 1 : LANES, :]
    for q in range(2):
        beyond = past[2 * q] * tail0 + past[2 * q + 1] * tail1
        rows_ref[LANES + q : LANES + q + 1, :] = beyond - (head0, head1)[q]
        beyond = ahead[2 * q] * head0 + ahead[2 * q + 1] * head1
        rows_ref[2 * LANES - 2 + q : 2 * LANES - 1 + q, :] = beyond - (tail0, tail1)[q]
    first, second = halves(rows_ref[...])
    matrix[:, 0:LANES] = first
    matrix[:, LANES : 2 * LANES] = second

    cell = lax.axis_index("gy") * wy
    row = cell // LANES
    total = planes * (wy + EXTRA)
    unit = (1.0, 0.0, 0.0, 1.0)
    lane = lax.broadcasted_iota(jnp.int32, (1, LANES), 1)
    even = (lane & 1) == 0

    def chain(number):
        return tuple(factors[number + k, pl.ds(row, 1), :] for k in range(4))

    def turned(x, by):
        return pltpu.roll(x, lax.rem(by + 2 * LANES, LANES), 1)

    def tiled(x, period):
        x = jnp.where(lane < period, x, 0.0)
        while period < LANES:
            x = x + lane_roll(x, period)
            period *= 2
        return x

    up, down, before, after = chain(12), chain(16), chain(20), chain(24)
    past_up, past_down = mm(before, up), mm(after, down)
    plane_row = lax.broadcasted_iota(jnp.int32, (planes, LANES), 0)
    wide_lane = lax.broadcasted_iota(jnp.int32, (planes, LANES), 1)
    for column in range(2):
        same = jnp.where(even, unit[column], unit[2 + column])
        for number, inside, early, late in (
            (column, up, turned(cell_weights(past_up, column, even), -start_y(cell)), same),
            (
                2 + column,
                down,
                same,
                turned(cell_weights(past_down, column, even), 4 - wy - start_y(cell)),
            ),
        ):
            inside = tiled(turned(cell_weights(inside, column, even), -start_y(cell)), wy)
            past = jnp.where(lane < 2, early, jnp.where(lane < 4, late, 0.0))
            past = tiled(past, EXTRA)
            rows = slice(number * planes, (number + 1) * planes)
            for begin in range(0, total, LANES):
                if begin < planes * wy:
                    owner, value = (begin + wide_lane) // wy, inside
                else:
                    owner, value = (begin - planes * wy + wide_lane) // EXTRA, past
                size = min(LANES, total - begin)
                first, second = halves(jnp.where(plane_row == owner, value, 0.0))
                spread_high[rows, begin : begin + size] = first[:, 0:size]
                spread_low[rows, begin : begin + size] = second[:, 0:size]


def whole_rows(matrix, row):
    start = row // 16 * 16
    both = matrix[start : start + 16, :].astype(jnp.float32)
    value = both[:, 0:LANES] + both[:, LANES : 2 * LANES]
    return value[row - start : row - start + 1]


def second_kernel(
    ny, nz, count_z, wy, partners, paired, chains, factors, matrix, high, low, local, moments, entering, *scratch
):
    columns, weights_y = scratch
    me_z, me_y = lax.axis_index("gz"), lax.axis_index("gy")
    planes = moments.shape[0] // 4
    head0, head1 = whole_rows(matrix, 0), whole_rows(matrix, 1)
    tail0, tail1 = whole_rows(matrix, LANES - 2), whole_rows(matrix, LANES - 1)

    if paired:
        pair = me_z // 2 * 2
        begins, ends = [me_z, pair], [me_z + 1, pair + 2]
        lowers = [me_z % 2 == 1, pair > 0]
    else:
        others = [jnp.bitwise_xor(me_z, k) for k in range(1, partners + 1)]
        begins, ends = [other + 1 for other in others], others
        lowers = [other < me_z for other in others]
    size = len(begins)
    up = chain_products(
        chains, 0, lambda b: (ny + b, 0), count_z, begins, [me_z] * size, [1.0] * size, False
    )
    down = chain_products(
        chains, 4, lambda b: (ny + b, LANES - 1), count_z, [me_z + 1] * size, ends, [1.0] * size, True
    )
    stack = []
    for k, lower in enumerate(lowers):
        for p in range(2):
            from_low = up[2 * p][k : k + 1] * head0 + up[2 * p + 1][k : k + 1] * head1
            from_high = down[2 * p][k : k + 1] * tail0 + down[2 * p + 1][k : k + 1] * tail1
            stack.append(jnp.where(lower, from_low, from_high))
    while len(stack) % 8:
        stack.append(jnp.zeros((1, LANES), jnp.float32))
    stack = jnp.concatenate(stack, axis=0)
    first = stack.astype(jnp.bfloat16).astype(jnp.float32)
    entering[...] = jnp.concatenate([first, stack - first, first], axis=0)

    cell = me_y * wy
    columns[0:LANES, 0:32] = transposed(factors, cell // LANES)
    start = lax.rem(cell, LANES)
    row = lax.broadcasted_iota(jnp.int32, (wy, LANES), 0)
    extra_row = lax.broadcasted_iota(jnp.int32, (EXTRA, LANES), 0)
    unit = (1.0, 0.0, 0.0, 1.0)

    def head(number):
        return tuple(columns[pl.ds(start, 1), number + k : number + k + 1] for k in range(4))

    def tail(number):
        return tuple(columns[pl.ds(start + wy - 1, 1), number + k : number + k + 1] for k in range(4))

    past_up, past_down = mm(head(12), head(20)), mm(tail(16), tail(24))
    for column in range(2):
        for output, number in ((column, 20), (2 + column, 24)):
            even = columns[pl.ds(start, wy), number + column : number + column + 1]
            odd = columns[pl.ds(start, wy), number + 2 + column : number + 3 + column]
            weights_y[output, 0:wy, :] = jnp.where((row & 1) == 0, even, odd)
        for output, early, late in (
            (column, (past_up[column], past_up[2 + column]), (unit[column], unit[2 + column])),
            (2 + column, (unit[column], unit[2 + column]), (past_down[column], past_down[2 + column])),
        ):
            value = jnp.zeros((EXTRA, LANES), jnp.float32)
            for r, v in enumerate(early + late):
                value = jnp.where(extra_row == r, v, value)
            weights_y[output, wy : wy + EXTRA, :] = value

    total = planes * (wy + EXTRA)

    def solve(begin, size):
        rows = slice(begin, begin + size)
        both = matmul(high[rows, :], matrix[...])
        value = both[:, 0:LANES] + (both[:, LANES : 2 * LANES] + matmul(low[rows, :], matrix[:, 0:LANES]))
        local[rows, :] = value
        return value

    extra = solve(planes * wy, planes * EXTRA)
    for part in range(planes // 8):
        core = solve(part * 8 * wy, 8 * wy)
        for number in range(4):
            lines = []
            for k in range(8):
                index = part * 8 + k
                value = jnp.sum(core[k * wy : (k + 1) * wy] * weights_y[number, 0:wy, :], axis=0, keepdims=True)
                past = extra[index * EXTRA : (index + 1) * EXTRA] * weights_y[number, wy : wy + EXTRA, :]
                lines.append(value + jnp.sum(past, axis=0, keepdims=True))
            start = number * planes + part * 8
            moments[start : start + 8, :] = jnp.concatenate(lines, axis=0)


def start_y(cell):
    return lax.rem(cell, LANES)


def y_kernel(count_y, wy, chains, factors, unused, inverse_y, coefs, columns, stacked):
    me_y = lax.axis_index("gy")
    cell = me_y * wy
    columns[0:LANES, 0:32] = transposed(factors, cell // LANES)
    start = lax.rem(cell, LANES)
    inverse_y[...] = dense_inverse(columns, start, wy, stacked)

    up, down = ([], [], []), ([], [], [])
    plan = stage_plan(count_y)
    for number, (stride, radix) in enumerate(plan):
        group = me_y // stride
        first = (group // radix) * radix
        others = [first + jnp.bitwise_xor(group - first, k) for k in range(radix)]
        for other in others[1:]:
            for lists, values in (
                (up, ((other + 1) * stride, me_y, truth(other < group))),
                (down, (me_y + 1, other * stride, truth(other > group))),
            ):
                for one, value in zip(lists, values):
                    one.append(value)
        if number + 1 < len(plan):
            for other in others:
                for lists, values in (
                    (up, ((other + 1) * stride, (first + radix) * stride, 1.0)),
                    (down, (first * stride, other * stride, 1.0)),
                ):
                    for one, value in zip(lists, values):
                        one.append(value)

    def place(block):
        return block * wy // LANES, block * wy % LANES

    def place_end(block):
        return place(block)[0], place(block)[1] + wy - 1

    for base, value in (
        (0, chain_products(chains, 0, place, count_y, *up, False)),
        (4, chain_products(chains, 4, place_end, count_y, *down, True)),
    ):
        for k in range(4):
            coefs[base + k] = value[k]


def pair_kernel(own, received, unused, total):
    total[...] = own[2:4] + received[2:4]


def arrived_rows(messages, count):
    rows = [m[0:2] for m in messages]
    if count > 2 * len(messages):
        rows.append(jnp.zeros((count - 2 * len(messages), rows[0].shape[1]), jnp.float32))
    return jnp.concatenate(rows, axis=0)


def third_kernel(moments, spread_high, spread_low, entering, *refs):
    messages, carried = refs[:-1], refs[-1]
    count = entering.shape[0] // 3
    received = arrived_rows(messages, count)
    first = received.astype(jnp.bfloat16).astype(jnp.float32)
    both = jnp.concatenate([first, received - first], axis=0).astype(jnp.bfloat16)
    top = jnp.concatenate([first, jnp.zeros_like(first)], axis=0).astype(jnp.bfloat16)
    across = (((1,), (1,)), ((), ()))
    corner = matmul(spread_high[...], both, across) + matmul(spread_low[...], top, across)
    values = entering[0:count, :] + entering[count : 2 * count, :]
    added = lax.dot_general(
        corner,
        jnp.concatenate([values, values], axis=0),
        (((1,), (0,)), ((), ())),
        precision=lax.Precision.HIGHEST,
        preferred_element_type=jnp.float32,
    )
    planes = carried.shape[1]
    for number in range(4):
        rows = slice(number * planes, (number + 1) * planes)
        carried[number] = moments[rows, :] + added[rows]


def local_y_kernel(wy, local, entering, inverse_y, unused, *refs):
    messages, (out, solved) = refs[:-2], refs[-2:]
    planes = out.shape[0]
    count = entering.shape[0] // 3
    received = arrived_rows(messages, count)
    first = received.astype(jnp.bfloat16).astype(jnp.float32)
    received = jnp.concatenate([first, first, received - first], axis=0).T.astype(jnp.bfloat16)
    solved[...] = local[...] + matmul(received, entering[...].astype(jnp.bfloat16))
    first, second = halves(inverse_y[:, 0 : wy + EXTRA])
    left = jnp.concatenate([first, second, first], axis=1)

    def part(index, carry):
        for k in range(8):
            number = index * 8 + k
            start = pl.multiple_of(number * wy, 8)
            core = solved[pl.ds(start, wy), :]
            start = pl.multiple_of(planes * wy + number * EXTRA, 8)
            both = jnp.concatenate([core, solved[pl.ds(start, EXTRA), :]], axis=0)
            top, rest = halves(both)
            out[number] = matmul(left, jnp.concatenate([top, top, rest], axis=0))
        return carry

    lax.fori_loop(0, planes // 8, part, 0)


def combine(coefs, side, row, values):
    first = 0 if side == 0 else 2
    out = [None, None]
    for k, value in enumerate(values):
        for q in range(2):
            for p in range(2):
                term = coefs[side + 2 * p + q, row + k : row + k + 1, :] * value[first + p]
                out[q] = term if out[q] is None else out[q] + term
    return out


def stage_kernel(base, stride, radix, narrow, has_entered, coefs, *refs):
    values = (refs[0],) + tuple(refs[1:radix][::-1])
    position = radix
    entered = None
    if has_entered:
        entered = refs[position]
        position += 1
    message, entering = refs[position : position + 2]
    below = combine(coefs, 0, base, values[1:])
    above = combine(coefs, 4, base, values[1:])
    for row, value in enumerate(below + above):
        entering[row] = value if entered is None else value + entered[row]
    upward = combine(coefs, 0, base + radix - 1, values)
    downward = combine(coefs, 4, base + radix - 1, values)
    if narrow:
        group = lax.axis_index("gy") // (stride * radix)
        sends_up = lax.rem(group, 2) == 0
        for row in range(2):
            message[row] = jnp.where(sends_up, upward[row], downward[row])
    else:
        for row, value in enumerate(upward + downward):
            message[row] = value


def last_kernel(base, radix, narrow, wy, coefs, local, inverse_y, entered, *refs):
    messages, (out_hbm, out, sent) = refs[: radix - 1], refs[radix - 1 :]
    values = list(messages)
    if narrow:
        values = [(m[0], m[1], m[0], m[1]) for m in values]
    below = combine(coefs, 0, base, values)
    above = combine(coefs, 4, base, values)
    st = [value + entered[row] for row, value in enumerate(below + above)]
    sides = [
        jnp.broadcast_to(inverse_y[:, c : c + 1], (wy, LANES)) for c in (0, 1, wy - 2, wy - 1)
    ]
    fields, planes_x = out.shape[:2]
    copies = []
    for field in range(fields):
        for x in range(planes_x):
            index = field * planes_x + x
            value = local[index]
            for number in range(4):
                value = value + sides[number] * st[number][index : index + 1]
            out[field, x] = value
            if (x + 1) % 4 == 0:
                part = (field, pl.ds(x - 3, 4))
                copy = pltpu.make_async_copy(out.at[part], out_hbm.at[part], sent.at[len(copies)])
                copy.start()
                copies.append(copy)
    for copy in copies:
        copy.wait()


VMEM = pl.BlockSpec(memory_space=pltpu.VMEM)
HBM = pl.BlockSpec(memory_space=pltpu.HBM)
SMEM = pl.BlockSpec(memory_space=pltpu.SMEM)
PARAMS = pltpu.CompilerParams(vmem_limit_bytes=40 * 1024 * 1024)


def array(*shape):
    return jax.ShapeDtypeStruct(shape, jnp.float32)


def in_hbm(x):
    return pltpu.with_memory_space_constraint(x, pltpu.HBM)


def cost(flops, data):
    return pl.CostEstimate(flops=flops, bytes_accessed=data, transcendentals=0)


def on_device(mesh, flow, speed, metric_y, metric_z):
    fields, planes_x, wy, wz = flow.shape
    count_y, count_z = mesh.shape["gy"], mesh.shape["gz"]
    assert wz == LANES
    ny, nz = metric_y.shape[0] // LANES, metric_z.shape[0] // LANES
    planes = fields * planes_x
    rows = planes * (wy + EXTRA)
    partners = count_z - 1
    paired = count_z == 4
    arrivals = 2 if paired else partners
    entering_rows = -(-2 * arrivals // 8) * 8
    half = jax.ShapeDtypeStruct((rows, 2 * LANES), jnp.bfloat16)
    outputs = pl.pallas_call(
        functools.partial(first_kernel, ny, nz, partners, paired),
        out_shape=[half, half, array(28, ny + nz, LANES), array(8, ny + nz, LANES)]
        + ([array(4, rows)] if paired else [array(2, rows)] * partners),
        in_specs=[HBM] * 4,
        out_specs=[VMEM] * (5 if paired else 4 + partners),
        scratch_shapes=[
            pltpu.VMEM(flow.shape, jnp.float32),
            pltpu.VMEM(speed.shape, jnp.float32),
            pltpu.VMEM((ny + nz, LANES), jnp.float32),
            pltpu.VMEM((planes_x, 3, wy + 16, LANES), jnp.float32),
            pltpu.SemaphoreType.DMA((fields + 3,)),
        ],
        compiler_params=PARAMS,
        name="forcing_and_factor",
    )(*(in_hbm(x) for x in (flow, speed, metric_y.reshape(ny, LANES), metric_z.reshape(nz, LANES))))
    high, low, factors, chains = outputs[:4]

    def exchange(values, axis, count, stride, radix):
        received = {}
        for k in reversed(range(1, radix)):
            pairs = [(i, i ^ (k * stride)) for i in range(count)]
            received[k] = lax.ppermute(values[k - 1], axis, pairs)
        return [received[k] for k in range(1, radix)]

    plan = stage_plan(count_y)
    work = [pltpu.VMEM((LANES + 16, LANES), jnp.float32)] * 2
    spread = jax.ShapeDtypeStruct((4 * planes, rows), jnp.bfloat16)
    matrix, spread_high, spread_low = pl.pallas_call(
        functools.partial(inverse_z_kernel, ny, planes, wy),
        out_shape=[jax.ShapeDtypeStruct((2 * LANES, 2 * LANES), jnp.bfloat16), spread, spread],
        in_specs=[VMEM],
        out_specs=[VMEM] * 3,
        scratch_shapes=work + [pltpu.VMEM((2 * LANES, LANES), jnp.float32)],
        compiler_params=PARAMS,
        cost_estimate=cost(rows * 1024, 4 * rows * 64),
        name="inverse_z",
    )(factors)
    if paired:
        near = exchange(outputs[4:], "gz", count_z, 1, 2)
        total = pl.pallas_call(
            pair_kernel,
            out_shape=array(2, rows),
            in_specs=[VMEM] * 2 + [HBM],
            out_specs=VMEM,
            compiler_params=PARAMS,
            name="join_pair",
        )(outputs[4], near[0], matrix)
        received = near + exchange([total], "gz", count_z, 2, 2)
    else:
        received = exchange(outputs[4:], "gz", count_z, 1, count_z)
    local, moments, entering = pl.pallas_call(
        functools.partial(second_kernel, ny, nz, count_z, wy, partners, paired),
        out_shape=[
            array(rows, LANES),
            array(4 * planes, LANES),
            array(3 * entering_rows, LANES),
        ],
        in_specs=[SMEM] + [VMEM] * 4,
        out_specs=[VMEM] * 3,
        scratch_shapes=[
            pltpu.VMEM((LANES + 16, LANES), jnp.float32),
            pltpu.VMEM((4, wy + EXTRA, LANES), jnp.float32),
        ],
        compiler_params=PARAMS,
        cost_estimate=cost(2 * rows * 256 * 128 * 6, 4 * rows * 384),
        name="local_z",
    )(chains, factors, matrix, high, low)
    carried = pl.pallas_call(
        third_kernel,
        out_shape=array(4, planes, LANES),
        in_specs=[VMEM] * (4 + arrivals),
        out_specs=VMEM,
        compiler_params=PARAMS,
        name="carried_y",
    )(moments, spread_high, spread_low, entering, *received)
    arrived = received

    narrow = plan[-1][1] == 2 and len(plan) > 1
    base, entered, result = 0, None, None
    for number, (stride, radix) in enumerate(plan):
        received = exchange([carried] * (radix - 1), "gy", count_y, stride, radix)
        if number == 0:
            entries = sum(2 * radix - 1 for _, radix in plan[:-1]) + plan[-1][1] - 1
            inverse_y, coefs = pl.pallas_call(
                functools.partial(y_kernel, count_y, wy),
                out_shape=[array(wy, LANES), array(8, -(-entries // 8) * 8, LANES)],
                in_specs=[SMEM, VMEM, HBM],
                out_specs=[VMEM] * 2,
                scratch_shapes=work,
                compiler_params=PARAMS,
                cost_estimate=cost(2 * rows * 128 * 128 * 6, 4 * rows * 256),
                name="inverse_y",
            )(chains, factors, carried)
        if number + 1 < len(plan):
            slim = narrow and number + 2 == len(plan)
            inputs = [carried] + received[::-1] + ([entered] if entered is not None else [])
            carried, entered = pl.pallas_call(
                functools.partial(stage_kernel, base, stride, radix, slim, entered is not None),
                out_shape=[array(2 if slim else 4, planes, LANES), array(4, planes, LANES)],
                in_specs=[VMEM] * (1 + len(inputs)),
                out_specs=[VMEM] * 2,
                compiler_params=PARAMS,
                name="join_groups",
            )(coefs, *inputs)
            base += 2 * radix - 1
            if number == 0:
                result = pl.pallas_call(
                    functools.partial(local_y_kernel, wy),
                    out_shape=array(planes, wy, LANES),
                    in_specs=[VMEM] * 3 + [HBM] + [VMEM] * arrivals,
                    out_specs=VMEM,
                    scratch_shapes=[pltpu.VMEM((rows, LANES), jnp.float32)],
                    compiler_params=PARAMS,
                    cost_estimate=cost(2 * rows * 128 * 128 * 6, 4 * rows * 256),
                    name="local_y",
                )(local, entering, inverse_y, entered, *arrived)
        else:
            return pl.pallas_call(
                functools.partial(last_kernel, base, radix, narrow, wy),
                out_shape=array(fields, planes_x, wy, wz),
                in_specs=[VMEM] * (4 + len(received)),
                out_specs=HBM,
                scratch_shapes=[
                    pltpu.VMEM(flow.shape, jnp.float32),
                    pltpu.SemaphoreType.DMA((planes // 4,)),
                ],
                compiler_params=PARAMS,
                name="finish_y",
            )(coefs, result, inverse_y, entered, *received)


def solution(mesh):
    placed = (P(None, None, "gy", "gz"), P(None, "gy", "gz"), P(), P())
    return jax.shard_map(
        functools.partial(on_device, mesh),
        mesh=mesh,
        in_specs=placed,
        out_specs=P(None, None, "gy", "gz"),
        check_vma=False,
    )
```

```python
import functools

import jax
import jax.numpy as jnp
from jax import lax
from jax.experimental import pallas as pl
from jax.experimental.pallas import tpu as pltpu
from jax.sharding import PartitionSpec as P

viscous = 0.25
explicit_fourth = 0.04
implicit_fourth = 0.05
time_step = 1048576.0
LANES = 128
EXTRA = 8


def mm(a, b):
    return (
        a[0] * b[0] + a[1] * b[2],
        a[0] * b[1] + a[1] * b[3],
        a[2] * b[0] + a[3] * b[2],
        a[2] * b[1] + a[3] * b[3],
    )


def inverse_of_one_minus(a):
    p, q, r, s = 1.0 - a[0], -a[1], -a[2], 1.0 - a[3]
    d = 1.0 / (p * s - q * r)
    return (s * d, -q * d, -r * d, p * d)


def pick(condition, a, b):
    return tuple(jnp.where(condition, x, y) for x, y in zip(a, b))


def halves(x):
    high = x.astype(jnp.bfloat16)
    return high, (x - high.astype(jnp.float32)).astype(jnp.bfloat16)


def matmul(a, b, dims=(((1,), (0,)), ((), ()))):
    return lax.dot_general(a, b, dims, preferred_element_type=jnp.float32)


def scan(m, ahead, count, step, shift, product):
    unit = (1.0, 0.0, 0.0, 1.0)

    def moved(by):
        return tuple(jnp.where(ahead >= by, shift(x, by), u) for x, u in zip(m, unit))

    while step < count:
        if 2 * step < count:
            m = product(product(m, moved(step)), product(moved(2 * step), moved(3 * step)))
            step *= 4
        else:
            m = product(m, moved(step))
            step *= 2
    return m


def lane_roll(x, by):
    return pltpu.roll(x, by % LANES, 1)


def row_roll(x, by):
    by = by % x.shape[0]
    return jnp.concatenate([x[x.shape[0] - by :], x[: x.shape[0] - by]], axis=0)


class Factor:
    def __init__(self, metric, ny, nz, wy):
        self.ny, self.nz, self.wy, self.rows = ny, nz, wy, ny + nz
        self.lane = lax.broadcasted_iota(jnp.int32, (self.rows, LANES), 1)
        self.row = lax.broadcasted_iota(jnp.int32, (self.rows, LANES), 0)
        self.block = jnp.where(self.row < ny, self.row, self.row - ny)
        self.to_end = jnp.where(self.row < ny, ny, nz) - 1 - self.block
        first = (self.lane == 0) & (self.block == 0)
        last = (self.lane == LANES - 1) & (self.to_end == 0)
        self.face_low = 0.5 * (jnp.where(first, metric, self.before(metric, 1)) + metric)
        self.face_high = 0.5 * (metric + jnp.where(last, metric, self.after(metric, 1)))

    def before(self, x, by):
        rolled = lane_roll(x, by)
        value = jnp.where(self.lane < by, row_roll(rolled, 1), rolled)
        return jnp.where((self.lane < by) & (self.block == 0), 0.0, value)

    def after(self, x, by):
        rolled = lane_roll(x, -by)
        value = jnp.where(self.lane >= LANES - by, row_roll(rolled, -1), rolled)
        return jnp.where((self.lane >= LANES - by) & (self.to_end == 0), 0.0, value)

    def guess(self, sign):
        face = self.face_high if sign > 0 else self.face_low
        if sign > 0:
            cell = self.lane + LANES * self.block
        else:
            cell = LANES - 1 - self.lane + LANES * self.to_end
        near = face / (cell + 1).astype(jnp.float32)
        one_over = 1.0 / (face + jnp.sqrt(face + near * near))
        return face * one_over, implicit_fourth * one_over, one_over

    def sweep(self, sign, ratio, far):
        rows = self.rows
        back = self.before if sign > 0 else self.after
        if sign > 0:
            face_in, face_out, place = self.face_low, self.face_high, self.block
        else:
            face_in, face_out, place = self.face_high, self.face_low, self.to_end
        eps = 4.0 * implicit_fourth - implicit_fourth * back(ratio, 1)
        mass = (1.0 + 6.0 * implicit_fourth) - implicit_fourth * back(far, 2) - 2.0 * eps
        eps_in = back(eps, 1)
        scale = 1.0 / (face_in + 2.0 * eps_in)
        m = ((mass + face_in) * scale, mass - eps_in * eps_in * scale, scale, jnp.ones_like(scale))
        ahead = self.lane if sign > 0 else LANES - 1 - self.lane
        m = scan(m, ahead, LANES, 1, lambda x, by: lane_roll(x, sign * by), mm)
        edge = LANES - 1 if sign > 0 else 0
        total = tuple(jnp.broadcast_to(x[:, edge : edge + 1], (rows, LANES)) for x in m)
        total = scan(
            total, place, max(self.ny, self.nz), 1, lambda x, by: row_roll(x, sign * by), mm
        )
        top = jnp.where(place >= 1, row_roll(total[0], sign), 1.0)
        low = jnp.where(place >= 1, row_roll(total[2], sign), 0.0)
        eta = (m[0] * top + m[1] * low) / (m[2] * top + m[3] * low)
        one_over = 1.0 / (face_out + (eta + 2.0 * eps))
        return (face_out + eps) * one_over, implicit_fourth * one_over, one_over

    def finish(self, near_l, far_l, pivot_l, near_r, far_r):
        lane, block, to_end = self.lane, self.block, self.to_end
        even = (lane & 1) == 0
        near_l = jnp.where((to_end == 0) & (lane >= LANES - 1), 0.0, near_l)
        far_l = jnp.where((to_end == 0) & (lane >= LANES - 2), 0.0, far_l)
        near_r = jnp.where((block == 0) & (lane < 1), 0.0, near_r)
        far_r = jnp.where((block == 0) & (lane < 2), 0.0, far_r)

        def of_even(x):
            return jnp.where(even, x, lane_roll(x, 1))

        def of_odd(x):
            return jnp.where(even, lane_roll(x, -1), x)

        t0, t1, r0, r1 = of_even(near_l), of_odd(near_l), of_even(far_l), of_odd(far_l)
        from_right = (t0 * t1 - r0, -t0 * r1, t1, -r1)
        p1 = of_odd(pivot_l)
        left_inverse = (of_even(pivot_l) + t0 * t0 * p1, t0 * p1, t0 * p1, p1)
        s0, s1, q0, q1 = of_even(near_r), of_odd(near_r), of_even(far_r), of_odd(far_r)
        from_left = (-q0, s0, -s1 * q0, s1 * s0 - q1)
        from_left_after = tuple(self.after(x, 2) for x in from_left)
        from_right_before = tuple(self.before(x, 2) for x in from_right)
        diagonal = mm(inverse_of_one_minus(mm(from_right, from_left_after)), left_inverse)
        width = jnp.where(self.row < self.ny, self.wy, LANES)
        place = lane & (width - 1)
        right = scan(from_right, width - 1 - place, LANES, 2, lambda x, by: lane_roll(x, -by), mm)
        left = scan(from_left, place, LANES, 2, lane_roll, mm)
        return from_right, from_left, diagonal, right, left, from_right_before, from_left_after


def cell_weights(chain, column, even):
    return jnp.where(even, chain[column], chain[2 + column])


def first_kernel(ny, nz, partners, paired, flow_hbm, speed_hbm, metric_y, metric_z, *refs):
    high, low, factors, chains = refs[:4]
    count = 1 if paired else partners
    messages = refs[4 : 4 + count]
    flow, speed, metric, spread, arrived = refs[4 + count :]
    fields, planes_x, wy, _ = flow.shape
    rows = ny + nz
    core_rows = fields * planes_x * wy

    copies = [
        pltpu.make_async_copy(metric_y, metric.at[0:ny], arrived.at[fields]),
        pltpu.make_async_copy(metric_z, metric.at[ny:rows], arrived.at[fields + 1]),
        pltpu.make_async_copy(speed_hbm, speed, arrived.at[fields + 2]),
    ]
    for copy in copies:
        copy.start()
    for field in range(fields):
        pltpu.make_async_copy(flow_hbm.at[field], flow.at[field], arrived.at[field]).start()

    lane = lax.broadcasted_iota(jnp.int32, (wy, LANES), 1)
    extra_row = lax.broadcasted_iota(jnp.int32, (EXTRA, LANES), 0)
    for slot in range(planes_x):
        for part in range(3):
            spread[slot, part, 0:8, :] = jnp.zeros((8, LANES), jnp.float32)
            spread[slot, part, wy + 8 : wy + 16, :] = jnp.zeros((8, LANES), jnp.float32)
    side = time_step * (viscous + 4.0 * explicit_fourth)
    half = time_step * 0.5
    centre = time_step * (-6.0 * viscous - 12.0 * explicit_fourth)
    fourth = -time_step * explicit_fourth

    def store(start, column, value):
        first, second = halves(value)
        high[pl.ds(start, value.shape[0]), column : column + LANES] = first
        low[pl.ds(start, value.shape[0]), column : column + LANES] = second

    def one_field(field):
        values = [flow[field, x] for x in range(planes_x)]
        fluxes = [values[x] * speed[x] for x in range(planes_x)]
        aside = [(time_step * viscous) * u for u in values]
        extras = []
        for x in range(planes_x):
            u, flux, slot = values[x], fluxes[x], x
            total = centre * u
            if x + 1 < planes_x:
                total = total + (aside[x + 1] - fluxes[x + 1])
            if x > 0:
                total = total + (aside[x - 1] + fluxes[x - 1])
            scaled = side * u
            onward, backward, far = scaled + flux, scaled - flux, fourth * u
            spread[slot, 0, 8 : wy + 8, :] = onward
            spread[slot, 1, 8 : wy + 8, :] = backward
            spread[slot, 2, 8 : wy + 8, :] = far
            total = total + (spread[slot, 0, 7 : wy + 7, :] + spread[slot, 1, 9 : wy + 9, :])
            total = total + (spread[slot, 2, 6 : wy + 6, :] + spread[slot, 2, 10 : wy + 10, :])
            a, b = lane_roll(onward, 1), lane_roll(backward, -1)
            c, d = lane_roll(far, 2), lane_roll(far, -2)
            from_low, from_high = a + c, b + d
            ends = jnp.where(lane == 0, from_low, jnp.where(lane == 1, c, 0.0))
            ends = jnp.where(lane == LANES - 1, from_high, jnp.where(lane == LANES - 2, d, ends))
            index = field * planes_x + x
            start = index * wy
            store(start, 0, total + (from_low + from_high))
            store(start, LANES, ends)
            above = spread[slot, 1, 7:15, :] + spread[slot, 2, 8:16, :]
            below = spread[slot, 0, wy + 5 : wy + 13, :] + spread[slot, 2, wy + 4 : wy + 12, :]
            extras.append(jnp.where(extra_row < 2, above, jnp.where(extra_row < 4, below, 0.0)))
            if len(extras) == 2:
                start = core_rows + (index - 1) * EXTRA
                store(start, 0, jnp.concatenate(extras, axis=0))
                for ref in (high, low):
                    ref[pl.ds(start, 2 * EXTRA), LANES : 2 * LANES] = jnp.zeros(
                        (2 * EXTRA, LANES), jnp.bfloat16
                    )
                extras = []

    copies[0].wait()
    copies[1].wait()
    factor = Factor(metric[...], ny, nz, wy)

    guess_l, guess_r = factor.guess(1), factor.guess(-1)
    left, right = factor.sweep(1, *guess_l[:2]), factor.sweep(-1, *guess_r[:2])
    copies[2].wait()
    for x in range(planes_x):
        speed[x] = half * speed[x]
    for field in range(fields):
        pltpu.make_async_copy(flow_hbm.at[field], flow.at[field], arrived.at[field]).wait()
    left, right = factor.sweep(1, *left[:2]), factor.sweep(-1, *right[:2])
    for field in range(fields // 2):
        one_field(field)
    parts = factor.finish(*left, *right[:2])
    from_right, from_left, diagonal, to_right, to_left, before, after = parts
    for number, value in enumerate(v for part in parts for v in part):
        factors[number] = value
    for number, value in enumerate(to_right + to_left):
        chains[number] = value
    for field in range(fields // 2, fields):
        one_field(field)

    me = lax.axis_index("gz")
    mine = lax.broadcasted_iota(jnp.int32, (rows, LANES), 0) == ny + me
    even = (lax.broadcasted_iota(jnp.int32, (1, LANES), 1) & 1) == 0
    lane = lax.broadcasted_iota(jnp.int32, (1, LANES), 1)

    def own(values):
        return tuple(jnp.sum(jnp.where(mine, v, 0.0), axis=0, keepdims=True) for v in values)

    up, down = own(to_right), own(to_left)
    up_past, down_past = own(mm(before, to_right)), own(mm(after, to_left))
    unit = (1.0, 0.0, 0.0, 1.0)
    weights = []
    for column in range(2):
        same = jnp.where(even, unit[column], unit[2 + column])
        inside_up = cell_weights(up, column, even)
        inside_down = cell_weights(down, column, even)
        past_up = lane_roll(cell_weights(up_past, column, even), -2)
        past_down = lane_roll(cell_weights(down_past, column, even), 2)
        ends_up = jnp.where(lane < 2, same, past_up) - inside_up
        ends_down = jnp.where(lane < 2, past_down, same) - inside_down
        at_end = (lane < 2) | (lane >= LANES - 2)
        ends_up, ends_down = jnp.where(at_end, ends_up, 0.0), jnp.where(at_end, ends_down, 0.0)
        weights.append(
            (
                jnp.concatenate([inside_up, ends_up], axis=1),
                jnp.concatenate([inside_down, ends_down], axis=1),
            )
        )
    if paired:
        lower = (me & 1) == 0
        stack = [jnp.where(lower, w[0], w[1]) for w in weights]
        peer = lax.broadcasted_iota(jnp.int32, (rows, LANES), 0) == ny + jnp.bitwise_xor(me, 1)

        def of_peer(values, place):
            chosen = tuple(jnp.sum(jnp.where(peer, v, 0.0), axis=0, keepdims=True) for v in values)
            return tuple(jnp.broadcast_to(v[:, place : place + 1], (1, 2 * LANES)) for v in chosen)

        over, under = of_peer(to_right, 0), of_peer(to_left, LANES - 1)
        (up0, down0), (up1, down1) = weights
        for q in range(2):
            upward = jnp.where(lower, over[q] * up0 + over[2 + q] * up1, weights[q][0])
            downward = jnp.where(lower, weights[q][1], under[q] * down0 + under[2 + q] * down1)
            stack.append(jnp.where(me < 2, upward, downward))
    else:
        stack = []
        for k in range(1, partners + 1):
            upward = jnp.bitwise_xor(me, k) > me
            stack += [jnp.where(upward, w[0], w[1]) for w in weights]
    while len(stack) % 8:
        stack.append(jnp.zeros((1, 2 * LANES), jnp.float32))
    count = len(stack)
    stack = jnp.concatenate(stack, axis=0)
    first = stack.astype(jnp.bfloat16).astype(jnp.float32)
    both = jnp.concatenate([first, stack - first], axis=0).astype(jnp.bfloat16)
    across = (((1,), (1,)), ((), ()))
    total = high.shape[0]
    size = planes_x * wy
    for begin in range(0, total, size):
        rows = slice(begin, min(begin + size, total))
        on_high = matmul(both, high[rows, :], across)
        on_low = matmul(both, low[rows, :], across)
        moments = (on_high[:count] + on_high[count:]) + on_low[:count]
        if paired:
            messages[0][:, rows] = moments[0:4]
        else:
            for k in range(partners):
                messages[k][:, rows] = moments[2 * k : 2 * k + 2]


def dense_inverse(columns, start, width, stack):
    parts = 8
    steps = width // (2 * parts)
    lane = lax.broadcasted_iota(jnp.int32, (parts, LANES), 1)
    part = lax.broadcasted_iota(jnp.int32, (parts, LANES), 0)
    fits = width + 4 <= LANES
    values = [columns[pl.ds(start + 2 * i, parts, stride=2 * steps), :] for i in range(steps)]

    def wide(i, number):
        return tuple(
            jnp.broadcast_to(values[i][:, number + k : number + k + 1], (parts, LANES)) for k in range(4)
        )

    blocks = [wide(i, 8) for i in range(steps)]
    zero, one = jnp.zeros((parts, LANES), jnp.float32), jnp.ones((parts, LANES), jnp.float32)

    def put(rows, i, extra, extra_lane, owner):
        first = 2 * (part * steps + i)
        out = []
        for r in range(2):
            row = jnp.where(lane == first, blocks[i][2 * r], rows[r])
            row = jnp.where(lane == first + 1, blocks[i][2 * r + 1], row)
            if extra is not None and fits:
                row = jnp.where((part == owner) & (lane == extra_lane), extra[2 * r], row)
                row = jnp.where((part == owner) & (lane == extra_lane + 1), extra[2 * r + 1], row)
            out.append(row)
        return tuple(out)

    def run(order, number, ends, extra_lane, owner):
        rows, product, out = (zero, zero), (one, zero, zero, one), {}
        for i in order:
            t = wide(i, number)
            rows = (t[0] * rows[0] + t[1] * rows[1], t[2] * rows[0] + t[3] * rows[1])
            extra = None
            if i == order[0]:
                e = wide(i, ends)
                extra = mm(blocks[i], (e[0], e[2], e[1], e[3]))
            rows = put(rows, i, extra, extra_lane, owner)
            product = mm(t, product)
            out[i] = rows, product
        rows, product = out[order[-1]]
        entering, last = [None] * parts, (jnp.zeros((1, LANES), jnp.float32),) * 2
        sequence = range(parts) if number == 4 else range(parts - 1, -1, -1)
        for p in sequence:
            entering[p] = last
            own, across = [r[p : p + 1] for r in rows], [x[p : p + 1] for x in product]
            last = (
                own[0] + across[0] * last[0] + across[1] * last[1],
                own[1] + across[2] * last[0] + across[3] * last[1],
            )
        entering = [jnp.concatenate([e[r] for e in entering], axis=0) for r in range(2)]
        result = []
        for i in range(steps):
            rows, product = out[i]
            for r in range(2):
                result.append(rows[r] + product[2 * r] * entering[0] + product[2 * r + 1] * entering[1])
        return result

    low = run(list(range(steps)), 4, 12, width, 0)
    high = run(list(range(steps - 1, -1, -1)), 0, 16, width + 2, parts - 1)
    for k in range(2 * steps):
        lower = lane <= 2 * (part * steps + k // 2) + 1
        if fits:
            lower = lower & (lane < width) | ((lane >= width) & (lane < width + 2))
        stack[parts * k : parts * (k + 1), :] = jnp.where(lower, low[k], high[k])
    rows = [stack[pl.ds(p, 2 * steps, stride=parts), :] for p in range(parts)]
    return jnp.concatenate(rows, axis=0)


def stage_plan(count):
    plan, stride = [], 1
    while stride < count:
        radix = 4 if count // stride >= 4 else 2
        plan.append((stride, radix))
        stride *= radix
    return plan


def transposed(factors, row):
    rows = [factors[number, pl.ds(row, 1), :] for number in range(12)]
    rows += [factors[20 + number, pl.ds(row, 1), :] for number in range(8)]
    rows += [factors[12 + number, pl.ds(row, 1), :] for number in range(8)]
    rows.append(jnp.zeros((4, LANES), jnp.float32))
    return jnp.concatenate(rows, axis=0).T


def chain_products(chains, number, place, blocks, begins, ends, masks, reverse):
    count = -(-len(begins) // 8) * 8
    row = lax.broadcasted_iota(jnp.int32, (count, LANES), 0)
    begin = jnp.zeros((count, LANES), jnp.int32)
    end, mask = begin, jnp.zeros((count, LANES), jnp.float32)
    for r, (b, e, m) in enumerate(zip(begins, ends, masks)):
        begin, end = jnp.where(row == r, b, begin), jnp.where(row == r, e, end)
        mask = jnp.where(row == r, m, mask)
    one, zero = jnp.ones((count, LANES), jnp.float32), jnp.zeros((count, LANES), jnp.float32)
    product = (one, zero, zero, one)
    for block in range(blocks - 1, -1, -1) if reverse else range(blocks):
        where = place(block)
        value = tuple(chains[number + k, where[0], where[1]] for k in range(4))
        product = pick((begin <= block) & (block < end), mm(product, value), product)
    return tuple(x * mask for x in product)


def truth(condition):
    return jnp.where(condition, 1.0, 0.0)


def inverse_z_kernel(ny, planes, wy, factors, matrix, spread_high, spread_low, columns, stacked, rows_ref):
    me_z = lax.axis_index("gz")
    columns[0:LANES, 0:32] = transposed(factors, ny + me_z)
    inverse = dense_inverse(columns, 0, LANES, stacked)
    rows_ref[0:LANES, :] = inverse
    rows_ref[LANES : 2 * LANES, :] = jnp.zeros((LANES, LANES), jnp.float32)
    past = tuple(columns[LANES - 1 : LANES, 16 + k : 17 + k] for k in range(4))
    ahead = tuple(columns[0:1, 12 + k : 13 + k] for k in range(4))
    head0, head1 = rows_ref[0:1, :], rows_ref[1:2, :]
    tail0, tail1 = rows_ref[LANES - 2 : LANES - 1, :], rows_ref[LANES - 1 : LANES, :]
    for q in range(2):
        beyond = past[2 * q] * tail0 + past[2 * q + 1] * tail1
        rows_ref[LANES + q : LANES + q + 1, :] = beyond - (head0, head1)[q]
        beyond = ahead[2 * q] * head0 + ahead[2 * q + 1] * head1
        rows_ref[2 * LANES - 2 + q : 2 * LANES - 1 + q, :] = beyond - (tail0, tail1)[q]
    first, second = halves(rows_ref[...])
    matrix[:, 0:LANES] = first
    matrix[:, LANES : 2 * LANES] = second

    cell = lax.axis_index("gy") * wy
    row = cell // LANES
    total = planes * (wy + EXTRA)
    unit = (1.0, 0.0, 0.0, 1.0)
    lane = lax.broadcasted_iota(jnp.int32, (1, LANES), 1)
    even = (lane & 1) == 0

    def chain(number):
        return tuple(factors[number + k, pl.ds(row, 1), :] for k in range(4))

    def turned(x, by):
        return pltpu.roll(x, lax.rem(by + 2 * LANES, LANES), 1)

    def tiled(x, period):
        x = jnp.where(lane < period, x, 0.0)
        while period < LANES:
            x = x + lane_roll(x, period)
            period *= 2
        return x

    up, down, before, after = chain(12), chain(16), chain(20), chain(24)
    past_up, past_down = mm(before, up), mm(after, down)
    plane_row = lax.broadcasted_iota(jnp.int32, (planes, LANES), 0)
    wide_lane = lax.broadcasted_iota(jnp.int32, (planes, LANES), 1)
    for column in range(2):
        same = jnp.where(even, unit[column], unit[2 + column])
        for number, inside, early, late in (
            (column, up, turned(cell_weights(past_up, column, even), -start_y(cell)), same),
            (
                2 + column,
                down,
                same,
                turned(cell_weights(past_down, column, even), 4 - wy - start_y(cell)),
            ),
        ):
            inside = tiled(turned(cell_weights(inside, column, even), -start_y(cell)), wy)
            past = jnp.where(lane < 2, early, jnp.where(lane < 4, late, 0.0))
            past = tiled(past, EXTRA)
            rows = slice(number * planes, (number + 1) * planes)
            for begin in range(0, total, LANES):
                if begin < planes * wy:
                    owner, value = (begin + wide_lane) // wy, inside
                else:
                    owner, value = (begin - planes * wy + wide_lane) // EXTRA, past
                size = min(LANES, total - begin)
                first, second = halves(jnp.where(plane_row == owner, value, 0.0))
                spread_high[rows, begin : begin + size] = first[:, 0:size]
                spread_low[rows, begin : begin + size] = second[:, 0:size]


def whole_rows(matrix, row):
    start = row // 16 * 16
    both = matrix[start : start + 16, :].astype(jnp.float32)
    value = both[:, 0:LANES] + both[:, LANES : 2 * LANES]
    return value[row - start : row - start + 1]


def second_kernel(
    ny, nz, count_z, wy, partners, paired, chains, factors, matrix, high, low, local, moments, entering, *scratch
):
    columns, weights_y = scratch
    me_z, me_y = lax.axis_index("gz"), lax.axis_index("gy")
    planes = moments.shape[0] // 4
    head0, head1 = whole_rows(matrix, 0), whole_rows(matrix, 1)
    tail0, tail1 = whole_rows(matrix, LANES - 2), whole_rows(matrix, LANES - 1)

    if paired:
        pair = me_z // 2 * 2
        begins, ends = [me_z, pair], [me_z + 1, pair + 2]
        lowers = [me_z % 2 == 1, pair > 0]
    else:
        others = [jnp.bitwise_xor(me_z, k) for k in range(1, partners + 1)]
        begins, ends = [other + 1 for other in others], others
        lowers = [other < me_z for other in others]
    size = len(begins)
    up = chain_products(
        chains, 0, lambda b: (ny + b, 0), count_z, begins, [me_z] * size, [1.0] * size, False
    )
    down = chain_products(
        chains, 4, lambda b: (ny + b, LANES - 1), count_z, [me_z + 1] * size, ends, [1.0] * size, True
    )
    stack = []
    for k, lower in enumerate(lowers):
        for p in range(2):
            from_low = up[2 * p][k : k + 1] * head0 + up[2 * p + 1][k : k + 1] * head1
            from_high = down[2 * p][k : k + 1] * tail0 + down[2 * p + 1][k : k + 1] * tail1
            stack.append(jnp.where(lower, from_low, from_high))
    while len(stack) % 8:
        stack.append(jnp.zeros((1, LANES), jnp.float32))
    stack = jnp.concatenate(stack, axis=0)
    first = stack.astype(jnp.bfloat16).astype(jnp.float32)
    entering[...] = jnp.concatenate([first, stack - first, first], axis=0)

    cell = me_y * wy
    columns[0:LANES, 0:32] = transposed(factors, cell // LANES)
    start = lax.rem(cell, LANES)
    row = lax.broadcasted_iota(jnp.int32, (wy, LANES), 0)
    extra_row = lax.broadcasted_iota(jnp.int32, (EXTRA, LANES), 0)
    unit = (1.0, 0.0, 0.0, 1.0)

    def head(number):
        return tuple(columns[pl.ds(start, 1), number + k : number + k + 1] for k in range(4))

    def tail(number):
        return tuple(columns[pl.ds(start + wy - 1, 1), number + k : number + k + 1] for k in range(4))

    past_up, past_down = mm(head(12), head(20)), mm(tail(16), tail(24))
    for column in range(2):
        for output, number in ((column, 20), (2 + column, 24)):
            even = columns[pl.ds(start, wy), number + column : number + column + 1]
            odd = columns[pl.ds(start, wy), number + 2 + column : number + 3 + column]
            weights_y[output, 0:wy, :] = jnp.where((row & 1) == 0, even, odd)
        for output, early, late in (
            (column, (past_up[column], past_up[2 + column]), (unit[column], unit[2 + column])),
            (2 + column, (unit[column], unit[2 + column]), (past_down[column], past_down[2 + column])),
        ):
            value = jnp.zeros((EXTRA, LANES), jnp.float32)
            for r, v in enumerate(early + late):
                value = jnp.where(extra_row == r, v, value)
            weights_y[output, wy : wy + EXTRA, :] = value

    total = planes * (wy + EXTRA)

    def solve(begin, size):
        rows = slice(begin, begin + size)
        both = matmul(high[rows, :], matrix[...])
        value = both[:, 0:LANES] + (both[:, LANES : 2 * LANES] + matmul(low[rows, :], matrix[:, 0:LANES]))
        local[rows, :] = value
        return value

    extra = solve(planes * wy, planes * EXTRA)
    for part in range(planes // 8):
        core = solve(part * 8 * wy, 8 * wy)
        for number in range(4):
            lines = []
            for k in range(8):
                index = part * 8 + k
                value = jnp.sum(core[k * wy : (k + 1) * wy] * weights_y[number, 0:wy, :], axis=0, keepdims=True)
                past = extra[index * EXTRA : (index + 1) * EXTRA] * weights_y[number, wy : wy + EXTRA, :]
                lines.append(value + jnp.sum(past, axis=0, keepdims=True))
            start = number * planes + part * 8
            moments[start : start + 8, :] = jnp.concatenate(lines, axis=0)


def start_y(cell):
    return lax.rem(cell, LANES)


def y_kernel(count_y, wy, chains, factors, unused, inverse_y, coefs, columns, stacked):
    me_y = lax.axis_index("gy")
    cell = me_y * wy
    columns[0:LANES, 0:32] = transposed(factors, cell // LANES)
    start = lax.rem(cell, LANES)
    inverse_y[...] = dense_inverse(columns, start, wy, stacked)

    up, down = ([], [], []), ([], [], [])
    plan = stage_plan(count_y)
    for number, (stride, radix) in enumerate(plan):
        group = me_y // stride
        first = (group // radix) * radix
        others = [first + jnp.bitwise_xor(group - first, k) for k in range(radix)]
        for other in others[1:]:
            for lists, values in (
                (up, ((other + 1) * stride, me_y, truth(other < group))),
                (down, (me_y + 1, other * stride, truth(other > group))),
            ):
                for one, value in zip(lists, values):
                    one.append(value)
        if number + 1 < len(plan):
            for other in others:
                for lists, values in (
                    (up, ((other + 1) * stride, (first + radix) * stride, 1.0)),
                    (down, (first * stride, other * stride, 1.0)),
                ):
                    for one, value in zip(lists, values):
                        one.append(value)

    def place(block):
        return block * wy // LANES, block * wy % LANES

    def place_end(block):
        return place(block)[0], place(block)[1] + wy - 1

    for base, value in (
        (0, chain_products(chains, 0, place, count_y, *up, False)),
        (4, chain_products(chains, 4, place_end, count_y, *down, True)),
    ):
        for k in range(4):
            coefs[base + k] = value[k]


def pair_kernel(own, received, unused, total):
    total[...] = own[2:4] + received[2:4]


def arrived_rows(messages, count):
    rows = [m[0:2] for m in messages]
    if count > 2 * len(messages):
        rows.append(jnp.zeros((count - 2 * len(messages), rows[0].shape[1]), jnp.float32))
    return jnp.concatenate(rows, axis=0)


def third_kernel(moments, spread_high, spread_low, entering, *refs):
    messages, carried = refs[:-1], refs[-1]
    count = entering.shape[0] // 3
    received = arrived_rows(messages, count)
    first = received.astype(jnp.bfloat16).astype(jnp.float32)
    both = jnp.concatenate([first, received - first], axis=0).astype(jnp.bfloat16)
    top = jnp.concatenate([first, jnp.zeros_like(first)], axis=0).astype(jnp.bfloat16)
    across = (((1,), (1,)), ((), ()))
    corner = matmul(spread_high[...], both, across) + matmul(spread_low[...], top, across)
    values = entering[0:count, :] + entering[count : 2 * count, :]
    added = lax.dot_general(
        corner,
        jnp.concatenate([values, values], axis=0),
        (((1,), (0,)), ((), ())),
        precision=lax.Precision.HIGHEST,
        preferred_element_type=jnp.float32,
    )
    planes = carried.shape[1]
    for number in range(4):
        rows = slice(number * planes, (number + 1) * planes)
        carried[number] = moments[rows, :] + added[rows]


def local_y_kernel(wy, local, entering, inverse_y, unused, *refs):
    messages, (out, solved) = refs[:-2], refs[-2:]
    planes = out.shape[0]
    count = entering.shape[0] // 3
    received = arrived_rows(messages, count)
    first = received.astype(jnp.bfloat16).astype(jnp.float32)
    received = jnp.concatenate([first, first, received - first], axis=0).T.astype(jnp.bfloat16)
    solved[...] = local[...] + matmul(received, entering[...].astype(jnp.bfloat16))
    first, second = halves(inverse_y[:, 0 : wy + EXTRA])
    left = jnp.concatenate([first, second, first], axis=1)

    def part(index, carry):
        for k in range(8):
            number = index * 8 + k
            start = pl.multiple_of(number * wy, 8)
            core = solved[pl.ds(start, wy), :]
            start = pl.multiple_of(planes * wy + number * EXTRA, 8)
            both = jnp.concatenate([core, solved[pl.ds(start, EXTRA), :]], axis=0)
            top, rest = halves(both)
            out[number] = matmul(left, jnp.concatenate([top, top, rest], axis=0))
        return carry

    lax.fori_loop(0, planes // 8, part, 0)


def combine(coefs, side, row, values):
    first = 0 if side == 0 else 2
    out = [None, None]
    for k, value in enumerate(values):
        for q in range(2):
            for p in range(2):
                term = coefs[side + 2 * p + q, row + k : row + k + 1, :] * value[first + p]
                out[q] = term if out[q] is None else out[q] + term
    return out


def stage_kernel(base, stride, radix, narrow, has_entered, split, coefs, *refs):
    values = (refs[0],) + tuple(refs[1:radix][::-1])
    position = radix
    entered = None
    if has_entered:
        entered = refs[position]
        position += 1
    entering, messages = refs[position], refs[position + 1 :]
    below = combine(coefs, 0, base, values[1:])
    above = combine(coefs, 4, base, values[1:])
    for row, value in enumerate(below + above):
        entering[row] = value if entered is None else value + entered[row]
    upward = combine(coefs, 0, base + radix - 1, values)
    downward = combine(coefs, 4, base + radix - 1, values)
    if narrow:
        group = lax.axis_index("gy") // (stride * radix)
        sends_up = lax.rem(group, 2) == 0
        values = [jnp.where(sends_up, upward[row], downward[row]) for row in range(2)]
    else:
        values = upward + downward
    for row, value in enumerate(values):
        for message, (begin, end) in zip(messages, split):
            message[row] = value[begin:end]


def last_kernel(base, radix, narrow, wy, begin, end, has_out, coefs, local, inverse_y, entered, *refs):
    messages, (out_hbm, out, sent) = refs[: radix - 1], refs[radix - 1 + has_out :]
    planes_x = out.shape[1]
    rows = slice(begin * planes_x, end * planes_x)
    values = list(messages)
    if narrow:
        values = [(m[0], m[1], m[0], m[1]) for m in values]
    below = combine(coefs, 0, base, values)
    above = combine(coefs, 4, base, values)
    st = [value + entered[row, rows] for row, value in enumerate(below + above)]
    sides = [
        jnp.broadcast_to(inverse_y[:, c : c + 1], (wy, LANES)) for c in (0, 1, wy - 2, wy - 1)
    ]
    copies = []
    for field in range(begin, end):
        for x in range(planes_x):
            index = (field - begin) * planes_x + x
            value = local[field * planes_x + x]
            for number in range(4):
                value = value + sides[number] * st[number][index : index + 1]
            out[field - begin, x] = value
            if (x + 1) % 4 == 0:
                part = pl.ds(x - 3, 4)
                copy = pltpu.make_async_copy(
                    out.at[field - begin, part], out_hbm.at[field, part], sent.at[len(copies)]
                )
                copy.start()
                copies.append(copy)
    for copy in copies:
        copy.wait()


VMEM = pl.BlockSpec(memory_space=pltpu.VMEM)
HBM = pl.BlockSpec(memory_space=pltpu.HBM)
SMEM = pl.BlockSpec(memory_space=pltpu.SMEM)
PARAMS = pltpu.CompilerParams(vmem_limit_bytes=40 * 1024 * 1024)


def array(*shape):
    return jax.ShapeDtypeStruct(shape, jnp.float32)


def in_hbm(x):
    return pltpu.with_memory_space_constraint(x, pltpu.HBM)


def cost(flops, data):
    return pl.CostEstimate(flops=flops, bytes_accessed=data, transcendentals=0)


def on_device(mesh, flow, speed, metric_y, metric_z):
    fields, planes_x, wy, wz = flow.shape
    count_y, count_z = mesh.shape["gy"], mesh.shape["gz"]
    assert wz == LANES
    ny, nz = metric_y.shape[0] // LANES, metric_z.shape[0] // LANES
    planes = fields * planes_x
    rows = planes * (wy + EXTRA)
    partners = count_z - 1
    paired = count_z == 4
    arrivals = 2 if paired else partners
    entering_rows = -(-2 * arrivals // 8) * 8
    half = jax.ShapeDtypeStruct((rows, 2 * LANES), jnp.bfloat16)
    outputs = pl.pallas_call(
        functools.partial(first_kernel, ny, nz, partners, paired),
        out_shape=[half, half, array(28, ny + nz, LANES), array(8, ny + nz, LANES)]
        + ([array(4, rows)] if paired else [array(2, rows)] * partners),
        in_specs=[HBM] * 4,
        out_specs=[VMEM] * (5 if paired else 4 + partners),
        scratch_shapes=[
            pltpu.VMEM(flow.shape, jnp.float32),
            pltpu.VMEM(speed.shape, jnp.float32),
            pltpu.VMEM((ny + nz, LANES), jnp.float32),
            pltpu.VMEM((planes_x, 3, wy + 16, LANES), jnp.float32),
            pltpu.SemaphoreType.DMA((fields + 3,)),
        ],
        compiler_params=PARAMS,
        name="forcing_and_factor",
    )(*(in_hbm(x) for x in (flow, speed, metric_y.reshape(ny, LANES), metric_z.reshape(nz, LANES))))
    high, low, factors, chains = outputs[:4]

    def exchange(values, axis, count, stride, radix):
        received = {}
        for k in reversed(range(1, radix)):
            pairs = [(i, i ^ (k * stride)) for i in range(count)]
            received[k] = lax.ppermute(values[k - 1], axis, pairs)
        return [received[k] for k in range(1, radix)]

    plan = stage_plan(count_y)
    work = [pltpu.VMEM((LANES + 16, LANES), jnp.float32)] * 2
    spread = jax.ShapeDtypeStruct((4 * planes, rows), jnp.bfloat16)
    matrix, spread_high, spread_low = pl.pallas_call(
        functools.partial(inverse_z_kernel, ny, planes, wy),
        out_shape=[jax.ShapeDtypeStruct((2 * LANES, 2 * LANES), jnp.bfloat16), spread, spread],
        in_specs=[VMEM],
        out_specs=[VMEM] * 3,
        scratch_shapes=work + [pltpu.VMEM((2 * LANES, LANES), jnp.float32)],
        compiler_params=PARAMS,
        cost_estimate=cost(rows * 1024, 4 * rows * 64),
        name="inverse_z",
    )(factors)
    if paired:
        near = exchange(outputs[4:], "gz", count_z, 1, 2)
        total = pl.pallas_call(
            pair_kernel,
            out_shape=array(2, rows),
            in_specs=[VMEM] * 2 + [HBM],
            out_specs=VMEM,
            compiler_params=PARAMS,
            name="join_pair",
        )(outputs[4], near[0], matrix)
        received = near + exchange([total], "gz", count_z, 2, 2)
    else:
        received = exchange(outputs[4:], "gz", count_z, 1, count_z)
    local, moments, entering = pl.pallas_call(
        functools.partial(second_kernel, ny, nz, count_z, wy, partners, paired),
        out_shape=[
            array(rows, LANES),
            array(4 * planes, LANES),
            array(3 * entering_rows, LANES),
        ],
        in_specs=[SMEM] + [VMEM] * 4,
        out_specs=[VMEM] * 3,
        scratch_shapes=[
            pltpu.VMEM((LANES + 16, LANES), jnp.float32),
            pltpu.VMEM((4, wy + EXTRA, LANES), jnp.float32),
        ],
        compiler_params=PARAMS,
        cost_estimate=cost(2 * rows * 256 * 128 * 6, 4 * rows * 384),
        name="local_z",
    )(chains, factors, matrix, high, low)
    carried = pl.pallas_call(
        third_kernel,
        out_shape=array(4, planes, LANES),
        in_specs=[VMEM] * (4 + arrivals),
        out_specs=VMEM,
        compiler_params=PARAMS,
        name="carried_y",
    )(moments, spread_high, spread_low, entering, *received)
    arrived = received

    narrow = plan[-1][1] == 2 and len(plan) > 1
    cut = (fields + 1) // 2
    ranges = [(0, cut), (cut, fields)]
    base, entered, result = 0, None, None
    for number, (stride, radix) in enumerate(plan):
        if number + 1 == len(plan):
            parts = carried if number else [carried[:, b * planes_x : e * planes_x] for b, e in ranges]
            received = [exchange([part] * (radix - 1), "gy", count_y, stride, radix) for part in parts]
            out = None
            for (begin, end), messages in zip(ranges, received):
                inputs = [coefs, result, inverse_y, entered, *messages]
                out = pl.pallas_call(
                    functools.partial(
                        last_kernel, base, radix, narrow, wy, begin, end, int(out is not None)
                    ),
                    out_shape=array(fields, planes_x, wy, wz),
                    in_specs=[VMEM] * len(inputs) + ([HBM] if out is not None else []),
                    out_specs=HBM,
                    scratch_shapes=[
                        pltpu.VMEM((end - begin, planes_x, wy, wz), jnp.float32),
                        pltpu.SemaphoreType.DMA(((end - begin) * planes_x // 4,)),
                    ],
                    input_output_aliases={len(inputs): 0} if out is not None else {},
                    compiler_params=PARAMS,
                    name="finish_y",
                )(*inputs, *([out] if out is not None else []))
            return out
        received = exchange([carried] * (radix - 1), "gy", count_y, stride, radix)
        if number == 0:
            entries = sum(2 * radix - 1 for _, radix in plan[:-1]) + plan[-1][1] - 1
            inverse_y, coefs = pl.pallas_call(
                functools.partial(y_kernel, count_y, wy),
                out_shape=[array(wy, LANES), array(8, -(-entries // 8) * 8, LANES)],
                in_specs=[SMEM, VMEM, HBM],
                out_specs=[VMEM] * 2,
                scratch_shapes=work,
                compiler_params=PARAMS,
                cost_estimate=cost(2 * rows * 128 * 128 * 6, 4 * rows * 256),
                name="inverse_y",
            )(chains, factors, carried)
        before_last = number + 2 == len(plan)
        slim = narrow and before_last
        split = [(b * planes_x, e * planes_x) for b, e in ranges] if before_last else [(0, planes)]
        inputs = [carried] + received[::-1] + ([entered] if entered is not None else [])
        entered, *carried = pl.pallas_call(
            functools.partial(stage_kernel, base, stride, radix, slim, entered is not None, split),
            out_shape=[array(4, planes, LANES)]
            + [array(2 if slim else 4, end - begin, LANES) for begin, end in split],
            in_specs=[VMEM] * (1 + len(inputs)),
            out_specs=[VMEM] * (1 + len(split)),
            compiler_params=PARAMS,
            name="join_groups",
        )(coefs, *inputs)
        carried = carried if before_last else carried[0]
        base += 2 * radix - 1
        if number == 0:
            result = pl.pallas_call(
                functools.partial(local_y_kernel, wy),
                out_shape=array(planes, wy, LANES),
                in_specs=[VMEM] * 3 + [HBM] + [VMEM] * arrivals,
                out_specs=VMEM,
                scratch_shapes=[pltpu.VMEM((rows, LANES), jnp.float32)],
                compiler_params=PARAMS,
                cost_estimate=cost(2 * rows * 128 * 128 * 6, 4 * rows * 256),
                name="local_y",
            )(local, entering, inverse_y, entered, *arrived)


def solution(mesh):
    placed = (P(None, None, "gy", "gz"), P(None, "gy", "gz"), P(), P())
    return jax.shard_map(
        functools.partial(on_device, mesh),
        mesh=mesh,
        in_specs=placed,
        out_specs=P(None, None, "gy", "gz"),
        check_vma=False,
    )
```

```python
import functools

import jax
import jax.numpy as jnp
from jax import lax
from jax.experimental import pallas as pl
from jax.experimental.pallas import tpu as pltpu
from jax.sharding import PartitionSpec as P

viscous = 0.25
explicit_fourth = 0.04
implicit_fourth = 0.05
time_step = 1048576.0
LANES = 128
EXTRA = 8


def mm(a, b):
    return (
        a[0] * b[0] + a[1] * b[2],
        a[0] * b[1] + a[1] * b[3],
        a[2] * b[0] + a[3] * b[2],
        a[2] * b[1] + a[3] * b[3],
    )


def inverse_of_one_minus(a):
    p, q, r, s = 1.0 - a[0], -a[1], -a[2], 1.0 - a[3]
    d = 1.0 / (p * s - q * r)
    return (s * d, -q * d, -r * d, p * d)


def pick(condition, a, b):
    return tuple(jnp.where(condition, x, y) for x, y in zip(a, b))


def halves(x):
    high = x.astype(jnp.bfloat16)
    return high, (x - high.astype(jnp.float32)).astype(jnp.bfloat16)


def matmul(a, b, dims=(((1,), (0,)), ((), ()))):
    return lax.dot_general(a, b, dims, preferred_element_type=jnp.float32)


def scan(m, ahead, count, step, shift, product):
    unit = (1.0, 0.0, 0.0, 1.0)

    def moved(by):
        return tuple(jnp.where(ahead >= by, shift(x, by), u) for x, u in zip(m, unit))

    while step < count:
        if 2 * step < count:
            m = product(product(m, moved(step)), product(moved(2 * step), moved(3 * step)))
            step *= 4
        else:
            m = product(m, moved(step))
            step *= 2
    return m


def lane_roll(x, by):
    return pltpu.roll(x, by % LANES, 1)


def row_roll(x, by):
    by = by % x.shape[0]
    return jnp.concatenate([x[x.shape[0] - by :], x[: x.shape[0] - by]], axis=0)


class Factor:
    def __init__(self, metric, ny, nz, wy):
        self.ny, self.nz, self.wy, self.rows = ny, nz, wy, ny + nz
        self.lane = lax.broadcasted_iota(jnp.int32, (self.rows, LANES), 1)
        self.row = lax.broadcasted_iota(jnp.int32, (self.rows, LANES), 0)
        self.block = jnp.where(self.row < ny, self.row, self.row - ny)
        self.to_end = jnp.where(self.row < ny, ny, nz) - 1 - self.block
        first = (self.lane == 0) & (self.block == 0)
        last = (self.lane == LANES - 1) & (self.to_end == 0)
        self.face_low = 0.5 * (jnp.where(first, metric, self.before(metric, 1)) + metric)
        self.face_high = 0.5 * (metric + jnp.where(last, metric, self.after(metric, 1)))

    def before(self, x, by):
        rolled = lane_roll(x, by)
        value = jnp.where(self.lane < by, row_roll(rolled, 1), rolled)
        return jnp.where((self.lane < by) & (self.block == 0), 0.0, value)

    def after(self, x, by):
        rolled = lane_roll(x, -by)
        value = jnp.where(self.lane >= LANES - by, row_roll(rolled, -1), rolled)
        return jnp.where((self.lane >= LANES - by) & (self.to_end == 0), 0.0, value)

    def guess(self, sign):
        face = self.face_high if sign > 0 else self.face_low
        if sign > 0:
            cell = self.lane + LANES * self.block
        else:
            cell = LANES - 1 - self.lane + LANES * self.to_end
        near = face / (cell + 1).astype(jnp.float32)
        one_over = 1.0 / (face + jnp.sqrt(face + near * near))
        return face * one_over, implicit_fourth * one_over, one_over

    def sweep(self, sign, ratio, far):
        rows = self.rows
        back = self.before if sign > 0 else self.after
        if sign > 0:
            face_in, face_out, place = self.face_low, self.face_high, self.block
        else:
            face_in, face_out, place = self.face_high, self.face_low, self.to_end
        eps = 4.0 * implicit_fourth - implicit_fourth * back(ratio, 1)
        mass = (1.0 + 6.0 * implicit_fourth) - implicit_fourth * back(far, 2) - 2.0 * eps
        eps_in = back(eps, 1)
        scale = 1.0 / (face_in + 2.0 * eps_in)
        m = ((mass + face_in) * scale, mass - eps_in * eps_in * scale, scale, jnp.ones_like(scale))
        ahead = self.lane if sign > 0 else LANES - 1 - self.lane
        m = scan(m, ahead, LANES, 1, lambda x, by: lane_roll(x, sign * by), mm)
        edge = LANES - 1 if sign > 0 else 0
        total = tuple(jnp.broadcast_to(x[:, edge : edge + 1], (rows, LANES)) for x in m)
        total = scan(
            total, place, max(self.ny, self.nz), 1, lambda x, by: row_roll(x, sign * by), mm
        )
        top = jnp.where(place >= 1, row_roll(total[0], sign), 1.0)
        low = jnp.where(place >= 1, row_roll(total[2], sign), 0.0)
        eta = (m[0] * top + m[1] * low) / (m[2] * top + m[3] * low)
        one_over = 1.0 / (face_out + (eta + 2.0 * eps))
        return (face_out + eps) * one_over, implicit_fourth * one_over, one_over

    def finish(self, near_l, far_l, pivot_l, near_r, far_r):
        lane, block, to_end = self.lane, self.block, self.to_end
        even = (lane & 1) == 0
        near_l = jnp.where((to_end == 0) & (lane >= LANES - 1), 0.0, near_l)
        far_l = jnp.where((to_end == 0) & (lane >= LANES - 2), 0.0, far_l)
        near_r = jnp.where((block == 0) & (lane < 1), 0.0, near_r)
        far_r = jnp.where((block == 0) & (lane < 2), 0.0, far_r)

        def of_even(x):
            return jnp.where(even, x, lane_roll(x, 1))

        def of_odd(x):
            return jnp.where(even, lane_roll(x, -1), x)

        t0, t1, r0, r1 = of_even(near_l), of_odd(near_l), of_even(far_l), of_odd(far_l)
        from_right = (t0 * t1 - r0, -t0 * r1, t1, -r1)
        p1 = of_odd(pivot_l)
        left_inverse = (of_even(pivot_l) + t0 * t0 * p1, t0 * p1, t0 * p1, p1)
        s0, s1, q0, q1 = of_even(near_r), of_odd(near_r), of_even(far_r), of_odd(far_r)
        from_left = (-q0, s0, -s1 * q0, s1 * s0 - q1)
        from_left_after = tuple(self.after(x, 2) for x in from_left)
        from_right_before = tuple(self.before(x, 2) for x in from_right)
        diagonal = mm(inverse_of_one_minus(mm(from_right, from_left_after)), left_inverse)
        width = jnp.where(self.row < self.ny, self.wy, LANES)
        place = lane & (width - 1)
        right = scan(from_right, width - 1 - place, LANES, 2, lambda x, by: lane_roll(x, -by), mm)
        left = scan(from_left, place, LANES, 2, lane_roll, mm)
        return from_right, from_left, diagonal, right, left, from_right_before, from_left_after


def cell_weights(chain, column, even):
    return jnp.where(even, chain[column], chain[2 + column])


def first_kernel(ny, nz, partners, paired, flow_hbm, speed_hbm, metric_y, metric_z, *refs):
    high, low, factors, chains = refs[:4]
    count = 1 if paired else partners
    messages = refs[4 : 4 + count]
    flow, speed, metric, spread, arrived = refs[4 + count :]
    fields, planes_x, wy, _ = flow.shape
    rows = ny + nz
    core_rows = fields * planes_x * wy

    copies = [
        pltpu.make_async_copy(metric_y, metric.at[0:ny], arrived.at[fields]),
        pltpu.make_async_copy(metric_z, metric.at[ny:rows], arrived.at[fields + 1]),
        pltpu.make_async_copy(speed_hbm, speed, arrived.at[fields + 2]),
    ]
    for copy in copies:
        copy.start()
    for field in range(fields):
        pltpu.make_async_copy(flow_hbm.at[field], flow.at[field], arrived.at[field]).start()

    lane = lax.broadcasted_iota(jnp.int32, (wy, LANES), 1)
    extra_row = lax.broadcasted_iota(jnp.int32, (EXTRA, LANES), 0)
    for slot in range(planes_x):
        for part in range(3):
            spread[slot, part, 0:8, :] = jnp.zeros((8, LANES), jnp.float32)
            spread[slot, part, wy + 8 : wy + 16, :] = jnp.zeros((8, LANES), jnp.float32)
    side = time_step * (viscous + 4.0 * explicit_fourth)
    half = time_step * 0.5
    centre = time_step * (-6.0 * viscous - 12.0 * explicit_fourth)
    fourth = -time_step * explicit_fourth

    def store(start, column, value):
        first, second = halves(value)
        high[pl.ds(start, value.shape[0]), column : column + LANES] = first
        low[pl.ds(start, value.shape[0]), column : column + LANES] = second

    def one_field(field):
        values = [flow[field, x] for x in range(planes_x)]
        fluxes = [values[x] * speed[x] for x in range(planes_x)]
        aside = [(time_step * viscous) * u for u in values]
        extras = []
        for x in range(planes_x):
            u, flux, slot = values[x], fluxes[x], x
            total = centre * u
            if x + 1 < planes_x:
                total = total + (aside[x + 1] - fluxes[x + 1])
            if x > 0:
                total = total + (aside[x - 1] + fluxes[x - 1])
            scaled = side * u
            onward, backward, far = scaled + flux, scaled - flux, fourth * u
            spread[slot, 0, 8 : wy + 8, :] = onward
            spread[slot, 1, 8 : wy + 8, :] = backward
            spread[slot, 2, 8 : wy + 8, :] = far
            total = total + (spread[slot, 0, 7 : wy + 7, :] + spread[slot, 1, 9 : wy + 9, :])
            total = total + (spread[slot, 2, 6 : wy + 6, :] + spread[slot, 2, 10 : wy + 10, :])
            a, b = lane_roll(onward, 1), lane_roll(backward, -1)
            c, d = lane_roll(far, 2), lane_roll(far, -2)
            from_low, from_high = a + c, b + d
            ends = jnp.where(lane == 0, from_low, jnp.where(lane == 1, c, 0.0))
            ends = jnp.where(lane == LANES - 1, from_high, jnp.where(lane == LANES - 2, d, ends))
            index = field * planes_x + x
            start = index * wy
            store(start, 0, total + (from_low + from_high))
            store(start, LANES, ends)
            above = spread[slot, 1, 7:15, :] + spread[slot, 2, 8:16, :]
            below = spread[slot, 0, wy + 5 : wy + 13, :] + spread[slot, 2, wy + 4 : wy + 12, :]
            extras.append(jnp.where(extra_row < 2, above, jnp.where(extra_row < 4, below, 0.0)))
            if len(extras) == 2:
                start = core_rows + (index - 1) * EXTRA
                store(start, 0, jnp.concatenate(extras, axis=0))
                for ref in (high, low):
                    ref[pl.ds(start, 2 * EXTRA), LANES : 2 * LANES] = jnp.zeros(
                        (2 * EXTRA, LANES), jnp.bfloat16
                    )
                extras = []

    copies[0].wait()
    copies[1].wait()
    factor = Factor(metric[...], ny, nz, wy)

    guess_l, guess_r = factor.guess(1), factor.guess(-1)
    left, right = factor.sweep(1, *guess_l[:2]), factor.sweep(-1, *guess_r[:2])
    copies[2].wait()
    for x in range(planes_x):
        speed[x] = half * speed[x]
    for field in range(fields):
        pltpu.make_async_copy(flow_hbm.at[field], flow.at[field], arrived.at[field]).wait()
    left, right = factor.sweep(1, *left[:2]), factor.sweep(-1, *right[:2])
    for field in range(fields // 2):
        one_field(field)
    parts = factor.finish(*left, *right[:2])
    from_right, from_left, diagonal, to_right, to_left, before, after = parts
    for number, value in enumerate(v for part in parts for v in part):
        factors[number] = value
    for number, value in enumerate(to_right + to_left):
        chains[number] = value
    for field in range(fields // 2, fields):
        one_field(field)

    me = lax.axis_index("gz")
    mine = lax.broadcasted_iota(jnp.int32, (rows, LANES), 0) == ny + me
    even = (lax.broadcasted_iota(jnp.int32, (1, LANES), 1) & 1) == 0
    lane = lax.broadcasted_iota(jnp.int32, (1, LANES), 1)

    def own(values):
        return tuple(jnp.sum(jnp.where(mine, v, 0.0), axis=0, keepdims=True) for v in values)

    up, down = own(to_right), own(to_left)
    up_past, down_past = own(mm(before, to_right)), own(mm(after, to_left))
    unit = (1.0, 0.0, 0.0, 1.0)
    weights = []
    for column in range(2):
        same = jnp.where(even, unit[column], unit[2 + column])
        inside_up = cell_weights(up, column, even)
        inside_down = cell_weights(down, column, even)
        past_up = lane_roll(cell_weights(up_past, column, even), -2)
        past_down = lane_roll(cell_weights(down_past, column, even), 2)
        ends_up = jnp.where(lane < 2, same, past_up) - inside_up
        ends_down = jnp.where(lane < 2, past_down, same) - inside_down
        at_end = (lane < 2) | (lane >= LANES - 2)
        ends_up, ends_down = jnp.where(at_end, ends_up, 0.0), jnp.where(at_end, ends_down, 0.0)
        weights.append(
            (
                jnp.concatenate([inside_up, ends_up], axis=1),
                jnp.concatenate([inside_down, ends_down], axis=1),
            )
        )
    if paired:
        lower = (me & 1) == 0
        stack = [jnp.where(lower, w[0], w[1]) for w in weights]
        peer = lax.broadcasted_iota(jnp.int32, (rows, LANES), 0) == ny + jnp.bitwise_xor(me, 1)

        def of_peer(values, place):
            chosen = tuple(jnp.sum(jnp.where(peer, v, 0.0), axis=0, keepdims=True) for v in values)
            return tuple(jnp.broadcast_to(v[:, place : place + 1], (1, 2 * LANES)) for v in chosen)

        over, under = of_peer(to_right, 0), of_peer(to_left, LANES - 1)
        (up0, down0), (up1, down1) = weights
        for q in range(2):
            upward = jnp.where(lower, over[q] * up0 + over[2 + q] * up1, weights[q][0])
            downward = jnp.where(lower, weights[q][1], under[q] * down0 + under[2 + q] * down1)
            stack.append(jnp.where(me < 2, upward, downward))
    else:
        stack = []
        for k in range(1, partners + 1):
            upward = jnp.bitwise_xor(me, k) > me
            stack += [jnp.where(upward, w[0], w[1]) for w in weights]
    while len(stack) % 8:
        stack.append(jnp.zeros((1, 2 * LANES), jnp.float32))
    count = len(stack)
    stack = jnp.concatenate(stack, axis=0)
    first = stack.astype(jnp.bfloat16).astype(jnp.float32)
    both = jnp.concatenate([first, stack - first], axis=0).astype(jnp.bfloat16)
    across = (((1,), (1,)), ((), ()))
    total = high.shape[0]
    size = planes_x * wy
    for begin in range(0, total, size):
        rows = slice(begin, min(begin + size, total))
        on_high = matmul(both, high[rows, :], across)
        on_low = matmul(both, low[rows, :], across)
        moments = (on_high[:count] + on_high[count:]) + on_low[:count]
        if paired:
            messages[0][:, rows] = moments[0:4]
        else:
            for k in range(partners):
                messages[k][:, rows] = moments[2 * k : 2 * k + 2]


def dense_inverse(columns, start, width, stack):
    parts = 8
    steps = width // (2 * parts)
    lane = lax.broadcasted_iota(jnp.int32, (parts, LANES), 1)
    part = lax.broadcasted_iota(jnp.int32, (parts, LANES), 0)
    fits = width + 4 <= LANES
    values = [columns[pl.ds(start + 2 * i, parts, stride=2 * steps), :] for i in range(steps)]

    def wide(i, number):
        return tuple(
            jnp.broadcast_to(values[i][:, number + k : number + k + 1], (parts, LANES)) for k in range(4)
        )

    blocks = [wide(i, 8) for i in range(steps)]
    zero, one = jnp.zeros((parts, LANES), jnp.float32), jnp.ones((parts, LANES), jnp.float32)

    def put(rows, i, extra, extra_lane, owner):
        first = 2 * (part * steps + i)
        out = []
        for r in range(2):
            row = jnp.where(lane == first, blocks[i][2 * r], rows[r])
            row = jnp.where(lane == first + 1, blocks[i][2 * r + 1], row)
            if extra is not None and fits:
                row = jnp.where((part == owner) & (lane == extra_lane), extra[2 * r], row)
                row = jnp.where((part == owner) & (lane == extra_lane + 1), extra[2 * r + 1], row)
            out.append(row)
        return tuple(out)

    def run(order, number, ends, extra_lane, owner):
        rows, product, out = (zero, zero), (one, zero, zero, one), {}
        for i in order:
            t = wide(i, number)
            rows = (t[0] * rows[0] + t[1] * rows[1], t[2] * rows[0] + t[3] * rows[1])
            extra = None
            if i == order[0]:
                e = wide(i, ends)
                extra = mm(blocks[i], (e[0], e[2], e[1], e[3]))
            rows = put(rows, i, extra, extra_lane, owner)
            product = mm(t, product)
            out[i] = rows, product
        rows, product = out[order[-1]]
        entering, last = [None] * parts, (jnp.zeros((1, LANES), jnp.float32),) * 2
        sequence = range(parts) if number == 4 else range(parts - 1, -1, -1)
        for p in sequence:
            entering[p] = last
            own, across = [r[p : p + 1] for r in rows], [x[p : p + 1] for x in product]
            last = (
                own[0] + across[0] * last[0] + across[1] * last[1],
                own[1] + across[2] * last[0] + across[3] * last[1],
            )
        entering = [jnp.concatenate([e[r] for e in entering], axis=0) for r in range(2)]
        result = []
        for i in range(steps):
            rows, product = out[i]
            for r in range(2):
                result.append(rows[r] + product[2 * r] * entering[0] + product[2 * r + 1] * entering[1])
        return result

    low = run(list(range(steps)), 4, 12, width, 0)
    high = run(list(range(steps - 1, -1, -1)), 0, 16, width + 2, parts - 1)
    for k in range(2 * steps):
        lower = lane <= 2 * (part * steps + k // 2) + 1
        if fits:
            lower = lower & (lane < width) | ((lane >= width) & (lane < width + 2))
        stack[parts * k : parts * (k + 1), :] = jnp.where(lower, low[k], high[k])
    rows = [stack[pl.ds(p, 2 * steps, stride=parts), :] for p in range(parts)]
    return jnp.concatenate(rows, axis=0)


def stage_plan(count):
    plan, stride = [], 1
    while stride < count:
        radix = 4 if count // stride >= 4 else 2
        plan.append((stride, radix))
        stride *= radix
    return plan


def transposed(factors, row):
    rows = [factors[number, pl.ds(row, 1), :] for number in range(12)]
    rows += [factors[20 + number, pl.ds(row, 1), :] for number in range(8)]
    rows += [factors[12 + number, pl.ds(row, 1), :] for number in range(8)]
    rows.append(jnp.zeros((4, LANES), jnp.float32))
    return jnp.concatenate(rows, axis=0).T


def chain_products(chains, number, place, blocks, begins, ends, masks, reverse):
    count = -(-len(begins) // 8) * 8
    row = lax.broadcasted_iota(jnp.int32, (count, LANES), 0)
    begin = jnp.zeros((count, LANES), jnp.int32)
    end, mask = begin, jnp.zeros((count, LANES), jnp.float32)
    for r, (b, e, m) in enumerate(zip(begins, ends, masks)):
        begin, end = jnp.where(row == r, b, begin), jnp.where(row == r, e, end)
        mask = jnp.where(row == r, m, mask)
    one, zero = jnp.ones((count, LANES), jnp.float32), jnp.zeros((count, LANES), jnp.float32)
    product = (one, zero, zero, one)
    for block in range(blocks - 1, -1, -1) if reverse else range(blocks):
        where = place(block)
        value = tuple(chains[number + k, where[0], where[1]] for k in range(4))
        product = pick((begin <= block) & (block < end), mm(product, value), product)
    return tuple(x * mask for x in product)


def truth(condition):
    return jnp.where(condition, 1.0, 0.0)


def inverse_z_kernel(ny, planes, wy, factors, matrix, spread_high, spread_low, columns, stacked, rows_ref):
    me_z = lax.axis_index("gz")
    columns[0:LANES, 0:32] = transposed(factors, ny + me_z)
    inverse = dense_inverse(columns, 0, LANES, stacked)
    rows_ref[0:LANES, :] = inverse
    rows_ref[LANES : 2 * LANES, :] = jnp.zeros((LANES, LANES), jnp.float32)
    past = tuple(columns[LANES - 1 : LANES, 16 + k : 17 + k] for k in range(4))
    ahead = tuple(columns[0:1, 12 + k : 13 + k] for k in range(4))
    head0, head1 = rows_ref[0:1, :], rows_ref[1:2, :]
    tail0, tail1 = rows_ref[LANES - 2 : LANES - 1, :], rows_ref[LANES - 1 : LANES, :]
    for q in range(2):
        beyond = past[2 * q] * tail0 + past[2 * q + 1] * tail1
        rows_ref[LANES + q : LANES + q + 1, :] = beyond - (head0, head1)[q]
        beyond = ahead[2 * q] * head0 + ahead[2 * q + 1] * head1
        rows_ref[2 * LANES - 2 + q : 2 * LANES - 1 + q, :] = beyond - (tail0, tail1)[q]
    first, second = halves(rows_ref[...])
    matrix[:, 0:LANES] = first
    matrix[:, LANES : 2 * LANES] = second

    cell = lax.axis_index("gy") * wy
    row = cell // LANES
    total = planes * (wy + EXTRA)
    unit = (1.0, 0.0, 0.0, 1.0)
    lane = lax.broadcasted_iota(jnp.int32, (1, LANES), 1)
    even = (lane & 1) == 0

    def chain(number):
        return tuple(factors[number + k, pl.ds(row, 1), :] for k in range(4))

    def turned(x, by):
        return pltpu.roll(x, lax.rem(by + 2 * LANES, LANES), 1)

    def tiled(x, period):
        x = jnp.where(lane < period, x, 0.0)
        while period < LANES:
            x = x + lane_roll(x, period)
            period *= 2
        return x

    up, down, before, after = chain(12), chain(16), chain(20), chain(24)
    past_up, past_down = mm(before, up), mm(after, down)
    plane_row = lax.broadcasted_iota(jnp.int32, (planes, LANES), 0)
    wide_lane = lax.broadcasted_iota(jnp.int32, (planes, LANES), 1)
    for column in range(2):
        same = jnp.where(even, unit[column], unit[2 + column])
        for number, inside, early, late in (
            (column, up, turned(cell_weights(past_up, column, even), -start_y(cell)), same),
            (
                2 + column,
                down,
                same,
                turned(cell_weights(past_down, column, even), 4 - wy - start_y(cell)),
            ),
        ):
            inside = tiled(turned(cell_weights(inside, column, even), -start_y(cell)), wy)
            past = jnp.where(lane < 2, early, jnp.where(lane < 4, late, 0.0))
            past = tiled(past, EXTRA)
            rows = slice(number * planes, (number + 1) * planes)
            for begin in range(0, total, LANES):
                if begin < planes * wy:
                    owner, value = (begin + wide_lane) // wy, inside
                else:
                    owner, value = (begin - planes * wy + wide_lane) // EXTRA, past
                size = min(LANES, total - begin)
                first, second = halves(jnp.where(plane_row == owner, value, 0.0))
                spread_high[rows, begin : begin + size] = first[:, 0:size]
                spread_low[rows, begin : begin + size] = second[:, 0:size]


def whole_rows(matrix, row):
    start = row // 16 * 16
    both = matrix[start : start + 16, :].astype(jnp.float32)
    value = both[:, 0:LANES] + both[:, LANES : 2 * LANES]
    return value[row - start : row - start + 1]


def second_kernel(
    ny, nz, count_z, wy, partners, paired, chains, factors, matrix, high, low, local, moments, entering, *scratch
):
    columns, weights_y = scratch
    me_z, me_y = lax.axis_index("gz"), lax.axis_index("gy")
    planes = moments.shape[0] // 4
    head0, head1 = whole_rows(matrix, 0), whole_rows(matrix, 1)
    tail0, tail1 = whole_rows(matrix, LANES - 2), whole_rows(matrix, LANES - 1)

    if paired:
        pair = me_z // 2 * 2
        begins, ends = [me_z, pair], [me_z + 1, pair + 2]
        lowers = [me_z % 2 == 1, pair > 0]
    else:
        others = [jnp.bitwise_xor(me_z, k) for k in range(1, partners + 1)]
        begins, ends = [other + 1 for other in others], others
        lowers = [other < me_z for other in others]
    size = len(begins)
    up = chain_products(
        chains, 0, lambda b: (ny + b, 0), count_z, begins, [me_z] * size, [1.0] * size, False
    )
    down = chain_products(
        chains, 4, lambda b: (ny + b, LANES - 1), count_z, [me_z + 1] * size, ends, [1.0] * size, True
    )
    stack = []
    for k, lower in enumerate(lowers):
        for p in range(2):
            from_low = up[2 * p][k : k + 1] * head0 + up[2 * p + 1][k : k + 1] * head1
            from_high = down[2 * p][k : k + 1] * tail0 + down[2 * p + 1][k : k + 1] * tail1
            stack.append(jnp.where(lower, from_low, from_high))
    while len(stack) % 8:
        stack.append(jnp.zeros((1, LANES), jnp.float32))
    stack = jnp.concatenate(stack, axis=0)
    first = stack.astype(jnp.bfloat16).astype(jnp.float32)
    entering[...] = jnp.concatenate([first, stack - first, first], axis=0)

    cell = me_y * wy
    columns[0:LANES, 0:32] = transposed(factors, cell // LANES)
    start = lax.rem(cell, LANES)
    row = lax.broadcasted_iota(jnp.int32, (wy, LANES), 0)
    extra_row = lax.broadcasted_iota(jnp.int32, (EXTRA, LANES), 0)
    unit = (1.0, 0.0, 0.0, 1.0)

    def head(number):
        return tuple(columns[pl.ds(start, 1), number + k : number + k + 1] for k in range(4))

    def tail(number):
        return tuple(columns[pl.ds(start + wy - 1, 1), number + k : number + k + 1] for k in range(4))

    past_up, past_down = mm(head(12), head(20)), mm(tail(16), tail(24))
    for column in range(2):
        for output, number in ((column, 20), (2 + column, 24)):
            even = columns[pl.ds(start, wy), number + column : number + column + 1]
            odd = columns[pl.ds(start, wy), number + 2 + column : number + 3 + column]
            weights_y[output, 0:wy, :] = jnp.where((row & 1) == 0, even, odd)
        for output, early, late in (
            (column, (past_up[column], past_up[2 + column]), (unit[column], unit[2 + column])),
            (2 + column, (unit[column], unit[2 + column]), (past_down[column], past_down[2 + column])),
        ):
            value = jnp.zeros((EXTRA, LANES), jnp.float32)
            for r, v in enumerate(early + late):
                value = jnp.where(extra_row == r, v, value)
            weights_y[output, wy : wy + EXTRA, :] = value

    total = planes * (wy + EXTRA)

    def solve(begin, size):
        rows = slice(begin, begin + size)
        both = matmul(high[rows, :], matrix[...])
        value = both[:, 0:LANES] + (both[:, LANES : 2 * LANES] + matmul(low[rows, :], matrix[:, 0:LANES]))
        local[rows, :] = value
        return value

    extra = solve(planes * wy, planes * EXTRA)
    for part in range(planes // 8):
        core = solve(part * 8 * wy, 8 * wy)
        for number in range(4):
            lines = []
            for k in range(8):
                index = part * 8 + k
                value = jnp.sum(core[k * wy : (k + 1) * wy] * weights_y[number, 0:wy, :], axis=0, keepdims=True)
                past = extra[index * EXTRA : (index + 1) * EXTRA] * weights_y[number, wy : wy + EXTRA, :]
                lines.append(value + jnp.sum(past, axis=0, keepdims=True))
            start = number * planes + part * 8
            moments[start : start + 8, :] = jnp.concatenate(lines, axis=0)


def start_y(cell):
    return lax.rem(cell, LANES)


def y_kernel(count_y, wy, chains, factors, unused, inverse_y, coefs, columns, stacked):
    me_y = lax.axis_index("gy")
    cell = me_y * wy
    columns[0:LANES, 0:32] = transposed(factors, cell // LANES)
    start = lax.rem(cell, LANES)
    inverse_y[...] = dense_inverse(columns, start, wy, stacked)

    up, down = ([], [], []), ([], [], [])
    plan = stage_plan(count_y)
    for number, (stride, radix) in enumerate(plan):
        group = me_y // stride
        first = (group // radix) * radix
        others = [first + jnp.bitwise_xor(group - first, k) for k in range(radix)]
        for other in others[1:]:
            for lists, values in (
                (up, ((other + 1) * stride, me_y, truth(other < group))),
                (down, (me_y + 1, other * stride, truth(other > group))),
            ):
                for one, value in zip(lists, values):
                    one.append(value)
        if number + 1 < len(plan):
            for other in others:
                for lists, values in (
                    (up, ((other + 1) * stride, (first + radix) * stride, 1.0)),
                    (down, (first * stride, other * stride, 1.0)),
                ):
                    for one, value in zip(lists, values):
                        one.append(value)

    def place(block):
        return block * wy // LANES, block * wy % LANES

    def place_end(block):
        return place(block)[0], place(block)[1] + wy - 1

    for base, value in (
        (0, chain_products(chains, 0, place, count_y, *up, False)),
        (4, chain_products(chains, 4, place_end, count_y, *down, True)),
    ):
        for k in range(4):
            coefs[base + k] = value[k]


def pair_kernel(own, received, unused, total):
    total[...] = own[2:4] + received[2:4]


def arrived_rows(messages, count):
    rows = [m[0:2] for m in messages]
    if count > 2 * len(messages):
        rows.append(jnp.zeros((count - 2 * len(messages), rows[0].shape[1]), jnp.float32))
    return jnp.concatenate(rows, axis=0)


def third_kernel(moments, spread_high, spread_low, entering, *refs):
    messages, carried = refs[:-1][::-1], refs[-1]
    count = entering.shape[0] // 3
    received = arrived_rows(messages, count)
    first = received.astype(jnp.bfloat16).astype(jnp.float32)
    both = jnp.concatenate([first, received - first], axis=0).astype(jnp.bfloat16)
    top = jnp.concatenate([first, jnp.zeros_like(first)], axis=0).astype(jnp.bfloat16)
    across = (((1,), (1,)), ((), ()))
    corner = matmul(spread_high[...], both, across) + matmul(spread_low[...], top, across)
    values = entering[0:count, :] + entering[count : 2 * count, :]
    added = lax.dot_general(
        corner,
        jnp.concatenate([values, values], axis=0),
        (((1,), (0,)), ((), ())),
        precision=lax.Precision.HIGHEST,
        preferred_element_type=jnp.float32,
    )
    planes = carried.shape[1]
    for number in range(4):
        rows = slice(number * planes, (number + 1) * planes)
        carried[number] = moments[rows, :] + added[rows]


def local_y_kernel(wy, local, entering, inverse_y, unused, *refs):
    messages, (out, solved) = refs[:-2], refs[-2:]
    planes = out.shape[0]
    count = entering.shape[0] // 3
    received = arrived_rows(messages, count)
    first = received.astype(jnp.bfloat16).astype(jnp.float32)
    received = jnp.concatenate([first, first, received - first], axis=0).T.astype(jnp.bfloat16)
    solved[...] = local[...] + matmul(received, entering[...].astype(jnp.bfloat16))
    first, second = halves(inverse_y[:, 0 : wy + EXTRA])
    left = jnp.concatenate([first, second, first], axis=1)

    def part(index, carry):
        for k in range(8):
            number = index * 8 + k
            start = pl.multiple_of(number * wy, 8)
            core = solved[pl.ds(start, wy), :]
            start = pl.multiple_of(planes * wy + number * EXTRA, 8)
            both = jnp.concatenate([core, solved[pl.ds(start, EXTRA), :]], axis=0)
            top, rest = halves(both)
            out[number] = matmul(left, jnp.concatenate([top, top, rest], axis=0))
        return carry

    lax.fori_loop(0, planes // 8, part, 0)


def combine(coefs, side, row, values):
    first = 0 if side == 0 else 2
    out = [None, None]
    for k, value in enumerate(values):
        for q in range(2):
            for p in range(2):
                term = coefs[side + 2 * p + q, row + k : row + k + 1, :] * value[first + p]
                out[q] = term if out[q] is None else out[q] + term
    return out


def stage_kernel(base, stride, radix, narrow, has_entered, coefs, *refs):
    values = (refs[0],) + tuple(refs[1:radix][::-1])
    position = radix
    entered = None
    if has_entered:
        entered = refs[position]
        position += 1
    message, entering = refs[position : position + 2]
    below = combine(coefs, 0, base, values[1:])
    above = combine(coefs, 4, base, values[1:])
    for row, value in enumerate(below + above):
        entering[row] = value if entered is None else value + entered[row]
    upward = combine(coefs, 0, base + radix - 1, values)
    downward = combine(coefs, 4, base + radix - 1, values)
    if narrow:
        group = lax.axis_index("gy") // (stride * radix)
        sends_up = lax.rem(group, 2) == 0
        for row in range(2):
            message[row] = jnp.where(sends_up, upward[row], downward[row])
    else:
        for row, value in enumerate(upward + downward):
            message[row] = value


def last_kernel(base, radix, narrow, wy, coefs, local, inverse_y, entered, *refs):
    messages, (out_hbm, out, sent) = refs[: radix - 1], refs[radix - 1 :]
    values = list(messages)
    if narrow:
        values = [(m[0], m[1], m[0], m[1]) for m in values]
    below = combine(coefs, 0, base, values)
    above = combine(coefs, 4, base, values)
    st = [value + entered[row] for row, value in enumerate(below + above)]
    sides = [
        jnp.broadcast_to(inverse_y[:, c : c + 1], (wy, LANES)) for c in (0, 1, wy - 2, wy - 1)
    ]
    fields, planes_x = out.shape[:2]
    copies = []
    for field in range(fields):
        for x in range(planes_x):
            index = field * planes_x + x
            value = local[index]
            for number in range(4):
                value = value + sides[number] * st[number][index : index + 1]
            out[field, x] = value
            if (x + 1) % 4 == 0:
                part = (field, pl.ds(x - 3, 4))
                copy = pltpu.make_async_copy(out.at[part], out_hbm.at[part], sent.at[len(copies)])
                copy.start()
                copies.append(copy)
    for copy in copies:
        copy.wait()


VMEM = pl.BlockSpec(memory_space=pltpu.VMEM)
HBM = pl.BlockSpec(memory_space=pltpu.HBM)
SMEM = pl.BlockSpec(memory_space=pltpu.SMEM)
PARAMS = pltpu.CompilerParams(vmem_limit_bytes=40 * 1024 * 1024)


def array(*shape):
    return jax.ShapeDtypeStruct(shape, jnp.float32)


def in_hbm(x):
    return pltpu.with_memory_space_constraint(x, pltpu.HBM)


def cost(flops, data):
    return pl.CostEstimate(flops=flops, bytes_accessed=data, transcendentals=0)


def on_device(mesh, flow, speed, metric_y, metric_z):
    fields, planes_x, wy, wz = flow.shape
    count_y, count_z = mesh.shape["gy"], mesh.shape["gz"]
    assert wz == LANES
    ny, nz = metric_y.shape[0] // LANES, metric_z.shape[0] // LANES
    planes = fields * planes_x
    rows = planes * (wy + EXTRA)
    partners = count_z - 1
    paired = False
    arrivals = 2 if paired else partners
    entering_rows = -(-2 * arrivals // 8) * 8
    half = jax.ShapeDtypeStruct((rows, 2 * LANES), jnp.bfloat16)
    outputs = pl.pallas_call(
        functools.partial(first_kernel, ny, nz, partners, paired),
        out_shape=[half, half, array(28, ny + nz, LANES), array(8, ny + nz, LANES)]
        + ([array(4, rows)] if paired else [array(2, rows)] * partners),
        in_specs=[HBM] * 4,
        out_specs=[VMEM] * (5 if paired else 4 + partners),
        scratch_shapes=[
            pltpu.VMEM(flow.shape, jnp.float32),
            pltpu.VMEM(speed.shape, jnp.float32),
            pltpu.VMEM((ny + nz, LANES), jnp.float32),
            pltpu.VMEM((planes_x, 3, wy + 16, LANES), jnp.float32),
            pltpu.SemaphoreType.DMA((fields + 3,)),
        ],
        compiler_params=PARAMS,
        name="forcing_and_factor",
    )(*(in_hbm(x) for x in (flow, speed, metric_y.reshape(ny, LANES), metric_z.reshape(nz, LANES))))
    high, low, factors, chains = outputs[:4]

    def exchange(values, axis, count, stride, radix):
        received = {}
        for k in reversed(range(1, radix)):
            pairs = [(i, i ^ (k * stride)) for i in range(count)]
            received[k] = lax.ppermute(values[k - 1], axis, pairs)
        return [received[k] for k in range(1, radix)]

    plan = stage_plan(count_y)
    work = [pltpu.VMEM((LANES + 16, LANES), jnp.float32)] * 2
    spread = jax.ShapeDtypeStruct((4 * planes, rows), jnp.bfloat16)
    matrix, spread_high, spread_low = pl.pallas_call(
        functools.partial(inverse_z_kernel, ny, planes, wy),
        out_shape=[jax.ShapeDtypeStruct((2 * LANES, 2 * LANES), jnp.bfloat16), spread, spread],
        in_specs=[VMEM],
        out_specs=[VMEM] * 3,
        scratch_shapes=work + [pltpu.VMEM((2 * LANES, LANES), jnp.float32)],
        compiler_params=PARAMS,
        cost_estimate=cost(rows * 1024, 4 * rows * 64),
        name="inverse_z",
    )(factors)
    if paired:
        near = exchange(outputs[4:], "gz", count_z, 1, 2)
        total = pl.pallas_call(
            pair_kernel,
            out_shape=array(2, rows),
            in_specs=[VMEM] * 2 + [HBM],
            out_specs=VMEM,
            compiler_params=PARAMS,
            name="join_pair",
        )(outputs[4], near[0], matrix)
        received = near + exchange([total], "gz", count_z, 2, 2)
    else:
        received = exchange(outputs[4:], "gz", count_z, 1, count_z)
    local, moments, entering = pl.pallas_call(
        functools.partial(second_kernel, ny, nz, count_z, wy, partners, paired),
        out_shape=[
            array(rows, LANES),
            array(4 * planes, LANES),
            array(3 * entering_rows, LANES),
        ],
        in_specs=[SMEM] + [VMEM] * 4,
        out_specs=[VMEM] * 3,
        scratch_shapes=[
            pltpu.VMEM((LANES + 16, LANES), jnp.float32),
            pltpu.VMEM((4, wy + EXTRA, LANES), jnp.float32),
        ],
        compiler_params=PARAMS,
        cost_estimate=cost(2 * rows * 256 * 128 * 6, 4 * rows * 384),
        name="local_z",
    )(chains, factors, matrix, high, low)
    carried = pl.pallas_call(
        third_kernel,
        out_shape=array(4, planes, LANES),
        in_specs=[VMEM] * (4 + arrivals),
        out_specs=VMEM,
        compiler_params=PARAMS,
        name="carried_y",
    )(moments, spread_high, spread_low, entering, *received[::-1])
    arrived = received

    narrow = plan[-1][1] == 2 and len(plan) > 1
    base, entered, result = 0, None, None
    for number, (stride, radix) in enumerate(plan):
        received = exchange([carried] * (radix - 1), "gy", count_y, stride, radix)
        if number == 0:
            entries = sum(2 * radix - 1 for _, radix in plan[:-1]) + plan[-1][1] - 1
            inverse_y, coefs = pl.pallas_call(
                functools.partial(y_kernel, count_y, wy),
                out_shape=[array(wy, LANES), array(8, -(-entries // 8) * 8, LANES)],
                in_specs=[SMEM, VMEM, HBM],
                out_specs=[VMEM] * 2,
                scratch_shapes=work,
                compiler_params=PARAMS,
                cost_estimate=cost(2 * rows * 128 * 128 * 6, 4 * rows * 256),
                name="inverse_y",
            )(chains, factors, carried)
        if number + 1 < len(plan):
            slim = narrow and number + 2 == len(plan)
            inputs = [carried] + received[::-1] + ([entered] if entered is not None else [])
            carried, entered = pl.pallas_call(
                functools.partial(stage_kernel, base, stride, radix, slim, entered is not None),
                out_shape=[array(2 if slim else 4, planes, LANES), array(4, planes, LANES)],
                in_specs=[VMEM] * (1 + len(inputs)),
                out_specs=[VMEM] * 2,
                compiler_params=PARAMS,
                name="join_groups",
            )(coefs, *inputs)
            base += 2 * radix - 1
            if number == 0:
                result = pl.pallas_call(
                    functools.partial(local_y_kernel, wy),
                    out_shape=array(planes, wy, LANES),
                    in_specs=[VMEM] * 3 + [HBM] + [VMEM] * arrivals,
                    out_specs=VMEM,
                    scratch_shapes=[pltpu.VMEM((rows, LANES), jnp.float32)],
                    compiler_params=PARAMS,
                    cost_estimate=cost(2 * rows * 128 * 128 * 6, 4 * rows * 256),
                    name="local_y",
                )(local, entering, inverse_y, entered, *arrived)
        else:
            return pl.pallas_call(
                functools.partial(last_kernel, base, radix, narrow, wy),
                out_shape=array(fields, planes_x, wy, wz),
                in_specs=[VMEM] * (4 + len(received)),
                out_specs=HBM,
                scratch_shapes=[
                    pltpu.VMEM(flow.shape, jnp.float32),
                    pltpu.SemaphoreType.DMA((planes // 4,)),
                ],
                compiler_params=PARAMS,
                name="finish_y",
            )(coefs, result, inverse_y, entered, *received)


def solution(mesh):
    placed = (P(None, None, "gy", "gz"), P(None, "gy", "gz"), P(), P())
    return jax.shard_map(
        functools.partial(on_device, mesh),
        mesh=mesh,
        in_specs=placed,
        out_specs=P(None, None, "gy", "gz"),
        check_vma=False,
    )
```

```python
import functools

import jax
import jax.numpy as jnp
from jax import lax
from jax.experimental import pallas as pl
from jax.experimental.pallas import tpu as pltpu
from jax.sharding import PartitionSpec as P

viscous = 0.25
explicit_fourth = 0.04
implicit_fourth = 0.05
time_step = 1048576.0
LANES = 128
EXTRA = 8


def mm(a, b):
    return (
        a[0] * b[0] + a[1] * b[2],
        a[0] * b[1] + a[1] * b[3],
        a[2] * b[0] + a[3] * b[2],
        a[2] * b[1] + a[3] * b[3],
    )


def inverse_of_one_minus(a):
    p, q, r, s = 1.0 - a[0], -a[1], -a[2], 1.0 - a[3]
    d = 1.0 / (p * s - q * r)
    return (s * d, -q * d, -r * d, p * d)


def pick(condition, a, b):
    return tuple(jnp.where(condition, x, y) for x, y in zip(a, b))


def halves(x):
    high = x.astype(jnp.bfloat16)
    return high, (x - high.astype(jnp.float32)).astype(jnp.bfloat16)


def matmul(a, b, dims=(((1,), (0,)), ((), ()))):
    return lax.dot_general(a, b, dims, preferred_element_type=jnp.float32)


def scan(m, ahead, count, step, shift, product):
    unit = (1.0, 0.0, 0.0, 1.0)

    def moved(by):
        return tuple(jnp.where(ahead >= by, shift(x, by), u) for x, u in zip(m, unit))

    while step < count:
        if 2 * step < count:
            m = product(product(m, moved(step)), product(moved(2 * step), moved(3 * step)))
            step *= 4
        else:
            m = product(m, moved(step))
            step *= 2
    return m


def lane_roll(x, by):
    return pltpu.roll(x, by % LANES, 1)


def row_roll(x, by):
    by = by % x.shape[0]
    return jnp.concatenate([x[x.shape[0] - by :], x[: x.shape[0] - by]], axis=0)


class Factor:
    def __init__(self, metric, ny, nz, wy):
        self.ny, self.nz, self.wy, self.rows = ny, nz, wy, ny + nz
        self.lane = lax.broadcasted_iota(jnp.int32, (self.rows, LANES), 1)
        self.row = lax.broadcasted_iota(jnp.int32, (self.rows, LANES), 0)
        self.block = jnp.where(self.row < ny, self.row, self.row - ny)
        self.to_end = jnp.where(self.row < ny, ny, nz) - 1 - self.block
        first = (self.lane == 0) & (self.block == 0)
        last = (self.lane == LANES - 1) & (self.to_end == 0)
        self.face_low = 0.5 * (jnp.where(first, metric, self.before(metric, 1)) + metric)
        self.face_high = 0.5 * (metric + jnp.where(last, metric, self.after(metric, 1)))

    def before(self, x, by):
        rolled = lane_roll(x, by)
        value = jnp.where(self.lane < by, row_roll(rolled, 1), rolled)
        return jnp.where((self.lane < by) & (self.block == 0), 0.0, value)

    def after(self, x, by):
        rolled = lane_roll(x, -by)
        value = jnp.where(self.lane >= LANES - by, row_roll(rolled, -1), rolled)
        return jnp.where((self.lane >= LANES - by) & (self.to_end == 0), 0.0, value)

    def guess(self, sign):
        face = self.face_high if sign > 0 else self.face_low
        if sign > 0:
            cell = self.lane + LANES * self.block
        else:
            cell = LANES - 1 - self.lane + LANES * self.to_end
        near = face / (cell + 1).astype(jnp.float32)
        one_over = 1.0 / (face + jnp.sqrt(face + near * near))
        return face * one_over, implicit_fourth * one_over, one_over

    def sweep(self, sign, ratio, far):
        rows = self.rows
        back = self.before if sign > 0 else self.after
        if sign > 0:
            face_in, face_out, place = self.face_low, self.face_high, self.block
        else:
            face_in, face_out, place = self.face_high, self.face_low, self.to_end
        eps = 4.0 * implicit_fourth - implicit_fourth * back(ratio, 1)
        mass = (1.0 + 6.0 * implicit_fourth) - implicit_fourth * back(far, 2) - 2.0 * eps
        eps_in = back(eps, 1)
        scale = 1.0 / (face_in + 2.0 * eps_in)
        m = ((mass + face_in) * scale, mass - eps_in * eps_in * scale, scale, jnp.ones_like(scale))
        ahead = self.lane if sign > 0 else LANES - 1 - self.lane
        m = scan(m, ahead, LANES, 1, lambda x, by: lane_roll(x, sign * by), mm)
        edge = LANES - 1 if sign > 0 else 0
        total = tuple(jnp.broadcast_to(x[:, edge : edge + 1], (rows, LANES)) for x in m)
        total = scan(
            total, place, max(self.ny, self.nz), 1, lambda x, by: row_roll(x, sign * by), mm
        )
        top = jnp.where(place >= 1, row_roll(total[0], sign), 1.0)
        low = jnp.where(place >= 1, row_roll(total[2], sign), 0.0)
        eta = (m[0] * top + m[1] * low) / (m[2] * top + m[3] * low)
        one_over = 1.0 / (face_out + (eta + 2.0 * eps))
        return (face_out + eps) * one_over, implicit_fourth * one_over, one_over

    def finish(self, near_l, far_l, pivot_l, near_r, far_r):
        lane, block, to_end = self.lane, self.block, self.to_end
        even = (lane & 1) == 0
        near_l = jnp.where((to_end == 0) & (lane >= LANES - 1), 0.0, near_l)
        far_l = jnp.where((to_end == 0) & (lane >= LANES - 2), 0.0, far_l)
        near_r = jnp.where((block == 0) & (lane < 1), 0.0, near_r)
        far_r = jnp.where((block == 0) & (lane < 2), 0.0, far_r)

        def of_even(x):
            return jnp.where(even, x, lane_roll(x, 1))

        def of_odd(x):
            return jnp.where(even, lane_roll(x, -1), x)

        t0, t1, r0, r1 = of_even(near_l), of_odd(near_l), of_even(far_l), of_odd(far_l)
        from_right = (t0 * t1 - r0, -t0 * r1, t1, -r1)
        p1 = of_odd(pivot_l)
        left_inverse = (of_even(pivot_l) + t0 * t0 * p1, t0 * p1, t0 * p1, p1)
        s0, s1, q0, q1 = of_even(near_r), of_odd(near_r), of_even(far_r), of_odd(far_r)
        from_left = (-q0, s0, -s1 * q0, s1 * s0 - q1)
        from_left_after = tuple(self.after(x, 2) for x in from_left)
        from_right_before = tuple(self.before(x, 2) for x in from_right)
        diagonal = mm(inverse_of_one_minus(mm(from_right, from_left_after)), left_inverse)
        width = jnp.where(self.row < self.ny, self.wy, LANES)
        place = lane & (width - 1)
        right = scan(from_right, width - 1 - place, LANES, 2, lambda x, by: lane_roll(x, -by), mm)
        left = scan(from_left, place, LANES, 2, lane_roll, mm)
        return from_right, from_left, diagonal, right, left, from_right_before, from_left_after


def cell_weights(chain, column, even):
    return jnp.where(even, chain[column], chain[2 + column])


def first_kernel(ny, nz, partners, paired, flow_hbm, speed_hbm, metric_y, metric_z, *refs):
    high, low, factors, chains = refs[:4]
    count = 1 if paired else partners
    messages = refs[4 : 4 + count]
    flow, speed, metric, spread, arrived = refs[4 + count :]
    fields, planes_x, wy, _ = flow.shape
    rows = ny + nz
    core_rows = fields * planes_x * wy

    copies = [
        pltpu.make_async_copy(metric_y, metric.at[0:ny], arrived.at[fields]),
        pltpu.make_async_copy(metric_z, metric.at[ny:rows], arrived.at[fields + 1]),
        pltpu.make_async_copy(speed_hbm, speed, arrived.at[fields + 2]),
    ]
    for copy in copies:
        copy.start()
    for field in range(fields):
        pltpu.make_async_copy(flow_hbm.at[field], flow.at[field], arrived.at[field]).start()

    lane = lax.broadcasted_iota(jnp.int32, (wy, LANES), 1)
    extra_row = lax.broadcasted_iota(jnp.int32, (EXTRA, LANES), 0)
    for slot in range(planes_x):
        for part in range(3):
            spread[slot, part, 0:8, :] = jnp.zeros((8, LANES), jnp.float32)
            spread[slot, part, wy + 8 : wy + 16, :] = jnp.zeros((8, LANES), jnp.float32)
    side = time_step * (viscous + 4.0 * explicit_fourth)
    half = time_step * 0.5
    centre = time_step * (-6.0 * viscous - 12.0 * explicit_fourth)
    fourth = -time_step * explicit_fourth

    def store(start, column, value):
        first, second = halves(value)
        high[pl.ds(start, value.shape[0]), column : column + LANES] = first
        low[pl.ds(start, value.shape[0]), column : column + LANES] = second

    def one_field(field):
        values = [flow[field, x] for x in range(planes_x)]
        fluxes = [values[x] * speed[x] for x in range(planes_x)]
        aside = [(time_step * viscous) * u for u in values]
        extras = []
        for x in range(planes_x):
            u, flux, slot = values[x], fluxes[x], x
            total = centre * u
            if x + 1 < planes_x:
                total = total + (aside[x + 1] - fluxes[x + 1])
            if x > 0:
                total = total + (aside[x - 1] + fluxes[x - 1])
            scaled = side * u
            onward, backward, far = scaled + flux, scaled - flux, fourth * u
            spread[slot, 0, 8 : wy + 8, :] = onward
            spread[slot, 1, 8 : wy + 8, :] = backward
            spread[slot, 2, 8 : wy + 8, :] = far
            total = total + (spread[slot, 0, 7 : wy + 7, :] + spread[slot, 1, 9 : wy + 9, :])
            total = total + (spread[slot, 2, 6 : wy + 6, :] + spread[slot, 2, 10 : wy + 10, :])
            a, b = lane_roll(onward, 1), lane_roll(backward, -1)
            c, d = lane_roll(far, 2), lane_roll(far, -2)
            from_low, from_high = a + c, b + d
            ends = jnp.where(lane == 0, from_low, jnp.where(lane == 1, c, 0.0))
            ends = jnp.where(lane == LANES - 1, from_high, jnp.where(lane == LANES - 2, d, ends))
            index = field * planes_x + x
            start = index * wy
            store(start, 0, total + (from_low + from_high))
            store(start, LANES, ends)
            above = spread[slot, 1, 7:15, :] + spread[slot, 2, 8:16, :]
            below = spread[slot, 0, wy + 5 : wy + 13, :] + spread[slot, 2, wy + 4 : wy + 12, :]
            extras.append(jnp.where(extra_row < 2, above, jnp.where(extra_row < 4, below, 0.0)))
            if len(extras) == 2:
                start = core_rows + (index - 1) * EXTRA
                store(start, 0, jnp.concatenate(extras, axis=0))
                for ref in (high, low):
                    ref[pl.ds(start, 2 * EXTRA), LANES : 2 * LANES] = jnp.zeros(
                        (2 * EXTRA, LANES), jnp.bfloat16
                    )
                extras = []

    copies[0].wait()
    copies[1].wait()
    factor = Factor(metric[...], ny, nz, wy)

    guess_l, guess_r = factor.guess(1), factor.guess(-1)
    left, right = factor.sweep(1, *guess_l[:2]), factor.sweep(-1, *guess_r[:2])
    copies[2].wait()
    for x in range(planes_x):
        speed[x] = half * speed[x]
    for field in range(fields):
        pltpu.make_async_copy(flow_hbm.at[field], flow.at[field], arrived.at[field]).wait()
    left, right = factor.sweep(1, *left[:2]), factor.sweep(-1, *right[:2])
    for field in range(fields // 2):
        one_field(field)
    parts = factor.finish(*left, *right[:2])
    from_right, from_left, diagonal, to_right, to_left, before, after = parts
    for number, value in enumerate(v for part in parts for v in part):
        factors[number] = value
    for number, value in enumerate(to_right + to_left):
        chains[number] = value
    for field in range(fields // 2, fields):
        one_field(field)

    me = lax.axis_index("gz")
    mine = lax.broadcasted_iota(jnp.int32, (rows, LANES), 0) == ny + me
    even = (lax.broadcasted_iota(jnp.int32, (1, LANES), 1) & 1) == 0
    lane = lax.broadcasted_iota(jnp.int32, (1, LANES), 1)

    def own(values):
        return tuple(jnp.sum(jnp.where(mine, v, 0.0), axis=0, keepdims=True) for v in values)

    up, down = own(to_right), own(to_left)
    up_past, down_past = own(mm(before, to_right)), own(mm(after, to_left))
    unit = (1.0, 0.0, 0.0, 1.0)
    weights = []
    for column in range(2):
        same = jnp.where(even, unit[column], unit[2 + column])
        inside_up = cell_weights(up, column, even)
        inside_down = cell_weights(down, column, even)
        past_up = lane_roll(cell_weights(up_past, column, even), -2)
        past_down = lane_roll(cell_weights(down_past, column, even), 2)
        ends_up = jnp.where(lane < 2, same, past_up) - inside_up
        ends_down = jnp.where(lane < 2, past_down, same) - inside_down
        at_end = (lane < 2) | (lane >= LANES - 2)
        ends_up, ends_down = jnp.where(at_end, ends_up, 0.0), jnp.where(at_end, ends_down, 0.0)
        weights.append(
            (
                jnp.concatenate([inside_up, ends_up], axis=1),
                jnp.concatenate([inside_down, ends_down], axis=1),
            )
        )
    if paired:
        lower = (me & 1) == 0
        stack = [jnp.where(lower, w[0], w[1]) for w in weights]
        peer = lax.broadcasted_iota(jnp.int32, (rows, LANES), 0) == ny + jnp.bitwise_xor(me, 1)

        def of_peer(values, place):
            chosen = tuple(jnp.sum(jnp.where(peer, v, 0.0), axis=0, keepdims=True) for v in values)
            return tuple(jnp.broadcast_to(v[:, place : place + 1], (1, 2 * LANES)) for v in chosen)

        over, under = of_peer(to_right, 0), of_peer(to_left, LANES - 1)
        (up0, down0), (up1, down1) = weights
        for q in range(2):
            upward = jnp.where(lower, over[q] * up0 + over[2 + q] * up1, weights[q][0])
            downward = jnp.where(lower, weights[q][1], under[q] * down0 + under[2 + q] * down1)
            stack.append(jnp.where(me < 2, upward, downward))
    else:
        stack = []
        for k in range(1, partners + 1):
            upward = jnp.bitwise_xor(me, k) > me
            stack += [jnp.where(upward, w[0], w[1]) for w in weights]
    while len(stack) % 8:
        stack.append(jnp.zeros((1, 2 * LANES), jnp.float32))
    count = len(stack)
    stack = jnp.concatenate(stack, axis=0)
    first = stack.astype(jnp.bfloat16).astype(jnp.float32)
    both = jnp.concatenate([first, stack - first], axis=0).astype(jnp.bfloat16)
    across = (((1,), (1,)), ((), ()))
    total = high.shape[0]
    size = planes_x * wy
    for begin in range(0, total, size):
        rows = slice(begin, min(begin + size, total))
        on_high = matmul(both, high[rows, :], across)
        on_low = matmul(both, low[rows, :], across)
        moments = (on_high[:count] + on_high[count:]) + on_low[:count]
        if paired:
            messages[0][:, rows] = moments[0:4]
        else:
            for k in range(partners):
                messages[k][:, rows] = moments[2 * k : 2 * k + 2]


def dense_inverse(columns, start, width, stack):
    parts = 8
    steps = width // (2 * parts)
    lane = lax.broadcasted_iota(jnp.int32, (parts, LANES), 1)
    part = lax.broadcasted_iota(jnp.int32, (parts, LANES), 0)
    fits = width + 4 <= LANES
    values = [columns[pl.ds(start + 2 * i, parts, stride=2 * steps), :] for i in range(steps)]

    def wide(i, number):
        return tuple(
            jnp.broadcast_to(values[i][:, number + k : number + k + 1], (parts, LANES)) for k in range(4)
        )

    blocks = [wide(i, 8) for i in range(steps)]
    zero, one = jnp.zeros((parts, LANES), jnp.float32), jnp.ones((parts, LANES), jnp.float32)

    def put(rows, i, extra, extra_lane, owner):
        first = 2 * (part * steps + i)
        out = []
        for r in range(2):
            row = jnp.where(lane == first, blocks[i][2 * r], rows[r])
            row = jnp.where(lane == first + 1, blocks[i][2 * r + 1], row)
            if extra is not None and fits:
                row = jnp.where((part == owner) & (lane == extra_lane), extra[2 * r], row)
                row = jnp.where((part == owner) & (lane == extra_lane + 1), extra[2 * r + 1], row)
            out.append(row)
        return tuple(out)

    def run(order, number, ends, extra_lane, owner):
        rows, product, out = (zero, zero), (one, zero, zero, one), {}
        for i in order:
            t = wide(i, number)
            rows = (t[0] * rows[0] + t[1] * rows[1], t[2] * rows[0] + t[3] * rows[1])
            extra = None
            if i == order[0]:
                e = wide(i, ends)
                extra = mm(blocks[i], (e[0], e[2], e[1], e[3]))
            rows = put(rows, i, extra, extra_lane, owner)
            product = mm(t, product)
            out[i] = rows, product
        rows, product = out[order[-1]]
        entering, last = [None] * parts, (jnp.zeros((1, LANES), jnp.float32),) * 2
        sequence = range(parts) if number == 4 else range(parts - 1, -1, -1)
        for p in sequence:
            entering[p] = last
            own, across = [r[p : p + 1] for r in rows], [x[p : p + 1] for x in product]
            last = (
                own[0] + across[0] * last[0] + across[1] * last[1],
                own[1] + across[2] * last[0] + across[3] * last[1],
            )
        entering = [jnp.concatenate([e[r] for e in entering], axis=0) for r in range(2)]
        result = []
        for i in range(steps):
            rows, product = out[i]
            for r in range(2):
                result.append(rows[r] + product[2 * r] * entering[0] + product[2 * r + 1] * entering[1])
        return result

    low = run(list(range(steps)), 4, 12, width, 0)
    high = run(list(range(steps - 1, -1, -1)), 0, 16, width + 2, parts - 1)
    for k in range(2 * steps):
        lower = lane <= 2 * (part * steps + k // 2) + 1
        if fits:
            lower = lower & (lane < width) | ((lane >= width) & (lane < width + 2))
        stack[parts * k : parts * (k + 1), :] = jnp.where(lower, low[k], high[k])
    rows = [stack[pl.ds(p, 2 * steps, stride=parts), :] for p in range(parts)]
    return jnp.concatenate(rows, axis=0)


def stage_plan(count):
    plan, stride = [], 1
    while stride < count:
        radix = 4 if count // stride >= 4 else 2
        plan.append((stride, radix))
        stride *= radix
    return plan


def transposed(factors, row):
    rows = [factors[number, pl.ds(row, 1), :] for number in range(12)]
    rows += [factors[20 + number, pl.ds(row, 1), :] for number in range(8)]
    rows += [factors[12 + number, pl.ds(row, 1), :] for number in range(8)]
    rows.append(jnp.zeros((4, LANES), jnp.float32))
    return jnp.concatenate(rows, axis=0).T


def chain_products(chains, number, place, blocks, begins, ends, masks, reverse):
    count = -(-len(begins) // 8) * 8
    row = lax.broadcasted_iota(jnp.int32, (count, LANES), 0)
    begin = jnp.zeros((count, LANES), jnp.int32)
    end, mask = begin, jnp.zeros((count, LANES), jnp.float32)
    for r, (b, e, m) in enumerate(zip(begins, ends, masks)):
        begin, end = jnp.where(row == r, b, begin), jnp.where(row == r, e, end)
        mask = jnp.where(row == r, m, mask)
    one, zero = jnp.ones((count, LANES), jnp.float32), jnp.zeros((count, LANES), jnp.float32)
    product = (one, zero, zero, one)
    for block in range(blocks - 1, -1, -1) if reverse else range(blocks):
        where = place(block)
        value = tuple(chains[number + k, where[0], where[1]] for k in range(4))
        product = pick((begin <= block) & (block < end), mm(product, value), product)
    return tuple(x * mask for x in product)


def truth(condition):
    return jnp.where(condition, 1.0, 0.0)


def inverse_z_kernel(ny, planes, wy, factors, matrix, spread_high, spread_low, columns, stacked, rows_ref):
    me_z = lax.axis_index("gz")
    columns[0:LANES, 0:32] = transposed(factors, ny + me_z)
    inverse = dense_inverse(columns, 0, LANES, stacked)
    rows_ref[0:LANES, :] = inverse
    rows_ref[LANES : 2 * LANES, :] = jnp.zeros((LANES, LANES), jnp.float32)
    past = tuple(columns[LANES - 1 : LANES, 16 + k : 17 + k] for k in range(4))
    ahead = tuple(columns[0:1, 12 + k : 13 + k] for k in range(4))
    head0, head1 = rows_ref[0:1, :], rows_ref[1:2, :]
    tail0, tail1 = rows_ref[LANES - 2 : LANES - 1, :], rows_ref[LANES - 1 : LANES, :]
    for q in range(2):
        beyond = past[2 * q] * tail0 + past[2 * q + 1] * tail1
        rows_ref[LANES + q : LANES + q + 1, :] = beyond - (head0, head1)[q]
        beyond = ahead[2 * q] * head0 + ahead[2 * q + 1] * head1
        rows_ref[2 * LANES - 2 + q : 2 * LANES - 1 + q, :] = beyond - (tail0, tail1)[q]
    first, second = halves(rows_ref[...])
    matrix[:, 0:LANES] = first
    matrix[:, LANES : 2 * LANES] = second

    cell = lax.axis_index("gy") * wy
    row = cell // LANES
    total = planes * (wy + EXTRA)
    unit = (1.0, 0.0, 0.0, 1.0)
    lane = lax.broadcasted_iota(jnp.int32, (1, LANES), 1)
    even = (lane & 1) == 0

    def chain(number):
        return tuple(factors[number + k, pl.ds(row, 1), :] for k in range(4))

    def turned(x, by):
        return pltpu.roll(x, lax.rem(by + 2 * LANES, LANES), 1)

    def tiled(x, period):
        x = jnp.where(lane < period, x, 0.0)
        while period < LANES:
            x = x + lane_roll(x, period)
            period *= 2
        return x

    up, down, before, after = chain(12), chain(16), chain(20), chain(24)
    past_up, past_down = mm(before, up), mm(after, down)
    plane_row = lax.broadcasted_iota(jnp.int32, (planes, LANES), 0)
    wide_lane = lax.broadcasted_iota(jnp.int32, (planes, LANES), 1)
    for column in range(2):
        same = jnp.where(even, unit[column], unit[2 + column])
        for number, inside, early, late in (
            (column, up, turned(cell_weights(past_up, column, even), -start_y(cell)), same),
            (
                2 + column,
                down,
                same,
                turned(cell_weights(past_down, column, even), 4 - wy - start_y(cell)),
            ),
        ):
            inside = tiled(turned(cell_weights(inside, column, even), -start_y(cell)), wy)
            past = jnp.where(lane < 2, early, jnp.where(lane < 4, late, 0.0))
            past = tiled(past, EXTRA)
            rows = slice(number * planes, (number + 1) * planes)
            for begin in range(0, total, LANES):
                if begin < planes * wy:
                    owner, value = (begin + wide_lane) // wy, inside
                else:
                    owner, value = (begin - planes * wy + wide_lane) // EXTRA, past
                size = min(LANES, total - begin)
                first, second = halves(jnp.where(plane_row == owner, value, 0.0))
                spread_high[rows, begin : begin + size] = first[:, 0:size]
                spread_low[rows, begin : begin + size] = second[:, 0:size]


def whole_rows(matrix, row):
    start = row // 16 * 16
    both = matrix[start : start + 16, :].astype(jnp.float32)
    value = both[:, 0:LANES] + both[:, LANES : 2 * LANES]
    return value[row - start : row - start + 1]


def second_kernel(
    ny, nz, count_z, wy, partners, paired, chains, factors, matrix, high, low, local, moments, entering, *scratch
):
    columns, weights_y = scratch
    me_z, me_y = lax.axis_index("gz"), lax.axis_index("gy")
    planes = moments.shape[0] // 4
    head0, head1 = whole_rows(matrix, 0), whole_rows(matrix, 1)
    tail0, tail1 = whole_rows(matrix, LANES - 2), whole_rows(matrix, LANES - 1)

    if paired:
        pair = me_z // 2 * 2
        begins, ends = [me_z, pair], [me_z + 1, pair + 2]
        lowers = [me_z % 2 == 1, pair > 0]
    else:
        others = [jnp.bitwise_xor(me_z, k) for k in range(1, partners + 1)]
        begins, ends = [other + 1 for other in others], others
        lowers = [other < me_z for other in others]
    size = len(begins)
    up = chain_products(
        chains, 0, lambda b: (ny + b, 0), count_z, begins, [me_z] * size, [1.0] * size, False
    )
    down = chain_products(
        chains, 4, lambda b: (ny + b, LANES - 1), count_z, [me_z + 1] * size, ends, [1.0] * size, True
    )
    stack = []
    for k, lower in enumerate(lowers):
        for p in range(2):
            from_low = up[2 * p][k : k + 1] * head0 + up[2 * p + 1][k : k + 1] * head1
            from_high = down[2 * p][k : k + 1] * tail0 + down[2 * p + 1][k : k + 1] * tail1
            stack.append(jnp.where(lower, from_low, from_high))
    while len(stack) % 8:
        stack.append(jnp.zeros((1, LANES), jnp.float32))
    stack = jnp.concatenate(stack, axis=0)
    first = stack.astype(jnp.bfloat16).astype(jnp.float32)
    entering[...] = jnp.concatenate([first, stack - first, first], axis=0)

    cell = me_y * wy
    columns[0:LANES, 0:32] = transposed(factors, cell // LANES)
    start = lax.rem(cell, LANES)
    row = lax.broadcasted_iota(jnp.int32, (wy, LANES), 0)
    extra_row = lax.broadcasted_iota(jnp.int32, (EXTRA, LANES), 0)
    unit = (1.0, 0.0, 0.0, 1.0)

    def head(number):
        return tuple(columns[pl.ds(start, 1), number + k : number + k + 1] for k in range(4))

    def tail(number):
        return tuple(columns[pl.ds(start + wy - 1, 1), number + k : number + k + 1] for k in range(4))

    past_up, past_down = mm(head(12), head(20)), mm(tail(16), tail(24))
    for column in range(2):
        for output, number in ((column, 20), (2 + column, 24)):
            even = columns[pl.ds(start, wy), number + column : number + column + 1]
            odd = columns[pl.ds(start, wy), number + 2 + column : number + 3 + column]
            weights_y[output, 0:wy, :] = jnp.where((row & 1) == 0, even, odd)
        for output, early, late in (
            (column, (past_up[column], past_up[2 + column]), (unit[column], unit[2 + column])),
            (2 + column, (unit[column], unit[2 + column]), (past_down[column], past_down[2 + column])),
        ):
            value = jnp.zeros((EXTRA, LANES), jnp.float32)
            for r, v in enumerate(early + late):
                value = jnp.where(extra_row == r, v, value)
            weights_y[output, wy : wy + EXTRA, :] = value

    total = planes * (wy + EXTRA)

    def solve(begin, size):
        rows = slice(begin, begin + size)
        both = matmul(high[rows, :], matrix[...])
        value = both[:, 0:LANES] + (both[:, LANES : 2 * LANES] + matmul(low[rows, :], matrix[:, 0:LANES]))
        local[rows, :] = value
        return value

    extra = solve(planes * wy, planes * EXTRA)
    for part in range(planes // 8):
        core = solve(part * 8 * wy, 8 * wy)
        for number in range(4):
            lines = []
            for k in range(8):
                index = part * 8 + k
                value = jnp.sum(core[k * wy : (k + 1) * wy] * weights_y[number, 0:wy, :], axis=0, keepdims=True)
                past = extra[index * EXTRA : (index + 1) * EXTRA] * weights_y[number, wy : wy + EXTRA, :]
                lines.append(value + jnp.sum(past, axis=0, keepdims=True))
            start = number * planes + part * 8
            moments[start : start + 8, :] = jnp.concatenate(lines, axis=0)


def start_y(cell):
    return lax.rem(cell, LANES)


def y_kernel(count_y, wy, chains, factors, unused, inverse_y, coefs, columns, stacked):
    me_y = lax.axis_index("gy")
    cell = me_y * wy
    columns[0:LANES, 0:32] = transposed(factors, cell // LANES)
    start = lax.rem(cell, LANES)
    inverse_y[...] = dense_inverse(columns, start, wy, stacked)

    up, down = ([], [], []), ([], [], [])
    plan = stage_plan(count_y)
    for number, (stride, radix) in enumerate(plan):
        group = me_y // stride
        first = (group // radix) * radix
        others = [first + jnp.bitwise_xor(group - first, k) for k in range(radix)]
        for other in others[1:]:
            for lists, values in (
                (up, ((other + 1) * stride, me_y, truth(other < group))),
                (down, (me_y + 1, other * stride, truth(other > group))),
            ):
                for one, value in zip(lists, values):
                    one.append(value)
        if number + 1 < len(plan):
            for other in others:
                for lists, values in (
                    (up, ((other + 1) * stride, (first + radix) * stride, 1.0)),
                    (down, (first * stride, other * stride, 1.0)),
                ):
                    for one, value in zip(lists, values):
                        one.append(value)

    def place(block):
        return block * wy // LANES, block * wy % LANES

    def place_end(block):
        return place(block)[0], place(block)[1] + wy - 1

    for base, value in (
        (0, chain_products(chains, 0, place, count_y, *up, False)),
        (4, chain_products(chains, 4, place_end, count_y, *down, True)),
    ):
        for k in range(4):
            coefs[base + k] = value[k]


def pair_kernel(own, received, unused, total):
    total[...] = own[2:4] + received[2:4]


def arrived_rows(messages, count):
    rows = [m[0:2] for m in messages]
    if count > 2 * len(messages):
        rows.append(jnp.zeros((count - 2 * len(messages), rows[0].shape[1]), jnp.float32))
    return jnp.concatenate(rows, axis=0)


def third_kernel(moments, spread_high, spread_low, entering, *refs):
    messages, carried = refs[:-1][::-1], refs[-1]
    count = entering.shape[0] // 3
    received = arrived_rows(messages, count)
    first = received.astype(jnp.bfloat16).astype(jnp.float32)
    both = jnp.concatenate([first, received - first], axis=0).astype(jnp.bfloat16)
    top = jnp.concatenate([first, jnp.zeros_like(first)], axis=0).astype(jnp.bfloat16)
    across = (((1,), (1,)), ((), ()))
    corner = matmul(spread_high[...], both, across) + matmul(spread_low[...], top, across)
    values = entering[0:count, :] + entering[count : 2 * count, :]
    added = lax.dot_general(
        corner,
        jnp.concatenate([values, values], axis=0),
        (((1,), (0,)), ((), ())),
        precision=lax.Precision.HIGHEST,
        preferred_element_type=jnp.float32,
    )
    planes = carried.shape[1]
    for number in range(4):
        rows = slice(number * planes, (number + 1) * planes)
        carried[number] = moments[rows, :] + added[rows]


def local_y_kernel(wy, local, entering, inverse_y, unused, *refs):
    messages, (out, solved) = refs[:-2], refs[-2:]
    planes = out.shape[0]
    count = entering.shape[0] // 3
    received = arrived_rows(messages, count)
    first = received.astype(jnp.bfloat16).astype(jnp.float32)
    received = jnp.concatenate([first, first, received - first], axis=0).T.astype(jnp.bfloat16)
    solved[...] = local[...] + matmul(received, entering[...].astype(jnp.bfloat16))
    first, second = halves(inverse_y[:, 0 : wy + EXTRA])
    left = jnp.concatenate([first, second, first], axis=1)

    def part(index, carry):
        for k in range(8):
            number = index * 8 + k
            start = pl.multiple_of(number * wy, 8)
            core = solved[pl.ds(start, wy), :]
            start = pl.multiple_of(planes * wy + number * EXTRA, 8)
            both = jnp.concatenate([core, solved[pl.ds(start, EXTRA), :]], axis=0)
            top, rest = halves(both)
            out[number] = matmul(left, jnp.concatenate([top, top, rest], axis=0))
        return carry

    lax.fori_loop(0, planes // 8, part, 0)


def combine(coefs, side, row, values):
    first = 0 if side == 0 else 2
    out = [None, None]
    for k, value in enumerate(values):
        for q in range(2):
            for p in range(2):
                term = coefs[side + 2 * p + q, row + k : row + k + 1, :] * value[first + p]
                out[q] = term if out[q] is None else out[q] + term
    return out


def stage_kernel(base, stride, radix, narrow, has_entered, coefs, *refs):
    values = refs[:radix]
    position = radix
    entered = None
    if has_entered:
        entered = refs[position]
        position += 1
    message, entering = refs[position : position + 2]
    below = combine(coefs, 0, base, values[1:])
    above = combine(coefs, 4, base, values[1:])
    for row, value in enumerate(below + above):
        entering[row] = value if entered is None else value + entered[row]
    upward = combine(coefs, 0, base + radix - 1, values)
    downward = combine(coefs, 4, base + radix - 1, values)
    if narrow:
        group = lax.axis_index("gy") // (stride * radix)
        sends_up = lax.rem(group, 2) == 0
        for row in range(2):
            message[row] = jnp.where(sends_up, upward[row], downward[row])
    else:
        for row, value in enumerate(upward + downward):
            message[row] = value


def last_kernel(base, radix, narrow, wy, coefs, local, inverse_y, entered, *refs):
    messages, (out_hbm, out, sent) = refs[: radix - 1], refs[radix - 1 :]
    values = list(messages)
    if narrow:
        values = [(m[0], m[1], m[0], m[1]) for m in values]
    below = combine(coefs, 0, base, values)
    above = combine(coefs, 4, base, values)
    st = [value + entered[row] for row, value in enumerate(below + above)]
    sides = [
        jnp.broadcast_to(inverse_y[:, c : c + 1], (wy, LANES)) for c in (0, 1, wy - 2, wy - 1)
    ]
    fields, planes_x = out.shape[:2]
    copies = []
    for field in range(fields):
        for x in range(planes_x):
            index = field * planes_x + x
            value = local[index]
            for number in range(4):
                value = value + sides[number] * st[number][index : index + 1]
            out[field, x] = value
            if (x + 1) % 4 == 0:
                part = (field, pl.ds(x - 3, 4))
                copy = pltpu.make_async_copy(out.at[part], out_hbm.at[part], sent.at[len(copies)])
                copy.start()
                copies.append(copy)
    for copy in copies:
        copy.wait()


VMEM = pl.BlockSpec(memory_space=pltpu.VMEM)
HBM = pl.BlockSpec(memory_space=pltpu.HBM)
SMEM = pl.BlockSpec(memory_space=pltpu.SMEM)
PARAMS = pltpu.CompilerParams(vmem_limit_bytes=40 * 1024 * 1024)


def array(*shape):
    return jax.ShapeDtypeStruct(shape, jnp.float32)


def in_hbm(x):
    return pltpu.with_memory_space_constraint(x, pltpu.HBM)


def cost(flops, data):
    return pl.CostEstimate(flops=flops, bytes_accessed=data, transcendentals=0)


def on_device(mesh, flow, speed, metric_y, metric_z):
    fields, planes_x, wy, wz = flow.shape
    count_y, count_z = mesh.shape["gy"], mesh.shape["gz"]
    assert wz == LANES
    ny, nz = metric_y.shape[0] // LANES, metric_z.shape[0] // LANES
    planes = fields * planes_x
    rows = planes * (wy + EXTRA)
    partners = count_z - 1
    paired = False
    arrivals = 2 if paired else partners
    entering_rows = -(-2 * arrivals // 8) * 8
    half = jax.ShapeDtypeStruct((rows, 2 * LANES), jnp.bfloat16)
    outputs = pl.pallas_call(
        functools.partial(first_kernel, ny, nz, partners, paired),
        out_shape=[half, half, array(28, ny + nz, LANES), array(8, ny + nz, LANES)]
        + ([array(4, rows)] if paired else [array(2, rows)] * partners),
        in_specs=[HBM] * 4,
        out_specs=[VMEM] * (5 if paired else 4 + partners),
        scratch_shapes=[
            pltpu.VMEM(flow.shape, jnp.float32),
            pltpu.VMEM(speed.shape, jnp.float32),
            pltpu.VMEM((ny + nz, LANES), jnp.float32),
            pltpu.VMEM((planes_x, 3, wy + 16, LANES), jnp.float32),
            pltpu.SemaphoreType.DMA((fields + 3,)),
        ],
        compiler_params=PARAMS,
        name="forcing_and_factor",
    )(*(in_hbm(x) for x in (flow, speed, metric_y.reshape(ny, LANES), metric_z.reshape(nz, LANES))))
    high, low, factors, chains = outputs[:4]

    def exchange(values, axis, count, stride, radix):
        received = {}
        for k in reversed(range(1, radix)):
            pairs = [(i, i ^ (k * stride)) for i in range(count)]
            received[k] = lax.ppermute(values[k - 1], axis, pairs)
        return [received[k] for k in range(1, radix)]

    plan = stage_plan(count_y)
    work = [pltpu.VMEM((LANES + 16, LANES), jnp.float32)] * 2
    spread = jax.ShapeDtypeStruct((4 * planes, rows), jnp.bfloat16)
    matrix, spread_high, spread_low = pl.pallas_call(
        functools.partial(inverse_z_kernel, ny, planes, wy),
        out_shape=[jax.ShapeDtypeStruct((2 * LANES, 2 * LANES), jnp.bfloat16), spread, spread],
        in_specs=[VMEM],
        out_specs=[VMEM] * 3,
        scratch_shapes=work + [pltpu.VMEM((2 * LANES, LANES), jnp.float32)],
        compiler_params=PARAMS,
        cost_estimate=cost(rows * 1024, 4 * rows * 64),
        name="inverse_z",
    )(factors)
    if paired:
        near = exchange(outputs[4:], "gz", count_z, 1, 2)
        total = pl.pallas_call(
            pair_kernel,
            out_shape=array(2, rows),
            in_specs=[VMEM] * 2 + [HBM],
            out_specs=VMEM,
            compiler_params=PARAMS,
            name="join_pair",
        )(outputs[4], near[0], matrix)
        received = near + exchange([total], "gz", count_z, 2, 2)
    else:
        received = exchange(outputs[4:], "gz", count_z, 1, count_z)
    local, moments, entering = pl.pallas_call(
        functools.partial(second_kernel, ny, nz, count_z, wy, partners, paired),
        out_shape=[
            array(rows, LANES),
            array(4 * planes, LANES),
            array(3 * entering_rows, LANES),
        ],
        in_specs=[SMEM] + [VMEM] * 4,
        out_specs=[VMEM] * 3,
        scratch_shapes=[
            pltpu.VMEM((LANES + 16, LANES), jnp.float32),
            pltpu.VMEM((4, wy + EXTRA, LANES), jnp.float32),
        ],
        compiler_params=PARAMS,
        cost_estimate=cost(2 * rows * 256 * 128 * 6, 4 * rows * 384),
        name="local_z",
    )(chains, factors, matrix, high, low)
    carried = pl.pallas_call(
        third_kernel,
        out_shape=array(4, planes, LANES),
        in_specs=[VMEM] * (4 + arrivals),
        out_specs=VMEM,
        compiler_params=PARAMS,
        name="carried_y",
    )(moments, spread_high, spread_low, entering, *received[::-1])
    arrived = received

    narrow = plan[-1][1] == 2 and len(plan) > 1
    base, entered, result = 0, None, None
    for number, (stride, radix) in enumerate(plan):
        received = exchange([carried] * (radix - 1), "gy", count_y, stride, radix)
        if number == 0:
            entries = sum(2 * radix - 1 for _, radix in plan[:-1]) + plan[-1][1] - 1
            inverse_y, coefs = pl.pallas_call(
                functools.partial(y_kernel, count_y, wy),
                out_shape=[array(wy, LANES), array(8, -(-entries // 8) * 8, LANES)],
                in_specs=[SMEM, VMEM, HBM],
                out_specs=[VMEM] * 2,
                scratch_shapes=work,
                compiler_params=PARAMS,
                cost_estimate=cost(2 * rows * 128 * 128 * 6, 4 * rows * 256),
                name="inverse_y",
            )(chains, factors, carried)
        if number + 1 < len(plan):
            slim = narrow and number + 2 == len(plan)
            inputs = [carried] + received + ([entered] if entered is not None else [])
            carried, entered = pl.pallas_call(
                functools.partial(stage_kernel, base, stride, radix, slim, entered is not None),
                out_shape=[array(2 if slim else 4, planes, LANES), array(4, planes, LANES)],
                in_specs=[VMEM] * (1 + len(inputs)),
                out_specs=[VMEM] * 2,
                compiler_params=PARAMS,
                name="join_groups",
            )(coefs, *inputs)
            base += 2 * radix - 1
            if number == 0:
                result = pl.pallas_call(
                    functools.partial(local_y_kernel, wy),
                    out_shape=array(planes, wy, LANES),
                    in_specs=[VMEM] * 3 + [HBM] + [VMEM] * arrivals,
                    out_specs=VMEM,
                    scratch_shapes=[pltpu.VMEM((rows, LANES), jnp.float32)],
                    compiler_params=PARAMS,
                    cost_estimate=cost(2 * rows * 128 * 128 * 6, 4 * rows * 256),
                    name="local_y",
                )(local, entering, inverse_y, entered, *arrived)
        else:
            return pl.pallas_call(
                functools.partial(last_kernel, base, radix, narrow, wy),
                out_shape=array(fields, planes_x, wy, wz),
                in_specs=[VMEM] * (4 + len(received)),
                out_specs=HBM,
                scratch_shapes=[
                    pltpu.VMEM(flow.shape, jnp.float32),
                    pltpu.SemaphoreType.DMA((planes // 4,)),
                ],
                compiler_params=PARAMS,
                name="finish_y",
            )(coefs, result, inverse_y, entered, *received)


def solution(mesh):
    placed = (P(None, None, "gy", "gz"), P(None, "gy", "gz"), P(), P())
    return jax.shard_map(
        functools.partial(on_device, mesh),
        mesh=mesh,
        in_specs=placed,
        out_specs=P(None, None, "gy", "gz"),
        check_vma=False,
    )
```

```python
import functools

import jax
import jax.numpy as jnp
from jax import lax
from jax.experimental import pallas as pl
from jax.experimental.pallas import tpu as pltpu
from jax.sharding import PartitionSpec as P

viscous = 0.25
explicit_fourth = 0.04
implicit_fourth = 0.05
time_step = 1048576.0
LANES = 128
EXTRA = 8


def mm(a, b):
    return (
        a[0] * b[0] + a[1] * b[2],
        a[0] * b[1] + a[1] * b[3],
        a[2] * b[0] + a[3] * b[2],
        a[2] * b[1] + a[3] * b[3],
    )


def inverse_of_one_minus(a):
    p, q, r, s = 1.0 - a[0], -a[1], -a[2], 1.0 - a[3]
    d = 1.0 / (p * s - q * r)
    return (s * d, -q * d, -r * d, p * d)


def pick(condition, a, b):
    return tuple(jnp.where(condition, x, y) for x, y in zip(a, b))


def halves(x):
    high = x.astype(jnp.bfloat16)
    return high, (x - high.astype(jnp.float32)).astype(jnp.bfloat16)


def matmul(a, b, dims=(((1,), (0,)), ((), ()))):
    return lax.dot_general(a, b, dims, preferred_element_type=jnp.float32)


def scan(m, ahead, count, step, shift, product):
    unit = (1.0, 0.0, 0.0, 1.0)

    def moved(by):
        return tuple(jnp.where(ahead >= by, shift(x, by), u) for x, u in zip(m, unit))

    while step < count:
        if 2 * step < count:
            m = product(product(m, moved(step)), product(moved(2 * step), moved(3 * step)))
            step *= 4
        else:
            m = product(m, moved(step))
            step *= 2
    return m


def lane_roll(x, by):
    return pltpu.roll(x, by % LANES, 1)


def row_roll(x, by):
    by = by % x.shape[0]
    return jnp.concatenate([x[x.shape[0] - by :], x[: x.shape[0] - by]], axis=0)


class Factor:
    def __init__(self, metric, ny, nz, wy):
        self.ny, self.nz, self.wy, self.rows = ny, nz, wy, ny + nz
        self.lane = lax.broadcasted_iota(jnp.int32, (self.rows, LANES), 1)
        self.row = lax.broadcasted_iota(jnp.int32, (self.rows, LANES), 0)
        self.block = jnp.where(self.row < ny, self.row, self.row - ny)
        self.to_end = jnp.where(self.row < ny, ny, nz) - 1 - self.block
        first = (self.lane == 0) & (self.block == 0)
        last = (self.lane == LANES - 1) & (self.to_end == 0)
        self.face_low = 0.5 * (jnp.where(first, metric, self.before(metric, 1)) + metric)
        self.face_high = 0.5 * (metric + jnp.where(last, metric, self.after(metric, 1)))

    def before(self, x, by):
        rolled = lane_roll(x, by)
        value = jnp.where(self.lane < by, row_roll(rolled, 1), rolled)
        return jnp.where((self.lane < by) & (self.block == 0), 0.0, value)

    def after(self, x, by):
        rolled = lane_roll(x, -by)
        value = jnp.where(self.lane >= LANES - by, row_roll(rolled, -1), rolled)
        return jnp.where((self.lane >= LANES - by) & (self.to_end == 0), 0.0, value)

    def guess(self, sign):
        face = self.face_high if sign > 0 else self.face_low
        if sign > 0:
            cell = self.lane + LANES * self.block
        else:
            cell = LANES - 1 - self.lane + LANES * self.to_end
        near = face / (cell + 1).astype(jnp.float32)
        one_over = 1.0 / (face + jnp.sqrt(face + near * near))
        return face * one_over, implicit_fourth * one_over, one_over

    def sweep(self, sign, ratio, far):
        rows = self.rows
        back = self.before if sign > 0 else self.after
        if sign > 0:
            face_in, face_out, place = self.face_low, self.face_high, self.block
        else:
            face_in, face_out, place = self.face_high, self.face_low, self.to_end
        eps = 4.0 * implicit_fourth - implicit_fourth * back(ratio, 1)
        mass = (1.0 + 6.0 * implicit_fourth) - implicit_fourth * back(far, 2) - 2.0 * eps
        eps_in = back(eps, 1)
        scale = 1.0 / (face_in + 2.0 * eps_in)
        m = ((mass + face_in) * scale, mass - eps_in * eps_in * scale, scale, jnp.ones_like(scale))
        ahead = self.lane if sign > 0 else LANES - 1 - self.lane
        m = scan(m, ahead, LANES, 1, lambda x, by: lane_roll(x, sign * by), mm)
        edge = LANES - 1 if sign > 0 else 0
        total = tuple(jnp.broadcast_to(x[:, edge : edge + 1], (rows, LANES)) for x in m)
        total = scan(
            total, place, max(self.ny, self.nz), 1, lambda x, by: row_roll(x, sign * by), mm
        )
        top = jnp.where(place >= 1, row_roll(total[0], sign), 1.0)
        low = jnp.where(place >= 1, row_roll(total[2], sign), 0.0)
        eta = (m[0] * top + m[1] * low) / (m[2] * top + m[3] * low)
        one_over = 1.0 / (face_out + (eta + 2.0 * eps))
        return (face_out + eps) * one_over, implicit_fourth * one_over, one_over

    def finish(self, near_l, far_l, pivot_l, near_r, far_r):
        lane, block, to_end = self.lane, self.block, self.to_end
        even = (lane & 1) == 0
        near_l = jnp.where((to_end == 0) & (lane >= LANES - 1), 0.0, near_l)
        far_l = jnp.where((to_end == 0) & (lane >= LANES - 2), 0.0, far_l)
        near_r = jnp.where((block == 0) & (lane < 1), 0.0, near_r)
        far_r = jnp.where((block == 0) & (lane < 2), 0.0, far_r)

        def of_even(x):
            return jnp.where(even, x, lane_roll(x, 1))

        def of_odd(x):
            return jnp.where(even, lane_roll(x, -1), x)

        t0, t1, r0, r1 = of_even(near_l), of_odd(near_l), of_even(far_l), of_odd(far_l)
        from_right = (t0 * t1 - r0, -t0 * r1, t1, -r1)
        p1 = of_odd(pivot_l)
        left_inverse = (of_even(pivot_l) + t0 * t0 * p1, t0 * p1, t0 * p1, p1)
        s0, s1, q0, q1 = of_even(near_r), of_odd(near_r), of_even(far_r), of_odd(far_r)
        from_left = (-q0, s0, -s1 * q0, s1 * s0 - q1)
        from_left_after = tuple(self.after(x, 2) for x in from_left)
        from_right_before = tuple(self.before(x, 2) for x in from_right)
        diagonal = mm(inverse_of_one_minus(mm(from_right, from_left_after)), left_inverse)
        width = jnp.where(self.row < self.ny, self.wy, LANES)
        place = lane & (width - 1)
        right = scan(from_right, width - 1 - place, LANES, 2, lambda x, by: lane_roll(x, -by), mm)
        left = scan(from_left, place, LANES, 2, lane_roll, mm)
        return from_right, from_left, diagonal, right, left, from_right_before, from_left_after


def cell_weights(chain, column, even):
    return jnp.where(even, chain[column], chain[2 + column])


def first_kernel(ny, nz, partners, flow_hbm, speed_hbm, metric_y, metric_z, *refs):
    high, low, factors, chains = refs[:4]
    messages = refs[4 : 4 + partners]
    flow, speed, metric, spread, arrived = refs[4 + partners :]
    fields, planes_x, wy, _ = flow.shape
    rows = ny + nz
    core_rows = fields * planes_x * wy

    copies = [
        pltpu.make_async_copy(metric_y, metric.at[0:ny], arrived.at[fields]),
        pltpu.make_async_copy(metric_z, metric.at[ny:rows], arrived.at[fields + 1]),
        pltpu.make_async_copy(speed_hbm, speed, arrived.at[fields + 2]),
    ]
    for copy in copies:
        copy.start()
    for field in range(fields):
        pltpu.make_async_copy(flow_hbm.at[field], flow.at[field], arrived.at[field]).start()

    lane = lax.broadcasted_iota(jnp.int32, (wy, LANES), 1)
    extra_row = lax.broadcasted_iota(jnp.int32, (EXTRA, LANES), 0)
    for slot in range(planes_x):
        for part in range(3):
            spread[slot, part, 0:8, :] = jnp.zeros((8, LANES), jnp.float32)
            spread[slot, part, wy + 8 : wy + 16, :] = jnp.zeros((8, LANES), jnp.float32)
    side = time_step * (viscous + 4.0 * explicit_fourth)
    half = time_step * 0.5
    centre = time_step * (-6.0 * viscous - 12.0 * explicit_fourth)
    fourth = -time_step * explicit_fourth

    def store(start, column, value):
        first, second = halves(value)
        high[pl.ds(start, value.shape[0]), column : column + LANES] = first
        low[pl.ds(start, value.shape[0]), column : column + LANES] = second

    def one_field(field):
        values = [flow[field, x] for x in range(planes_x)]
        fluxes = [values[x] * speed[x] for x in range(planes_x)]
        aside = [(time_step * viscous) * u for u in values]
        extras = []
        for x in range(planes_x):
            u, flux, slot = values[x], fluxes[x], x
            total = centre * u
            if x + 1 < planes_x:
                total = total + (aside[x + 1] - fluxes[x + 1])
            if x > 0:
                total = total + (aside[x - 1] + fluxes[x - 1])
            scaled = side * u
            onward, backward, far = scaled + flux, scaled - flux, fourth * u
            spread[slot, 0, 8 : wy + 8, :] = onward
            spread[slot, 1, 8 : wy + 8, :] = backward
            spread[slot, 2, 8 : wy + 8, :] = far
            total = total + (spread[slot, 0, 7 : wy + 7, :] + spread[slot, 1, 9 : wy + 9, :])
            total = total + (spread[slot, 2, 6 : wy + 6, :] + spread[slot, 2, 10 : wy + 10, :])
            a, b = lane_roll(onward, 1), lane_roll(backward, -1)
            c, d = lane_roll(far, 2), lane_roll(far, -2)
            from_low, from_high = a + c, b + d
            ends = jnp.where(lane == 0, from_low, jnp.where(lane == 1, c, 0.0))
            ends = jnp.where(lane == LANES - 1, from_high, jnp.where(lane == LANES - 2, d, ends))
            index = field * planes_x + x
            start = index * wy
            store(start, 0, total + (from_low + from_high))
            store(start, LANES, ends)
            above = spread[slot, 1, 7:15, :] + spread[slot, 2, 8:16, :]
            below = spread[slot, 0, wy + 5 : wy + 13, :] + spread[slot, 2, wy + 4 : wy + 12, :]
            extras.append(jnp.where(extra_row < 2, above, jnp.where(extra_row < 4, below, 0.0)))
            if len(extras) == 2:
                start = core_rows + (index - 1) * EXTRA
                store(start, 0, jnp.concatenate(extras, axis=0))
                for ref in (high, low):
                    ref[pl.ds(start, 2 * EXTRA), LANES : 2 * LANES] = jnp.zeros(
                        (2 * EXTRA, LANES), jnp.bfloat16
                    )
                extras = []

    copies[0].wait()
    copies[1].wait()
    factor = Factor(metric[...], ny, nz, wy)

    guess_l, guess_r = factor.guess(1), factor.guess(-1)
    left, right = factor.sweep(1, *guess_l[:2]), factor.sweep(-1, *guess_r[:2])
    copies[2].wait()
    for x in range(planes_x):
        speed[x] = half * speed[x]
    for field in range(fields):
        pltpu.make_async_copy(flow_hbm.at[field], flow.at[field], arrived.at[field]).wait()
    left, right = factor.sweep(1, *left[:2]), factor.sweep(-1, *right[:2])
    for field in range(fields // 2):
        one_field(field)
    parts = factor.finish(*left, *right[:2])
    from_right, from_left, diagonal, to_right, to_left, before, after = parts
    for number, value in enumerate(v for part in parts for v in part):
        factors[number] = value
    for number, value in enumerate(to_right + to_left):
        chains[number] = value
    for field in range(fields // 2, fields):
        one_field(field)

    me = lax.axis_index("gz")
    mine = lax.broadcasted_iota(jnp.int32, (rows, LANES), 0) == ny + me
    even = (lax.broadcasted_iota(jnp.int32, (1, LANES), 1) & 1) == 0
    lane = lax.broadcasted_iota(jnp.int32, (1, LANES), 1)

    def own(values):
        return tuple(jnp.sum(jnp.where(mine, v, 0.0), axis=0, keepdims=True) for v in values)

    up, down = own(to_right), own(to_left)
    up_past, down_past = own(mm(before, to_right)), own(mm(after, to_left))
    unit = (1.0, 0.0, 0.0, 1.0)
    weights = []
    for column in range(2):
        same = jnp.where(even, unit[column], unit[2 + column])
        inside_up = cell_weights(up, column, even)
        inside_down = cell_weights(down, column, even)
        past_up = lane_roll(cell_weights(up_past, column, even), -2)
        past_down = lane_roll(cell_weights(down_past, column, even), 2)
        ends_up = jnp.where(lane < 2, same, past_up) - inside_up
        ends_down = jnp.where(lane < 2, past_down, same) - inside_down
        at_end = (lane < 2) | (lane >= LANES - 2)
        ends_up, ends_down = jnp.where(at_end, ends_up, 0.0), jnp.where(at_end, ends_down, 0.0)
        weights.append(
            (
                jnp.concatenate([inside_up, ends_up], axis=1),
                jnp.concatenate([inside_down, ends_down], axis=1),
            )
        )
    stack = []
    for k in range(1, partners + 1):
        upward = jnp.bitwise_xor(me, k) > me
        stack += [jnp.where(upward, w[0], w[1]) for w in weights]
    while len(stack) % 8:
        stack.append(jnp.zeros((1, 2 * LANES), jnp.float32))
    count = len(stack)
    stack = jnp.concatenate(stack, axis=0)
    first = stack.astype(jnp.bfloat16).astype(jnp.float32)
    both = jnp.concatenate([first, stack - first], axis=0).astype(jnp.bfloat16)
    across = (((1,), (1,)), ((), ()))
    total = high.shape[0]
    size = planes_x * wy
    for begin in range(0, total, size):
        rows = slice(begin, min(begin + size, total))
        on_high = matmul(both, high[rows, :], across)
        on_low = matmul(both, low[rows, :], across)
        moments = (on_high[:count] + on_high[count:]) + on_low[:count]
        for k in range(partners):
            messages[k][:, rows] = moments[2 * k : 2 * k + 2]


def dense_inverse(columns, start, width, stack):
    parts = 8
    steps = width // (2 * parts)
    lane = lax.broadcasted_iota(jnp.int32, (parts, LANES), 1)
    part = lax.broadcasted_iota(jnp.int32, (parts, LANES), 0)
    fits = width + 4 <= LANES
    values = [columns[pl.ds(start + 2 * i, parts, stride=2 * steps), :] for i in range(steps)]

    def wide(i, number):
        return tuple(
            jnp.broadcast_to(values[i][:, number + k : number + k + 1], (parts, LANES)) for k in range(4)
        )

    blocks = [wide(i, 8) for i in range(steps)]
    zero, one = jnp.zeros((parts, LANES), jnp.float32), jnp.ones((parts, LANES), jnp.float32)

    def put(rows, i, extra, extra_lane, owner):
        first = 2 * (part * steps + i)
        out = []
        for r in range(2):
            row = jnp.where(lane == first, blocks[i][2 * r], rows[r])
            row = jnp.where(lane == first + 1, blocks[i][2 * r + 1], row)
            if extra is not None and fits:
                row = jnp.where((part == owner) & (lane == extra_lane), extra[2 * r], row)
                row = jnp.where((part == owner) & (lane == extra_lane + 1), extra[2 * r + 1], row)
            out.append(row)
        return tuple(out)

    def run(order, number, ends, extra_lane, owner):
        rows, product, out = (zero, zero), (one, zero, zero, one), {}
        for i in order:
            t = wide(i, number)
            rows = (t[0] * rows[0] + t[1] * rows[1], t[2] * rows[0] + t[3] * rows[1])
            extra = None
            if i == order[0]:
                e = wide(i, ends)
                extra = mm(blocks[i], (e[0], e[2], e[1], e[3]))
            rows = put(rows, i, extra, extra_lane, owner)
            product = mm(t, product)
            out[i] = rows, product
        rows, product = out[order[-1]]
        entering, last = [None] * parts, (jnp.zeros((1, LANES), jnp.float32),) * 2
        sequence = range(parts) if number == 4 else range(parts - 1, -1, -1)
        for p in sequence:
            entering[p] = last
            own, across = [r[p : p + 1] for r in rows], [x[p : p + 1] for x in product]
            last = (
                own[0] + across[0] * last[0] + across[1] * last[1],
                own[1] + across[2] * last[0] + across[3] * last[1],
            )
        entering = [jnp.concatenate([e[r] for e in entering], axis=0) for r in range(2)]
        result = []
        for i in range(steps):
            rows, product = out[i]
            for r in range(2):
                result.append(rows[r] + product[2 * r] * entering[0] + product[2 * r + 1] * entering[1])
        return result

    low = run(list(range(steps)), 4, 12, width, 0)
    high = run(list(range(steps - 1, -1, -1)), 0, 16, width + 2, parts - 1)
    for k in range(2 * steps):
        lower = lane <= 2 * (part * steps + k // 2) + 1
        if fits:
            lower = lower & (lane < width) | ((lane >= width) & (lane < width + 2))
        stack[parts * k : parts * (k + 1), :] = jnp.where(lower, low[k], high[k])
    rows = [stack[pl.ds(p, 2 * steps, stride=parts), :] for p in range(parts)]
    return jnp.concatenate(rows, axis=0)


def stage_plan(count):
    plan, stride = [], 1
    while stride < count:
        radix = 4 if count // stride >= 4 else 2
        plan.append((stride, radix))
        stride *= radix
    return plan


def transposed(factors, row):
    rows = [factors[number, pl.ds(row, 1), :] for number in range(12)]
    rows += [factors[20 + number, pl.ds(row, 1), :] for number in range(8)]
    rows += [factors[12 + number, pl.ds(row, 1), :] for number in range(8)]
    rows.append(jnp.zeros((4, LANES), jnp.float32))
    return jnp.concatenate(rows, axis=0).T


def chain_products(chains, number, place, blocks, begins, ends, masks, reverse):
    count = -(-len(begins) // 8) * 8
    row = lax.broadcasted_iota(jnp.int32, (count, LANES), 0)
    begin = jnp.zeros((count, LANES), jnp.int32)
    end, mask = begin, jnp.zeros((count, LANES), jnp.float32)
    for r, (b, e, m) in enumerate(zip(begins, ends, masks)):
        begin, end = jnp.where(row == r, b, begin), jnp.where(row == r, e, end)
        mask = jnp.where(row == r, m, mask)
    one, zero = jnp.ones((count, LANES), jnp.float32), jnp.zeros((count, LANES), jnp.float32)
    product = (one, zero, zero, one)
    for block in range(blocks - 1, -1, -1) if reverse else range(blocks):
        where = place(block)
        value = tuple(chains[number + k, where[0], where[1]] for k in range(4))
        product = pick((begin <= block) & (block < end), mm(product, value), product)
    return tuple(x * mask for x in product)


def truth(condition):
    return jnp.where(condition, 1.0, 0.0)


def second_kernel(
    ny, nz, count_z, wy, partners, chains, factors, high, low, local, moments, entering, spread_core, spread_extra, *scratch
):
    columns, stacked, rows_ref, matrix, weights_y = scratch
    planes = (moments.shape[0] - 8) // 4
    me_z, me_y = lax.axis_index("gz"), lax.axis_index("gy")
    columns[0:LANES, 0:32] = transposed(factors, ny + me_z)
    inverse = dense_inverse(columns, 0, LANES, stacked)
    rows_ref[0:LANES, :] = inverse
    rows_ref[LANES : 2 * LANES, :] = jnp.zeros((LANES, LANES), jnp.float32)
    past = tuple(columns[LANES - 1 : LANES, 16 + k : 17 + k] for k in range(4))
    ahead = tuple(columns[0:1, 12 + k : 13 + k] for k in range(4))
    head0, head1 = rows_ref[0:1, :], rows_ref[1:2, :]
    tail0, tail1 = rows_ref[LANES - 2 : LANES - 1, :], rows_ref[LANES - 1 : LANES, :]
    for q in range(2):
        beyond = past[2 * q] * tail0 + past[2 * q + 1] * tail1
        rows_ref[LANES + q : LANES + q + 1, :] = beyond - (head0, head1)[q]
        beyond = ahead[2 * q] * head0 + ahead[2 * q + 1] * head1
        rows_ref[2 * LANES - 2 + q : 2 * LANES - 1 + q, :] = beyond - (tail0, tail1)[q]
    first, second = halves(rows_ref[...])
    matrix[:, 0:LANES] = first
    matrix[:, LANES : 2 * LANES] = second

    cell = me_y * wy
    start = lax.rem(cell, LANES)
    row = cell // LANES
    unit = (1.0, 0.0, 0.0, 1.0)
    lane = lax.broadcasted_iota(jnp.int32, (1, LANES), 1)
    even = (lane & 1) == 0

    def chain(number):
        return tuple(factors[number + k, pl.ds(row, 1), :] for k in range(4))

    def turned(x, by):
        return pltpu.roll(x, lax.rem(by + 2 * LANES, LANES), 1)

    def tiled(x, period):
        x = jnp.where(lane < period, x, 0.0)
        while period < LANES:
            x = x + lane_roll(x, period)
            period *= 2
        return x

    up, down, before, after = chain(12), chain(16), chain(20), chain(24)
    past_up, past_down = mm(before, up), mm(after, down)
    core_rows, extra_rows = [], []
    for column in range(2):
        same = jnp.where(even, unit[column], unit[2 + column])
        early = turned(cell_weights(past_up, column, even), -start)
        late = turned(cell_weights(past_down, column, even), 4 - wy - start)
        for inside, first, second in ((up, early, same), (down, same, late)):
            core_rows.append(tiled(turned(cell_weights(inside, column, even), -start), wy))
            past = jnp.where(lane < 2, first, jnp.where(lane < 4, second, 0.0))
            extra_rows.append(tiled(past, EXTRA))
    for number, source in enumerate((0, 2, 1, 3)):
        for rows, out, width in ((core_rows, spread_core, wy), (extra_rows, spread_extra, EXTRA)):
            per = LANES // width
            owner = lax.broadcasted_iota(jnp.int32, (per, LANES), 0)
            wide_lane = lax.broadcasted_iota(jnp.int32, (per, LANES), 1)
            value = jnp.where(owner == wide_lane // width, rows[source], 0.0)
            out[number * per : (number + 1) * per, :] = value

    others = [jnp.bitwise_xor(me_z, k) for k in range(1, partners + 1)]
    begins, ends = [other + 1 for other in others], others
    lowers = [other < me_z for other in others]
    size = len(begins)
    up = chain_products(
        chains, 0, lambda b: (ny + b, 0), count_z, begins, [me_z] * size, [1.0] * size, False
    )
    down = chain_products(
        chains, 4, lambda b: (ny + b, LANES - 1), count_z, [me_z + 1] * size, ends, [1.0] * size, True
    )
    stack = []
    for k, lower in enumerate(lowers):
        for p in range(2):
            from_low = up[2 * p][k : k + 1] * head0 + up[2 * p + 1][k : k + 1] * head1
            from_high = down[2 * p][k : k + 1] * tail0 + down[2 * p + 1][k : k + 1] * tail1
            stack.append(jnp.where(lower, from_low, from_high))
    while len(stack) % 8:
        stack.append(jnp.zeros((1, LANES), jnp.float32))
    stack = jnp.concatenate(stack, axis=0)
    first = stack.astype(jnp.bfloat16).astype(jnp.float32)
    entering[...] = jnp.concatenate([first, stack - first, first], axis=0)

    columns[0:LANES, 0:32] = transposed(factors, cell // LANES)
    row = lax.broadcasted_iota(jnp.int32, (wy, LANES), 0)
    extra_row = lax.broadcasted_iota(jnp.int32, (EXTRA, LANES), 0)
    unit = (1.0, 0.0, 0.0, 1.0)

    def head(number):
        return tuple(columns[pl.ds(start, 1), number + k : number + k + 1] for k in range(4))

    def tail(number):
        return tuple(columns[pl.ds(start + wy - 1, 1), number + k : number + k + 1] for k in range(4))

    past_up, past_down = mm(head(12), head(20)), mm(tail(16), tail(24))
    for column in range(2):
        for output, number in ((column, 20), (2 + column, 24)):
            even = columns[pl.ds(start, wy), number + column : number + column + 1]
            odd = columns[pl.ds(start, wy), number + 2 + column : number + 3 + column]
            weights_y[output, 0:wy, :] = jnp.where((row & 1) == 0, even, odd)
        for output, early, late in (
            (column, (past_up[column], past_up[2 + column]), (unit[column], unit[2 + column])),
            (2 + column, (unit[column], unit[2 + column]), (past_down[column], past_down[2 + column])),
        ):
            value = jnp.zeros((EXTRA, LANES), jnp.float32)
            for r, v in enumerate(early + late):
                value = jnp.where(extra_row == r, v, value)
            weights_y[output, wy : wy + EXTRA, :] = value

    total = planes * (wy + EXTRA)

    def solve(begin, size):
        rows = slice(begin, begin + size)
        both = matmul(high[rows, :], matrix[...])
        value = both[:, 0:LANES] + (both[:, LANES : 2 * LANES] + matmul(low[rows, :], matrix[:, 0:LANES]))
        local[rows, :] = value
        return value

    extra = solve(planes * wy, planes * EXTRA)
    for part in range(planes // 8):
        core = solve(part * 8 * wy, 8 * wy)
        for number in range(4):
            lines = []
            for k in range(8):
                index = part * 8 + k
                value = jnp.sum(core[k * wy : (k + 1) * wy] * weights_y[number, 0:wy, :], axis=0, keepdims=True)
                past = extra[index * EXTRA : (index + 1) * EXTRA] * weights_y[number, wy : wy + EXTRA, :]
                lines.append(value + jnp.sum(past, axis=0, keepdims=True))
            start = number * planes + part * 8
            moments[start : start + 8, :] = jnp.concatenate(lines, axis=0)


def y_kernel(count_y, wy, chains, factors, unused, inverse_y, coefs, columns, stacked):
    me_y = lax.axis_index("gy")
    cell = me_y * wy
    columns[0:LANES, 0:32] = transposed(factors, cell // LANES)
    start = lax.rem(cell, LANES)
    inverse_y[...] = dense_inverse(columns, start, wy, stacked)

    up, down = ([], [], []), ([], [], [])
    plan = stage_plan(count_y)
    for number, (stride, radix) in enumerate(plan):
        group = me_y // stride
        first = (group // radix) * radix
        others = [first + jnp.bitwise_xor(group - first, k) for k in range(radix)]
        for other in others[1:]:
            for lists, values in (
                (up, ((other + 1) * stride, me_y, truth(other < group))),
                (down, (me_y + 1, other * stride, truth(other > group))),
            ):
                for one, value in zip(lists, values):
                    one.append(value)
        if number + 1 < len(plan):
            for other in others:
                for lists, values in (
                    (up, ((other + 1) * stride, (first + radix) * stride, 1.0)),
                    (down, (first * stride, other * stride, 1.0)),
                ):
                    for one, value in zip(lists, values):
                        one.append(value)

    def place(block):
        return block * wy // LANES, block * wy % LANES

    def place_end(block):
        return place(block)[0], place(block)[1] + wy - 1

    for base, value in (
        (0, chain_products(chains, 0, place, count_y, *up, False)),
        (4, chain_products(chains, 4, place_end, count_y, *down, True)),
    ):
        for k in range(4):
            coefs[base + k] = value[k]


def arrived_rows(messages, count):
    rows = [m[0:2] for m in messages]
    if count > 2 * len(messages):
        rows.append(jnp.zeros((count - 2 * len(messages), rows[0].shape[1]), jnp.float32))
    return jnp.concatenate(rows, axis=0)


def third_kernel(wy, moments, spread_core, spread_extra, entering, *refs):
    messages, (carried, held, result) = refs[:-3][::-1], refs[-3:]
    planes = carried.shape[1]
    count = entering.shape[0] // 3
    received = arrived_rows(messages, count)
    first = received.astype(jnp.bfloat16).astype(jnp.float32)
    both = jnp.concatenate([first, received - first], axis=0)
    values = entering[0:count, :] + entering[count : 2 * count, :]
    across = (((1,), (1,)), ((), ()))
    used = 2 * len(messages)

    def chunks(begin, end):
        parts = [both[:, at : min(at + LANES, end)] for at in range(begin, end, LANES)]
        if parts[-1].shape[1] < LANES:
            missing = jnp.zeros((2 * count, LANES - parts[-1].shape[1]), jnp.float32)
            parts[-1] = jnp.concatenate([parts[-1], missing], axis=1)
        return jnp.concatenate(parts, axis=0).astype(jnp.bfloat16), len(parts)

    per = LANES // wy
    stack, number = chunks(0, planes * wy)
    top, rest = halves(spread_core[...])
    held[0 : number * 2 * count, 0 : 4 * per] = matmul(stack, top, across) + matmul(stack, rest, across)
    columns = [
        held[pl.ds(r, number, stride=2 * count), :] + held[pl.ds(count + r, number, stride=2 * count), :]
        for r in range(used)
    ]
    for m in range(4):
        for p in range(per):
            lane = m * per + p
            value = moments[pl.ds(m * planes + p, number, stride=per), :]
            for r in range(used):
                value = value + columns[r][:, lane : lane + 1] * values[r : r + 1]
            result[pl.ds(m * planes + p, number, stride=per), :] = value

    per = LANES // EXTRA
    stack, number = chunks(planes * wy, planes * (wy + EXTRA))
    top, rest = halves(spread_extra[...])
    corner = matmul(top, stack, across) + matmul(rest, stack, across)
    for m in range(4):
        for chunk in range(number):
            size = min(per, planes - chunk * per)
            rows = slice(chunk * per, chunk * per + size)
            value = result[m * planes + chunk * per : m * planes + chunk * per + size, :]
            for r in range(used):
                lane = chunk * 2 * count + r
                part = corner[m * per : m * per + size]
                column = part[:, lane : lane + 1] + part[:, lane + count : lane + count + 1]
                value = value + column * values[r : r + 1]
            carried[m, rows, :] = value


def local_y_kernel(wy, local, entering, inverse_y, unused, *refs):
    messages, (out, solved) = refs[:-2], refs[-2:]
    planes = out.shape[0]
    count = entering.shape[0] // 3
    received = arrived_rows(messages, count)
    first = received.astype(jnp.bfloat16).astype(jnp.float32)
    received = jnp.concatenate([first, first, received - first], axis=0).T.astype(jnp.bfloat16)
    solved[...] = local[...] + matmul(received, entering[...].astype(jnp.bfloat16))
    first, second = halves(inverse_y[:, 0 : wy + EXTRA])
    left = jnp.concatenate([first, second, first], axis=1)

    def part(index, carry):
        for k in range(8):
            number = index * 8 + k
            start = pl.multiple_of(number * wy, 8)
            core = solved[pl.ds(start, wy), :]
            start = pl.multiple_of(planes * wy + number * EXTRA, 8)
            both = jnp.concatenate([core, solved[pl.ds(start, EXTRA), :]], axis=0)
            top, rest = halves(both)
            out[number] = matmul(left, jnp.concatenate([top, top, rest], axis=0))
        return carry

    lax.fori_loop(0, planes // 8, part, 0)


def combine(coefs, side, row, values):
    first = 0 if side == 0 else 2
    out = [None, None]
    for k, value in enumerate(values):
        for q in range(2):
            for p in range(2):
                term = coefs[side + 2 * p + q, row + k : row + k + 1, :] * value[first + p]
                out[q] = term if out[q] is None else out[q] + term
    return out


def stage_kernel(base, stride, radix, narrow, has_entered, coefs, *refs):
    values = refs[:radix]
    position = radix
    entered = None
    if has_entered:
        entered = refs[position]
        position += 1
    message, entering = refs[position : position + 2]
    below = combine(coefs, 0, base, values[1:])
    above = combine(coefs, 4, base, values[1:])
    for row, value in enumerate(below + above):
        entering[row] = value if entered is None else value + entered[row]
    upward = combine(coefs, 0, base + radix - 1, values)
    downward = combine(coefs, 4, base + radix - 1, values)
    if narrow:
        group = lax.axis_index("gy") // (stride * radix)
        sends_up = lax.rem(group, 2) == 0
        for row in range(2):
            message[row] = jnp.where(sends_up, upward[row], downward[row])
    else:
        for row, value in enumerate(upward + downward):
            message[row] = value


def last_kernel(base, radix, narrow, wy, coefs, local, inverse_y, entered, *refs):
    messages, (out_hbm, out, sent) = refs[: radix - 1], refs[radix - 1 :]
    values = list(messages)
    if narrow:
        values = [(m[0], m[1], m[0], m[1]) for m in values]
    below = combine(coefs, 0, base, values)
    above = combine(coefs, 4, base, values)
    st = [value + entered[row] for row, value in enumerate(below + above)]
    sides = [
        jnp.broadcast_to(inverse_y[:, c : c + 1], (wy, LANES)) for c in (0, 1, wy - 2, wy - 1)
    ]
    fields, planes_x = out.shape[:2]
    copies = []
    for field in range(fields):
        for x in range(planes_x):
            index = field * planes_x + x
            value = local[index]
            for number in range(4):
                value = value + sides[number] * st[number][index : index + 1]
            out[field, x] = value
            if (x + 1) % 4 == 0:
                part = (field, pl.ds(x - 3, 4))
                copy = pltpu.make_async_copy(out.at[part], out_hbm.at[part], sent.at[len(copies)])
                copy.start()
                copies.append(copy)
    for copy in copies:
        copy.wait()


VMEM = pl.BlockSpec(memory_space=pltpu.VMEM)
HBM = pl.BlockSpec(memory_space=pltpu.HBM)
SMEM = pl.BlockSpec(memory_space=pltpu.SMEM)
PARAMS = pltpu.CompilerParams(vmem_limit_bytes=40 * 1024 * 1024)


def array(*shape):
    return jax.ShapeDtypeStruct(shape, jnp.float32)


def in_hbm(x):
    return pltpu.with_memory_space_constraint(x, pltpu.HBM)


def cost(flops, data):
    return pl.CostEstimate(flops=flops, bytes_accessed=data, transcendentals=0)


def on_device(mesh, flow, speed, metric_y, metric_z):
    fields, planes_x, wy, wz = flow.shape
    count_y, count_z = mesh.shape["gy"], mesh.shape["gz"]
    assert wz == LANES
    ny, nz = metric_y.shape[0] // LANES, metric_z.shape[0] // LANES
    planes = fields * planes_x
    rows = planes * (wy + EXTRA)
    partners = count_z - 1
    arrivals = partners
    entering_rows = -(-2 * arrivals // 8) * 8
    half = jax.ShapeDtypeStruct((rows, 2 * LANES), jnp.bfloat16)
    outputs = pl.pallas_call(
        functools.partial(first_kernel, ny, nz, partners),
        out_shape=[half, half, array(28, ny + nz, LANES), array(8, ny + nz, LANES)]
        + [array(2, rows)] * partners,
        in_specs=[HBM] * 4,
        out_specs=[VMEM] * (4 + partners),
        scratch_shapes=[
            pltpu.VMEM(flow.shape, jnp.float32),
            pltpu.VMEM(speed.shape, jnp.float32),
            pltpu.VMEM((ny + nz, LANES), jnp.float32),
            pltpu.VMEM((planes_x, 3, wy + 16, LANES), jnp.float32),
            pltpu.SemaphoreType.DMA((fields + 3,)),
        ],
        compiler_params=PARAMS,
        name="forcing_and_factor",
    )(*(in_hbm(x) for x in (flow, speed, metric_y.reshape(ny, LANES), metric_z.reshape(nz, LANES))))
    high, low, factors, chains = outputs[:4]

    def exchange(values, axis, count, stride, radix):
        received = {}
        for k in reversed(range(1, radix)):
            pairs = [(i, i ^ (k * stride)) for i in range(count)]
            received[k] = lax.ppermute(values[k - 1], axis, pairs)
        return [received[k] for k in range(1, radix)]

    plan = stage_plan(count_y)
    work = [pltpu.VMEM((LANES + 16, LANES), jnp.float32)] * 2
    received = exchange(outputs[4:], "gz", count_z, 1, count_z)
    local, moments, entering, spread_core, spread_extra = pl.pallas_call(
        functools.partial(second_kernel, ny, nz, count_z, wy, partners),
        out_shape=[
            array(rows, LANES),
            array(4 * planes + 8, LANES),
            array(3 * entering_rows, LANES),
            array(4 * (LANES // wy), LANES),
            array(4 * (LANES // EXTRA), LANES),
        ],
        in_specs=[SMEM] + [VMEM] * 3,
        out_specs=[VMEM] * 5,
        scratch_shapes=work
        + [
            pltpu.VMEM((2 * LANES, LANES), jnp.float32),
            pltpu.VMEM((2 * LANES, 2 * LANES), jnp.bfloat16),
            pltpu.VMEM((4, wy + EXTRA, LANES), jnp.float32),
        ],
        compiler_params=PARAMS,
        cost_estimate=cost(2 * rows * 256 * 128 * 6, 4 * rows * 384),
        name="local_z",
    )(chains, factors, high, low)
    carried = pl.pallas_call(
        functools.partial(third_kernel, wy),
        out_shape=array(4, planes, LANES),
        in_specs=[VMEM] * (4 + arrivals),
        out_specs=VMEM,
        scratch_shapes=[
            pltpu.VMEM((planes * wy // LANES * 2 * entering_rows + 2 * entering_rows, LANES), jnp.float32),
            pltpu.VMEM((4 * planes + 8, LANES), jnp.float32),
        ],
        compiler_params=PARAMS,
        name="carried_y",
    )(moments, spread_core, spread_extra, entering, *received[::-1])
    arrived = received

    narrow = plan[-1][1] == 2 and len(plan) > 1
    base, entered, result = 0, None, None
    for number, (stride, radix) in enumerate(plan):
        received = exchange([carried] * (radix - 1), "gy", count_y, stride, radix)
        if number == 0:
            entries = sum(2 * radix - 1 for _, radix in plan[:-1]) + plan[-1][1] - 1
            inverse_y, coefs = pl.pallas_call(
                functools.partial(y_kernel, count_y, wy),
                out_shape=[array(wy, LANES), array(8, -(-entries // 8) * 8, LANES)],
                in_specs=[SMEM, VMEM, HBM],
                out_specs=[VMEM] * 2,
                scratch_shapes=work,
                compiler_params=PARAMS,
                cost_estimate=cost(2 * rows * 128 * 128 * 6, 4 * rows * 256),
                name="inverse_y",
            )(chains, factors, carried)
        if number + 1 < len(plan):
            slim = narrow and number + 2 == len(plan)
            inputs = [carried] + received + ([entered] if entered is not None else [])
            carried, entered = pl.pallas_call(
                functools.partial(stage_kernel, base, stride, radix, slim, entered is not None),
                out_shape=[array(2 if slim else 4, planes, LANES), array(4, planes, LANES)],
                in_specs=[VMEM] * (1 + len(inputs)),
                out_specs=[VMEM] * 2,
                compiler_params=PARAMS,
                name="join_groups",
            )(coefs, *inputs)
            base += 2 * radix - 1
            if number == 0:
                result = pl.pallas_call(
                    functools.partial(local_y_kernel, wy),
                    out_shape=array(planes, wy, LANES),
                    in_specs=[VMEM] * 3 + [HBM] + [VMEM] * arrivals,
                    out_specs=VMEM,
                    scratch_shapes=[pltpu.VMEM((rows, LANES), jnp.float32)],
                    compiler_params=PARAMS,
                    cost_estimate=cost(2 * rows * 128 * 128 * 6, 4 * rows * 256),
                    name="local_y",
                )(local, entering, inverse_y, entered, *arrived)
        else:
            return pl.pallas_call(
                functools.partial(last_kernel, base, radix, narrow, wy),
                out_shape=array(fields, planes_x, wy, wz),
                in_specs=[VMEM] * (4 + len(received)),
                out_specs=HBM,
                scratch_shapes=[
                    pltpu.VMEM(flow.shape, jnp.float32),
                    pltpu.SemaphoreType.DMA((planes // 4,)),
                ],
                compiler_params=PARAMS,
                name="finish_y",
            )(coefs, result, inverse_y, entered, *received)


def solution(mesh):
    placed = (P(None, None, "gy", "gz"), P(None, "gy", "gz"), P(), P())
    return jax.shard_map(
        functools.partial(on_device, mesh),
        mesh=mesh,
        in_specs=placed,
        out_specs=P(None, None, "gy", "gz"),
        check_vma=False,
    )
```

```python
import functools

import jax
import jax.numpy as jnp
from jax import lax
from jax.experimental import pallas as pl
from jax.experimental.pallas import tpu as pltpu
from jax.sharding import PartitionSpec as P

viscous = 0.25
explicit_fourth = 0.04
implicit_fourth = 0.05
time_step = 1048576.0
LANES = 128
EXTRA = 8


def mm(a, b):
    return (
        a[0] * b[0] + a[1] * b[2],
        a[0] * b[1] + a[1] * b[3],
        a[2] * b[0] + a[3] * b[2],
        a[2] * b[1] + a[3] * b[3],
    )


def inverse_of_one_minus(a):
    p, q, r, s = 1.0 - a[0], -a[1], -a[2], 1.0 - a[3]
    d = 1.0 / (p * s - q * r)
    return (s * d, -q * d, -r * d, p * d)


def pick(condition, a, b):
    return tuple(jnp.where(condition, x, y) for x, y in zip(a, b))


def halves(x):
    high = x.astype(jnp.bfloat16)
    return high, (x - high.astype(jnp.float32)).astype(jnp.bfloat16)


def matmul(a, b, dims=(((1,), (0,)), ((), ()))):
    return lax.dot_general(a, b, dims, preferred_element_type=jnp.float32)


def scan(m, ahead, count, step, shift, product):
    unit = (1.0, 0.0, 0.0, 1.0)

    def moved(by):
        return tuple(jnp.where(ahead >= by, shift(x, by), u) for x, u in zip(m, unit))

    while step < count:
        if 2 * step < count:
            m = product(product(m, moved(step)), product(moved(2 * step), moved(3 * step)))
            step *= 4
        else:
            m = product(m, moved(step))
            step *= 2
    return m


def lane_roll(x, by):
    return pltpu.roll(x, by % LANES, 1)


def row_roll(x, by):
    by = by % x.shape[0]
    return jnp.concatenate([x[x.shape[0] - by :], x[: x.shape[0] - by]], axis=0)


class Factor:
    def __init__(self, metric, ny, nz, wy):
        self.ny, self.nz, self.wy, self.rows = ny, nz, wy, ny + nz
        self.lane = lax.broadcasted_iota(jnp.int32, (self.rows, LANES), 1)
        self.row = lax.broadcasted_iota(jnp.int32, (self.rows, LANES), 0)
        self.block = jnp.where(self.row < ny, self.row, self.row - ny)
        self.to_end = jnp.where(self.row < ny, ny, nz) - 1 - self.block
        first = (self.lane == 0) & (self.block == 0)
        last = (self.lane == LANES - 1) & (self.to_end == 0)
        self.face_low = 0.5 * (jnp.where(first, metric, self.before(metric, 1)) + metric)
        self.face_high = 0.5 * (metric + jnp.where(last, metric, self.after(metric, 1)))

    def before(self, x, by):
        rolled = lane_roll(x, by)
        value = jnp.where(self.lane < by, row_roll(rolled, 1), rolled)
        return jnp.where((self.lane < by) & (self.block == 0), 0.0, value)

    def after(self, x, by):
        rolled = lane_roll(x, -by)
        value = jnp.where(self.lane >= LANES - by, row_roll(rolled, -1), rolled)
        return jnp.where((self.lane >= LANES - by) & (self.to_end == 0), 0.0, value)

    def guess(self, sign):
        face = self.face_high if sign > 0 else self.face_low
        if sign > 0:
            cell = self.lane + LANES * self.block
        else:
            cell = LANES - 1 - self.lane + LANES * self.to_end
        near = face / (cell + 1).astype(jnp.float32)
        one_over = 1.0 / (face + jnp.sqrt(face + near * near))
        return face * one_over, implicit_fourth * one_over, one_over

    def sweep(self, sign, ratio, far):
        rows = self.rows
        back = self.before if sign > 0 else self.after
        if sign > 0:
            face_in, face_out, place = self.face_low, self.face_high, self.block
        else:
            face_in, face_out, place = self.face_high, self.face_low, self.to_end
        eps = 4.0 * implicit_fourth - implicit_fourth * back(ratio, 1)
        mass = (1.0 + 6.0 * implicit_fourth) - implicit_fourth * back(far, 2) - 2.0 * eps
        eps_in = back(eps, 1)
        scale = 1.0 / (face_in + 2.0 * eps_in)
        m = ((mass + face_in) * scale, mass - eps_in * eps_in * scale, scale, jnp.ones_like(scale))
        ahead = self.lane if sign > 0 else LANES - 1 - self.lane
        m = scan(m, ahead, LANES, 1, lambda x, by: lane_roll(x, sign * by), mm)
        edge = LANES - 1 if sign > 0 else 0
        total = tuple(jnp.broadcast_to(x[:, edge : edge + 1], (rows, LANES)) for x in m)
        total = scan(
            total, place, max(self.ny, self.nz), 1, lambda x, by: row_roll(x, sign * by), mm
        )
        top = jnp.where(place >= 1, row_roll(total[0], sign), 1.0)
        low = jnp.where(place >= 1, row_roll(total[2], sign), 0.0)
        eta = (m[0] * top + m[1] * low) / (m[2] * top + m[3] * low)
        one_over = 1.0 / (face_out + (eta + 2.0 * eps))
        return (face_out + eps) * one_over, implicit_fourth * one_over, one_over

    def finish(self, near_l, far_l, pivot_l, near_r, far_r):
        lane, block, to_end = self.lane, self.block, self.to_end
        even = (lane & 1) == 0
        near_l = jnp.where((to_end == 0) & (lane >= LANES - 1), 0.0, near_l)
        far_l = jnp.where((to_end == 0) & (lane >= LANES - 2), 0.0, far_l)
        near_r = jnp.where((block == 0) & (lane < 1), 0.0, near_r)
        far_r = jnp.where((block == 0) & (lane < 2), 0.0, far_r)

        def of_even(x):
            return jnp.where(even, x, lane_roll(x, 1))

        def of_odd(x):
            return jnp.where(even, lane_roll(x, -1), x)

        t0, t1, r0, r1 = of_even(near_l), of_odd(near_l), of_even(far_l), of_odd(far_l)
        from_right = (t0 * t1 - r0, -t0 * r1, t1, -r1)
        p1 = of_odd(pivot_l)
        left_inverse = (of_even(pivot_l) + t0 * t0 * p1, t0 * p1, t0 * p1, p1)
        s0, s1, q0, q1 = of_even(near_r), of_odd(near_r), of_even(far_r), of_odd(far_r)
        from_left = (-q0, s0, -s1 * q0, s1 * s0 - q1)
        from_left_after = tuple(self.after(x, 2) for x in from_left)
        from_right_before = tuple(self.before(x, 2) for x in from_right)
        diagonal = mm(inverse_of_one_minus(mm(from_right, from_left_after)), left_inverse)
        width = jnp.where(self.row < self.ny, self.wy, LANES)
        place = lane & (width - 1)
        right = scan(from_right, width - 1 - place, LANES, 2, lambda x, by: lane_roll(x, -by), mm)
        left = scan(from_left, place, LANES, 2, lane_roll, mm)
        return from_right, from_left, diagonal, right, left, from_right_before, from_left_after


def cell_weights(chain, column, even):
    return jnp.where(even, chain[column], chain[2 + column])


def first_kernel(ny, nz, partners, flow_hbm, speed_hbm, metric_y, metric_z, *refs):
    high, low, factors = refs[:3]
    messages = refs[3 : 3 + partners]
    flow, speed, metric, spread, arrived = refs[3 + partners :]
    fields, planes_x, wy, _ = flow.shape
    rows = ny + nz
    core_rows = fields * planes_x * wy

    copies = [
        pltpu.make_async_copy(metric_y, metric.at[0:ny], arrived.at[fields]),
        pltpu.make_async_copy(metric_z, metric.at[ny:rows], arrived.at[fields + 1]),
        pltpu.make_async_copy(speed_hbm, speed, arrived.at[fields + 2]),
    ]
    for copy in copies:
        copy.start()
    for field in range(fields):
        pltpu.make_async_copy(flow_hbm.at[field], flow.at[field], arrived.at[field]).start()

    lane = lax.broadcasted_iota(jnp.int32, (wy, LANES), 1)
    extra_row = lax.broadcasted_iota(jnp.int32, (EXTRA, LANES), 0)
    for slot in range(planes_x):
        for part in range(3):
            spread[slot, part, 0:8, :] = jnp.zeros((8, LANES), jnp.float32)
            spread[slot, part, wy + 8 : wy + 16, :] = jnp.zeros((8, LANES), jnp.float32)
    side = time_step * (viscous + 4.0 * explicit_fourth)
    half = time_step * 0.5
    centre = time_step * (-6.0 * viscous - 12.0 * explicit_fourth)
    fourth = -time_step * explicit_fourth

    def store(start, column, value):
        first, second = halves(value)
        high[pl.ds(start, value.shape[0]), column : column + LANES] = first
        low[pl.ds(start, value.shape[0]), column : column + LANES] = second

    def one_field(field):
        values = [flow[field, x] for x in range(planes_x)]
        fluxes = [values[x] * speed[x] for x in range(planes_x)]
        aside = [(time_step * viscous) * u for u in values]
        extras = []
        for x in range(planes_x):
            u, flux, slot = values[x], fluxes[x], x
            total = centre * u
            if x + 1 < planes_x:
                total = total + (aside[x + 1] - fluxes[x + 1])
            if x > 0:
                total = total + (aside[x - 1] + fluxes[x - 1])
            scaled = side * u
            onward, backward, far = scaled + flux, scaled - flux, fourth * u
            spread[slot, 0, 8 : wy + 8, :] = onward
            spread[slot, 1, 8 : wy + 8, :] = backward
            spread[slot, 2, 8 : wy + 8, :] = far
            total = total + (spread[slot, 0, 7 : wy + 7, :] + spread[slot, 1, 9 : wy + 9, :])
            total = total + (spread[slot, 2, 6 : wy + 6, :] + spread[slot, 2, 10 : wy + 10, :])
            a, b = lane_roll(onward, 1), lane_roll(backward, -1)
            c, d = lane_roll(far, 2), lane_roll(far, -2)
            from_low, from_high = a + c, b + d
            ends = jnp.where(lane == 0, from_low, jnp.where(lane == 1, c, 0.0))
            ends = jnp.where(lane == LANES - 1, from_high, jnp.where(lane == LANES - 2, d, ends))
            index = field * planes_x + x
            start = index * wy
            store(start, 0, total + (from_low + from_high))
            store(start, LANES, ends)
            above = spread[slot, 1, 7:15, :] + spread[slot, 2, 8:16, :]
            below = spread[slot, 0, wy + 5 : wy + 13, :] + spread[slot, 2, wy + 4 : wy + 12, :]
            extras.append(jnp.where(extra_row < 2, above, jnp.where(extra_row < 4, below, 0.0)))
            if len(extras) == 2:
                start = core_rows + (index - 1) * EXTRA
                store(start, 0, jnp.concatenate(extras, axis=0))
                for ref in (high, low):
                    ref[pl.ds(start, 2 * EXTRA), LANES : 2 * LANES] = jnp.zeros(
                        (2 * EXTRA, LANES), jnp.bfloat16
                    )
                extras = []

    copies[0].wait()
    copies[1].wait()
    factor = Factor(metric[...], ny, nz, wy)

    guess_l, guess_r = factor.guess(1), factor.guess(-1)
    left, right = factor.sweep(1, *guess_l[:2]), factor.sweep(-1, *guess_r[:2])
    copies[2].wait()
    for x in range(planes_x):
        speed[x] = half * speed[x]
    for field in range(fields):
        pltpu.make_async_copy(flow_hbm.at[field], flow.at[field], arrived.at[field]).wait()
    left, right = factor.sweep(1, *left[:2]), factor.sweep(-1, *right[:2])
    for field in range(fields // 2):
        one_field(field)
    parts = factor.finish(*left, *right[:2])
    from_right, from_left, diagonal, to_right, to_left, before, after = parts
    for number, value in enumerate(v for part in parts for v in part):
        factors[number] = value
    for field in range(fields // 2, fields):
        one_field(field)

    me = lax.axis_index("gz")
    mine = lax.broadcasted_iota(jnp.int32, (rows, LANES), 0) == ny + me
    even = (lax.broadcasted_iota(jnp.int32, (1, LANES), 1) & 1) == 0
    lane = lax.broadcasted_iota(jnp.int32, (1, LANES), 1)

    def own(values):
        return tuple(jnp.sum(jnp.where(mine, v, 0.0), axis=0, keepdims=True) for v in values)

    up, down = own(to_right), own(to_left)
    up_past, down_past = own(mm(before, to_right)), own(mm(after, to_left))
    unit = (1.0, 0.0, 0.0, 1.0)
    weights = []
    for column in range(2):
        same = jnp.where(even, unit[column], unit[2 + column])
        inside_up = cell_weights(up, column, even)
        inside_down = cell_weights(down, column, even)
        past_up = lane_roll(cell_weights(up_past, column, even), -2)
        past_down = lane_roll(cell_weights(down_past, column, even), 2)
        ends_up = jnp.where(lane < 2, same, past_up) - inside_up
        ends_down = jnp.where(lane < 2, past_down, same) - inside_down
        at_end = (lane < 2) | (lane >= LANES - 2)
        ends_up, ends_down = jnp.where(at_end, ends_up, 0.0), jnp.where(at_end, ends_down, 0.0)
        weights.append(
            (
                jnp.concatenate([inside_up, ends_up], axis=1),
                jnp.concatenate([inside_down, ends_down], axis=1),
            )
        )
    stack = []
    for k in range(1, partners + 1):
        upward = jnp.bitwise_xor(me, k) > me
        stack += [jnp.where(upward, w[0], w[1]) for w in weights]
    while len(stack) % 8:
        stack.append(jnp.zeros((1, 2 * LANES), jnp.float32))
    count = len(stack)
    stack = jnp.concatenate(stack, axis=0)
    first = stack.astype(jnp.bfloat16).astype(jnp.float32)
    both = jnp.concatenate([first, stack - first], axis=0).astype(jnp.bfloat16)
    across = (((1,), (1,)), ((), ()))
    total = high.shape[0]
    size = planes_x * wy
    for begin in range(0, total, size):
        rows = slice(begin, min(begin + size, total))
        on_high = matmul(both, high[rows, :], across)
        on_low = matmul(both, low[rows, :], across)
        moments = (on_high[:count] + on_high[count:]) + on_low[:count]
        for k in range(partners):
            messages[k][:, rows] = moments[2 * k : 2 * k + 2]


def dense_inverse(columns, start, width, stack):
    parts = 8
    steps = width // (2 * parts)
    lane = lax.broadcasted_iota(jnp.int32, (parts, LANES), 1)
    part = lax.broadcasted_iota(jnp.int32, (parts, LANES), 0)
    fits = width + 4 <= LANES
    values = [columns[pl.ds(start + 2 * i, parts, stride=2 * steps), :] for i in range(steps)]

    def wide(i, number):
        return tuple(
            jnp.broadcast_to(values[i][:, number + k : number + k + 1], (parts, LANES)) for k in range(4)
        )

    blocks = [wide(i, 8) for i in range(steps)]
    zero, one = jnp.zeros((parts, LANES), jnp.float32), jnp.ones((parts, LANES), jnp.float32)

    def put(rows, i, extra, extra_lane, owner):
        first = 2 * (part * steps + i)
        out = []
        for r in range(2):
            row = jnp.where(lane == first, blocks[i][2 * r], rows[r])
            row = jnp.where(lane == first + 1, blocks[i][2 * r + 1], row)
            if extra is not None and fits:
                row = jnp.where((part == owner) & (lane == extra_lane), extra[2 * r], row)
                row = jnp.where((part == owner) & (lane == extra_lane + 1), extra[2 * r + 1], row)
            out.append(row)
        return tuple(out)

    def run(order, number, ends, extra_lane, owner):
        rows, product, out = (zero, zero), (one, zero, zero, one), {}
        for i in order:
            t = wide(i, number)
            rows = (t[0] * rows[0] + t[1] * rows[1], t[2] * rows[0] + t[3] * rows[1])
            extra = None
            if i == order[0]:
                e = wide(i, ends)
                extra = mm(blocks[i], (e[0], e[2], e[1], e[3]))
            rows = put(rows, i, extra, extra_lane, owner)
            product = mm(t, product)
            out[i] = rows, product
        rows, product = out[order[-1]]
        entering, last = [None] * parts, (jnp.zeros((1, LANES), jnp.float32),) * 2
        sequence = range(parts) if number == 4 else range(parts - 1, -1, -1)
        for p in sequence:
            entering[p] = last
            own, across = [r[p : p + 1] for r in rows], [x[p : p + 1] for x in product]
            last = (
                own[0] + across[0] * last[0] + across[1] * last[1],
                own[1] + across[2] * last[0] + across[3] * last[1],
            )
        entering = [jnp.concatenate([e[r] for e in entering], axis=0) for r in range(2)]
        result = []
        for i in range(steps):
            rows, product = out[i]
            for r in range(2):
                result.append(rows[r] + product[2 * r] * entering[0] + product[2 * r + 1] * entering[1])
        return result

    low = run(list(range(steps)), 4, 12, width, 0)
    high = run(list(range(steps - 1, -1, -1)), 0, 16, width + 2, parts - 1)
    for k in range(2 * steps):
        lower = lane <= 2 * (part * steps + k // 2) + 1
        if fits:
            lower = lower & (lane < width) | ((lane >= width) & (lane < width + 2))
        stack[parts * k : parts * (k + 1), :] = jnp.where(lower, low[k], high[k])
    rows = [stack[pl.ds(p, 2 * steps, stride=parts), :] for p in range(parts)]
    return jnp.concatenate(rows, axis=0)


def stage_plan(count):
    plan, stride = [], 1
    while stride < count:
        radix = 4 if count // stride >= 4 else 2
        plan.append((stride, radix))
        stride *= radix
    return plan


def transposed(factors, row):
    rows = [factors[number, pl.ds(row, 1), :] for number in range(12)]
    rows += [factors[20 + number, pl.ds(row, 1), :] for number in range(8)]
    rows += [factors[12 + number, pl.ds(row, 1), :] for number in range(8)]
    rows.append(jnp.zeros((4, LANES), jnp.float32))
    return jnp.concatenate(rows, axis=0).T


def chain_products(factors, number, place, blocks, begins, ends, masks, reverse):
    count = -(-len(begins) // 8) * 8
    row = lax.broadcasted_iota(jnp.int32, (count, LANES), 0)
    begin = jnp.zeros((count, LANES), jnp.int32)
    end, mask = begin, jnp.zeros((count, LANES), jnp.float32)
    for r, (b, e, m) in enumerate(zip(begins, ends, masks)):
        begin, end = jnp.where(row == r, b, begin), jnp.where(row == r, e, end)
        mask = jnp.where(row == r, m, mask)
    one, zero = jnp.ones((count, LANES), jnp.float32), jnp.zeros((count, LANES), jnp.float32)
    product = (one, zero, zero, one)
    for block in range(blocks - 1, -1, -1) if reverse else range(blocks):
        where = place(block)
        at = (slice(where[0], where[0] + 1), slice(where[1], where[1] + 1))
        value = tuple(factors[(number + k, *at)] for k in range(4))
        product = pick((begin <= block) & (block < end), mm(product, value), product)
    return tuple(x * mask for x in product)


def truth(condition):
    return jnp.where(condition, 1.0, 0.0)


def second_kernel(
    ny, nz, count_z, wy, partners, factors, high, low, local, moments, entering, spread_core, spread_extra, *scratch
):
    columns, stacked, rows_ref, matrix, weights_y = scratch
    planes = (moments.shape[0] - 8) // 4
    me_z, me_y = lax.axis_index("gz"), lax.axis_index("gy")
    columns[0:LANES, 0:32] = transposed(factors, ny + me_z)
    inverse = dense_inverse(columns, 0, LANES, stacked)
    rows_ref[0:LANES, :] = inverse
    rows_ref[LANES : 2 * LANES, :] = jnp.zeros((LANES, LANES), jnp.float32)
    past = tuple(columns[LANES - 1 : LANES, 16 + k : 17 + k] for k in range(4))
    ahead = tuple(columns[0:1, 12 + k : 13 + k] for k in range(4))
    head0, head1 = rows_ref[0:1, :], rows_ref[1:2, :]
    tail0, tail1 = rows_ref[LANES - 2 : LANES - 1, :], rows_ref[LANES - 1 : LANES, :]
    for q in range(2):
        beyond = past[2 * q] * tail0 + past[2 * q + 1] * tail1
        rows_ref[LANES + q : LANES + q + 1, :] = beyond - (head0, head1)[q]
        beyond = ahead[2 * q] * head0 + ahead[2 * q + 1] * head1
        rows_ref[2 * LANES - 2 + q : 2 * LANES - 1 + q, :] = beyond - (tail0, tail1)[q]
    first, second = halves(rows_ref[...])
    matrix[:, 0:LANES] = first
    matrix[:, LANES : 2 * LANES] = second

    cell = me_y * wy
    start = lax.rem(cell, LANES)
    row = cell // LANES
    unit = (1.0, 0.0, 0.0, 1.0)
    lane = lax.broadcasted_iota(jnp.int32, (1, LANES), 1)
    even = (lane & 1) == 0

    def chain(number):
        return tuple(factors[number + k, pl.ds(row, 1), :] for k in range(4))

    def turned(x, by):
        return pltpu.roll(x, lax.rem(by + 2 * LANES, LANES), 1)

    def tiled(x, period):
        x = jnp.where(lane < period, x, 0.0)
        while period < LANES:
            x = x + lane_roll(x, period)
            period *= 2
        return x

    up, down, before, after = chain(12), chain(16), chain(20), chain(24)
    past_up, past_down = mm(before, up), mm(after, down)
    core_rows, extra_rows = [], []
    for column in range(2):
        same = jnp.where(even, unit[column], unit[2 + column])
        early = turned(cell_weights(past_up, column, even), -start)
        late = turned(cell_weights(past_down, column, even), 4 - wy - start)
        for inside, first, second in ((up, early, same), (down, same, late)):
            core_rows.append(tiled(turned(cell_weights(inside, column, even), -start), wy))
            past = jnp.where(lane < 2, first, jnp.where(lane < 4, second, 0.0))
            extra_rows.append(tiled(past, EXTRA))
    for number, source in enumerate((0, 2, 1, 3)):
        for rows, out, width in ((core_rows, spread_core, wy), (extra_rows, spread_extra, EXTRA)):
            per = LANES // width
            owner = lax.broadcasted_iota(jnp.int32, (per, LANES), 0)
            wide_lane = lax.broadcasted_iota(jnp.int32, (per, LANES), 1)
            value = jnp.where(owner == wide_lane // width, rows[source], 0.0)
            out[number * per : (number + 1) * per, :] = value

    others = [jnp.bitwise_xor(me_z, k) for k in range(1, partners + 1)]
    begins, ends = [other + 1 for other in others], others
    lowers = [other < me_z for other in others]
    size = len(begins)
    up = chain_products(
        factors, 12, lambda b: (ny + b, 0), count_z, begins, [me_z] * size, [1.0] * size, False
    )
    down = chain_products(
        factors, 16, lambda b: (ny + b, LANES - 1), count_z, [me_z + 1] * size, ends, [1.0] * size, True
    )
    stack = []
    for k, lower in enumerate(lowers):
        for p in range(2):
            from_low = up[2 * p][k : k + 1] * head0 + up[2 * p + 1][k : k + 1] * head1
            from_high = down[2 * p][k : k + 1] * tail0 + down[2 * p + 1][k : k + 1] * tail1
            stack.append(jnp.where(lower, from_low, from_high))
    while len(stack) % 8:
        stack.append(jnp.zeros((1, LANES), jnp.float32))
    stack = jnp.concatenate(stack, axis=0)
    first = stack.astype(jnp.bfloat16).astype(jnp.float32)
    entering[...] = jnp.concatenate([first, stack - first, first], axis=0)

    columns[0:LANES, 0:32] = transposed(factors, cell // LANES)
    row = lax.broadcasted_iota(jnp.int32, (wy, LANES), 0)
    extra_row = lax.broadcasted_iota(jnp.int32, (EXTRA, LANES), 0)
    unit = (1.0, 0.0, 0.0, 1.0)

    def head(number):
        return tuple(columns[pl.ds(start, 1), number + k : number + k + 1] for k in range(4))

    def tail(number):
        return tuple(columns[pl.ds(start + wy - 1, 1), number + k : number + k + 1] for k in range(4))

    past_up, past_down = mm(head(12), head(20)), mm(tail(16), tail(24))
    for column in range(2):
        for output, number in ((column, 20), (2 + column, 24)):
            even = columns[pl.ds(start, wy), number + column : number + column + 1]
            odd = columns[pl.ds(start, wy), number + 2 + column : number + 3 + column]
            weights_y[output, 0:wy, :] = jnp.where((row & 1) == 0, even, odd)
        for output, early, late in (
            (column, (past_up[column], past_up[2 + column]), (unit[column], unit[2 + column])),
            (2 + column, (unit[column], unit[2 + column]), (past_down[column], past_down[2 + column])),
        ):
            value = jnp.zeros((EXTRA, LANES), jnp.float32)
            for r, v in enumerate(early + late):
                value = jnp.where(extra_row == r, v, value)
            weights_y[output, wy : wy + EXTRA, :] = value

    total = planes * (wy + EXTRA)

    def solve(begin, size):
        rows = slice(begin, begin + size)
        both = matmul(high[rows, :], matrix[...])
        value = both[:, 0:LANES] + (both[:, LANES : 2 * LANES] + matmul(low[rows, :], matrix[:, 0:LANES]))
        local[rows, :] = value
        return value

    extra = solve(planes * wy, planes * EXTRA)
    for part in range(planes // 8):
        core = solve(part * 8 * wy, 8 * wy)
        for number in range(4):
            lines = []
            for k in range(8):
                index = part * 8 + k
                value = jnp.sum(core[k * wy : (k + 1) * wy] * weights_y[number, 0:wy, :], axis=0, keepdims=True)
                past = extra[index * EXTRA : (index + 1) * EXTRA] * weights_y[number, wy : wy + EXTRA, :]
                lines.append(value + jnp.sum(past, axis=0, keepdims=True))
            start = number * planes + part * 8
            moments[start : start + 8, :] = jnp.concatenate(lines, axis=0)


def y_kernel(count_y, wy, factors, unused, inverse_y, coefs, columns, stacked):
    me_y = lax.axis_index("gy")
    cell = me_y * wy
    columns[0:LANES, 0:32] = transposed(factors, cell // LANES)
    start = lax.rem(cell, LANES)
    inverse_y[...] = dense_inverse(columns, start, wy, stacked)

    up, down = ([], [], []), ([], [], [])
    plan = stage_plan(count_y)
    for number, (stride, radix) in enumerate(plan):
        group = me_y // stride
        first = (group // radix) * radix
        others = [first + jnp.bitwise_xor(group - first, k) for k in range(radix)]
        for other in others[1:]:
            for lists, values in (
                (up, ((other + 1) * stride, me_y, truth(other < group))),
                (down, (me_y + 1, other * stride, truth(other > group))),
            ):
                for one, value in zip(lists, values):
                    one.append(value)
        if number + 1 < len(plan):
            for other in others:
                for lists, values in (
                    (up, ((other + 1) * stride, (first + radix) * stride, 1.0)),
                    (down, (first * stride, other * stride, 1.0)),
                ):
                    for one, value in zip(lists, values):
                        one.append(value)

    def place(block):
        return block * wy // LANES, block * wy % LANES

    def place_end(block):
        return place(block)[0], place(block)[1] + wy - 1

    for base, value in (
        (0, chain_products(factors, 12, place, count_y, *up, False)),
        (4, chain_products(factors, 16, place_end, count_y, *down, True)),
    ):
        for k in range(4):
            coefs[base + k] = value[k]


def arrived_rows(messages, count):
    rows = [m[0:2] for m in messages]
    if count > 2 * len(messages):
        rows.append(jnp.zeros((count - 2 * len(messages), rows[0].shape[1]), jnp.float32))
    return jnp.concatenate(rows, axis=0)


def third_kernel(wy, moments, spread_core, spread_extra, entering, *refs):
    messages, (carried, held, result) = refs[:-3][::-1], refs[-3:]
    planes = carried.shape[1]
    count = entering.shape[0] // 3
    received = arrived_rows(messages, count)
    first = received.astype(jnp.bfloat16).astype(jnp.float32)
    both = jnp.concatenate([first, received - first], axis=0)
    values = entering[0:count, :] + entering[count : 2 * count, :]
    across = (((1,), (1,)), ((), ()))
    used = 2 * len(messages)

    def chunks(begin, end):
        parts = [both[:, at : min(at + LANES, end)] for at in range(begin, end, LANES)]
        if parts[-1].shape[1] < LANES:
            missing = jnp.zeros((2 * count, LANES - parts[-1].shape[1]), jnp.float32)
            parts[-1] = jnp.concatenate([parts[-1], missing], axis=1)
        return jnp.concatenate(parts, axis=0).astype(jnp.bfloat16), len(parts)

    per = LANES // wy
    stack, number = chunks(0, planes * wy)
    top, rest = halves(spread_core[...])
    held[0 : number * 2 * count, 0 : 4 * per] = matmul(stack, top, across) + matmul(stack, rest, across)
    columns = [
        held[pl.ds(r, number, stride=2 * count), :] + held[pl.ds(count + r, number, stride=2 * count), :]
        for r in range(used)
    ]
    for m in range(4):
        for p in range(per):
            lane = m * per + p
            value = moments[pl.ds(m * planes + p, number, stride=per), :]
            for r in range(used):
                value = value + columns[r][:, lane : lane + 1] * values[r : r + 1]
            result[pl.ds(m * planes + p, number, stride=per), :] = value

    per = LANES // EXTRA
    stack, number = chunks(planes * wy, planes * (wy + EXTRA))
    top, rest = halves(spread_extra[...])
    corner = matmul(top, stack, across) + matmul(rest, stack, across)
    spare = jnp.zeros((corner.shape[0], -corner.shape[1] % LANES), jnp.float32)
    corner = jnp.concatenate([corner, spare], axis=1)
    corner = corner + pltpu.roll(corner, corner.shape[1] - count, 1)
    for m in range(4):
        for chunk in range(number):
            size = min(per, planes - chunk * per)
            rows = slice(chunk * per, chunk * per + size)
            value = result[m * planes + chunk * per : m * planes + chunk * per + size, :]
            for r in range(used):
                lane = chunk * 2 * count + r
                part = corner[m * per : m * per + size]
                value = value + part[:, lane : lane + 1] * values[r : r + 1]
            carried[m, rows, :] = value


def local_y_kernel(wy, local, entering, inverse_y, unused, *refs):
    messages, (out, solved) = refs[:-2], refs[-2:]
    planes = out.shape[0]
    count = entering.shape[0] // 3
    received = arrived_rows(messages, count)
    first = received.astype(jnp.bfloat16).astype(jnp.float32)
    received = jnp.concatenate([first, first, received - first], axis=0).T.astype(jnp.bfloat16)
    solved[...] = local[...] + matmul(received, entering[...].astype(jnp.bfloat16))
    first, second = halves(inverse_y[:, 0 : wy + EXTRA])
    left = jnp.concatenate([first, second, first], axis=1)

    def part(index, carry):
        for k in range(8):
            number = index * 8 + k
            start = pl.multiple_of(number * wy, 8)
            core = solved[pl.ds(start, wy), :]
            start = pl.multiple_of(planes * wy + number * EXTRA, 8)
            both = jnp.concatenate([core, solved[pl.ds(start, EXTRA), :]], axis=0)
            top, rest = halves(both)
            out[number] = matmul(left, jnp.concatenate([top, top, rest], axis=0))
        return carry

    lax.fori_loop(0, planes // 8, part, 0)


def combine(coefs, side, row, values):
    first = 0 if side == 0 else 2
    out = [None, None]
    for k, value in enumerate(values):
        for q in range(2):
            for p in range(2):
                term = coefs[side + 2 * p + q, row + k : row + k + 1, :] * value[first + p]
                out[q] = term if out[q] is None else out[q] + term
    return out


def stage_kernel(base, stride, radix, narrow, has_entered, coefs, *refs):
    values = refs[:radix]
    position = radix
    entered = None
    if has_entered:
        entered = refs[position]
        position += 1
    message, entering = refs[position : position + 2]
    below = combine(coefs, 0, base, values[1:])
    above = combine(coefs, 4, base, values[1:])
    for row, value in enumerate(below + above):
        entering[row] = value if entered is None else value + entered[row]
    upward = combine(coefs, 0, base + radix - 1, values)
    downward = combine(coefs, 4, base + radix - 1, values)
    if narrow:
        group = lax.axis_index("gy") // (stride * radix)
        sends_up = lax.rem(group, 2) == 0
        for row in range(2):
            message[row] = jnp.where(sends_up, upward[row], downward[row])
    else:
        for row, value in enumerate(upward + downward):
            message[row] = value


def last_kernel(base, radix, narrow, wy, coefs, local, inverse_y, entered, *refs):
    messages, (out_hbm, out, sent) = refs[: radix - 1], refs[radix - 1 :]
    values = list(messages)
    if narrow:
        values = [(m[0], m[1], m[0], m[1]) for m in values]
    below = combine(coefs, 0, base, values)
    above = combine(coefs, 4, base, values)
    st = [value + entered[row] for row, value in enumerate(below + above)]
    sides = [
        jnp.broadcast_to(inverse_y[:, c : c + 1], (wy, LANES)) for c in (0, 1, wy - 2, wy - 1)
    ]
    fields, planes_x = out.shape[:2]
    copies = []
    for field in range(fields):
        for x in range(planes_x):
            index = field * planes_x + x
            value = local[index]
            for number in range(4):
                value = value + sides[number] * st[number][index : index + 1]
            out[field, x] = value
            if (x + 1) % 4 == 0:
                part = (field, pl.ds(x - 3, 4))
                copy = pltpu.make_async_copy(out.at[part], out_hbm.at[part], sent.at[len(copies)])
                copy.start()
                copies.append(copy)
    for copy in copies:
        copy.wait()


VMEM = pl.BlockSpec(memory_space=pltpu.VMEM)
HBM = pl.BlockSpec(memory_space=pltpu.HBM)
PARAMS = pltpu.CompilerParams(vmem_limit_bytes=40 * 1024 * 1024)


def array(*shape):
    return jax.ShapeDtypeStruct(shape, jnp.float32)


def in_hbm(x):
    return pltpu.with_memory_space_constraint(x, pltpu.HBM)


def cost(flops, data):
    return pl.CostEstimate(flops=flops, bytes_accessed=data, transcendentals=0)


def on_device(mesh, flow, speed, metric_y, metric_z):
    fields, planes_x, wy, wz = flow.shape
    count_y, count_z = mesh.shape["gy"], mesh.shape["gz"]
    assert wz == LANES
    ny, nz = metric_y.shape[0] // LANES, metric_z.shape[0] // LANES
    planes = fields * planes_x
    rows = planes * (wy + EXTRA)
    partners = count_z - 1
    arrivals = partners
    entering_rows = -(-2 * arrivals // 8) * 8
    half = jax.ShapeDtypeStruct((rows, 2 * LANES), jnp.bfloat16)
    outputs = pl.pallas_call(
        functools.partial(first_kernel, ny, nz, partners),
        out_shape=[half, half, array(28, ny + nz, LANES)]
        + [array(2, rows)] * partners,
        in_specs=[HBM] * 4,
        out_specs=[VMEM] * (3 + partners),
        scratch_shapes=[
            pltpu.VMEM(flow.shape, jnp.float32),
            pltpu.VMEM(speed.shape, jnp.float32),
            pltpu.VMEM((ny + nz, LANES), jnp.float32),
            pltpu.VMEM((planes_x, 3, wy + 16, LANES), jnp.float32),
            pltpu.SemaphoreType.DMA((fields + 3,)),
        ],
        compiler_params=PARAMS,
        name="forcing_and_factor",
    )(*(in_hbm(x) for x in (flow, speed, metric_y.reshape(ny, LANES), metric_z.reshape(nz, LANES))))
    high, low, factors = outputs[:3]

    def exchange(values, axis, count, stride, radix):
        received = {}
        for k in reversed(range(1, radix)):
            pairs = [(i, i ^ (k * stride)) for i in range(count)]
            received[k] = lax.ppermute(values[k - 1], axis, pairs)
        return [received[k] for k in range(1, radix)]

    plan = stage_plan(count_y)
    work = [pltpu.VMEM((LANES + 16, LANES), jnp.float32)] * 2
    received = exchange(outputs[3:], "gz", count_z, 1, count_z)
    local, moments, entering, spread_core, spread_extra = pl.pallas_call(
        functools.partial(second_kernel, ny, nz, count_z, wy, partners),
        out_shape=[
            array(rows, LANES),
            array(4 * planes + 8, LANES),
            array(3 * entering_rows, LANES),
            array(4 * (LANES // wy), LANES),
            array(4 * (LANES // EXTRA), LANES),
        ],
        in_specs=[VMEM] * 3,
        out_specs=[VMEM] * 5,
        scratch_shapes=work
        + [
            pltpu.VMEM((2 * LANES, LANES), jnp.float32),
            pltpu.VMEM((2 * LANES, 2 * LANES), jnp.bfloat16),
            pltpu.VMEM((4, wy + EXTRA, LANES), jnp.float32),
        ],
        compiler_params=PARAMS,
        cost_estimate=cost(2 * rows * 256 * 128 * 6, 4 * rows * 384),
        name="local_z",
    )(factors, high, low)
    carried = pl.pallas_call(
        functools.partial(third_kernel, wy),
        out_shape=array(4, planes, LANES),
        in_specs=[VMEM] * (4 + arrivals),
        out_specs=VMEM,
        scratch_shapes=[
            pltpu.VMEM((planes * wy // LANES * 2 * entering_rows + 2 * entering_rows, LANES), jnp.float32),
            pltpu.VMEM((4 * planes + 8, LANES), jnp.float32),
        ],
        compiler_params=PARAMS,
        name="carried_y",
    )(moments, spread_core, spread_extra, entering, *received[::-1])
    arrived = received

    narrow = plan[-1][1] == 2 and len(plan) > 1
    base, entered, result = 0, None, None
    for number, (stride, radix) in enumerate(plan):
        received = exchange([carried] * (radix - 1), "gy", count_y, stride, radix)
        if number == 0:
            entries = sum(2 * radix - 1 for _, radix in plan[:-1]) + plan[-1][1] - 1
            inverse_y, coefs = pl.pallas_call(
                functools.partial(y_kernel, count_y, wy),
                out_shape=[array(wy, LANES), array(8, -(-entries // 8) * 8, LANES)],
                in_specs=[VMEM, HBM],
                out_specs=[VMEM] * 2,
                scratch_shapes=work,
                compiler_params=PARAMS,
                cost_estimate=cost(2 * rows * 128 * 128 * 6, 4 * rows * 256),
                name="inverse_y",
            )(factors, carried)
        if number + 1 < len(plan):
            slim = narrow and number + 2 == len(plan)
            inputs = [carried] + received + ([entered] if entered is not None else [])
            carried, entered = pl.pallas_call(
                functools.partial(stage_kernel, base, stride, radix, slim, entered is not None),
                out_shape=[array(2 if slim else 4, planes, LANES), array(4, planes, LANES)],
                in_specs=[VMEM] * (1 + len(inputs)),
                out_specs=[VMEM] * 2,
                compiler_params=PARAMS,
                name="join_groups",
            )(coefs, *inputs)
            base += 2 * radix - 1
            if number == 0:
                result = pl.pallas_call(
                    functools.partial(local_y_kernel, wy),
                    out_shape=array(planes, wy, LANES),
                    in_specs=[VMEM] * 3 + [HBM] + [VMEM] * arrivals,
                    out_specs=VMEM,
                    scratch_shapes=[pltpu.VMEM((rows, LANES), jnp.float32)],
                    compiler_params=PARAMS,
                    cost_estimate=cost(2 * rows * 128 * 128 * 6, 4 * rows * 256),
                    name="local_y",
                )(local, entering, inverse_y, entered, *arrived)
        else:
            return pl.pallas_call(
                functools.partial(last_kernel, base, radix, narrow, wy),
                out_shape=array(fields, planes_x, wy, wz),
                in_specs=[VMEM] * (4 + len(received)),
                out_specs=HBM,
                scratch_shapes=[
                    pltpu.VMEM(flow.shape, jnp.float32),
                    pltpu.SemaphoreType.DMA((planes // 4,)),
                ],
                compiler_params=PARAMS,
                name="finish_y",
            )(coefs, result, inverse_y, entered, *received)


def solution(mesh):
    placed = (P(None, None, "gy", "gz"), P(None, "gy", "gz"), P(), P())
    return jax.shard_map(
        functools.partial(on_device, mesh),
        mesh=mesh,
        in_specs=placed,
        out_specs=P(None, None, "gy", "gz"),
        check_vma=False,
    )
```

```python
import functools

import jax
import jax.numpy as jnp
from jax import lax
from jax.experimental import pallas as pl
from jax.experimental.pallas import tpu as pltpu
from jax.sharding import PartitionSpec as P

viscous = 0.25
explicit_fourth = 0.04
implicit_fourth = 0.05
time_step = 1048576.0
LANES = 128
EXTRA = 8


def mm(a, b):
    return (
        a[0] * b[0] + a[1] * b[2],
        a[0] * b[1] + a[1] * b[3],
        a[2] * b[0] + a[3] * b[2],
        a[2] * b[1] + a[3] * b[3],
    )


def inverse_of_one_minus(a):
    p, q, r, s = 1.0 - a[0], -a[1], -a[2], 1.0 - a[3]
    d = 1.0 / (p * s - q * r)
    return (s * d, -q * d, -r * d, p * d)


def pick(condition, a, b):
    return tuple(jnp.where(condition, x, y) for x, y in zip(a, b))


def halves(x):
    high = x.astype(jnp.bfloat16)
    return high, (x - high.astype(jnp.float32)).astype(jnp.bfloat16)


def matmul(a, b, dims=(((1,), (0,)), ((), ()))):
    return lax.dot_general(a, b, dims, preferred_element_type=jnp.float32)


def scan(m, ahead, count, step, shift, product):
    unit = (1.0, 0.0, 0.0, 1.0)

    def moved(by):
        return tuple(jnp.where(ahead >= by, shift(x, by), u) for x, u in zip(m, unit))

    while step < count:
        if 2 * step < count:
            m = product(product(m, moved(step)), product(moved(2 * step), moved(3 * step)))
            step *= 4
        else:
            m = product(m, moved(step))
            step *= 2
    return m


def lane_roll(x, by):
    return pltpu.roll(x, by % LANES, 1)


def row_roll(x, by):
    by = by % x.shape[0]
    return jnp.concatenate([x[x.shape[0] - by :], x[: x.shape[0] - by]], axis=0)


class Factor:
    def __init__(self, metric, ny, nz, wy):
        self.ny, self.nz, self.wy, self.rows = ny, nz, wy, ny + nz
        self.lane = lax.broadcasted_iota(jnp.int32, (self.rows, LANES), 1)
        self.row = lax.broadcasted_iota(jnp.int32, (self.rows, LANES), 0)
        self.block = jnp.where(self.row < ny, self.row, self.row - ny)
        self.to_end = jnp.where(self.row < ny, ny, nz) - 1 - self.block
        first = (self.lane == 0) & (self.block == 0)
        last = (self.lane == LANES - 1) & (self.to_end == 0)
        self.face_low = 0.5 * (jnp.where(first, metric, self.before(metric, 1)) + metric)
        self.face_high = 0.5 * (metric + jnp.where(last, metric, self.after(metric, 1)))

    def before(self, x, by):
        rolled = lane_roll(x, by)
        value = jnp.where(self.lane < by, row_roll(rolled, 1), rolled)
        return jnp.where((self.lane < by) & (self.block == 0), 0.0, value)

    def after(self, x, by):
        rolled = lane_roll(x, -by)
        value = jnp.where(self.lane >= LANES - by, row_roll(rolled, -1), rolled)
        return jnp.where((self.lane >= LANES - by) & (self.to_end == 0), 0.0, value)

    def guess(self, sign):
        face = self.face_high if sign > 0 else self.face_low
        if sign > 0:
            cell = self.lane + LANES * self.block
        else:
            cell = LANES - 1 - self.lane + LANES * self.to_end
        near = face / (cell + 1).astype(jnp.float32)
        one_over = 1.0 / (face + jnp.sqrt(face + near * near))
        return face * one_over, implicit_fourth * one_over, one_over

    def sweep(self, sign, ratio, far):
        rows = self.rows
        back = self.before if sign > 0 else self.after
        if sign > 0:
            face_in, face_out, place = self.face_low, self.face_high, self.block
        else:
            face_in, face_out, place = self.face_high, self.face_low, self.to_end
        eps = 4.0 * implicit_fourth - implicit_fourth * back(ratio, 1)
        mass = (1.0 + 6.0 * implicit_fourth) - implicit_fourth * back(far, 2) - 2.0 * eps
        eps_in = back(eps, 1)
        scale = 1.0 / (face_in + 2.0 * eps_in)
        m = ((mass + face_in) * scale, mass - eps_in * eps_in * scale, scale, jnp.ones_like(scale))
        ahead = self.lane if sign > 0 else LANES - 1 - self.lane
        m = scan(m, ahead, LANES, 1, lambda x, by: lane_roll(x, sign * by), mm)
        edge = LANES - 1 if sign > 0 else 0
        total = tuple(jnp.broadcast_to(x[:, edge : edge + 1], (rows, LANES)) for x in m)
        total = scan(
            total, place, max(self.ny, self.nz), 1, lambda x, by: row_roll(x, sign * by), mm
        )
        top = jnp.where(place >= 1, row_roll(total[0], sign), 1.0)
        low = jnp.where(place >= 1, row_roll(total[2], sign), 0.0)
        eta = (m[0] * top + m[1] * low) / (m[2] * top + m[3] * low)
        one_over = 1.0 / (face_out + (eta + 2.0 * eps))
        return (face_out + eps) * one_over, implicit_fourth * one_over, one_over

    def finish(self, near_l, far_l, pivot_l, near_r, far_r):
        lane, block, to_end = self.lane, self.block, self.to_end
        even = (lane & 1) == 0
        near_l = jnp.where((to_end == 0) & (lane >= LANES - 1), 0.0, near_l)
        far_l = jnp.where((to_end == 0) & (lane >= LANES - 2), 0.0, far_l)
        near_r = jnp.where((block == 0) & (lane < 1), 0.0, near_r)
        far_r = jnp.where((block == 0) & (lane < 2), 0.0, far_r)

        def of_even(x):
            return jnp.where(even, x, lane_roll(x, 1))

        def of_odd(x):
            return jnp.where(even, lane_roll(x, -1), x)

        t0, t1, r0, r1 = of_even(near_l), of_odd(near_l), of_even(far_l), of_odd(far_l)
        from_right = (t0 * t1 - r0, -t0 * r1, t1, -r1)
        p1 = of_odd(pivot_l)
        left_inverse = (of_even(pivot_l) + t0 * t0 * p1, t0 * p1, t0 * p1, p1)
        s0, s1, q0, q1 = of_even(near_r), of_odd(near_r), of_even(far_r), of_odd(far_r)
        from_left = (-q0, s0, -s1 * q0, s1 * s0 - q1)
        from_left_after = tuple(self.after(x, 2) for x in from_left)
        from_right_before = tuple(self.before(x, 2) for x in from_right)
        diagonal = mm(inverse_of_one_minus(mm(from_right, from_left_after)), left_inverse)
        width = jnp.where(self.row < self.ny, self.wy, LANES)
        place = lane & (width - 1)
        right = scan(from_right, width - 1 - place, LANES, 2, lambda x, by: lane_roll(x, -by), mm)
        left = scan(from_left, place, LANES, 2, lane_roll, mm)
        return from_right, from_left, diagonal, right, left, from_right_before, from_left_after


def cell_weights(chain, column, even):
    return jnp.where(even, chain[column], chain[2 + column])


def first_kernel(ny, nz, partners, flow_hbm, speed_hbm, metric_y, metric_z, *refs):
    high, low, factors = refs[:3]
    messages = refs[3 : 3 + partners]
    flow, speed, metric, spread, arrived = refs[3 + partners :]
    fields, planes_x, wy, _ = flow.shape
    rows = ny + nz
    core_rows = fields * planes_x * wy

    copies = [
        pltpu.make_async_copy(metric_y, metric.at[0:ny], arrived.at[fields]),
        pltpu.make_async_copy(metric_z, metric.at[ny:rows], arrived.at[fields + 1]),
        pltpu.make_async_copy(speed_hbm, speed, arrived.at[fields + 2]),
    ]
    for copy in copies:
        copy.start()
    for field in range(fields):
        pltpu.make_async_copy(flow_hbm.at[field], flow.at[field], arrived.at[field]).start()

    lane = lax.broadcasted_iota(jnp.int32, (wy, LANES), 1)
    extra_row = lax.broadcasted_iota(jnp.int32, (EXTRA, LANES), 0)
    for slot in range(planes_x):
        for part in range(3):
            spread[slot, part, 0:8, :] = jnp.zeros((8, LANES), jnp.float32)
            spread[slot, part, wy + 8 : wy + 16, :] = jnp.zeros((8, LANES), jnp.float32)
    side = time_step * (viscous + 4.0 * explicit_fourth)
    half = time_step * 0.5
    centre = time_step * (-6.0 * viscous - 12.0 * explicit_fourth)
    fourth = -time_step * explicit_fourth

    def store(start, column, value):
        first, second = halves(value)
        high[pl.ds(start, value.shape[0]), column : column + LANES] = first
        low[pl.ds(start, value.shape[0]), column : column + LANES] = second

    def one_field(field):
        values = [flow[field, x] for x in range(planes_x)]
        fluxes = [values[x] * speed[x] for x in range(planes_x)]
        aside = [(time_step * viscous) * u for u in values]
        extras = []
        for x in range(planes_x):
            u, flux, slot = values[x], fluxes[x], x
            total = centre * u
            if x + 1 < planes_x:
                total = total + (aside[x + 1] - fluxes[x + 1])
            if x > 0:
                total = total + (aside[x - 1] + fluxes[x - 1])
            scaled = side * u
            onward, backward, far = scaled + flux, scaled - flux, fourth * u
            spread[slot, 0, 8 : wy + 8, :] = onward
            spread[slot, 1, 8 : wy + 8, :] = backward
            spread[slot, 2, 8 : wy + 8, :] = far
            total = total + (spread[slot, 0, 7 : wy + 7, :] + spread[slot, 1, 9 : wy + 9, :])
            total = total + (spread[slot, 2, 6 : wy + 6, :] + spread[slot, 2, 10 : wy + 10, :])
            a, b = lane_roll(onward, 1), lane_roll(backward, -1)
            c, d = lane_roll(far, 2), lane_roll(far, -2)
            from_low, from_high = a + c, b + d
            ends = jnp.where(lane == 0, from_low, jnp.where(lane == 1, c, 0.0))
            ends = jnp.where(lane == LANES - 1, from_high, jnp.where(lane == LANES - 2, d, ends))
            index = field * planes_x + x
            start = index * wy
            store(start, 0, total + (from_low + from_high))
            store(start, LANES, ends)
            above = spread[slot, 1, 7:15, :] + spread[slot, 2, 8:16, :]
            below = spread[slot, 0, wy + 5 : wy + 13, :] + spread[slot, 2, wy + 4 : wy + 12, :]
            extras.append(jnp.where(extra_row < 2, above, jnp.where(extra_row < 4, below, 0.0)))
            if len(extras) == 2:
                start = core_rows + (index - 1) * EXTRA
                store(start, 0, jnp.concatenate(extras, axis=0))
                for ref in (high, low):
                    ref[pl.ds(start, 2 * EXTRA), LANES : 2 * LANES] = jnp.zeros(
                        (2 * EXTRA, LANES), jnp.bfloat16
                    )
                extras = []

    copies[0].wait()
    copies[1].wait()
    factor = Factor(metric[...], ny, nz, wy)

    guess_l, guess_r = factor.guess(1), factor.guess(-1)
    left, right = factor.sweep(1, *guess_l[:2]), factor.sweep(-1, *guess_r[:2])
    copies[2].wait()
    for x in range(planes_x):
        speed[x] = half * speed[x]
    for field in range(fields):
        pltpu.make_async_copy(flow_hbm.at[field], flow.at[field], arrived.at[field]).wait()
    left, right = factor.sweep(1, *left[:2]), factor.sweep(-1, *right[:2])
    for field in range(fields // 2):
        one_field(field)
    parts = factor.finish(*left, *right[:2])
    from_right, from_left, diagonal, to_right, to_left, before, after = parts
    for number, value in enumerate(v for part in parts for v in part):
        factors[number] = value
    for field in range(fields // 2, fields):
        one_field(field)

    me = lax.axis_index("gz")
    mine = lax.broadcasted_iota(jnp.int32, (rows, LANES), 0) == ny + me
    even = (lax.broadcasted_iota(jnp.int32, (1, LANES), 1) & 1) == 0
    lane = lax.broadcasted_iota(jnp.int32, (1, LANES), 1)

    def own(values):
        return tuple(jnp.sum(jnp.where(mine, v, 0.0), axis=0, keepdims=True) for v in values)

    up, down = own(to_right), own(to_left)
    up_past, down_past = own(mm(before, to_right)), own(mm(after, to_left))
    unit = (1.0, 0.0, 0.0, 1.0)
    weights = []
    for column in range(2):
        same = jnp.where(even, unit[column], unit[2 + column])
        inside_up = cell_weights(up, column, even)
        inside_down = cell_weights(down, column, even)
        past_up = lane_roll(cell_weights(up_past, column, even), -2)
        past_down = lane_roll(cell_weights(down_past, column, even), 2)
        ends_up = jnp.where(lane < 2, same, past_up) - inside_up
        ends_down = jnp.where(lane < 2, past_down, same) - inside_down
        at_end = (lane < 2) | (lane >= LANES - 2)
        ends_up, ends_down = jnp.where(at_end, ends_up, 0.0), jnp.where(at_end, ends_down, 0.0)
        weights.append(
            (
                jnp.concatenate([inside_up, ends_up], axis=1),
                jnp.concatenate([inside_down, ends_down], axis=1),
            )
        )
    stack = []
    for k in range(1, partners + 1):
        upward = jnp.bitwise_xor(me, k) > me
        stack += [jnp.where(upward, w[0], w[1]) for w in weights]
    while len(stack) % 8:
        stack.append(jnp.zeros((1, 2 * LANES), jnp.float32))
    count = len(stack)
    stack = jnp.concatenate(stack, axis=0)
    first = stack.astype(jnp.bfloat16).astype(jnp.float32)
    both = jnp.concatenate([first, stack - first], axis=0).astype(jnp.bfloat16)
    across = (((1,), (1,)), ((), ()))
    total = high.shape[0]
    size = planes_x * wy
    for begin in range(0, total, size):
        rows = slice(begin, min(begin + size, total))
        on_high = matmul(both, high[rows, :], across)
        on_low = matmul(both, low[rows, :], across)
        moments = (on_high[:count] + on_high[count:]) + on_low[:count]
        for k in range(partners):
            messages[k][:, rows] = moments[2 * k : 2 * k + 2]


def dense_inverse(columns, start, width, stack):
    parts = 8
    steps = width // (2 * parts)
    lane = lax.broadcasted_iota(jnp.int32, (parts, LANES), 1)
    part = lax.broadcasted_iota(jnp.int32, (parts, LANES), 0)
    fits = width + 4 <= LANES
    values = [columns[pl.ds(start + 2 * i, parts, stride=2 * steps), :] for i in range(steps)]

    def wide(i, number):
        return tuple(
            jnp.broadcast_to(values[i][:, number + k : number + k + 1], (parts, LANES)) for k in range(4)
        )

    blocks = [wide(i, 8) for i in range(steps)]
    zero, one = jnp.zeros((parts, LANES), jnp.float32), jnp.ones((parts, LANES), jnp.float32)

    def put(rows, i, extra, extra_lane, owner):
        first = 2 * (part * steps + i)
        out = []
        for r in range(2):
            row = jnp.where(lane == first, blocks[i][2 * r], rows[r])
            row = jnp.where(lane == first + 1, blocks[i][2 * r + 1], row)
            if extra is not None and fits:
                row = jnp.where((part == owner) & (lane == extra_lane), extra[2 * r], row)
                row = jnp.where((part == owner) & (lane == extra_lane + 1), extra[2 * r + 1], row)
            out.append(row)
        return tuple(out)

    def run(order, number, ends, extra_lane, owner):
        rows, product, out = (zero, zero), (one, zero, zero, one), {}
        for i in order:
            t = wide(i, number)
            rows = (t[0] * rows[0] + t[1] * rows[1], t[2] * rows[0] + t[3] * rows[1])
            extra = None
            if i == order[0]:
                e = wide(i, ends)
                extra = mm(blocks[i], (e[0], e[2], e[1], e[3]))
            rows = put(rows, i, extra, extra_lane, owner)
            product = mm(t, product)
            out[i] = rows, product
        rows, product = out[order[-1]]
        entering, last = [None] * parts, (jnp.zeros((1, LANES), jnp.float32),) * 2
        sequence = range(parts) if number == 4 else range(parts - 1, -1, -1)
        for p in sequence:
            entering[p] = last
            own, across = [r[p : p + 1] for r in rows], [x[p : p + 1] for x in product]
            last = (
                own[0] + across[0] * last[0] + across[1] * last[1],
                own[1] + across[2] * last[0] + across[3] * last[1],
            )
        entering = [jnp.concatenate([e[r] for e in entering], axis=0) for r in range(2)]
        result = []
        for i in range(steps):
            rows, product = out[i]
            for r in range(2):
                result.append(rows[r] + product[2 * r] * entering[0] + product[2 * r + 1] * entering[1])
        return result

    low = run(list(range(steps)), 4, 12, width, 0)
    high = run(list(range(steps - 1, -1, -1)), 0, 16, width + 2, parts - 1)
    for k in range(2 * steps):
        lower = lane <= 2 * (part * steps + k // 2) + 1
        if fits:
            lower = lower & (lane < width) | ((lane >= width) & (lane < width + 2))
        stack[parts * k : parts * (k + 1), :] = jnp.where(lower, low[k], high[k])
    rows = [stack[pl.ds(p, 2 * steps, stride=parts), :] for p in range(parts)]
    return jnp.concatenate(rows, axis=0)


def stage_plan(count):
    plan, stride = [], 1
    while stride < count:
        radix = 4 if count // stride >= 4 else 2
        plan.append((stride, radix))
        stride *= radix
    return plan


def transposed(factors, row):
    rows = [factors[number, pl.ds(row, 1), :] for number in range(12)]
    rows += [factors[20 + number, pl.ds(row, 1), :] for number in range(8)]
    rows += [factors[12 + number, pl.ds(row, 1), :] for number in range(8)]
    rows.append(jnp.zeros((4, LANES), jnp.float32))
    return jnp.concatenate(rows, axis=0).T


def chain_products(factors, number, place, blocks, begins, ends, masks, reverse):
    count = -(-len(begins) // 8) * 8
    row = lax.broadcasted_iota(jnp.int32, (count, LANES), 0)
    begin = jnp.zeros((count, LANES), jnp.int32)
    end, mask = begin, jnp.zeros((count, LANES), jnp.float32)
    for r, (b, e, m) in enumerate(zip(begins, ends, masks)):
        begin, end = jnp.where(row == r, b, begin), jnp.where(row == r, e, end)
        mask = jnp.where(row == r, m, mask)
    one, zero = jnp.ones((count, LANES), jnp.float32), jnp.zeros((count, LANES), jnp.float32)
    product = (one, zero, zero, one)
    for block in range(blocks - 1, -1, -1) if reverse else range(blocks):
        where = place(block)
        at = (slice(where[0], where[0] + 1), slice(where[1], where[1] + 1))
        value = tuple(factors[(number + k, *at)] for k in range(4))
        product = pick((begin <= block) & (block < end), mm(product, value), product)
    return tuple(x * mask for x in product)


def truth(condition):
    return jnp.where(condition, 1.0, 0.0)


def second_kernel(
    ny, nz, count_z, wy, partners, factors, high, low, local, moments, entering, spread_core, spread_extra, *scratch
):
    columns, stacked, rows_ref, matrix, weights_y = scratch
    planes = (moments.shape[0] - 8) // 4
    me_z, me_y = lax.axis_index("gz"), lax.axis_index("gy")
    columns[0:LANES, 0:32] = transposed(factors, ny + me_z)
    inverse = dense_inverse(columns, 0, LANES, stacked)
    rows_ref[0:LANES, :] = inverse
    rows_ref[LANES : 2 * LANES, :] = jnp.zeros((LANES, LANES), jnp.float32)
    past = tuple(columns[LANES - 1 : LANES, 16 + k : 17 + k] for k in range(4))
    ahead = tuple(columns[0:1, 12 + k : 13 + k] for k in range(4))
    head0, head1 = rows_ref[0:1, :], rows_ref[1:2, :]
    tail0, tail1 = rows_ref[LANES - 2 : LANES - 1, :], rows_ref[LANES - 1 : LANES, :]
    for q in range(2):
        beyond = past[2 * q] * tail0 + past[2 * q + 1] * tail1
        rows_ref[LANES + q : LANES + q + 1, :] = beyond - (head0, head1)[q]
        beyond = ahead[2 * q] * head0 + ahead[2 * q + 1] * head1
        rows_ref[2 * LANES - 2 + q : 2 * LANES - 1 + q, :] = beyond - (tail0, tail1)[q]
    first, second = halves(rows_ref[...])
    matrix[:, 0:LANES] = first
    matrix[:, LANES : 2 * LANES] = second

    cell = me_y * wy
    start = lax.rem(cell, LANES)
    row = cell // LANES
    unit = (1.0, 0.0, 0.0, 1.0)
    lane = lax.broadcasted_iota(jnp.int32, (1, LANES), 1)
    even = (lane & 1) == 0

    def chain(number):
        return tuple(factors[number + k, pl.ds(row, 1), :] for k in range(4))

    def turned(x, by):
        return pltpu.roll(x, lax.rem(by + 2 * LANES, LANES), 1)

    def tiled(x, period):
        x = jnp.where(lane < period, x, 0.0)
        while period < LANES:
            x = x + lane_roll(x, period)
            period *= 2
        return x

    up, down, before, after = chain(12), chain(16), chain(20), chain(24)
    past_up, past_down = mm(before, up), mm(after, down)
    core_rows, extra_rows = [], []
    for column in range(2):
        same = jnp.where(even, unit[column], unit[2 + column])
        early = turned(cell_weights(past_up, column, even), -start)
        late = turned(cell_weights(past_down, column, even), 4 - wy - start)
        for inside, first, second in ((up, early, same), (down, same, late)):
            core_rows.append(tiled(turned(cell_weights(inside, column, even), -start), wy))
            past = jnp.where(lane < 2, first, jnp.where(lane < 4, second, 0.0))
            extra_rows.append(tiled(past, EXTRA))
    for number, source in enumerate((0, 2, 1, 3)):
        for rows, out, width in ((core_rows, spread_core, wy), (extra_rows, spread_extra, EXTRA)):
            per = LANES // width
            owner = lax.broadcasted_iota(jnp.int32, (per, LANES), 0)
            wide_lane = lax.broadcasted_iota(jnp.int32, (per, LANES), 1)
            value = jnp.where(owner == wide_lane // width, rows[source], 0.0)
            out[number * per : (number + 1) * per, :] = value

    others = [jnp.bitwise_xor(me_z, k) for k in range(1, partners + 1)]
    begins, ends = [other + 1 for other in others], others
    lowers = [other < me_z for other in others]
    size = len(begins)
    up = chain_products(
        factors, 12, lambda b: (ny + b, 0), count_z, begins, [me_z] * size, [1.0] * size, False
    )
    down = chain_products(
        factors, 16, lambda b: (ny + b, LANES - 1), count_z, [me_z + 1] * size, ends, [1.0] * size, True
    )
    stack = []
    for k, lower in enumerate(lowers):
        for p in range(2):
            from_low = up[2 * p][k : k + 1] * head0 + up[2 * p + 1][k : k + 1] * head1
            from_high = down[2 * p][k : k + 1] * tail0 + down[2 * p + 1][k : k + 1] * tail1
            stack.append(jnp.where(lower, from_low, from_high))
    while len(stack) % 8:
        stack.append(jnp.zeros((1, LANES), jnp.float32))
    stack = jnp.concatenate(stack, axis=0)
    first = stack.astype(jnp.bfloat16).astype(jnp.float32)
    entering[...] = jnp.concatenate([first, stack - first, first], axis=0)

    columns[0:LANES, 0:32] = transposed(factors, cell // LANES)
    row = lax.broadcasted_iota(jnp.int32, (wy, LANES), 0)
    extra_row = lax.broadcasted_iota(jnp.int32, (EXTRA, LANES), 0)
    unit = (1.0, 0.0, 0.0, 1.0)

    def head(number):
        return tuple(columns[pl.ds(start, 1), number + k : number + k + 1] for k in range(4))

    def tail(number):
        return tuple(columns[pl.ds(start + wy - 1, 1), number + k : number + k + 1] for k in range(4))

    past_up, past_down = mm(head(12), head(20)), mm(tail(16), tail(24))
    for column in range(2):
        for output, number in ((column, 20), (2 + column, 24)):
            even = columns[pl.ds(start, wy), number + column : number + column + 1]
            odd = columns[pl.ds(start, wy), number + 2 + column : number + 3 + column]
            weights_y[output, 0:wy, :] = jnp.where((row & 1) == 0, even, odd)
        for output, early, late in (
            (column, (past_up[column], past_up[2 + column]), (unit[column], unit[2 + column])),
            (2 + column, (unit[column], unit[2 + column]), (past_down[column], past_down[2 + column])),
        ):
            value = jnp.zeros((EXTRA, LANES), jnp.float32)
            for r, v in enumerate(early + late):
                value = jnp.where(extra_row == r, v, value)
            weights_y[output, wy : wy + EXTRA, :] = value

    total = planes * (wy + EXTRA)

    def solve(begin, size):
        rows = slice(begin, begin + size)
        both = matmul(high[rows, :], matrix[...])
        value = both[:, 0:LANES] + (both[:, LANES : 2 * LANES] + matmul(low[rows, :], matrix[:, 0:LANES]))
        local[rows, :] = value
        return value

    extra = solve(planes * wy, planes * EXTRA)
    for part in range(planes // 8):
        core = solve(part * 8 * wy, 8 * wy)
        for number in range(4):
            lines = []
            for k in range(8):
                index = part * 8 + k
                value = jnp.sum(core[k * wy : (k + 1) * wy] * weights_y[number, 0:wy, :], axis=0, keepdims=True)
                past = extra[index * EXTRA : (index + 1) * EXTRA] * weights_y[number, wy : wy + EXTRA, :]
                lines.append(value + jnp.sum(past, axis=0, keepdims=True))
            start = number * planes + part * 8
            moments[start : start + 8, :] = jnp.concatenate(lines, axis=0)


def y_kernel(count_y, wy, factors, unused, inverse_y, coefs, columns, stacked):
    me_y = lax.axis_index("gy")
    cell = me_y * wy
    columns[0:LANES, 0:32] = transposed(factors, cell // LANES)
    start = lax.rem(cell, LANES)
    inverse_y[...] = dense_inverse(columns, start, wy, stacked)

    up, down = ([], [], []), ([], [], [])
    plan = stage_plan(count_y)
    for number, (stride, radix) in enumerate(plan):
        group = me_y // stride
        first = (group // radix) * radix
        others = [first + jnp.bitwise_xor(group - first, k) for k in range(radix)]
        for other in others[1:]:
            for lists, values in (
                (up, ((other + 1) * stride, me_y, truth(other < group))),
                (down, (me_y + 1, other * stride, truth(other > group))),
            ):
                for one, value in zip(lists, values):
                    one.append(value)
        if number + 1 < len(plan):
            for other in others:
                for lists, values in (
                    (up, ((other + 1) * stride, (first + radix) * stride, 1.0)),
                    (down, (first * stride, other * stride, 1.0)),
                ):
                    for one, value in zip(lists, values):
                        one.append(value)

    def place(block):
        return block * wy // LANES, block * wy % LANES

    def place_end(block):
        return place(block)[0], place(block)[1] + wy - 1

    for base, value in (
        (0, chain_products(factors, 12, place, count_y, *up, False)),
        (4, chain_products(factors, 16, place_end, count_y, *down, True)),
    ):
        for k in range(4):
            coefs[base + k] = value[k]


def arrived_rows(messages, count):
    rows = [m[0:2] for m in messages]
    if count > 2 * len(messages):
        rows.append(jnp.zeros((count - 2 * len(messages), rows[0].shape[1]), jnp.float32))
    return jnp.concatenate(rows, axis=0)


def third_kernel(planes, wy, chosen, moments, spread_core, spread_extra, entering, *refs):
    messages, (carried, held, result) = refs[:-3][::-1], refs[-3:]
    count = -(-2 * len(messages) // 8) * 8
    total = entering.shape[0] // 3
    received = arrived_rows(messages, count)
    first = received.astype(jnp.bfloat16).astype(jnp.float32)
    both = jnp.concatenate([first, received - first], axis=0)
    values = entering[0:total, :] + entering[total : 2 * total, :]
    values = [values[2 * (k - 1) + p : 2 * k - 1 + p] for k in chosen for p in range(2)]
    across = (((1,), (1,)), ((), ()))
    used = 2 * len(messages)

    def chunks(begin, end):
        parts = [both[:, at : min(at + LANES, end)] for at in range(begin, end, LANES)]
        if parts[-1].shape[1] < LANES:
            missing = jnp.zeros((2 * count, LANES - parts[-1].shape[1]), jnp.float32)
            parts[-1] = jnp.concatenate([parts[-1], missing], axis=1)
        return jnp.concatenate(parts, axis=0).astype(jnp.bfloat16), len(parts)

    per = LANES // wy
    stack, number = chunks(0, planes * wy)
    top, rest = halves(spread_core[...])
    held[0 : number * 2 * count, 0 : 4 * per] = matmul(stack, top, across) + matmul(stack, rest, across)
    columns = [
        held[pl.ds(r, number, stride=2 * count), :] + held[pl.ds(count + r, number, stride=2 * count), :]
        for r in range(used)
    ]
    for m in range(4):
        for p in range(per):
            lane = m * per + p
            value = moments[pl.ds(m * planes + p, number, stride=per), :]
            for r in range(used):
                value = value + columns[r][:, lane : lane + 1] * values[r]
            result[pl.ds(m * planes + p, number, stride=per), :] = value

    per = LANES // EXTRA
    stack, number = chunks(planes * wy, planes * (wy + EXTRA))
    top, rest = halves(spread_extra[...])
    corner = matmul(top, stack, across) + matmul(rest, stack, across)
    spare = jnp.zeros((corner.shape[0], -corner.shape[1] % LANES), jnp.float32)
    corner = jnp.concatenate([corner, spare], axis=1)
    corner = corner + pltpu.roll(corner, corner.shape[1] - count, 1)
    for m in range(4):
        for chunk in range(number):
            size = min(per, planes - chunk * per)
            rows = slice(chunk * per, chunk * per + size)
            value = result[m * planes + chunk * per : m * planes + chunk * per + size, :]
            for r in range(used):
                lane = chunk * 2 * count + r
                part = corner[m * per : m * per + size]
                value = value + part[:, lane : lane + 1] * values[r]
            if len(carried.shape) == 3:
                carried[m, rows, :] = value
            else:
                carried[m * planes + rows.start : m * planes + rows.stop, :] = value


def local_y_kernel(wy, local, entering, inverse_y, unused, *refs):
    messages, (out, solved) = refs[:-2], refs[-2:]
    planes = out.shape[0]
    count = entering.shape[0] // 3
    received = arrived_rows(messages, count)
    first = received.astype(jnp.bfloat16).astype(jnp.float32)
    received = jnp.concatenate([first, first, received - first], axis=0).T.astype(jnp.bfloat16)
    solved[...] = local[...] + matmul(received, entering[...].astype(jnp.bfloat16))
    first, second = halves(inverse_y[:, 0 : wy + EXTRA])
    left = jnp.concatenate([first, second, first], axis=1)

    def part(index, carry):
        for k in range(8):
            number = index * 8 + k
            start = pl.multiple_of(number * wy, 8)
            core = solved[pl.ds(start, wy), :]
            start = pl.multiple_of(planes * wy + number * EXTRA, 8)
            both = jnp.concatenate([core, solved[pl.ds(start, EXTRA), :]], axis=0)
            top, rest = halves(both)
            out[number] = matmul(left, jnp.concatenate([top, top, rest], axis=0))
        return carry

    lax.fori_loop(0, planes // 8, part, 0)


def combine(coefs, side, row, values):
    first = 0 if side == 0 else 2
    out = [None, None]
    for k, value in enumerate(values):
        for q in range(2):
            for p in range(2):
                term = coefs[side + 2 * p + q, row + k : row + k + 1, :] * value[first + p]
                out[q] = term if out[q] is None else out[q] + term
    return out


def stage_kernel(base, stride, radix, narrow, has_entered, coefs, *refs):
    values = refs[:radix]
    position = radix
    entered = None
    if has_entered:
        entered = refs[position]
        position += 1
    message, entering = refs[position : position + 2]
    below = combine(coefs, 0, base, values[1:])
    above = combine(coefs, 4, base, values[1:])
    for row, value in enumerate(below + above):
        entering[row] = value if entered is None else value + entered[row]
    upward = combine(coefs, 0, base + radix - 1, values)
    downward = combine(coefs, 4, base + radix - 1, values)
    if narrow:
        group = lax.axis_index("gy") // (stride * radix)
        sends_up = lax.rem(group, 2) == 0
        for row in range(2):
            message[row] = jnp.where(sends_up, upward[row], downward[row])
    else:
        for row, value in enumerate(upward + downward):
            message[row] = value


def last_kernel(base, radix, narrow, wy, coefs, local, inverse_y, entered, *refs):
    messages, (out_hbm, out, sent) = refs[: radix - 1], refs[radix - 1 :]
    values = list(messages)
    if narrow:
        values = [(m[0], m[1], m[0], m[1]) for m in values]
    below = combine(coefs, 0, base, values)
    above = combine(coefs, 4, base, values)
    st = [value + entered[row] for row, value in enumerate(below + above)]
    sides = [
        jnp.broadcast_to(inverse_y[:, c : c + 1], (wy, LANES)) for c in (0, 1, wy - 2, wy - 1)
    ]
    fields, planes_x = out.shape[:2]
    copies = []
    for field in range(fields):
        for x in range(planes_x):
            index = field * planes_x + x
            value = local[index]
            for number in range(4):
                value = value + sides[number] * st[number][index : index + 1]
            out[field, x] = value
            if (x + 1) % 4 == 0:
                part = (field, pl.ds(x - 3, 4))
                copy = pltpu.make_async_copy(out.at[part], out_hbm.at[part], sent.at[len(copies)])
                copy.start()
                copies.append(copy)
    for copy in copies:
        copy.wait()


VMEM = pl.BlockSpec(memory_space=pltpu.VMEM)
HBM = pl.BlockSpec(memory_space=pltpu.HBM)
PARAMS = pltpu.CompilerParams(vmem_limit_bytes=40 * 1024 * 1024)


def array(*shape):
    return jax.ShapeDtypeStruct(shape, jnp.float32)


def in_hbm(x):
    return pltpu.with_memory_space_constraint(x, pltpu.HBM)


def cost(flops, data):
    return pl.CostEstimate(flops=flops, bytes_accessed=data, transcendentals=0)


def on_device(mesh, flow, speed, metric_y, metric_z):
    fields, planes_x, wy, wz = flow.shape
    count_y, count_z = mesh.shape["gy"], mesh.shape["gz"]
    assert wz == LANES
    ny, nz = metric_y.shape[0] // LANES, metric_z.shape[0] // LANES
    planes = fields * planes_x
    rows = planes * (wy + EXTRA)
    partners = count_z - 1
    arrivals = partners
    entering_rows = -(-2 * arrivals // 8) * 8
    half = jax.ShapeDtypeStruct((rows, 2 * LANES), jnp.bfloat16)
    outputs = pl.pallas_call(
        functools.partial(first_kernel, ny, nz, partners),
        out_shape=[half, half, array(28, ny + nz, LANES)]
        + [array(2, rows)] * partners,
        in_specs=[HBM] * 4,
        out_specs=[VMEM] * (3 + partners),
        scratch_shapes=[
            pltpu.VMEM(flow.shape, jnp.float32),
            pltpu.VMEM(speed.shape, jnp.float32),
            pltpu.VMEM((ny + nz, LANES), jnp.float32),
            pltpu.VMEM((planes_x, 3, wy + 16, LANES), jnp.float32),
            pltpu.SemaphoreType.DMA((fields + 3,)),
        ],
        compiler_params=PARAMS,
        name="forcing_and_factor",
    )(*(in_hbm(x) for x in (flow, speed, metric_y.reshape(ny, LANES), metric_z.reshape(nz, LANES))))
    high, low, factors = outputs[:3]

    def exchange(values, axis, count, stride, radix):
        received = {}
        for k in reversed(range(1, radix)):
            pairs = [(i, i ^ (k * stride)) for i in range(count)]
            received[k] = lax.ppermute(values[k - 1], axis, pairs)
        return [received[k] for k in range(1, radix)]

    plan = stage_plan(count_y)
    work = [pltpu.VMEM((LANES + 16, LANES), jnp.float32)] * 2
    received = exchange(outputs[3:], "gz", count_z, 1, count_z)
    local, moments, entering, spread_core, spread_extra = pl.pallas_call(
        functools.partial(second_kernel, ny, nz, count_z, wy, partners),
        out_shape=[
            array(rows, LANES),
            array(4 * planes + 8, LANES),
            array(3 * entering_rows, LANES),
            array(4 * (LANES // wy), LANES),
            array(4 * (LANES // EXTRA), LANES),
        ],
        in_specs=[VMEM] * 3,
        out_specs=[VMEM] * 5,
        scratch_shapes=work
        + [
            pltpu.VMEM((2 * LANES, LANES), jnp.float32),
            pltpu.VMEM((2 * LANES, 2 * LANES), jnp.bfloat16),
            pltpu.VMEM((4, wy + EXTRA, LANES), jnp.float32),
        ],
        compiler_params=PARAMS,
        cost_estimate=cost(2 * rows * 256 * 128 * 6, 4 * rows * 384),
        name="local_z",
    )(factors, high, low)
    early = [k for k in range(1, partners + 1) if k > 2]
    late = [k for k in range(1, partners + 1) if k <= 2]
    carried = moments
    for chosen, shape in ((early, (4 * planes + 8, LANES)), (late, (4, planes, LANES))):
        room = 2 * (-(-2 * len(chosen) // 8) * 8)
        carried = pl.pallas_call(
            functools.partial(third_kernel, planes, wy, chosen),
            out_shape=array(*shape),
            in_specs=[VMEM] * (4 + len(chosen)),
            out_specs=VMEM,
            scratch_shapes=[
                pltpu.VMEM((planes * wy // LANES * room + room, LANES), jnp.float32),
                pltpu.VMEM((4 * planes + 8, LANES), jnp.float32),
            ],
            compiler_params=PARAMS,
            name="carried_y",
        )(carried, spread_core, spread_extra, entering, *[received[k - 1] for k in chosen[::-1]])
    arrived = received

    narrow = plan[-1][1] == 2 and len(plan) > 1
    base, entered, result = 0, None, None
    for number, (stride, radix) in enumerate(plan):
        received = exchange([carried] * (radix - 1), "gy", count_y, stride, radix)
        if number == 0:
            entries = sum(2 * radix - 1 for _, radix in plan[:-1]) + plan[-1][1] - 1
            inverse_y, coefs = pl.pallas_call(
                functools.partial(y_kernel, count_y, wy),
                out_shape=[array(wy, LANES), array(8, -(-entries // 8) * 8, LANES)],
                in_specs=[VMEM, HBM],
                out_specs=[VMEM] * 2,
                scratch_shapes=work,
                compiler_params=PARAMS,
                cost_estimate=cost(2 * rows * 128 * 128 * 6, 4 * rows * 256),
                name="inverse_y",
            )(factors, carried)
        if number + 1 < len(plan):
            slim = narrow and number + 2 == len(plan)
            inputs = [carried] + received + ([entered] if entered is not None else [])
            carried, entered = pl.pallas_call(
                functools.partial(stage_kernel, base, stride, radix, slim, entered is not None),
                out_shape=[array(2 if slim else 4, planes, LANES), array(4, planes, LANES)],
                in_specs=[VMEM] * (1 + len(inputs)),
                out_specs=[VMEM] * 2,
                compiler_params=PARAMS,
                name="join_groups",
            )(coefs, *inputs)
            base += 2 * radix - 1
            if number == 0:
                result = pl.pallas_call(
                    functools.partial(local_y_kernel, wy),
                    out_shape=array(planes, wy, LANES),
                    in_specs=[VMEM] * 3 + [HBM] + [VMEM] * arrivals,
                    out_specs=VMEM,
                    scratch_shapes=[pltpu.VMEM((rows, LANES), jnp.float32)],
                    compiler_params=PARAMS,
                    cost_estimate=cost(2 * rows * 128 * 128 * 6, 4 * rows * 256),
                    name="local_y",
                )(local, entering, inverse_y, entered, *arrived)
        else:
            return pl.pallas_call(
                functools.partial(last_kernel, base, radix, narrow, wy),
                out_shape=array(fields, planes_x, wy, wz),
                in_specs=[VMEM] * (4 + len(received)),
                out_specs=HBM,
                scratch_shapes=[
                    pltpu.VMEM(flow.shape, jnp.float32),
                    pltpu.SemaphoreType.DMA((planes // 4,)),
                ],
                compiler_params=PARAMS,
                name="finish_y",
            )(coefs, result, inverse_y, entered, *received)


def solution(mesh):
    placed = (P(None, None, "gy", "gz"), P(None, "gy", "gz"), P(), P())
    return jax.shard_map(
        functools.partial(on_device, mesh),
        mesh=mesh,
        in_specs=placed,
        out_specs=P(None, None, "gy", "gz"),
        check_vma=False,
    )
```

```python
import functools

import jax
import jax.numpy as jnp
from jax import lax
from jax.experimental import pallas as pl
from jax.experimental.pallas import tpu as pltpu
from jax.sharding import PartitionSpec as P

viscous = 0.25
explicit_fourth = 0.04
implicit_fourth = 0.05
time_step = 1048576.0
LANES = 128
EXTRA = 8


def mm(a, b):
    return (
        a[0] * b[0] + a[1] * b[2],
        a[0] * b[1] + a[1] * b[3],
        a[2] * b[0] + a[3] * b[2],
        a[2] * b[1] + a[3] * b[3],
    )


def inverse_of_one_minus(a):
    p, q, r, s = 1.0 - a[0], -a[1], -a[2], 1.0 - a[3]
    d = 1.0 / (p * s - q * r)
    return (s * d, -q * d, -r * d, p * d)


def pick(condition, a, b):
    return tuple(jnp.where(condition, x, y) for x, y in zip(a, b))


def halves(x):
    high = x.astype(jnp.bfloat16)
    return high, (x - high.astype(jnp.float32)).astype(jnp.bfloat16)


def matmul(a, b, dims=(((1,), (0,)), ((), ()))):
    return lax.dot_general(a, b, dims, preferred_element_type=jnp.float32)


def scan(m, ahead, count, step, shift, product):
    unit = (1.0, 0.0, 0.0, 1.0)

    def moved(by):
        return tuple(jnp.where(ahead >= by, shift(x, by), u) for x, u in zip(m, unit))

    while step < count:
        if 2 * step < count:
            m = product(product(m, moved(step)), product(moved(2 * step), moved(3 * step)))
            step *= 4
        else:
            m = product(m, moved(step))
            step *= 2
    return m


def lane_roll(x, by):
    return pltpu.roll(x, by % LANES, 1)


def row_roll(x, by):
    by = by % x.shape[0]
    return jnp.concatenate([x[x.shape[0] - by :], x[: x.shape[0] - by]], axis=0)


class Factor:
    def __init__(self, metric, ny, nz, wy):
        self.ny, self.nz, self.wy, self.rows = ny, nz, wy, ny + nz
        self.lane = lax.broadcasted_iota(jnp.int32, (self.rows, LANES), 1)
        self.row = lax.broadcasted_iota(jnp.int32, (self.rows, LANES), 0)
        self.block = jnp.where(self.row < ny, self.row, self.row - ny)
        self.to_end = jnp.where(self.row < ny, ny, nz) - 1 - self.block
        first = (self.lane == 0) & (self.block == 0)
        last = (self.lane == LANES - 1) & (self.to_end == 0)
        self.face_low = 0.5 * (jnp.where(first, metric, self.before(metric, 1)) + metric)
        self.face_high = 0.5 * (metric + jnp.where(last, metric, self.after(metric, 1)))

    def before(self, x, by):
        rolled = lane_roll(x, by)
        value = jnp.where(self.lane < by, row_roll(rolled, 1), rolled)
        return jnp.where((self.lane < by) & (self.block == 0), 0.0, value)

    def after(self, x, by):
        rolled = lane_roll(x, -by)
        value = jnp.where(self.lane >= LANES - by, row_roll(rolled, -1), rolled)
        return jnp.where((self.lane >= LANES - by) & (self.to_end == 0), 0.0, value)

    def guess(self, sign):
        face = self.face_high if sign > 0 else self.face_low
        if sign > 0:
            cell = self.lane + LANES * self.block
        else:
            cell = LANES - 1 - self.lane + LANES * self.to_end
        near = face / (cell + 1).astype(jnp.float32)
        one_over = 1.0 / (face + jnp.sqrt(face + near * near))
        return face * one_over, implicit_fourth * one_over, one_over

    def sweep(self, sign, ratio, far):
        rows = self.rows
        back = self.before if sign > 0 else self.after
        if sign > 0:
            face_in, face_out, place = self.face_low, self.face_high, self.block
        else:
            face_in, face_out, place = self.face_high, self.face_low, self.to_end
        eps = 4.0 * implicit_fourth - implicit_fourth * back(ratio, 1)
        mass = (1.0 + 6.0 * implicit_fourth) - implicit_fourth * back(far, 2) - 2.0 * eps
        eps_in = back(eps, 1)
        scale = 1.0 / (face_in + 2.0 * eps_in)
        m = ((mass + face_in) * scale, mass - eps_in * eps_in * scale, scale, jnp.ones_like(scale))
        ahead = self.lane if sign > 0 else LANES - 1 - self.lane
        m = scan(m, ahead, LANES, 1, lambda x, by: lane_roll(x, sign * by), mm)
        edge = LANES - 1 if sign > 0 else 0
        total = tuple(jnp.broadcast_to(x[:, edge : edge + 1], (rows, LANES)) for x in m)
        total = scan(
            total, place, max(self.ny, self.nz), 1, lambda x, by: row_roll(x, sign * by), mm
        )
        top = jnp.where(place >= 1, row_roll(total[0], sign), 1.0)
        low = jnp.where(place >= 1, row_roll(total[2], sign), 0.0)
        eta = (m[0] * top + m[1] * low) / (m[2] * top + m[3] * low)
        one_over = 1.0 / (face_out + (eta + 2.0 * eps))
        return (face_out + eps) * one_over, implicit_fourth * one_over, one_over

    def finish(self, near_l, far_l, pivot_l, near_r, far_r):
        lane, block, to_end = self.lane, self.block, self.to_end
        even = (lane & 1) == 0
        near_l = jnp.where((to_end == 0) & (lane >= LANES - 1), 0.0, near_l)
        far_l = jnp.where((to_end == 0) & (lane >= LANES - 2), 0.0, far_l)
        near_r = jnp.where((block == 0) & (lane < 1), 0.0, near_r)
        far_r = jnp.where((block == 0) & (lane < 2), 0.0, far_r)

        def of_even(x):
            return jnp.where(even, x, lane_roll(x, 1))

        def of_odd(x):
            return jnp.where(even, lane_roll(x, -1), x)

        t0, t1, r0, r1 = of_even(near_l), of_odd(near_l), of_even(far_l), of_odd(far_l)
        from_right = (t0 * t1 - r0, -t0 * r1, t1, -r1)
        p1 = of_odd(pivot_l)
        left_inverse = (of_even(pivot_l) + t0 * t0 * p1, t0 * p1, t0 * p1, p1)
        s0, s1, q0, q1 = of_even(near_r), of_odd(near_r), of_even(far_r), of_odd(far_r)
        from_left = (-q0, s0, -s1 * q0, s1 * s0 - q1)
        from_left_after = tuple(self.after(x, 2) for x in from_left)
        from_right_before = tuple(self.before(x, 2) for x in from_right)
        diagonal = mm(inverse_of_one_minus(mm(from_right, from_left_after)), left_inverse)
        width = jnp.where(self.row < self.ny, self.wy, LANES)
        place = lane & (width - 1)
        right = scan(from_right, width - 1 - place, LANES, 2, lambda x, by: lane_roll(x, -by), mm)
        left = scan(from_left, place, LANES, 2, lane_roll, mm)
        return from_right, from_left, diagonal, right, left, from_right_before, from_left_after


def cell_weights(chain, column, even):
    return jnp.where(even, chain[column], chain[2 + column])


def first_kernel(ny, nz, partners, flow_hbm, speed_hbm, metric_y, metric_z, *refs):
    high, low, factors = refs[:3]
    messages = refs[3 : 3 + partners]
    flow, speed, metric, spread, arrived = refs[3 + partners :]
    fields, planes_x, wy, _ = flow.shape
    rows = ny + nz
    core_rows = fields * planes_x * wy

    copies = [
        pltpu.make_async_copy(metric_y, metric.at[0:ny], arrived.at[fields]),
        pltpu.make_async_copy(metric_z, metric.at[ny:rows], arrived.at[fields + 1]),
        pltpu.make_async_copy(speed_hbm, speed, arrived.at[fields + 2]),
    ]
    for copy in copies:
        copy.start()
    for field in range(fields):
        pltpu.make_async_copy(flow_hbm.at[field], flow.at[field], arrived.at[field]).start()

    lane = lax.broadcasted_iota(jnp.int32, (wy, LANES), 1)
    extra_row = lax.broadcasted_iota(jnp.int32, (EXTRA, LANES), 0)
    for slot in range(planes_x):
        for part in range(3):
            spread[slot, part, 0:8, :] = jnp.zeros((8, LANES), jnp.float32)
            spread[slot, part, wy + 8 : wy + 16, :] = jnp.zeros((8, LANES), jnp.float32)
    side = time_step * (viscous + 4.0 * explicit_fourth)
    half = time_step * 0.5
    centre = time_step * (-6.0 * viscous - 12.0 * explicit_fourth)
    fourth = -time_step * explicit_fourth

    def store(start, column, value):
        first, second = halves(value)
        high[pl.ds(start, value.shape[0]), column : column + LANES] = first
        low[pl.ds(start, value.shape[0]), column : column + LANES] = second

    def one_field(field):
        values = [flow[field, x] for x in range(planes_x)]
        fluxes = [values[x] * speed[x] for x in range(planes_x)]
        aside = [(time_step * viscous) * u for u in values]
        extras = []
        for x in range(planes_x):
            u, flux, slot = values[x], fluxes[x], x
            total = centre * u
            if x + 1 < planes_x:
                total = total + (aside[x + 1] - fluxes[x + 1])
            if x > 0:
                total = total + (aside[x - 1] + fluxes[x - 1])
            scaled = side * u
            onward, backward, far = scaled + flux, scaled - flux, fourth * u
            spread[slot, 0, 8 : wy + 8, :] = onward
            spread[slot, 1, 8 : wy + 8, :] = backward
            spread[slot, 2, 8 : wy + 8, :] = far
            total = total + (spread[slot, 0, 7 : wy + 7, :] + spread[slot, 1, 9 : wy + 9, :])
            total = total + (spread[slot, 2, 6 : wy + 6, :] + spread[slot, 2, 10 : wy + 10, :])
            a, b = lane_roll(onward, 1), lane_roll(backward, -1)
            c, d = lane_roll(far, 2), lane_roll(far, -2)
            from_low, from_high = a + c, b + d
            ends = jnp.where(lane == 0, from_low, jnp.where(lane == 1, c, 0.0))
            ends = jnp.where(lane == LANES - 1, from_high, jnp.where(lane == LANES - 2, d, ends))
            index = field * planes_x + x
            start = index * wy
            store(start, 0, total + (from_low + from_high))
            store(start, LANES, ends)
            above = spread[slot, 1, 7:15, :] + spread[slot, 2, 8:16, :]
            below = spread[slot, 0, wy + 5 : wy + 13, :] + spread[slot, 2, wy + 4 : wy + 12, :]
            extras.append(jnp.where(extra_row < 2, above, jnp.where(extra_row < 4, below, 0.0)))
            if len(extras) == 2:
                start = core_rows + (index - 1) * EXTRA
                store(start, 0, jnp.concatenate(extras, axis=0))
                for ref in (high, low):
                    ref[pl.ds(start, 2 * EXTRA), LANES : 2 * LANES] = jnp.zeros(
                        (2 * EXTRA, LANES), jnp.bfloat16
                    )
                extras = []

    copies[0].wait()
    copies[1].wait()
    factor = Factor(metric[...], ny, nz, wy)

    guess_l, guess_r = factor.guess(1), factor.guess(-1)
    left, right = factor.sweep(1, *guess_l[:2]), factor.sweep(-1, *guess_r[:2])
    copies[2].wait()
    for x in range(planes_x):
        speed[x] = half * speed[x]
    for field in range(fields):
        pltpu.make_async_copy(flow_hbm.at[field], flow.at[field], arrived.at[field]).wait()
    left, right = factor.sweep(1, *left[:2]), factor.sweep(-1, *right[:2])
    for field in range(fields // 2):
        one_field(field)
    parts = factor.finish(*left, *right[:2])
    from_right, from_left, diagonal, to_right, to_left, before, after = parts
    for number, value in enumerate(v for part in parts for v in part):
        factors[number] = value
    for field in range(fields // 2, fields):
        one_field(field)

    me = lax.axis_index("gz")
    mine = lax.broadcasted_iota(jnp.int32, (rows, LANES), 0) == ny + me
    even = (lax.broadcasted_iota(jnp.int32, (1, LANES), 1) & 1) == 0
    lane = lax.broadcasted_iota(jnp.int32, (1, LANES), 1)

    def own(values):
        return tuple(jnp.sum(jnp.where(mine, v, 0.0), axis=0, keepdims=True) for v in values)

    up, down = own(to_right), own(to_left)
    up_past, down_past = own(mm(before, to_right)), own(mm(after, to_left))
    unit = (1.0, 0.0, 0.0, 1.0)
    weights = []
    for column in range(2):
        same = jnp.where(even, unit[column], unit[2 + column])
        inside_up = cell_weights(up, column, even)
        inside_down = cell_weights(down, column, even)
        past_up = lane_roll(cell_weights(up_past, column, even), -2)
        past_down = lane_roll(cell_weights(down_past, column, even), 2)
        ends_up = jnp.where(lane < 2, same, past_up) - inside_up
        ends_down = jnp.where(lane < 2, past_down, same) - inside_down
        at_end = (lane < 2) | (lane >= LANES - 2)
        ends_up, ends_down = jnp.where(at_end, ends_up, 0.0), jnp.where(at_end, ends_down, 0.0)
        weights.append(
            (
                jnp.concatenate([inside_up, ends_up], axis=1),
                jnp.concatenate([inside_down, ends_down], axis=1),
            )
        )
    stack = []
    for k in range(1, partners + 1):
        upward = jnp.bitwise_xor(me, k) > me
        stack += [jnp.where(upward, w[0], w[1]) for w in weights]
    while len(stack) % 8:
        stack.append(jnp.zeros((1, 2 * LANES), jnp.float32))
    count = len(stack)
    stack = jnp.concatenate(stack, axis=0)
    first = stack.astype(jnp.bfloat16).astype(jnp.float32)
    both = jnp.concatenate([first, stack - first], axis=0).astype(jnp.bfloat16)
    across = (((1,), (1,)), ((), ()))
    total = high.shape[0]
    size = planes_x * wy
    for begin in range(0, total, size):
        rows = slice(begin, min(begin + size, total))
        on_high = matmul(both, high[rows, :], across)
        on_low = matmul(both, low[rows, :], across)
        moments = (on_high[:count] + on_high[count:]) + on_low[:count]
        for k in range(partners):
            messages[k][:, rows] = moments[2 * k : 2 * k + 2]


def dense_inverse(columns, start, width, stack):
    parts = 8
    steps = width // (2 * parts)
    lane = lax.broadcasted_iota(jnp.int32, (parts, LANES), 1)
    part = lax.broadcasted_iota(jnp.int32, (parts, LANES), 0)
    fits = width + 4 <= LANES
    values = [columns[pl.ds(start + 2 * i, parts, stride=2 * steps), :] for i in range(steps)]

    def wide(i, number):
        return tuple(
            jnp.broadcast_to(values[i][:, number + k : number + k + 1], (parts, LANES)) for k in range(4)
        )

    blocks = [wide(i, 8) for i in range(steps)]
    zero, one = jnp.zeros((parts, LANES), jnp.float32), jnp.ones((parts, LANES), jnp.float32)

    def put(rows, i, extra, extra_lane, owner):
        first = 2 * (part * steps + i)
        out = []
        for r in range(2):
            row = jnp.where(lane == first, blocks[i][2 * r], rows[r])
            row = jnp.where(lane == first + 1, blocks[i][2 * r + 1], row)
            if extra is not None and fits:
                row = jnp.where((part == owner) & (lane == extra_lane), extra[2 * r], row)
                row = jnp.where((part == owner) & (lane == extra_lane + 1), extra[2 * r + 1], row)
            out.append(row)
        return tuple(out)

    def run(order, number, ends, extra_lane, owner):
        rows, product, out = (zero, zero), (one, zero, zero, one), {}
        for i in order:
            t = wide(i, number)
            rows = (t[0] * rows[0] + t[1] * rows[1], t[2] * rows[0] + t[3] * rows[1])
            extra = None
            if i == order[0]:
                e = wide(i, ends)
                extra = mm(blocks[i], (e[0], e[2], e[1], e[3]))
            rows = put(rows, i, extra, extra_lane, owner)
            product = mm(t, product)
            out[i] = rows, product
        rows, product = out[order[-1]]
        entering, last = [None] * parts, (jnp.zeros((1, LANES), jnp.float32),) * 2
        sequence = range(parts) if number == 4 else range(parts - 1, -1, -1)
        for p in sequence:
            entering[p] = last
            own, across = [r[p : p + 1] for r in rows], [x[p : p + 1] for x in product]
            last = (
                own[0] + across[0] * last[0] + across[1] * last[1],
                own[1] + across[2] * last[0] + across[3] * last[1],
            )
        entering = [jnp.concatenate([e[r] for e in entering], axis=0) for r in range(2)]
        result = []
        for i in range(steps):
            rows, product = out[i]
            for r in range(2):
                result.append(rows[r] + product[2 * r] * entering[0] + product[2 * r + 1] * entering[1])
        return result

    low = run(list(range(steps)), 4, 12, width, 0)
    high = run(list(range(steps - 1, -1, -1)), 0, 16, width + 2, parts - 1)
    for k in range(2 * steps):
        lower = lane <= 2 * (part * steps + k // 2) + 1
        if fits:
            lower = lower & (lane < width) | ((lane >= width) & (lane < width + 2))
        stack[parts * k : parts * (k + 1), :] = jnp.where(lower, low[k], high[k])
    rows = [stack[pl.ds(p, 2 * steps, stride=parts), :] for p in range(parts)]
    return jnp.concatenate(rows, axis=0)


def stage_plan(count):
    plan, stride = [], 1
    while stride < count:
        radix = 4 if count // stride >= 4 else 2
        plan.append((stride, radix))
        stride *= radix
    return plan


def transposed(factors, row):
    rows = [factors[number, pl.ds(row, 1), :] for number in range(12)]
    rows += [factors[20 + number, pl.ds(row, 1), :] for number in range(8)]
    rows += [factors[12 + number, pl.ds(row, 1), :] for number in range(8)]
    rows.append(jnp.zeros((4, LANES), jnp.float32))
    return jnp.concatenate(rows, axis=0).T


def chain_products(factors, number, place, blocks, begins, ends, masks, reverse):
    count = -(-len(begins) // 8) * 8
    row = lax.broadcasted_iota(jnp.int32, (count, LANES), 0)
    begin = jnp.zeros((count, LANES), jnp.int32)
    end, mask = begin, jnp.zeros((count, LANES), jnp.float32)
    for r, (b, e, m) in enumerate(zip(begins, ends, masks)):
        begin, end = jnp.where(row == r, b, begin), jnp.where(row == r, e, end)
        mask = jnp.where(row == r, m, mask)
    one, zero = jnp.ones((count, LANES), jnp.float32), jnp.zeros((count, LANES), jnp.float32)
    product = (one, zero, zero, one)
    for block in range(blocks - 1, -1, -1) if reverse else range(blocks):
        where = place(block)
        at = (slice(where[0], where[0] + 1), slice(where[1], where[1] + 1))
        value = tuple(factors[(number + k, *at)] for k in range(4))
        product = pick((begin <= block) & (block < end), mm(product, value), product)
    return tuple(x * mask for x in product)


def truth(condition):
    return jnp.where(condition, 1.0, 0.0)


def second_kernel(
    ny, nz, count_z, wy, partners, factors, high, low, local, moments, entering, spread_core, spread_extra, *scratch
):
    columns, stacked, rows_ref, matrix, weights_y = scratch
    planes = (moments.shape[0] - 8) // 4
    me_z, me_y = lax.axis_index("gz"), lax.axis_index("gy")
    columns[0:LANES, 0:32] = transposed(factors, ny + me_z)
    inverse = dense_inverse(columns, 0, LANES, stacked)
    rows_ref[0:LANES, :] = inverse
    rows_ref[LANES : 2 * LANES, :] = jnp.zeros((LANES, LANES), jnp.float32)
    past = tuple(columns[LANES - 1 : LANES, 16 + k : 17 + k] for k in range(4))
    ahead = tuple(columns[0:1, 12 + k : 13 + k] for k in range(4))
    head0, head1 = rows_ref[0:1, :], rows_ref[1:2, :]
    tail0, tail1 = rows_ref[LANES - 2 : LANES - 1, :], rows_ref[LANES - 1 : LANES, :]
    for q in range(2):
        beyond = past[2 * q] * tail0 + past[2 * q + 1] * tail1
        rows_ref[LANES + q : LANES + q + 1, :] = beyond - (head0, head1)[q]
        beyond = ahead[2 * q] * head0 + ahead[2 * q + 1] * head1
        rows_ref[2 * LANES - 2 + q : 2 * LANES - 1 + q, :] = beyond - (tail0, tail1)[q]
    first, second = halves(rows_ref[...])
    matrix[:, 0:LANES] = first
    matrix[:, LANES : 2 * LANES] = second

    cell = me_y * wy
    start = lax.rem(cell, LANES)
    row = cell // LANES
    unit = (1.0, 0.0, 0.0, 1.0)
    lane = lax.broadcasted_iota(jnp.int32, (1, LANES), 1)
    even = (lane & 1) == 0

    def chain(number):
        return tuple(factors[number + k, pl.ds(row, 1), :] for k in range(4))

    def turned(x, by):
        return pltpu.roll(x, lax.rem(by + 2 * LANES, LANES), 1)

    def tiled(x, period):
        x = jnp.where(lane < period, x, 0.0)
        while period < LANES:
            x = x + lane_roll(x, period)
            period *= 2
        return x

    up, down, before, after = chain(12), chain(16), chain(20), chain(24)
    past_up, past_down = mm(before, up), mm(after, down)
    core_rows, extra_rows = [], []
    for column in range(2):
        same = jnp.where(even, unit[column], unit[2 + column])
        early = turned(cell_weights(past_up, column, even), -start)
        late = turned(cell_weights(past_down, column, even), 4 - wy - start)
        for inside, first, second in ((up, early, same), (down, same, late)):
            core_rows.append(tiled(turned(cell_weights(inside, column, even), -start), wy))
            past = jnp.where(lane < 2, first, jnp.where(lane < 4, second, 0.0))
            extra_rows.append(tiled(past, EXTRA))
    for number, source in enumerate((0, 2, 1, 3)):
        for rows, out, width in ((core_rows, spread_core, wy), (extra_rows, spread_extra, EXTRA)):
            per = LANES // width
            owner = lax.broadcasted_iota(jnp.int32, (per, LANES), 0)
            wide_lane = lax.broadcasted_iota(jnp.int32, (per, LANES), 1)
            value = jnp.where(owner == wide_lane // width, rows[source], 0.0)
            out[number * per : (number + 1) * per, :] = value

    others = [jnp.bitwise_xor(me_z, k) for k in range(1, partners + 1)]
    begins, ends = [other + 1 for other in others], others
    lowers = [other < me_z for other in others]
    size = len(begins)
    up = chain_products(
        factors, 12, lambda b: (ny + b, 0), count_z, begins, [me_z] * size, [1.0] * size, False
    )
    down = chain_products(
        factors, 16, lambda b: (ny + b, LANES - 1), count_z, [me_z + 1] * size, ends, [1.0] * size, True
    )
    stack = []
    for k, lower in enumerate(lowers):
        for p in range(2):
            from_low = up[2 * p][k : k + 1] * head0 + up[2 * p + 1][k : k + 1] * head1
            from_high = down[2 * p][k : k + 1] * tail0 + down[2 * p + 1][k : k + 1] * tail1
            stack.append(jnp.where(lower, from_low, from_high))
    while len(stack) % 8:
        stack.append(jnp.zeros((1, LANES), jnp.float32))
    stack = jnp.concatenate(stack, axis=0)
    first = stack.astype(jnp.bfloat16).astype(jnp.float32)
    entering[...] = jnp.concatenate([first, stack - first, first], axis=0)

    columns[0:LANES, 0:32] = transposed(factors, cell // LANES)
    row = lax.broadcasted_iota(jnp.int32, (wy, LANES), 0)
    extra_row = lax.broadcasted_iota(jnp.int32, (EXTRA, LANES), 0)
    unit = (1.0, 0.0, 0.0, 1.0)

    def head(number):
        return tuple(columns[pl.ds(start, 1), number + k : number + k + 1] for k in range(4))

    def tail(number):
        return tuple(columns[pl.ds(start + wy - 1, 1), number + k : number + k + 1] for k in range(4))

    past_up, past_down = mm(head(12), head(20)), mm(tail(16), tail(24))
    for column in range(2):
        for output, number in ((column, 20), (2 + column, 24)):
            even = columns[pl.ds(start, wy), number + column : number + column + 1]
            odd = columns[pl.ds(start, wy), number + 2 + column : number + 3 + column]
            weights_y[output, 0:wy, :] = jnp.where((row & 1) == 0, even, odd)
        for output, early, late in (
            (column, (past_up[column], past_up[2 + column]), (unit[column], unit[2 + column])),
            (2 + column, (unit[column], unit[2 + column]), (past_down[column], past_down[2 + column])),
        ):
            value = jnp.zeros((EXTRA, LANES), jnp.float32)
            for r, v in enumerate(early + late):
                value = jnp.where(extra_row == r, v, value)
            weights_y[output, wy : wy + EXTRA, :] = value

    total = planes * (wy + EXTRA)

    def solve(begin, size):
        rows = slice(begin, begin + size)
        both = matmul(high[rows, :], matrix[...])
        value = both[:, 0:LANES] + (both[:, LANES : 2 * LANES] + matmul(low[rows, :], matrix[:, 0:LANES]))
        local[rows, :] = value
        return value

    extra = solve(planes * wy, planes * EXTRA)
    for part in range(planes // 8):
        core = solve(part * 8 * wy, 8 * wy)
        for number in range(4):
            lines = []
            for k in range(8):
                index = part * 8 + k
                value = jnp.sum(core[k * wy : (k + 1) * wy] * weights_y[number, 0:wy, :], axis=0, keepdims=True)
                past = extra[index * EXTRA : (index + 1) * EXTRA] * weights_y[number, wy : wy + EXTRA, :]
                lines.append(value + jnp.sum(past, axis=0, keepdims=True))
            start = number * planes + part * 8
            moments[start : start + 8, :] = jnp.concatenate(lines, axis=0)


def y_kernel(count_y, wy, factors, unused, inverse_y, coefs, columns, stacked):
    me_y = lax.axis_index("gy")
    cell = me_y * wy
    columns[0:LANES, 0:32] = transposed(factors, cell // LANES)
    start = lax.rem(cell, LANES)
    inverse_y[...] = dense_inverse(columns, start, wy, stacked)

    up, down = ([], [], []), ([], [], [])
    plan = stage_plan(count_y)
    for number, (stride, radix) in enumerate(plan):
        group = me_y // stride
        first = (group // radix) * radix
        others = [first + jnp.bitwise_xor(group - first, k) for k in range(radix)]
        for other in others[1:]:
            for lists, values in (
                (up, ((other + 1) * stride, me_y, truth(other < group))),
                (down, (me_y + 1, other * stride, truth(other > group))),
            ):
                for one, value in zip(lists, values):
                    one.append(value)
        if number + 1 < len(plan):
            for other in others:
                for lists, values in (
                    (up, ((other + 1) * stride, (first + radix) * stride, 1.0)),
                    (down, (first * stride, other * stride, 1.0)),
                ):
                    for one, value in zip(lists, values):
                        one.append(value)

    def place(block):
        return block * wy // LANES, block * wy % LANES

    def place_end(block):
        return place(block)[0], place(block)[1] + wy - 1

    for base, value in (
        (0, chain_products(factors, 12, place, count_y, *up, False)),
        (4, chain_products(factors, 16, place_end, count_y, *down, True)),
    ):
        for k in range(4):
            coefs[base + k] = value[k]


def arrived_rows(messages, count):
    rows = [m[0:2] for m in messages]
    if count > 2 * len(messages):
        rows.append(jnp.zeros((count - 2 * len(messages), rows[0].shape[1]), jnp.float32))
    return jnp.concatenate(rows, axis=0)


def third_kernel(planes, wy, chosen, moments, spread_core, spread_extra, entering, *refs):
    messages, (carried, held, result) = refs[:-3][::-1], refs[-3:]
    count = -(-2 * len(messages) // 8) * 8
    total = entering.shape[0] // 3
    received = arrived_rows(messages, count)
    first = received.astype(jnp.bfloat16).astype(jnp.float32)
    both = jnp.concatenate([first, received - first], axis=0)
    values = entering[0:total, :] + entering[total : 2 * total, :]
    values = [values[2 * (k - 1) + p : 2 * k - 1 + p] for k in chosen for p in range(2)]
    across = (((1,), (1,)), ((), ()))
    used = 2 * len(messages)

    def chunks(begin, end):
        parts = [both[:, at : min(at + LANES, end)] for at in range(begin, end, LANES)]
        if parts[-1].shape[1] < LANES:
            missing = jnp.zeros((2 * count, LANES - parts[-1].shape[1]), jnp.float32)
            parts[-1] = jnp.concatenate([parts[-1], missing], axis=1)
        return jnp.concatenate(parts, axis=0).astype(jnp.bfloat16), len(parts)

    per = LANES // wy
    stack, number = chunks(0, planes * wy)
    top, rest = halves(spread_core[...])
    held[0 : number * 2 * count, 0 : 4 * per] = matmul(stack, top, across) + matmul(stack, rest, across)
    columns = [
        held[pl.ds(r, number, stride=2 * count), :] + held[pl.ds(count + r, number, stride=2 * count), :]
        for r in range(used)
    ]
    for m in range(4):
        for p in range(per):
            lane = m * per + p
            value = moments[pl.ds(m * planes + p, number, stride=per), :]
            for r in range(used):
                value = value + columns[r][:, lane : lane + 1] * values[r]
            result[pl.ds(m * planes + p, number, stride=per), :] = value

    per = LANES // EXTRA
    stack, number = chunks(planes * wy, planes * (wy + EXTRA))
    top, rest = halves(spread_extra[...])
    corner = matmul(top, stack, across) + matmul(rest, stack, across)
    spare = jnp.zeros((corner.shape[0], -corner.shape[1] % LANES), jnp.float32)
    corner = jnp.concatenate([corner, spare], axis=1)
    corner = corner + pltpu.roll(corner, corner.shape[1] - count, 1)
    for m in range(4):
        for chunk in range(number):
            size = min(per, planes - chunk * per)
            rows = slice(chunk * per, chunk * per + size)
            value = result[m * planes + chunk * per : m * planes + chunk * per + size, :]
            for r in range(used):
                lane = chunk * 2 * count + r
                part = corner[m * per : m * per + size]
                value = value + part[:, lane : lane + 1] * values[r]
            if len(carried.shape) == 3:
                carried[m, rows, :] = value
            else:
                carried[m * planes + rows.start : m * planes + rows.stop, :] = value


def local_y_kernel(wy, local, entering, inverse_y, unused, *refs):
    messages, (out, sides, solved) = refs[:-3], refs[-3:]
    planes = out.shape[0]
    for number, c in enumerate((0, 1, wy - 2, wy - 1)):
        sides[number] = jnp.broadcast_to(inverse_y[:, c : c + 1], (wy, LANES))
    count = entering.shape[0] // 3
    received = arrived_rows(messages, count)
    first = received.astype(jnp.bfloat16).astype(jnp.float32)
    received = jnp.concatenate([first, first, received - first], axis=0).T.astype(jnp.bfloat16)
    solved[...] = local[...] + matmul(received, entering[...].astype(jnp.bfloat16))
    first, second = halves(inverse_y[:, 0 : wy + EXTRA])
    left = jnp.concatenate([first, second, first], axis=1)

    def part(index, carry):
        for k in range(8):
            number = index * 8 + k
            start = pl.multiple_of(number * wy, 8)
            core = solved[pl.ds(start, wy), :]
            start = pl.multiple_of(planes * wy + number * EXTRA, 8)
            both = jnp.concatenate([core, solved[pl.ds(start, EXTRA), :]], axis=0)
            top, rest = halves(both)
            out[number] = matmul(left, jnp.concatenate([top, top, rest], axis=0))
        return carry

    lax.fori_loop(0, planes // 8, part, 0)


def combine(coefs, side, row, values):
    first = 0 if side == 0 else 2
    out = [None, None]
    for k, value in enumerate(values):
        for q in range(2):
            for p in range(2):
                term = coefs[side + 2 * p + q, row + k : row + k + 1, :] * value[first + p]
                out[q] = term if out[q] is None else out[q] + term
    return out


def stage_kernel(base, stride, radix, narrow, has_entered, coefs, *refs):
    values = refs[:radix]
    position = radix
    entered = None
    if has_entered:
        entered = refs[position]
        position += 1
    message, entering = refs[position : position + 2]
    below = combine(coefs, 0, base, values[1:])
    above = combine(coefs, 4, base, values[1:])
    for row, value in enumerate(below + above):
        entering[row] = value if entered is None else value + entered[row]
    upward = combine(coefs, 0, base + radix - 1, values)
    downward = combine(coefs, 4, base + radix - 1, values)
    if narrow:
        group = lax.axis_index("gy") // (stride * radix)
        sends_up = lax.rem(group, 2) == 0
        for row in range(2):
            message[row] = jnp.where(sends_up, upward[row], downward[row])
    else:
        for row, value in enumerate(upward + downward):
            message[row] = value


def last_kernel(base, radix, narrow, wy, coefs, local, sides, entered, *refs):
    messages, (out_hbm, out, sent) = refs[: radix - 1], refs[radix - 1 :]
    values = list(messages)
    if narrow:
        values = [(m[0], m[1], m[0], m[1]) for m in values]
    below = combine(coefs, 0, base, values)
    above = combine(coefs, 4, base, values)
    st = [value + entered[row] for row, value in enumerate(below + above)]
    fields, planes_x = out.shape[:2]
    copies = []
    for field in range(fields):
        for x in range(planes_x):
            index = field * planes_x + x
            value = local[index]
            for number in range(4):
                value = value + sides[number] * st[number][index : index + 1]
            out[field, x] = value
            if (x + 1) % 4 == 0:
                part = (field, pl.ds(x - 3, 4))
                copy = pltpu.make_async_copy(out.at[part], out_hbm.at[part], sent.at[len(copies)])
                copy.start()
                copies.append(copy)
    for copy in copies:
        copy.wait()


VMEM = pl.BlockSpec(memory_space=pltpu.VMEM)
HBM = pl.BlockSpec(memory_space=pltpu.HBM)
PARAMS = pltpu.CompilerParams(vmem_limit_bytes=40 * 1024 * 1024)


def array(*shape):
    return jax.ShapeDtypeStruct(shape, jnp.float32)


def in_hbm(x):
    return pltpu.with_memory_space_constraint(x, pltpu.HBM)


def cost(flops, data):
    return pl.CostEstimate(flops=flops, bytes_accessed=data, transcendentals=0)


def on_device(mesh, flow, speed, metric_y, metric_z):
    fields, planes_x, wy, wz = flow.shape
    count_y, count_z = mesh.shape["gy"], mesh.shape["gz"]
    assert wz == LANES
    ny, nz = metric_y.shape[0] // LANES, metric_z.shape[0] // LANES
    planes = fields * planes_x
    rows = planes * (wy + EXTRA)
    partners = count_z - 1
    arrivals = partners
    entering_rows = -(-2 * arrivals // 8) * 8
    half = jax.ShapeDtypeStruct((rows, 2 * LANES), jnp.bfloat16)
    outputs = pl.pallas_call(
        functools.partial(first_kernel, ny, nz, partners),
        out_shape=[half, half, array(28, ny + nz, LANES)]
        + [array(2, rows)] * partners,
        in_specs=[HBM] * 4,
        out_specs=[VMEM] * (3 + partners),
        scratch_shapes=[
            pltpu.VMEM(flow.shape, jnp.float32),
            pltpu.VMEM(speed.shape, jnp.float32),
            pltpu.VMEM((ny + nz, LANES), jnp.float32),
            pltpu.VMEM((planes_x, 3, wy + 16, LANES), jnp.float32),
            pltpu.SemaphoreType.DMA((fields + 3,)),
        ],
        compiler_params=PARAMS,
        name="forcing_and_factor",
    )(*(in_hbm(x) for x in (flow, speed, metric_y.reshape(ny, LANES), metric_z.reshape(nz, LANES))))
    high, low, factors = outputs[:3]

    def exchange(values, axis, count, stride, radix):
        received = {}
        for k in reversed(range(1, radix)):
            pairs = [(i, i ^ (k * stride)) for i in range(count)]
            received[k] = lax.ppermute(values[k - 1], axis, pairs)
        return [received[k] for k in range(1, radix)]

    plan = stage_plan(count_y)
    work = [pltpu.VMEM((LANES + 16, LANES), jnp.float32)] * 2
    received = exchange(outputs[3:], "gz", count_z, 1, count_z)
    local, moments, entering, spread_core, spread_extra = pl.pallas_call(
        functools.partial(second_kernel, ny, nz, count_z, wy, partners),
        out_shape=[
            array(rows, LANES),
            array(4 * planes + 8, LANES),
            array(3 * entering_rows, LANES),
            array(4 * (LANES // wy), LANES),
            array(4 * (LANES // EXTRA), LANES),
        ],
        in_specs=[VMEM] * 3,
        out_specs=[VMEM] * 5,
        scratch_shapes=work
        + [
            pltpu.VMEM((2 * LANES, LANES), jnp.float32),
            pltpu.VMEM((2 * LANES, 2 * LANES), jnp.bfloat16),
            pltpu.VMEM((4, wy + EXTRA, LANES), jnp.float32),
        ],
        compiler_params=PARAMS,
        cost_estimate=cost(2 * rows * 256 * 128 * 6, 4 * rows * 384),
        name="local_z",
    )(factors, high, low)
    early = [k for k in range(1, partners + 1) if k > 2]
    late = [k for k in range(1, partners + 1) if k <= 2]
    carried = moments
    for chosen, shape in ((early, (4 * planes + 8, LANES)), (late, (4, planes, LANES))):
        room = 2 * (-(-2 * len(chosen) // 8) * 8)
        carried = pl.pallas_call(
            functools.partial(third_kernel, planes, wy, chosen),
            out_shape=array(*shape),
            in_specs=[VMEM] * (4 + len(chosen)),
            out_specs=VMEM,
            scratch_shapes=[
                pltpu.VMEM((planes * wy // LANES * room + room, LANES), jnp.float32),
                pltpu.VMEM((4 * planes + 8, LANES), jnp.float32),
            ],
            compiler_params=PARAMS,
            name="carried_y",
        )(carried, spread_core, spread_extra, entering, *[received[k - 1] for k in chosen[::-1]])
    arrived = received

    narrow = plan[-1][1] == 2 and len(plan) > 1
    base, entered, result = 0, None, None
    for number, (stride, radix) in enumerate(plan):
        received = exchange([carried] * (radix - 1), "gy", count_y, stride, radix)
        if number == 0:
            entries = sum(2 * radix - 1 for _, radix in plan[:-1]) + plan[-1][1] - 1
            inverse_y, coefs = pl.pallas_call(
                functools.partial(y_kernel, count_y, wy),
                out_shape=[array(wy, LANES), array(8, -(-entries // 8) * 8, LANES)],
                in_specs=[VMEM, HBM],
                out_specs=[VMEM] * 2,
                scratch_shapes=work,
                compiler_params=PARAMS,
                cost_estimate=cost(2 * rows * 128 * 128 * 6, 4 * rows * 256),
                name="inverse_y",
            )(factors, carried)
        if number + 1 < len(plan):
            slim = narrow and number + 2 == len(plan)
            inputs = [carried] + received + ([entered] if entered is not None else [])
            carried, entered = pl.pallas_call(
                functools.partial(stage_kernel, base, stride, radix, slim, entered is not None),
                out_shape=[array(2 if slim else 4, planes, LANES), array(4, planes, LANES)],
                in_specs=[VMEM] * (1 + len(inputs)),
                out_specs=[VMEM] * 2,
                compiler_params=PARAMS,
                name="join_groups",
            )(coefs, *inputs)
            base += 2 * radix - 1
            if number == 0:
                result, sides = pl.pallas_call(
                    functools.partial(local_y_kernel, wy),
                    out_shape=[array(planes, wy, LANES), array(4, wy, LANES)],
                    in_specs=[VMEM] * 3 + [HBM] + [VMEM] * arrivals,
                    out_specs=[VMEM] * 2,
                    scratch_shapes=[pltpu.VMEM((rows, LANES), jnp.float32)],
                    compiler_params=PARAMS,
                    cost_estimate=cost(2 * rows * 128 * 128 * 6, 4 * rows * 256),
                    name="local_y",
                )(local, entering, inverse_y, entered, *arrived)
        else:
            return pl.pallas_call(
                functools.partial(last_kernel, base, radix, narrow, wy),
                out_shape=array(fields, planes_x, wy, wz),
                in_specs=[VMEM] * (4 + len(received)),
                out_specs=HBM,
                scratch_shapes=[
                    pltpu.VMEM(flow.shape, jnp.float32),
                    pltpu.SemaphoreType.DMA((planes // 4,)),
                ],
                compiler_params=PARAMS,
                name="finish_y",
            )(coefs, result, sides, entered, *received)


def solution(mesh):
    placed = (P(None, None, "gy", "gz"), P(None, "gy", "gz"), P(), P())
    return jax.shard_map(
        functools.partial(on_device, mesh),
        mesh=mesh,
        in_specs=placed,
        out_specs=P(None, None, "gy", "gz"),
        check_vma=False,
    )
```

```python
import functools

import jax
import jax.numpy as jnp
from jax import lax
from jax.experimental import pallas as pl
from jax.experimental.pallas import tpu as pltpu
from jax.sharding import PartitionSpec as P

viscous = 0.25
explicit_fourth = 0.04
implicit_fourth = 0.05
time_step = 1048576.0
LANES = 128
EXTRA = 8


def mm(a, b):
    return (
        a[0] * b[0] + a[1] * b[2],
        a[0] * b[1] + a[1] * b[3],
        a[2] * b[0] + a[3] * b[2],
        a[2] * b[1] + a[3] * b[3],
    )


def inverse_of_one_minus(a):
    p, q, r, s = 1.0 - a[0], -a[1], -a[2], 1.0 - a[3]
    d = 1.0 / (p * s - q * r)
    return (s * d, -q * d, -r * d, p * d)


def pick(condition, a, b):
    return tuple(jnp.where(condition, x, y) for x, y in zip(a, b))


def halves(x):
    high = x.astype(jnp.bfloat16)
    return high, (x - high.astype(jnp.float32)).astype(jnp.bfloat16)


def matmul(a, b, dims=(((1,), (0,)), ((), ()))):
    return lax.dot_general(a, b, dims, preferred_element_type=jnp.float32)


def scan(m, ahead, count, step, shift, product):
    unit = (1.0, 0.0, 0.0, 1.0)

    def moved(by):
        return tuple(jnp.where(ahead >= by, shift(x, by), u) for x, u in zip(m, unit))

    while step < count:
        if 2 * step < count:
            m = product(product(m, moved(step)), product(moved(2 * step), moved(3 * step)))
            step *= 4
        else:
            m = product(m, moved(step))
            step *= 2
    return m


def lane_roll(x, by):
    return pltpu.roll(x, by % LANES, 1)


def row_roll(x, by):
    by = by % x.shape[0]
    return jnp.concatenate([x[x.shape[0] - by :], x[: x.shape[0] - by]], axis=0)


class Factor:
    def __init__(self, metric, ny, nz, wy):
        self.ny, self.nz, self.wy, self.rows = ny, nz, wy, ny + nz
        self.lane = lax.broadcasted_iota(jnp.int32, (self.rows, LANES), 1)
        self.row = lax.broadcasted_iota(jnp.int32, (self.rows, LANES), 0)
        self.block = jnp.where(self.row < ny, self.row, self.row - ny)
        self.to_end = jnp.where(self.row < ny, ny, nz) - 1 - self.block
        first = (self.lane == 0) & (self.block == 0)
        last = (self.lane == LANES - 1) & (self.to_end == 0)
        self.face_low = 0.5 * (jnp.where(first, metric, self.before(metric, 1)) + metric)
        self.face_high = 0.5 * (metric + jnp.where(last, metric, self.after(metric, 1)))

    def before(self, x, by):
        rolled = lane_roll(x, by)
        value = jnp.where(self.lane < by, row_roll(rolled, 1), rolled)
        return jnp.where((self.lane < by) & (self.block == 0), 0.0, value)

    def after(self, x, by):
        rolled = lane_roll(x, -by)
        value = jnp.where(self.lane >= LANES - by, row_roll(rolled, -1), rolled)
        return jnp.where((self.lane >= LANES - by) & (self.to_end == 0), 0.0, value)

    def guess(self, sign):
        face = self.face_high if sign > 0 else self.face_low
        if sign > 0:
            cell = self.lane + LANES * self.block
        else:
            cell = LANES - 1 - self.lane + LANES * self.to_end
        near = face / (cell + 1).astype(jnp.float32)
        one_over = 1.0 / (face + jnp.sqrt(face + near * near))
        return face * one_over, implicit_fourth * one_over, one_over

    def sweep(self, sign, ratio, far):
        rows = self.rows
        back = self.before if sign > 0 else self.after
        if sign > 0:
            face_in, face_out, place = self.face_low, self.face_high, self.block
        else:
            face_in, face_out, place = self.face_high, self.face_low, self.to_end
        eps = 4.0 * implicit_fourth - implicit_fourth * back(ratio, 1)
        mass = (1.0 + 6.0 * implicit_fourth) - implicit_fourth * back(far, 2) - 2.0 * eps
        eps_in = back(eps, 1)
        scale = 1.0 / (face_in + 2.0 * eps_in)
        m = ((mass + face_in) * scale, mass - eps_in * eps_in * scale, scale, jnp.ones_like(scale))
        ahead = self.lane if sign > 0 else LANES - 1 - self.lane
        m = scan(m, ahead, LANES, 1, lambda x, by: lane_roll(x, sign * by), mm)
        edge = LANES - 1 if sign > 0 else 0
        total = tuple(jnp.broadcast_to(x[:, edge : edge + 1], (rows, LANES)) for x in m)
        total = scan(
            total, place, max(self.ny, self.nz), 1, lambda x, by: row_roll(x, sign * by), mm
        )
        top = jnp.where(place >= 1, row_roll(total[0], sign), 1.0)
        low = jnp.where(place >= 1, row_roll(total[2], sign), 0.0)
        eta = (m[0] * top + m[1] * low) / (m[2] * top + m[3] * low)
        one_over = 1.0 / (face_out + (eta + 2.0 * eps))
        return (face_out + eps) * one_over, implicit_fourth * one_over, one_over

    def finish(self, near_l, far_l, pivot_l, near_r, far_r):
        lane, block, to_end = self.lane, self.block, self.to_end
        even = (lane & 1) == 0
        near_l = jnp.where((to_end == 0) & (lane >= LANES - 1), 0.0, near_l)
        far_l = jnp.where((to_end == 0) & (lane >= LANES - 2), 0.0, far_l)
        near_r = jnp.where((block == 0) & (lane < 1), 0.0, near_r)
        far_r = jnp.where((block == 0) & (lane < 2), 0.0, far_r)

        def of_even(x):
            return jnp.where(even, x, lane_roll(x, 1))

        def of_odd(x):
            return jnp.where(even, lane_roll(x, -1), x)

        t0, t1, r0, r1 = of_even(near_l), of_odd(near_l), of_even(far_l), of_odd(far_l)
        from_right = (t0 * t1 - r0, -t0 * r1, t1, -r1)
        p1 = of_odd(pivot_l)
        left_inverse = (of_even(pivot_l) + t0 * t0 * p1, t0 * p1, t0 * p1, p1)
        s0, s1, q0, q1 = of_even(near_r), of_odd(near_r), of_even(far_r), of_odd(far_r)
        from_left = (-q0, s0, -s1 * q0, s1 * s0 - q1)
        from_left_after = tuple(self.after(x, 2) for x in from_left)
        from_right_before = tuple(self.before(x, 2) for x in from_right)
        diagonal = mm(inverse_of_one_minus(mm(from_right, from_left_after)), left_inverse)
        width = jnp.where(self.row < self.ny, self.wy, LANES)
        place = lane & (width - 1)
        right = scan(from_right, width - 1 - place, LANES, 2, lambda x, by: lane_roll(x, -by), mm)
        left = scan(from_left, place, LANES, 2, lane_roll, mm)
        return from_right, from_left, diagonal, right, left, from_right_before, from_left_after


def cell_weights(chain, column, even):
    return jnp.where(even, chain[column], chain[2 + column])


def first_kernel(ny, nz, partners, flow_hbm, speed_hbm, metric_y, metric_z, *refs):
    high, low, factors = refs[:3]
    messages = refs[3 : 3 + partners]
    flow, speed, metric, spread, arrived = refs[3 + partners :]
    fields, planes_x, wy, _ = flow.shape
    rows = ny + nz
    core_rows = fields * planes_x * wy

    copies = [
        pltpu.make_async_copy(metric_y, metric.at[0:ny], arrived.at[fields]),
        pltpu.make_async_copy(metric_z, metric.at[ny:rows], arrived.at[fields + 1]),
        pltpu.make_async_copy(speed_hbm, speed, arrived.at[fields + 2]),
    ]
    for copy in copies:
        copy.start()
    for field in range(fields):
        pltpu.make_async_copy(flow_hbm.at[field], flow.at[field], arrived.at[field]).start()

    lane = lax.broadcasted_iota(jnp.int32, (wy, LANES), 1)
    extra_row = lax.broadcasted_iota(jnp.int32, (EXTRA, LANES), 0)
    for slot in range(planes_x):
        for part in range(3):
            spread[slot, part, 0:8, :] = jnp.zeros((8, LANES), jnp.float32)
            spread[slot, part, wy + 8 : wy + 16, :] = jnp.zeros((8, LANES), jnp.float32)
    side = time_step * (viscous + 4.0 * explicit_fourth)
    half = time_step * 0.5
    centre = time_step * (-6.0 * viscous - 12.0 * explicit_fourth)
    fourth = -time_step * explicit_fourth

    def store(start, column, value):
        first, second = halves(value)
        high[pl.ds(start, value.shape[0]), column : column + LANES] = first
        low[pl.ds(start, value.shape[0]), column : column + LANES] = second

    def one_field(field):
        values = [flow[field, x] for x in range(planes_x)]
        fluxes = [values[x] * speed[x] for x in range(planes_x)]
        aside = [(time_step * viscous) * u for u in values]
        extras = []
        for x in range(planes_x):
            u, flux, slot = values[x], fluxes[x], x
            total = centre * u
            if x + 1 < planes_x:
                total = total + (aside[x + 1] - fluxes[x + 1])
            if x > 0:
                total = total + (aside[x - 1] + fluxes[x - 1])
            scaled = side * u
            onward, backward, far = scaled + flux, scaled - flux, fourth * u
            spread[slot, 0, 8 : wy + 8, :] = onward
            spread[slot, 1, 8 : wy + 8, :] = backward
            spread[slot, 2, 8 : wy + 8, :] = far
            total = total + (spread[slot, 0, 7 : wy + 7, :] + spread[slot, 1, 9 : wy + 9, :])
            total = total + (spread[slot, 2, 6 : wy + 6, :] + spread[slot, 2, 10 : wy + 10, :])
            a, b = lane_roll(onward, 1), lane_roll(backward, -1)
            c, d = lane_roll(far, 2), lane_roll(far, -2)
            from_low, from_high = a + c, b + d
            ends = jnp.where(lane == 0, from_low, jnp.where(lane == 1, c, 0.0))
            ends = jnp.where(lane == LANES - 1, from_high, jnp.where(lane == LANES - 2, d, ends))
            index = field * planes_x + x
            start = index * wy
            store(start, 0, total + (from_low + from_high))
            store(start, LANES, ends)
            above = spread[slot, 1, 7:15, :] + spread[slot, 2, 8:16, :]
            below = spread[slot, 0, wy + 5 : wy + 13, :] + spread[slot, 2, wy + 4 : wy + 12, :]
            extras.append(jnp.where(extra_row < 2, above, jnp.where(extra_row < 4, below, 0.0)))
            if len(extras) == 2:
                start = core_rows + (index - 1) * EXTRA
                store(start, 0, jnp.concatenate(extras, axis=0))
                for ref in (high, low):
                    ref[pl.ds(start, 2 * EXTRA), LANES : 2 * LANES] = jnp.zeros(
                        (2 * EXTRA, LANES), jnp.bfloat16
                    )
                extras = []

    copies[0].wait()
    copies[1].wait()
    factor = Factor(metric[...], ny, nz, wy)

    guess_l, guess_r = factor.guess(1), factor.guess(-1)
    left, right = factor.sweep(1, *guess_l[:2]), factor.sweep(-1, *guess_r[:2])
    copies[2].wait()
    for x in range(planes_x):
        speed[x] = half * speed[x]
    for field in range(fields):
        pltpu.make_async_copy(flow_hbm.at[field], flow.at[field], arrived.at[field]).wait()
    left, right = factor.sweep(1, *left[:2]), factor.sweep(-1, *right[:2])
    for field in range(fields // 2):
        one_field(field)
    parts = factor.finish(*left, *right[:2])
    from_right, from_left, diagonal, to_right, to_left, before, after = parts
    for number, value in enumerate(v for part in parts for v in part):
        factors[number] = value
    for field in range(fields // 2, fields):
        one_field(field)

    me = lax.axis_index("gz")
    mine = lax.broadcasted_iota(jnp.int32, (rows, LANES), 0) == ny + me
    even = (lax.broadcasted_iota(jnp.int32, (1, LANES), 1) & 1) == 0
    lane = lax.broadcasted_iota(jnp.int32, (1, LANES), 1)

    def own(values):
        return tuple(jnp.sum(jnp.where(mine, v, 0.0), axis=0, keepdims=True) for v in values)

    up, down = own(to_right), own(to_left)
    up_past, down_past = own(mm(before, to_right)), own(mm(after, to_left))
    unit = (1.0, 0.0, 0.0, 1.0)
    weights = []
    for column in range(2):
        same = jnp.where(even, unit[column], unit[2 + column])
        inside_up = cell_weights(up, column, even)
        inside_down = cell_weights(down, column, even)
        past_up = lane_roll(cell_weights(up_past, column, even), -2)
        past_down = lane_roll(cell_weights(down_past, column, even), 2)
        ends_up = jnp.where(lane < 2, same, past_up) - inside_up
        ends_down = jnp.where(lane < 2, past_down, same) - inside_down
        at_end = (lane < 2) | (lane >= LANES - 2)
        ends_up, ends_down = jnp.where(at_end, ends_up, 0.0), jnp.where(at_end, ends_down, 0.0)
        weights.append(
            (
                jnp.concatenate([inside_up, ends_up], axis=1),
                jnp.concatenate([inside_down, ends_down], axis=1),
            )
        )
    stack = []
    for k in range(1, partners + 1):
        upward = jnp.bitwise_xor(me, k) > me
        stack += [jnp.where(upward, w[0], w[1]) for w in weights]
    while len(stack) % 8:
        stack.append(jnp.zeros((1, 2 * LANES), jnp.float32))
    count = len(stack)
    stack = jnp.concatenate(stack, axis=0)
    first = stack.astype(jnp.bfloat16).astype(jnp.float32)
    both = jnp.concatenate([first, stack - first], axis=0).astype(jnp.bfloat16)
    both = jnp.concatenate([both, both], axis=1)
    across = (((1,), (1,)), ((), ()))
    total = high.shape[0]
    size = planes_x * wy
    for begin in range(0, total, size):
        rows = slice(begin, min(begin + size, total))
        sources = jnp.concatenate([high[rows, :], low[rows, :]], axis=1)
        moments = matmul(both, sources, across)
        moments = moments[:count] + moments[count:]
        for k in range(partners):
            messages[k][:, rows] = moments[2 * k : 2 * k + 2]


def dense_inverse(columns, start, width, stack):
    parts = 8
    steps = width // (2 * parts)
    lane = lax.broadcasted_iota(jnp.int32, (parts, LANES), 1)
    part = lax.broadcasted_iota(jnp.int32, (parts, LANES), 0)
    fits = width + 4 <= LANES
    values = [columns[pl.ds(start + 2 * i, parts, stride=2 * steps), :] for i in range(steps)]

    def wide(i, number):
        return tuple(
            jnp.broadcast_to(values[i][:, number + k : number + k + 1], (parts, LANES)) for k in range(4)
        )

    blocks = [wide(i, 8) for i in range(steps)]
    zero, one = jnp.zeros((parts, LANES), jnp.float32), jnp.ones((parts, LANES), jnp.float32)

    def put(rows, i, extra, extra_lane, owner):
        first = 2 * (part * steps + i)
        out = []
        for r in range(2):
            row = jnp.where(lane == first, blocks[i][2 * r], rows[r])
            row = jnp.where(lane == first + 1, blocks[i][2 * r + 1], row)
            if extra is not None and fits:
                row = jnp.where((part == owner) & (lane == extra_lane), extra[2 * r], row)
                row = jnp.where((part == owner) & (lane == extra_lane + 1), extra[2 * r + 1], row)
            out.append(row)
        return tuple(out)

    def run(order, number, ends, extra_lane, owner):
        rows, product, out = (zero, zero), (one, zero, zero, one), {}
        for i in order:
            t = wide(i, number)
            rows = (t[0] * rows[0] + t[1] * rows[1], t[2] * rows[0] + t[3] * rows[1])
            extra = None
            if i == order[0]:
                e = wide(i, ends)
                extra = mm(blocks[i], (e[0], e[2], e[1], e[3]))
            rows = put(rows, i, extra, extra_lane, owner)
            product = mm(t, product)
            out[i] = rows, product
        rows, product = out[order[-1]]
        entering, last = [None] * parts, (jnp.zeros((1, LANES), jnp.float32),) * 2
        sequence = range(parts) if number == 4 else range(parts - 1, -1, -1)
        for p in sequence:
            entering[p] = last
            own, across = [r[p : p + 1] for r in rows], [x[p : p + 1] for x in product]
            last = (
                own[0] + across[0] * last[0] + across[1] * last[1],
                own[1] + across[2] * last[0] + across[3] * last[1],
            )
        entering = [jnp.concatenate([e[r] for e in entering], axis=0) for r in range(2)]
        result = []
        for i in range(steps):
            rows, product = out[i]
            for r in range(2):
                result.append(rows[r] + product[2 * r] * entering[0] + product[2 * r + 1] * entering[1])
        return result

    low = run(list(range(steps)), 4, 12, width, 0)
    high = run(list(range(steps - 1, -1, -1)), 0, 16, width + 2, parts - 1)
    for k in range(2 * steps):
        lower = lane <= 2 * (part * steps + k // 2) + 1
        if fits:
            lower = lower & (lane < width) | ((lane >= width) & (lane < width + 2))
        stack[parts * k : parts * (k + 1), :] = jnp.where(lower, low[k], high[k])
    rows = [stack[pl.ds(p, 2 * steps, stride=parts), :] for p in range(parts)]
    return jnp.concatenate(rows, axis=0)


def stage_plan(count):
    plan, stride = [], 1
    while stride < count:
        radix = 4 if count // stride >= 4 else 2
        plan.append((stride, radix))
        stride *= radix
    return plan


def transposed(factors, row):
    rows = [factors[number, pl.ds(row, 1), :] for number in range(12)]
    rows += [factors[20 + number, pl.ds(row, 1), :] for number in range(8)]
    rows += [factors[12 + number, pl.ds(row, 1), :] for number in range(8)]
    rows.append(jnp.zeros((4, LANES), jnp.float32))
    return jnp.concatenate(rows, axis=0).T


def chain_products(factors, number, place, blocks, begins, ends, masks, reverse):
    count = -(-len(begins) // 8) * 8
    row = lax.broadcasted_iota(jnp.int32, (count, LANES), 0)
    begin = jnp.zeros((count, LANES), jnp.int32)
    end, mask = begin, jnp.zeros((count, LANES), jnp.float32)
    for r, (b, e, m) in enumerate(zip(begins, ends, masks)):
        begin, end = jnp.where(row == r, b, begin), jnp.where(row == r, e, end)
        mask = jnp.where(row == r, m, mask)
    one, zero = jnp.ones((count, LANES), jnp.float32), jnp.zeros((count, LANES), jnp.float32)
    product = (one, zero, zero, one)
    for block in range(blocks - 1, -1, -1) if reverse else range(blocks):
        where = place(block)
        at = (slice(where[0], where[0] + 1), slice(where[1], where[1] + 1))
        value = tuple(factors[(number + k, *at)] for k in range(4))
        product = pick((begin <= block) & (block < end), mm(product, value), product)
    return tuple(x * mask for x in product)


def truth(condition):
    return jnp.where(condition, 1.0, 0.0)


def second_kernel(
    ny, nz, count_z, wy, partners, factors, high, low, local, moments, entering, spread_core, spread_extra, *scratch
):
    columns, stacked, rows_ref, matrix, weights_y = scratch
    planes = (moments.shape[0] - 8) // 4
    me_z, me_y = lax.axis_index("gz"), lax.axis_index("gy")
    columns[0:LANES, 0:32] = transposed(factors, ny + me_z)
    inverse = dense_inverse(columns, 0, LANES, stacked)
    rows_ref[0:LANES, :] = inverse
    rows_ref[LANES : 2 * LANES, :] = jnp.zeros((LANES, LANES), jnp.float32)
    past = tuple(columns[LANES - 1 : LANES, 16 + k : 17 + k] for k in range(4))
    ahead = tuple(columns[0:1, 12 + k : 13 + k] for k in range(4))
    head0, head1 = rows_ref[0:1, :], rows_ref[1:2, :]
    tail0, tail1 = rows_ref[LANES - 2 : LANES - 1, :], rows_ref[LANES - 1 : LANES, :]
    for q in range(2):
        beyond = past[2 * q] * tail0 + past[2 * q + 1] * tail1
        rows_ref[LANES + q : LANES + q + 1, :] = beyond - (head0, head1)[q]
        beyond = ahead[2 * q] * head0 + ahead[2 * q + 1] * head1
        rows_ref[2 * LANES - 2 + q : 2 * LANES - 1 + q, :] = beyond - (tail0, tail1)[q]
    first, second = halves(rows_ref[...])
    matrix[:, 0:LANES] = first
    matrix[:, LANES : 2 * LANES] = second

    cell = me_y * wy
    start = lax.rem(cell, LANES)
    row = cell // LANES
    unit = (1.0, 0.0, 0.0, 1.0)
    lane = lax.broadcasted_iota(jnp.int32, (1, LANES), 1)
    even = (lane & 1) == 0

    def chain(number):
        return tuple(factors[number + k, pl.ds(row, 1), :] for k in range(4))

    def turned(x, by):
        return pltpu.roll(x, lax.rem(by + 2 * LANES, LANES), 1)

    def tiled(x, period):
        x = jnp.where(lane < period, x, 0.0)
        while period < LANES:
            x = x + lane_roll(x, period)
            period *= 2
        return x

    up, down, before, after = chain(12), chain(16), chain(20), chain(24)
    past_up, past_down = mm(before, up), mm(after, down)
    core_rows, extra_rows = [], []
    for column in range(2):
        same = jnp.where(even, unit[column], unit[2 + column])
        early = turned(cell_weights(past_up, column, even), -start)
        late = turned(cell_weights(past_down, column, even), 4 - wy - start)
        for inside, first, second in ((up, early, same), (down, same, late)):
            core_rows.append(tiled(turned(cell_weights(inside, column, even), -start), wy))
            past = jnp.where(lane < 2, first, jnp.where(lane < 4, second, 0.0))
            extra_rows.append(tiled(past, EXTRA))
    for number, source in enumerate((0, 2, 1, 3)):
        for rows, out, width in ((core_rows, spread_core, wy), (extra_rows, spread_extra, EXTRA)):
            per = LANES // width
            owner = lax.broadcasted_iota(jnp.int32, (per, LANES), 0)
            wide_lane = lax.broadcasted_iota(jnp.int32, (per, LANES), 1)
            value = jnp.where(owner == wide_lane // width, rows[source], 0.0)
            out[number * per : (number + 1) * per, :] = value

    others = [jnp.bitwise_xor(me_z, k) for k in range(1, partners + 1)]
    begins, ends = [other + 1 for other in others], others
    lowers = [other < me_z for other in others]
    size = len(begins)
    up = chain_products(
        factors, 12, lambda b: (ny + b, 0), count_z, begins, [me_z] * size, [1.0] * size, False
    )
    down = chain_products(
        factors, 16, lambda b: (ny + b, LANES - 1), count_z, [me_z + 1] * size, ends, [1.0] * size, True
    )
    stack = []
    for k, lower in enumerate(lowers):
        for p in range(2):
            from_low = up[2 * p][k : k + 1] * head0 + up[2 * p + 1][k : k + 1] * head1
            from_high = down[2 * p][k : k + 1] * tail0 + down[2 * p + 1][k : k + 1] * tail1
            stack.append(jnp.where(lower, from_low, from_high))
    while len(stack) % 8:
        stack.append(jnp.zeros((1, LANES), jnp.float32))
    stack = jnp.concatenate(stack, axis=0)
    first = stack.astype(jnp.bfloat16).astype(jnp.float32)
    entering[...] = jnp.concatenate([first, stack - first, first], axis=0)

    columns[0:LANES, 0:32] = transposed(factors, cell // LANES)
    row = lax.broadcasted_iota(jnp.int32, (wy, LANES), 0)
    extra_row = lax.broadcasted_iota(jnp.int32, (EXTRA, LANES), 0)
    unit = (1.0, 0.0, 0.0, 1.0)

    def head(number):
        return tuple(columns[pl.ds(start, 1), number + k : number + k + 1] for k in range(4))

    def tail(number):
        return tuple(columns[pl.ds(start + wy - 1, 1), number + k : number + k + 1] for k in range(4))

    past_up, past_down = mm(head(12), head(20)), mm(tail(16), tail(24))
    for column in range(2):
        for output, number in ((column, 20), (2 + column, 24)):
            even = columns[pl.ds(start, wy), number + column : number + column + 1]
            odd = columns[pl.ds(start, wy), number + 2 + column : number + 3 + column]
            weights_y[output, 0:wy, :] = jnp.where((row & 1) == 0, even, odd)
        for output, early, late in (
            (column, (past_up[column], past_up[2 + column]), (unit[column], unit[2 + column])),
            (2 + column, (unit[column], unit[2 + column]), (past_down[column], past_down[2 + column])),
        ):
            value = jnp.zeros((EXTRA, LANES), jnp.float32)
            for r, v in enumerate(early + late):
                value = jnp.where(extra_row == r, v, value)
            weights_y[output, wy : wy + EXTRA, :] = value

    total = planes * (wy + EXTRA)

    def solve(begin, size):
        rows = slice(begin, begin + size)
        both = matmul(high[rows, :], matrix[...])
        value = both[:, 0:LANES] + (both[:, LANES : 2 * LANES] + matmul(low[rows, :], matrix[:, 0:LANES]))
        local[rows, :] = value
        return value

    extra = solve(planes * wy, planes * EXTRA)
    for part in range(planes // 8):
        core = solve(part * 8 * wy, 8 * wy)
        for number in range(4):
            lines = []
            for k in range(8):
                index = part * 8 + k
                value = jnp.sum(core[k * wy : (k + 1) * wy] * weights_y[number, 0:wy, :], axis=0, keepdims=True)
                past = extra[index * EXTRA : (index + 1) * EXTRA] * weights_y[number, wy : wy + EXTRA, :]
                lines.append(value + jnp.sum(past, axis=0, keepdims=True))
            start = number * planes + part * 8
            moments[start : start + 8, :] = jnp.concatenate(lines, axis=0)


def y_kernel(count_y, wy, factors, unused, inverse_y, coefs, columns, stacked):
    me_y = lax.axis_index("gy")
    cell = me_y * wy
    columns[0:LANES, 0:32] = transposed(factors, cell // LANES)
    start = lax.rem(cell, LANES)
    inverse_y[...] = dense_inverse(columns, start, wy, stacked)

    up, down = ([], [], []), ([], [], [])
    plan = stage_plan(count_y)
    for number, (stride, radix) in enumerate(plan):
        group = me_y // stride
        first = (group // radix) * radix
        others = [first + jnp.bitwise_xor(group - first, k) for k in range(radix)]
        for other in others[1:]:
            for lists, values in (
                (up, ((other + 1) * stride, me_y, truth(other < group))),
                (down, (me_y + 1, other * stride, truth(other > group))),
            ):
                for one, value in zip(lists, values):
                    one.append(value)
        if number + 1 < len(plan):
            for other in others:
                for lists, values in (
                    (up, ((other + 1) * stride, (first + radix) * stride, 1.0)),
                    (down, (first * stride, other * stride, 1.0)),
                ):
                    for one, value in zip(lists, values):
                        one.append(value)

    def place(block):
        return block * wy // LANES, block * wy % LANES

    def place_end(block):
        return place(block)[0], place(block)[1] + wy - 1

    for base, value in (
        (0, chain_products(factors, 12, place, count_y, *up, False)),
        (4, chain_products(factors, 16, place_end, count_y, *down, True)),
    ):
        for k in range(4):
            coefs[base + k] = value[k]


def arrived_rows(messages, count):
    rows = [m[0:2] for m in messages]
    if count > 2 * len(messages):
        rows.append(jnp.zeros((count - 2 * len(messages), rows[0].shape[1]), jnp.float32))
    return jnp.concatenate(rows, axis=0)


def third_kernel(planes, wy, chosen, moments, spread_core, spread_extra, entering, *refs):
    messages, (carried, held, result) = refs[:-3][::-1], refs[-3:]
    count = -(-2 * len(messages) // 8) * 8
    total = entering.shape[0] // 3
    received = arrived_rows(messages, count)
    first = received.astype(jnp.bfloat16).astype(jnp.float32)
    both = jnp.concatenate([first, received - first], axis=0)
    values = entering[0:total, :] + entering[total : 2 * total, :]
    values = [values[2 * (k - 1) + p : 2 * k - 1 + p] for k in chosen for p in range(2)]
    across = (((1,), (1,)), ((), ()))
    used = 2 * len(messages)

    def chunks(begin, end):
        parts = [both[:, at : min(at + LANES, end)] for at in range(begin, end, LANES)]
        if parts[-1].shape[1] < LANES:
            missing = jnp.zeros((2 * count, LANES - parts[-1].shape[1]), jnp.float32)
            parts[-1] = jnp.concatenate([parts[-1], missing], axis=1)
        stack = jnp.concatenate(parts, axis=0).astype(jnp.bfloat16)
        return jnp.concatenate([stack, stack], axis=1), len(parts)

    per = LANES // wy
    stack, number = chunks(0, planes * wy)
    weights = jnp.concatenate(halves(spread_core[...]), axis=1)
    held[0 : number * 2 * count, 0 : 4 * per] = matmul(stack, weights, across)
    columns = [
        held[pl.ds(r, number, stride=2 * count), :] + held[pl.ds(count + r, number, stride=2 * count), :]
        for r in range(used)
    ]
    for m in range(4):
        for p in range(per):
            lane = m * per + p
            value = moments[pl.ds(m * planes + p, number, stride=per), :]
            for r in range(used):
                value = value + columns[r][:, lane : lane + 1] * values[r]
            result[pl.ds(m * planes + p, number, stride=per), :] = value

    per = LANES // EXTRA
    stack, number = chunks(planes * wy, planes * (wy + EXTRA))
    weights = jnp.concatenate(halves(spread_extra[...]), axis=1)
    corner = matmul(weights, stack, across)
    spare = jnp.zeros((corner.shape[0], -corner.shape[1] % LANES), jnp.float32)
    corner = jnp.concatenate([corner, spare], axis=1)
    corner = corner + pltpu.roll(corner, corner.shape[1] - count, 1)
    for m in range(4):
        for chunk in range(number):
            size = min(per, planes - chunk * per)
            rows = slice(chunk * per, chunk * per + size)
            value = result[m * planes + chunk * per : m * planes + chunk * per + size, :]
            for r in range(used):
                lane = chunk * 2 * count + r
                part = corner[m * per : m * per + size]
                value = value + part[:, lane : lane + 1] * values[r]
            if len(carried.shape) == 3:
                carried[m, rows, :] = value
            else:
                carried[m * planes + rows.start : m * planes + rows.stop, :] = value


def local_y_kernel(wy, local, entering, inverse_y, unused, *refs):
    messages, (out, sides, solved) = refs[:-3], refs[-3:]
    planes = out.shape[0]
    for number, c in enumerate((0, 1, wy - 2, wy - 1)):
        sides[number] = jnp.broadcast_to(inverse_y[:, c : c + 1], (wy, LANES))
    count = entering.shape[0] // 3
    received = arrived_rows(messages, count)
    first = received.astype(jnp.bfloat16).astype(jnp.float32)
    received = jnp.concatenate([first, first, received - first], axis=0).T.astype(jnp.bfloat16)
    solved[...] = local[...] + matmul(received, entering[...].astype(jnp.bfloat16))
    first, second = halves(inverse_y[:, 0 : wy + EXTRA])
    left = jnp.concatenate([first, second, first], axis=1)

    def part(index, carry):
        for k in range(8):
            number = index * 8 + k
            start = pl.multiple_of(number * wy, 8)
            core = solved[pl.ds(start, wy), :]
            start = pl.multiple_of(planes * wy + number * EXTRA, 8)
            both = jnp.concatenate([core, solved[pl.ds(start, EXTRA), :]], axis=0)
            top, rest = halves(both)
            out[number] = matmul(left, jnp.concatenate([top, top, rest], axis=0))
        return carry

    lax.fori_loop(0, planes // 8, part, 0)


def combine(coefs, side, row, values):
    first = 0 if side == 0 else 2
    out = [None, None]
    for k, value in enumerate(values):
        for q in range(2):
            for p in range(2):
                term = coefs[side + 2 * p + q, row + k : row + k + 1, :] * value[first + p]
                out[q] = term if out[q] is None else out[q] + term
    return out


def stage_kernel(base, stride, radix, narrow, has_entered, coefs, *refs):
    values = refs[:radix]
    position = radix
    entered = None
    if has_entered:
        entered = refs[position]
        position += 1
    message, entering = refs[position : position + 2]
    below = combine(coefs, 0, base, values[1:])
    above = combine(coefs, 4, base, values[1:])
    for row, value in enumerate(below + above):
        entering[row] = value if entered is None else value + entered[row]
    upward = combine(coefs, 0, base + radix - 1, values)
    downward = combine(coefs, 4, base + radix - 1, values)
    if narrow:
        group = lax.axis_index("gy") // (stride * radix)
        sends_up = lax.rem(group, 2) == 0
        for row in range(2):
            message[row] = jnp.where(sends_up, upward[row], downward[row])
    else:
        for row, value in enumerate(upward + downward):
            message[row] = value


def last_kernel(base, radix, narrow, wy, coefs, local, sides, entered, *refs):
    messages, (out_hbm, out, sent) = refs[: radix - 1], refs[radix - 1 :]
    values = list(messages)
    if narrow:
        values = [(m[0], m[1], m[0], m[1]) for m in values]
    below = combine(coefs, 0, base, values)
    above = combine(coefs, 4, base, values)
    st = [value + entered[row] for row, value in enumerate(below + above)]
    fields, planes_x = out.shape[:2]
    copies = []
    for field in range(fields):
        for x in range(planes_x):
            index = field * planes_x + x
            value = local[index]
            for number in range(4):
                value = value + sides[number] * st[number][index : index + 1]
            out[field, x] = value
            if (x + 1) % 4 == 0:
                part = (field, pl.ds(x - 3, 4))
                copy = pltpu.make_async_copy(out.at[part], out_hbm.at[part], sent.at[len(copies)])
                copy.start()
                copies.append(copy)
    for copy in copies:
        copy.wait()


VMEM = pl.BlockSpec(memory_space=pltpu.VMEM)
HBM = pl.BlockSpec(memory_space=pltpu.HBM)
PARAMS = pltpu.CompilerParams(vmem_limit_bytes=40 * 1024 * 1024)


def array(*shape):
    return jax.ShapeDtypeStruct(shape, jnp.float32)


def in_hbm(x):
    return pltpu.with_memory_space_constraint(x, pltpu.HBM)


def cost(flops, data):
    return pl.CostEstimate(flops=flops, bytes_accessed=data, transcendentals=0)


def on_device(mesh, flow, speed, metric_y, metric_z):
    fields, planes_x, wy, wz = flow.shape
    count_y, count_z = mesh.shape["gy"], mesh.shape["gz"]
    assert wz == LANES
    ny, nz = metric_y.shape[0] // LANES, metric_z.shape[0] // LANES
    planes = fields * planes_x
    rows = planes * (wy + EXTRA)
    partners = count_z - 1
    arrivals = partners
    entering_rows = -(-2 * arrivals // 8) * 8
    half = jax.ShapeDtypeStruct((rows, 2 * LANES), jnp.bfloat16)
    outputs = pl.pallas_call(
        functools.partial(first_kernel, ny, nz, partners),
        out_shape=[half, half, array(28, ny + nz, LANES)]
        + [array(2, rows)] * partners,
        in_specs=[HBM] * 4,
        out_specs=[VMEM] * (3 + partners),
        scratch_shapes=[
            pltpu.VMEM(flow.shape, jnp.float32),
            pltpu.VMEM(speed.shape, jnp.float32),
            pltpu.VMEM((ny + nz, LANES), jnp.float32),
            pltpu.VMEM((planes_x, 3, wy + 16, LANES), jnp.float32),
            pltpu.SemaphoreType.DMA((fields + 3,)),
        ],
        compiler_params=PARAMS,
        name="forcing_and_factor",
    )(*(in_hbm(x) for x in (flow, speed, metric_y.reshape(ny, LANES), metric_z.reshape(nz, LANES))))
    high, low, factors = outputs[:3]

    def exchange(values, axis, count, stride, radix):
        received = {}
        for k in reversed(range(1, radix)):
            pairs = [(i, i ^ (k * stride)) for i in range(count)]
            received[k] = lax.ppermute(values[k - 1], axis, pairs)
        return [received[k] for k in range(1, radix)]

    plan = stage_plan(count_y)
    work = [pltpu.VMEM((LANES + 16, LANES), jnp.float32)] * 2
    received = exchange(outputs[3:], "gz", count_z, 1, count_z)
    local, moments, entering, spread_core, spread_extra = pl.pallas_call(
        functools.partial(second_kernel, ny, nz, count_z, wy, partners),
        out_shape=[
            array(rows, LANES),
            array(4 * planes + 8, LANES),
            array(3 * entering_rows, LANES),
            array(4 * (LANES // wy), LANES),
            array(4 * (LANES // EXTRA), LANES),
        ],
        in_specs=[VMEM] * 3,
        out_specs=[VMEM] * 5,
        scratch_shapes=work
        + [
            pltpu.VMEM((2 * LANES, LANES), jnp.float32),
            pltpu.VMEM((2 * LANES, 2 * LANES), jnp.bfloat16),
            pltpu.VMEM((4, wy + EXTRA, LANES), jnp.float32),
        ],
        compiler_params=PARAMS,
        cost_estimate=cost(2 * rows * 256 * 128 * 6, 4 * rows * 384),
        name="local_z",
    )(factors, high, low)
    early = [k for k in range(1, partners + 1) if k > 2]
    late = [k for k in range(1, partners + 1) if k <= 2]
    carried = moments
    for chosen, shape in ((early, (4 * planes + 8, LANES)), (late, (4, planes, LANES))):
        room = 2 * (-(-2 * len(chosen) // 8) * 8)
        carried = pl.pallas_call(
            functools.partial(third_kernel, planes, wy, chosen),
            out_shape=array(*shape),
            in_specs=[VMEM] * (4 + len(chosen)),
            out_specs=VMEM,
            scratch_shapes=[
                pltpu.VMEM((planes * wy // LANES * room + room, LANES), jnp.float32),
                pltpu.VMEM((4 * planes + 8, LANES), jnp.float32),
            ],
            compiler_params=PARAMS,
            name="carried_y",
        )(carried, spread_core, spread_extra, entering, *[received[k - 1] for k in chosen[::-1]])
    arrived = received

    narrow = plan[-1][1] == 2 and len(plan) > 1
    base, entered, result = 0, None, None
    for number, (stride, radix) in enumerate(plan):
        received = exchange([carried] * (radix - 1), "gy", count_y, stride, radix)
        if number == 0:
            entries = sum(2 * radix - 1 for _, radix in plan[:-1]) + plan[-1][1] - 1
            inverse_y, coefs = pl.pallas_call(
                functools.partial(y_kernel, count_y, wy),
                out_shape=[array(wy, LANES), array(8, -(-entries // 8) * 8, LANES)],
                in_specs=[VMEM, HBM],
                out_specs=[VMEM] * 2,
                scratch_shapes=work,
                compiler_params=PARAMS,
                cost_estimate=cost(2 * rows * 128 * 128 * 6, 4 * rows * 256),
                name="inverse_y",
            )(factors, carried)
        if number + 1 < len(plan):
            slim = narrow and number + 2 == len(plan)
            inputs = [carried] + received + ([entered] if entered is not None else [])
            carried, entered = pl.pallas_call(
                functools.partial(stage_kernel, base, stride, radix, slim, entered is not None),
                out_shape=[array(2 if slim else 4, planes, LANES), array(4, planes, LANES)],
                in_specs=[VMEM] * (1 + len(inputs)),
                out_specs=[VMEM] * 2,
                compiler_params=PARAMS,
                name="join_groups",
            )(coefs, *inputs)
            base += 2 * radix - 1
            if number == 0:
                result, sides = pl.pallas_call(
                    functools.partial(local_y_kernel, wy),
                    out_shape=[array(planes, wy, LANES), array(4, wy, LANES)],
                    in_specs=[VMEM] * 3 + [HBM] + [VMEM] * arrivals,
                    out_specs=[VMEM] * 2,
                    scratch_shapes=[pltpu.VMEM((rows, LANES), jnp.float32)],
                    compiler_params=PARAMS,
                    cost_estimate=cost(2 * rows * 128 * 128 * 6, 4 * rows * 256),
                    name="local_y",
                )(local, entering, inverse_y, entered, *arrived)
        else:
            return pl.pallas_call(
                functools.partial(last_kernel, base, radix, narrow, wy),
                out_shape=array(fields, planes_x, wy, wz),
                in_specs=[VMEM] * (4 + len(received)),
                out_specs=HBM,
                scratch_shapes=[
                    pltpu.VMEM(flow.shape, jnp.float32),
                    pltpu.SemaphoreType.DMA((planes // 4,)),
                ],
                compiler_params=PARAMS,
                name="finish_y",
            )(coefs, result, sides, entered, *received)


def solution(mesh):
    placed = (P(None, None, "gy", "gz"), P(None, "gy", "gz"), P(), P())
    return jax.shard_map(
        functools.partial(on_device, mesh),
        mesh=mesh,
        in_specs=placed,
        out_specs=P(None, None, "gy", "gz"),
        check_vma=False,
    )
```
